32 devices in a mesh: sect: 4 (over x, core), grp: 4 (over z), span: 2 (over y).
Axes of the slice: x: 2, y: 2, z: 4, core: 2. Of those that a mesh axis runs over, the one named last changes fastest.
Arguments:
- grad_out: bfloat16 [320, 8192], P('grp', 'span'), may hold values from -6 to 6
- destination: int32 [320], P('grp'), may hold values from 0 to 319, as said below
- w_down: bfloat16 [5120, 8192], P('sect', 'span'), may hold values from -0.078125 to 0.078125
- pre_act: bfloat16 [320, 5120], P('grp', ('sect', 'span')), may hold values from -6 to 6
- w_up: bfloat16 [5120, 5120], P(None, ('sect', 'span')), may hold values from -0.078125 to 0.078125
- queries: bfloat16 [1280, 1280], P('grp', ('sect', 'span')), may hold values from -16 to 16
- key_states: bfloat16 [1280, 1280], P('grp', ('sect', 'span')), may hold values from -16 to 16
- value_states: bfloat16 [1280, 1280], P('grp', ('sect', 'span')), may hold values from -6 to 6
- lengths: int32 [12], replicated, may hold values from 1 to 80, 320 in all
Outputs:
- grad_queries: bfloat16 [1280, 1280], P('grp', ('sect', 'span'))
- grad_keys: bfloat16 [1280, 1280], P('grp', ('sect', 'span'))
- grad_values: bfloat16 [1280, 1280], P('grp', ('sect', 'span'))
The draws below stay inside these ranges and needn't reach their ends.
Inputs may be any that keep to these rules, and one draw needn't show every extreme that they name: `destination`: a permutation of the merged tokens; the merged tokens on one index of grp go to exactly 4 indices of grp, exactly 20 to each. `lengths`: an image has 4 patches for each merged token; images lie one after another along the merged tokens.
All inputs are finite; a program needn't handle non-finite values.
Results may differ from the reference program's by a relative error of at most 0.015.
Values may be sent and summed in bfloat16 or wider, within the bound.
No kernel may reach another device: no remote copies, remote signals or barrier semaphores. Data moves between devices by JAX's collectives and lax.ppermute only.
A program may use at most 64 MiB of HBM per device.

```python
import math
import jax
import jax.numpy as jnp
import numpy as np
from jax import lax

HEADS = 16
HEAD_DIM = 80
MERGED = 8192
MERGED_DEV = 80
WIDTH = 1280
MERGE_IN = 5120
TOKENS = 320
PATCHES = 1280
IMAGES = 12
OFFS = 4
CAP = 20


def draw_destination(key, part):
    groups = TOKENS // MERGED_DEV
    ranks = jax.random.permutation(jax.random.fold_in(key, 1), groups).astype(jnp.int32)
    candidates = jnp.arange(groups, dtype=jnp.int32)
    priority = jnp.where(candidates == groups // 2, -2, jnp.where(candidates == 1 % groups, -1, ranks))
    shifts = jnp.argsort(priority, stable=True)[:OFFS].astype(jnp.int32)
    sources = jnp.arange(groups, dtype=jnp.int32)[:, None]
    slot_ids = jnp.arange(MERGED_DEV, dtype=jnp.int32)[None, :]
    classes = slot_ids // CAP
    targets = (sources + shifts[classes]) % groups
    positions = targets * MERGED_DEV + slot_ids
    orders = jax.vmap(lambda sub_key: jax.random.permutation(sub_key, MERGED_DEV))(jax.random.split(jax.random.fold_in(key, 2), groups))
    return jnp.take_along_axis(positions, orders, axis=1).reshape(-1).astype(jnp.int32)


def base_rows(key, salt_value):
    drawn = jnp.clip(jax.random.normal(jax.random.fold_in(key, salt_value), (PATCHES, HEADS * HEAD_DIM), jnp.float32), -4.0, 4.0)
    return drawn


def draw_queries(key, part):
    drawn = base_rows(key, 11)
    return drawn.astype(jnp.bfloat16)


def draw_key_states(key, part):
    drawn = base_rows(key, 21)
    return drawn.astype(jnp.bfloat16)


def block_scale(rng, dims, shards, smallest, top_value):
    loudness = 1.0
    for dim, blocks in shards:
        steps = jax.random.uniform(jax.random.fold_in(jax.random.fold_in(rng, 6), dim), (blocks,), jnp.float32, smallest / len(shards), top_value / len(shards))
        loudness = loudness * jnp.repeat(jnp.exp(steps), dims[dim] // blocks).reshape((-1,) + (1,) * (len(dims) - 1 - dim))
    return loudness


def length_profile(amount, total, most, slope):
    loads = [(1 << 20) // math.isqrt(grade ** slope) + 1 for grade in range(2, amount + 1)]
    rest, counts = total - most - (amount - 1), [1] * (amount - 1)
    while rest > 0:
        free = [i for i in range(amount - 1) if counts[i] < most]
        whole, budget = sum([loads[i] for i in free]), rest
        for i in free:
            more = min(most - counts[i], max(1, budget * loads[i] // whole), rest)
            counts[i] = counts[i] + more
            rest = rest - more
    return np.array([most] + counts)


def ragged(own_key, number_of, total, most, skew):
    if number_of == 2:
        one = jax.random.randint(own_key, (), max(1, total - most), min(most, total - 1) + 1)
        return jnp.stack([one, total - one])
    sizes = jnp.asarray(length_profile(number_of, total, most, skew), jnp.int32)
    pairs = (number_of - 1) // 2
    source_of, receiver = sizes[1:1 + 2 * pairs:2], sizes[2:2 + 2 * pairs:2]
    margin = jnp.minimum(source_of - 1, most - receiver)
    moved = jax.random.randint(jax.random.fold_in(own_key, 1), (pairs,), 0, 1 << 20) % (margin + 1)
    sizes = sizes.at[1:1 + 2 * pairs:2].set(source_of - moved).at[2:2 + 2 * pairs:2].set(receiver + moved)
    return sizes[jax.random.permutation(jax.random.fold_in(own_key, 2), number_of)]


def scatter_about(rng, shape, scale, limit, pieces=(), kind=jnp.bfloat16):
    entries = jax.random.normal(rng, shape, jnp.float32) * scale
    if len(pieces) > 0:
        entries = block_scale(rng, shape, pieces, -0.22, 0.18) * entries
    return jnp.clip(entries, min=-limit, max=limit).astype(kind)


def setup_inputs(seed: int = 0) -> dict:
    splits = jax.random.split(jax.random.key(seed), 10)
    return {
        "grad_out": scatter_about(splits[0], (TOKENS, MERGED), 1.0, 6.0, ((0, 4), (1, 2))),
        "destination": draw_destination(jax.random.fold_in(splits[9], 71), 0),
        "w_down": scatter_about(splits[2], (MERGE_IN, MERGED), MERGE_IN ** -0.5, 0.078125, ((0, 4), (1, 2))),
        "pre_act": scatter_about(splits[3], (TOKENS, MERGE_IN), 1.5, 6.0, ((0, 4), (1, 8))),
        "w_up": scatter_about(splits[4], (MERGE_IN, MERGE_IN), MERGE_IN ** -0.5, 0.078125, ((1, 8),)),
        "queries": draw_queries(jax.random.fold_in(splits[9], 71), 0),
        "key_states": draw_key_states(jax.random.fold_in(splits[9], 71), 0),
        "value_states": scatter_about(splits[7], (PATCHES, WIDTH), 1.0, 6.0, ((0, 4), (1, 8))),
        "lengths": ragged(splits[8], IMAGES, TOKENS, MERGED_DEV, 2).astype(jnp.int32),
    }


def gelu_slope(values):
    normal_cdf = 0.5 * (1.0 + jax.scipy.special.erf(values * 0.7071067811865476))
    return normal_cdf + values * jnp.exp(-0.5 * values * values) * 0.3989422804014327


def reference(grad_out, destination, w_down, pre_act, w_up, queries, key_states, value_states, lengths):
    grad_enc = jnp.zeros_like(grad_out).at[destination].set(grad_out)
    grad_hidden = lax.dot_general(grad_enc, w_down, (((1,), (1,)), ((), ())), preferred_element_type=jnp.float32)
    grad_pre = (grad_hidden * gelu_slope(pre_act.astype(jnp.float32))).astype(jnp.bfloat16)
    grad_merge = lax.dot_general(grad_pre, w_up, (((1,), (1,)), ((), ())), preferred_element_type=jnp.float32)
    grad_attn = grad_merge.reshape(PATCHES, WIDTH).astype(jnp.bfloat16)
    boundaries = jnp.cumsum(lengths).astype(jnp.int32)
    positions = jnp.arange(TOKENS, dtype=jnp.int32)
    token_image = jnp.sum((boundaries[None, :] <= positions[:, None]).astype(jnp.int32), 1)
    patch_image = jnp.repeat(token_image, 4)
    block = 4 * MERGED_DEV
    blocks = PATCHES // block
    keys_padded = jnp.pad(key_states, ((block, block), (0, 0)))
    values_padded = jnp.pad(value_states, ((block, block), (0, 0)))
    image_padded = jnp.pad(patch_image, (block, block), constant_values=-1)
    scale = HEAD_DIM ** -0.5

    def one_block(carry, index):
        key_total, value_total = carry
        start = (index * block).astype(jnp.int32)
        query_heads = lax.dynamic_slice_in_dim(queries, start, block, 0).reshape(block, HEADS, HEAD_DIM).astype(jnp.float32)
        grad_heads = lax.dynamic_slice_in_dim(grad_attn, start, block, 0).reshape(block, HEADS, HEAD_DIM).astype(jnp.float32)
        near_keys = lax.dynamic_slice_in_dim(keys_padded, start, 3 * block, 0).reshape(3 * block, HEADS, HEAD_DIM).astype(jnp.float32)
        near_values = lax.dynamic_slice_in_dim(values_padded, start, 3 * block, 0).reshape(3 * block, HEADS, HEAD_DIM).astype(jnp.float32)
        query_image = lax.dynamic_slice_in_dim(patch_image, start, block, 0)
        key_image = lax.dynamic_slice_in_dim(image_padded, start, 3 * block, 0)
        same_image = query_image[:, None] == key_image[None, :]
        scores = jnp.einsum('qhe,khe->hqk', query_heads, near_keys) * scale
        scores = jnp.where(same_image[None], scores, -jnp.inf)
        top_score = jnp.max(scores, -1, keepdims=True)
        weights = jnp.exp(scores - top_score)
        probs = weights / jnp.sum(weights, -1, keepdims=True)
        probs_low = probs.astype(jnp.bfloat16).astype(jnp.float32)
        attended = jnp.einsum('hqk,khe->qhe', probs_low, near_values)
        row_delta = jnp.sum(grad_heads * attended, -1)
        value_part = jnp.einsum('hqk,qhe->khe', probs_low, grad_heads)
        grad_probs = jnp.einsum('qhe,khe->hqk', grad_heads, near_values)
        grad_scores = (probs * (grad_probs - row_delta.T[:, :, None])).astype(jnp.bfloat16).astype(jnp.float32)
        grad_query = (jnp.einsum('hqk,khe->qhe', grad_scores, near_keys) * scale).astype(jnp.bfloat16)
        key_part = jnp.einsum('hqk,qhe->khe', grad_scores, query_heads) * scale
        key_total = lax.dynamic_update_slice_in_dim(key_total, lax.dynamic_slice_in_dim(key_total, start, 3 * block, 0) + key_part.reshape(3 * block, WIDTH), start, 0)
        value_total = lax.dynamic_update_slice_in_dim(value_total, lax.dynamic_slice_in_dim(value_total, start, 3 * block, 0) + value_part.reshape(3 * block, WIDTH), start, 0)
        return (key_total, value_total), grad_query.reshape(block, WIDTH)

    zeros_total = jnp.zeros((PATCHES + 2 * block, WIDTH), jnp.float32)
    (key_total, value_total), grad_blocks = lax.scan(one_block, (zeros_total, zeros_total), jnp.arange(blocks, dtype=jnp.int32))
    grad_queries = grad_blocks.reshape(PATCHES, WIDTH)
    grad_keys = key_total[block:block + PATCHES].astype(jnp.bfloat16)
    grad_values = value_total[block:block + PATCHES].astype(jnp.bfloat16)
    return (grad_queries, grad_keys, grad_values)
```

```python
import functools

import jax
import jax.numpy as jnp
from jax import lax
from jax.experimental import pallas as pl
from jax.experimental.pallas import tpu as pltpu
from jax.sharding import PartitionSpec as P

HEAD_DIM = 80
SCALE = HEAD_DIM**-0.5
MIB = 1024 * 1024
VMEM = pltpu.MemorySpace.VMEM
NT = (((1,), (1,)), ((), ()))
NN = (((1,), (0,)), ((), ()))
TN = (((0,), (0,)), ((), ()))


def dot(a, b, dims):
    return lax.dot_general(a, b, dims, preferred_element_type=jnp.float32)


def iota(shape, dim):
    return lax.broadcasted_iota(jnp.int32, shape, dim)


def params(mib):
    return pltpu.CompilerParams(vmem_limit_bytes=mib * MIB)


def in_vmem(count):
    return [pl.BlockSpec(memory_space=VMEM) for _ in range(count)]


def padded_slots(row_count, groups):
    offsets = min(groups, row_count // 2)
    capacity = row_count // offsets
    return capacity, -(-(capacity + 1) // 8) * 8


def down_kernel(groups, spans, capacity, slots, chunks, dest_ref, rows_ref, weight_ref, out_ref,
                held, sems):
    row_count = rows_ref.shape[0]
    hidden = weight_ref.shape[0] // spans
    depth = weight_ref.shape[1] // chunks
    copies = []
    for s in range(spans):
        for c in range(chunks):
            part = (pl.ds(s * hidden, hidden), pl.ds(c * depth, depth))
            copy = pltpu.make_async_copy(weight_ref.at[part], held.at[part], sems.at[s * chunks + c])
            copy.start()
            copies.append(copy)
    across = jnp.broadcast_to(dest_ref[...].astype(jnp.float32), (row_count, row_count))
    down = across.T
    group_across = jnp.floor((across + 0.5) * (1.0 / row_count))
    group_down = jnp.floor((down + 0.5) * (1.0 / row_count))
    slot_down = down - group_down * row_count
    same = group_across == group_down
    earlier = iota((row_count, row_count), 0) < iota((row_count, row_count), 1)
    later = iota((row_count, row_count), 1) < iota((row_count, row_count), 0)
    rank_across = jnp.sum(jnp.where(same & earlier, 1.0, 0.0), 0, keepdims=True)
    rank_down = jnp.sum(jnp.where(same & later, 1.0, 0.0), 1, keepdims=True)
    row_of = group_across[:1] * slots + rank_across
    places = iota((groups * slots, row_count), 0).astype(jnp.float32)
    pick = jnp.where(places == row_of, 1.0, 0.0).astype(jnp.bfloat16)
    lane = iota((row_count, hidden), 1).astype(jnp.float32)
    at_rank = lane == rank_down
    label_row = iota((slots, hidden), 0) == capacity
    labels = []
    for g in range(groups):
        hit = at_rank & (group_down[:, :1] == g)
        labels.append(jnp.sum(jnp.where(hit, slot_down[:, :1] + 1.0, 0.0), 0, keepdims=True) - 1.0)
    for s in range(spans):
        total = jnp.zeros((row_count, hidden), jnp.float32)
        for c in range(chunks):
            copies[s * chunks + c].wait()
            part = held[s * hidden : (s + 1) * hidden, c * depth : (c + 1) * depth]
            total = total + dot(rows_ref[:, c * depth : (c + 1) * depth], part, NT)
        moved = dot(pick, total.astype(jnp.bfloat16), NN)
        for g in range(groups):
            piece = jnp.where(label_row, labels[g], moved[g * slots : (g + 1) * slots])
            out_ref[g * spans + s] = piece.astype(jnp.bfloat16)


def down_pieces(dest, rows, weight, groups, spans):
    row_count = rows.shape[0]
    capacity, slots = padded_slots(row_count, groups)
    hidden = weight.shape[0] // spans
    chunks = 4
    return pl.pallas_call(
        functools.partial(down_kernel, groups, spans, capacity, slots, chunks),
        out_shape=jax.ShapeDtypeStruct((groups * spans, slots, hidden), jnp.bfloat16),
        in_specs=in_vmem(2) + [pl.BlockSpec(memory_space=pl.ANY)],
        out_specs=pl.BlockSpec(memory_space=VMEM),
        scratch_shapes=[
            pltpu.VMEM(weight.shape, jnp.bfloat16),
            pltpu.SemaphoreType.DMA((spans * chunks,)),
        ],
        compiler_params=params(40),
        name="down_product",
    )(dest.reshape(1, row_count), rows, weight)


def up_kernel(heads, capacity, pieces_ref, pre_ref, weight_ref, out_ref, held, sems):
    row_count, hidden = pre_ref.shape
    count, slots, _ = pieces_ref.shape
    width = weight_ref.shape[0] // (4 * heads)
    copies = []
    for h in range(heads):
        for j in range(4):
            copy = pltpu.make_async_copy(
                weight_ref.at[pl.ds((j * heads + h) * width, width)],
                held.at[h, pl.ds(j * width, width)],
                sems.at[h * 4 + j],
            )
            copy.start()
            copies.append(copy)
    row = iota((row_count, slots), 0).astype(jnp.float32)

    def placed(p, total):
        piece = pieces_ref[p]
        label = piece.astype(jnp.float32)[capacity : capacity + 1, :slots]
        put = jnp.where(row == label, 1.0, 0.0).astype(jnp.bfloat16)
        return total + dot(put, piece, NN)

    total = jnp.zeros((row_count, hidden), jnp.float32)
    if count <= 16:
        for p in range(count):
            total = placed(p, total)
    else:
        total = lax.fori_loop(0, count, placed, total)
    pre = pre_ref[...].astype(jnp.float32)
    cdf = 0.5 * (1.0 + lax.erf(pre * 0.7071067811865476))
    slope = cdf + pre * jnp.exp(-0.5 * pre * pre) * 0.3989422804014327
    grad_pre = (total * slope).astype(jnp.bfloat16)
    for h in range(heads):
        for j in range(4):
            copies[h * 4 + j].wait()
        out_ref[h] = dot(grad_pre, held[h], NT).astype(jnp.bfloat16)


def up_pieces(pieces, pre, weight, heads, capacity):
    width = weight.shape[0] // heads
    return pl.pallas_call(
        functools.partial(up_kernel, heads, capacity),
        out_shape=jax.ShapeDtypeStruct((heads, pre.shape[0], width), jnp.bfloat16),
        in_specs=in_vmem(2) + [pl.BlockSpec(memory_space=pl.ANY)],
        out_specs=pl.BlockSpec(memory_space=VMEM),
        scratch_shapes=[
            pltpu.VMEM((heads, width, weight.shape[1]), jnp.bfloat16),
            pltpu.SemaphoreType.DMA((heads * 4,)),
        ],
        compiler_params=params(32),
        name="up_product",
    )(pieces, pre, weight)


def softmax_kernel(lengths_ref, first_ref, own_ref, before_ref, after_ref, _, own_probs_ref,
                   side_probs_ref, attended_ref, values_ref):
    columns, patches = own_ref.shape[0] // 3, own_ref.shape[1]
    first = first_ref[0, 0]

    def image_of(shape, dim):
        token = iota(shape, dim) // 4 + first

        def step(i, state):
            image, bound = state
            bound = bound + lengths_ref[0, i]
            return image + jnp.where(token >= bound, 1, 0), bound

        start = (jnp.where(token < 0, -1, 0), jnp.int32(0))
        return lax.fori_loop(0, lengths_ref.shape[1], step, start)[0]

    key_image = image_of((3 * patches, 1), 0)
    query_image = image_of((1, 3 * patches), 1)
    blocks = (before_ref, own_ref, after_ref)
    heads = columns // HEAD_DIM
    for h in range(heads):
        q, k, v = [
            [b[t * columns + h * HEAD_DIM : t * columns + (h + 1) * HEAD_DIM] for b in blocks]
            for t in range(3)
        ]
        rows_of = lambda x: x.astype(jnp.float32).T.astype(jnp.bfloat16)
        k_rows = [rows_of(x) for x in k]
        for b in range(3):
            values_ref[h, b * patches : (b + 1) * patches] = rows_of(v[b])
        for qb, keys in ((0, (0, 1)), (1, (0, 1, 2)), (2, (1, 2))):
            scores = []
            image = query_image[:, qb * patches : (qb + 1) * patches]
            for kb in keys:
                same = key_image[kb * patches : (kb + 1) * patches] == image
                scores.append(jnp.where(same, dot(k_rows[kb], q[qb], NN) * SCALE, -jnp.inf))
            tops = [jnp.max(s, 0, keepdims=True) for s in scores]
            top = functools.reduce(jnp.maximum, tops)
            weights = [jnp.exp(s - top) for s in scores]
            over = 1.0 / functools.reduce(jnp.add, [jnp.sum(w, 0, keepdims=True) for w in weights])
            attended = jnp.zeros((HEAD_DIM, patches), jnp.float32)
            for kb, w in zip(keys, weights):
                probs = (w * over).astype(jnp.bfloat16)
                attended = attended + dot(v[kb], probs, NN)
                if qb == 1:
                    own_probs_ref[h, kb * patches : (kb + 1) * patches] = probs
                elif kb == 1:
                    side_probs_ref[h, qb // 2] = probs
            attended_ref[qb, h * HEAD_DIM : (h + 1) * HEAD_DIM] = attended


def softmax_parts(lengths, first, own, before, after, later):
    columns, patches = own.shape[0] // 3, own.shape[1]
    heads = columns // HEAD_DIM
    smem = pl.BlockSpec(memory_space=pltpu.MemorySpace.SMEM)
    return pl.pallas_call(
        softmax_kernel,
        out_shape=(
            jax.ShapeDtypeStruct((heads, 3 * patches, patches), jnp.bfloat16),
            jax.ShapeDtypeStruct((heads, 2, patches, patches), jnp.bfloat16),
            jax.ShapeDtypeStruct((3, columns, patches), jnp.float32),
            jax.ShapeDtypeStruct((heads, 3 * patches, HEAD_DIM), jnp.bfloat16),
        ),
        in_specs=[smem, smem] + in_vmem(3) + [pl.BlockSpec(memory_space=pl.ANY)],
        out_specs=tuple(in_vmem(4)),
        compiler_params=params(32),
        name="softmax_parts",
    )(lengths.reshape(1, -1), first.reshape(1, 1), own, before, after, later)


def gather_kernel(pieces_ref, out_ref):
    count, row_count, width = pieces_ref.shape
    total = pieces_ref[0].astype(jnp.float32)
    for p in range(1, count):
        total = total + pieces_ref[p].astype(jnp.float32)
    total = total.astype(jnp.bfloat16)
    columns = width // 4
    patch = iota((row_count, 4 * row_count), 1)
    token = iota((row_count, 4 * row_count), 0)
    result = jnp.zeros((columns, 4 * row_count), jnp.float32)
    for j in range(4):
        put = jnp.where(patch == 4 * token + j, 1.0, 0.0).astype(jnp.bfloat16)
        result = result + dot(total[:, j * columns : (j + 1) * columns], put, TN)
    out_ref[...] = result.astype(jnp.bfloat16)


def gathered(pieces):
    _, row_count, width = pieces.shape
    return pl.pallas_call(
        gather_kernel,
        out_shape=jax.ShapeDtypeStruct((width // 4, 4 * row_count), jnp.bfloat16),
        in_specs=in_vmem(1),
        out_specs=pl.BlockSpec(memory_space=VMEM),
        compiler_params=params(16),
        name="gather_sum",
    )(pieces)


def own_kernel(grad_ref, own_ref, before_ref, after_ref, probs_ref, attended_ref, values_ref,
               query_ref, key_ref, value_ref):
    columns, patches = grad_ref.shape
    for h in range(columns // HEAD_DIM):
        cols = slice(h * HEAD_DIM, (h + 1) * HEAD_DIM)
        grad = grad_ref[cols]
        delta = jnp.sum(grad.astype(jnp.float32) * attended_ref[1, cols], 0, keepdims=True)
        total = jnp.zeros((HEAD_DIM, patches), jnp.float32)
        for b, ref in enumerate((before_ref, own_ref, after_ref)):
            rows = slice(b * patches, (b + 1) * patches)
            probs = probs_ref[h, rows]
            slope = dot(values_ref[h, rows], grad, NN)
            scores = (probs.astype(jnp.float32) * (slope - delta)).astype(jnp.bfloat16)
            key = ref[columns + h * HEAD_DIM : columns + (h + 1) * HEAD_DIM]
            total = total + dot(key, scores, NN)
            if b == 1:
                key_ref[cols] = dot(ref[cols], scores, NT)
                value_ref[cols] = dot(grad, probs, NT)
        query_ref[cols] = (total * SCALE).astype(jnp.bfloat16)


def own_terms(grad, own, before, after, probs, attended, values):
    return pl.pallas_call(
        own_kernel,
        out_shape=(
            jax.ShapeDtypeStruct(grad.shape, jnp.bfloat16),
            jax.ShapeDtypeStruct(grad.shape, jnp.float32),
            jax.ShapeDtypeStruct(grad.shape, jnp.float32),
        ),
        in_specs=in_vmem(7),
        out_specs=tuple(in_vmem(3)),
        compiler_params=params(32),
        name="own_terms",
    )(grad, own, before, after, probs, attended, values)


def side_kernel(left_ref, right_ref, before_ref, after_ref, probs_ref, attended_ref, values_ref,
                key_part_ref, value_part_ref, key_ref, value_ref):
    columns, patches = left_ref.shape
    for h in range(columns // HEAD_DIM):
        cols = slice(h * HEAD_DIM, (h + 1) * HEAD_DIM)
        key, value = key_part_ref[cols], value_part_ref[cols]
        for side, (grad_ref, ref) in enumerate(((left_ref, before_ref), (right_ref, after_ref))):
            grad = grad_ref[cols]
            delta = jnp.sum(
                grad.astype(jnp.float32) * attended_ref[2 * side, cols], 0, keepdims=True
            )
            probs = probs_ref[h, side]
            slope = dot(values_ref[h, patches : 2 * patches], grad, NN)
            scores = (probs.astype(jnp.float32) * (slope - delta)).astype(jnp.bfloat16)
            key = key + dot(ref[cols], scores, NT)
            value = value + dot(grad, probs, NT)
        key_ref[cols] = (key * SCALE).astype(jnp.bfloat16)
        value_ref[cols] = value.astype(jnp.bfloat16)


def side_terms(left, right, before, after, probs, attended, values, key_part, value_part):
    shape = jax.ShapeDtypeStruct(left.shape, jnp.bfloat16)
    return pl.pallas_call(
        side_kernel,
        out_shape=(shape, shape),
        in_specs=in_vmem(9),
        out_specs=tuple(in_vmem(2)),
        compiler_params=params(32),
        name="side_terms",
    )(left, right, before, after, probs, attended, values, key_part, value_part)


def from_both_sides(x, axis):
    size = lax.axis_size(axis)
    up = [(i, i + 1) for i in range(size - 1)]
    return (
        lax.ppermute(x, axis, up),
        lax.ppermute(x, axis, [(j, i) for i, j in up]),
    )


def on_device(
    grad_out, destination, w_down, pre_act, w_up, queries, key_states, value_states, lengths
):
    groups = lax.axis_size("grp")
    spans = lax.axis_size("span")
    heads = lax.axis_size(("sect", "span"))
    row_count = grad_out.shape[0]
    capacity, _ = padded_slots(row_count, groups)
    pieces = down_pieces(destination, grad_out, w_down, groups, spans)
    own = jnp.concatenate([queries.T, key_states.T, value_states.T], 0)
    own, pieces = lax.optimization_barrier((own, pieces))
    arrived = lax.all_to_all(pieces, ("grp", "span"), split_axis=0, concat_axis=0, tiled=True)
    before, after = from_both_sides(own, "grp")
    shares = up_pieces(arrived, pre_act, w_up, heads, capacity)
    first = (lax.axis_index("grp") - 1) * row_count
    own_probs, side_probs, attended, values = softmax_parts(
        lengths, first, own, before, after, shares
    )
    shares = lax.all_to_all(shares, ("sect", "span"), split_axis=0, concat_axis=0, tiled=True)
    grad = gathered(shares)
    left, right = from_both_sides(grad, "grp")
    grad_query, key_part, value_part = own_terms(
        grad, own, before, after, own_probs, attended, values
    )
    grad_key, grad_value = side_terms(
        left, right, before, after, side_probs, attended, values, key_part, value_part
    )
    return grad_query.T, grad_key.T, grad_value.T


def solution(mesh):
    split = P("grp", ("sect", "span"))
    placed = (
        P("grp", "span"),
        P("grp"),
        P("sect", "span"),
        split,
        P(None, ("sect", "span")),
        split,
        split,
        split,
        P(),
    )
    return jax.shard_map(
        on_device,
        mesh=mesh,
        in_specs=placed,
        out_specs=(split, split, split),
        check_vma=False,
    )
```

```python
import functools

import jax
import jax.numpy as jnp
from jax import lax
from jax.experimental import pallas as pl
from jax.experimental.pallas import tpu as pltpu
from jax.sharding import PartitionSpec as P

HEAD_DIM = 80
SCALE = HEAD_DIM**-0.5
MIB = 1024 * 1024
VMEM = pltpu.MemorySpace.VMEM
NT = (((1,), (1,)), ((), ()))
NN = (((1,), (0,)), ((), ()))
TN = (((0,), (0,)), ((), ()))


def dot(a, b, dims):
    return lax.dot_general(a, b, dims, preferred_element_type=jnp.float32)


def iota(shape, dim):
    return lax.broadcasted_iota(jnp.int32, shape, dim)


def params(mib):
    return pltpu.CompilerParams(vmem_limit_bytes=mib * MIB)


def in_vmem(count):
    return [pl.BlockSpec(memory_space=VMEM) for _ in range(count)]


def padded_slots(row_count, groups):
    offsets = min(groups, row_count // 2)
    capacity = row_count // offsets
    return capacity, -(-(capacity + 1) // 8) * 8


def one_product(count, slots, hidden):
    return count * slots <= hidden


def down_kernel(groups, spans, capacity, slots, chunks, dest_hbm, rows_hbm, weight_ref, out_ref,
                dest_ref, rows_ref, held, sems, first_sems):
    row_count = rows_ref.shape[0]
    dest_copy = pltpu.make_async_copy(dest_hbm, dest_ref, first_sems.at[0])
    dest_copy.start()
    rows_copy = pltpu.make_async_copy(rows_hbm, rows_ref, first_sems.at[1])
    rows_copy.start()
    hidden = weight_ref.shape[0] // spans
    depth = weight_ref.shape[1] // chunks
    copies = []
    for s in range(spans):
        for c in range(chunks):
            part = (pl.ds(s * hidden, hidden), pl.ds(c * depth, depth))
            copy = pltpu.make_async_copy(weight_ref.at[part], held.at[part], sems.at[s * chunks + c])
            copy.start()
            copies.append(copy)
    dest_copy.wait()
    across = jnp.broadcast_to(dest_ref[...].astype(jnp.float32), (row_count, row_count))
    down = across.T
    group_across = jnp.floor((across + 0.5) * (1.0 / row_count))
    group_down = jnp.floor((down + 0.5) * (1.0 / row_count))
    slot_down = down - group_down * row_count
    same = group_across == group_down
    earlier = iota((row_count, row_count), 0) < iota((row_count, row_count), 1)
    later = iota((row_count, row_count), 1) < iota((row_count, row_count), 0)
    rank_across = jnp.sum(jnp.where(same & earlier, 1.0, 0.0), 0, keepdims=True)
    rank_down = jnp.sum(jnp.where(same & later, 1.0, 0.0), 1, keepdims=True)
    row_of = group_across[:1] * slots + rank_across
    places = iota((groups * slots, row_count), 0).astype(jnp.float32)
    pick = jnp.where(places == row_of, 1.0, 0.0).astype(jnp.bfloat16)
    lane = iota((row_count, hidden), 1).astype(jnp.float32)
    shift = 0.0
    if one_product(groups * spans, slots, hidden):
        device = lax.axis_index("grp") * spans + lax.axis_index("span")
        shift = (device * slots).astype(jnp.float32)
    at_rank = lane == rank_down + shift
    label_row = iota((slots, hidden), 0) == capacity
    labels = []
    for g in range(groups):
        hit = at_rank & (group_down[:, :1] == g)
        labels.append(jnp.sum(jnp.where(hit, slot_down[:, :1] + 1.0, 0.0), 0, keepdims=True) - 1.0)
    rows_copy.wait()
    for s in range(spans):
        total = jnp.zeros((row_count, hidden), jnp.float32)
        for c in range(chunks):
            copies[s * chunks + c].wait()
            part = held[s * hidden : (s + 1) * hidden, c * depth : (c + 1) * depth]
            total = total + dot(rows_ref[:, c * depth : (c + 1) * depth], part, NT)
        moved = dot(pick, total.astype(jnp.bfloat16), NN)
        for g in range(groups):
            piece = jnp.where(label_row, labels[g], moved[g * slots : (g + 1) * slots])
            out_ref[g * spans + s] = piece.astype(jnp.bfloat16)


def down_pieces(dest, rows, weight, groups, spans):
    row_count = rows.shape[0]
    capacity, slots = padded_slots(row_count, groups)
    hidden = weight.shape[0] // spans
    chunks = 4
    return pl.pallas_call(
        functools.partial(down_kernel, groups, spans, capacity, slots, chunks),
        out_shape=jax.ShapeDtypeStruct((groups * spans, slots, hidden), jnp.bfloat16),
        in_specs=[pl.BlockSpec(memory_space=pltpu.MemorySpace.HBM)] * 3,
        out_specs=pl.BlockSpec(memory_space=VMEM),
        scratch_shapes=[
            pltpu.VMEM((1, row_count), jnp.int32),
            pltpu.VMEM(rows.shape, jnp.bfloat16),
            pltpu.VMEM(weight.shape, jnp.bfloat16),
            pltpu.SemaphoreType.DMA((spans * chunks,)),
            pltpu.SemaphoreType.DMA((2,)),
        ],
        compiler_params=params(60),
        name="down_product",
    )(dest.reshape(1, row_count), rows, weight)


def up_kernel(heads, capacity, pieces_ref, pre_ref, weight_ref, out_ref, held, sems):
    row_count, hidden = pre_ref.shape
    count, slots, _ = pieces_ref.shape
    width = weight_ref.shape[0] // (4 * heads)
    copies = []
    for h in range(heads):
        for j in range(4):
            copy = pltpu.make_async_copy(
                weight_ref.at[pl.ds((j * heads + h) * width, width)],
                held.at[h, pl.ds(j * width, width)],
                sems.at[h * 4 + j],
            )
            copy.start()
            copies.append(copy)
    label_at = slice(capacity, capacity + 1)
    if one_product(count, slots, hidden):
        pieces = [pieces_ref[p].astype(jnp.float32) for p in range(count)]
        labels = functools.reduce(jnp.maximum, [x[label_at, : count * slots] for x in pieces])
        row = iota((row_count, count * slots), 0).astype(jnp.float32)
        put = jnp.where(row == labels, 1.0, 0.0).astype(jnp.bfloat16)
        total = dot(put, jnp.concatenate(pieces, 0).astype(jnp.bfloat16), NN)
    else:
        row = iota((row_count, slots), 0).astype(jnp.float32)

        def placed(p, total):
            piece = pieces_ref[p]
            labels = piece.astype(jnp.float32)[label_at, :slots]
            put = jnp.where(row == labels, 1.0, 0.0).astype(jnp.bfloat16)
            return total + dot(put, piece, NN)

        total = lax.fori_loop(0, count, placed, jnp.zeros((row_count, hidden), jnp.float32))
    pre = pre_ref[...].astype(jnp.float32)
    cdf = 0.5 * (1.0 + lax.erf(pre * 0.7071067811865476))
    slope = cdf + pre * jnp.exp(-0.5 * pre * pre) * 0.3989422804014327
    grad_pre = (total * slope).astype(jnp.bfloat16)
    for h in range(heads):
        for j in range(4):
            copies[h * 4 + j].wait()
        out_ref[h] = dot(held[h], grad_pre, NT).T.astype(jnp.bfloat16)


def up_pieces(pieces, pre, weight, heads, capacity):
    width = weight.shape[0] // heads
    return pl.pallas_call(
        functools.partial(up_kernel, heads, capacity),
        out_shape=jax.ShapeDtypeStruct((heads, pre.shape[0], width), jnp.bfloat16),
        in_specs=in_vmem(2) + [pl.BlockSpec(memory_space=pltpu.MemorySpace.HBM)],
        out_specs=pl.BlockSpec(memory_space=VMEM),
        scratch_shapes=[
            pltpu.VMEM((heads, width, weight.shape[1]), jnp.bfloat16),
            pltpu.SemaphoreType.DMA((heads * 4,)),
        ],
        compiler_params=params(60),
        name="up_product",
    )(pieces, pre, weight)


def softmax_kernel(lengths_ref, first_ref, own_ref, before_ref, after_ref, _, own_probs_ref,
                   side_probs_ref, attended_ref, values_ref):
    columns, patches = own_ref.shape[0] // 3, own_ref.shape[1]
    first = first_ref[0, 0]

    def image_of(shape, dim):
        token = iota(shape, dim) // 4 + first

        def step(i, state):
            image, bound = state
            bound = bound + lengths_ref[0, i]
            return image + jnp.where(token >= bound, 1, 0), bound

        start = (jnp.where(token < 0, -1, 0), jnp.int32(0))
        return lax.fori_loop(0, lengths_ref.shape[1], step, start)[0]

    key_image = image_of((3 * patches, 1), 0)
    query_image = image_of((1, 3 * patches), 1)
    blocks = (before_ref, own_ref, after_ref)
    heads = columns // HEAD_DIM
    for h in range(heads):
        q, k, v = [
            [b[t * columns + h * HEAD_DIM : t * columns + (h + 1) * HEAD_DIM] for b in blocks]
            for t in range(3)
        ]
        rows_of = lambda x: x.astype(jnp.float32).T.astype(jnp.bfloat16)
        k_rows = [rows_of(x) for x in k]
        for b in range(3):
            values_ref[h, b * patches : (b + 1) * patches] = rows_of(v[b])
        for qb, keys in ((0, (0, 1)), (1, (0, 1, 2)), (2, (1, 2))):
            scores = []
            image = query_image[:, qb * patches : (qb + 1) * patches]
            for kb in keys:
                same = key_image[kb * patches : (kb + 1) * patches] == image
                scores.append(jnp.where(same, dot(k_rows[kb], q[qb], NN) * SCALE, -jnp.inf))
            tops = [jnp.max(s, 0, keepdims=True) for s in scores]
            top = functools.reduce(jnp.maximum, tops)
            weights = [jnp.exp(s - top) for s in scores]
            over = 1.0 / functools.reduce(jnp.add, [jnp.sum(w, 0, keepdims=True) for w in weights])
            attended = jnp.zeros((HEAD_DIM, patches), jnp.float32)
            for kb, w in zip(keys, weights):
                probs = (w * over).astype(jnp.bfloat16)
                attended = attended + dot(v[kb], probs, NN)
                if qb == 1:
                    own_probs_ref[h, kb * patches : (kb + 1) * patches] = probs
                elif kb == 1:
                    side_probs_ref[h, qb // 2] = probs
            attended_ref[qb, h * HEAD_DIM : (h + 1) * HEAD_DIM] = attended


def softmax_parts(lengths, first, own, before, after, later):
    columns, patches = own.shape[0] // 3, own.shape[1]
    heads = columns // HEAD_DIM
    smem = pl.BlockSpec(memory_space=pltpu.MemorySpace.SMEM)
    return pl.pallas_call(
        softmax_kernel,
        out_shape=(
            jax.ShapeDtypeStruct((heads, 3 * patches, patches), jnp.bfloat16),
            jax.ShapeDtypeStruct((heads, 2, patches, patches), jnp.bfloat16),
            jax.ShapeDtypeStruct((3, columns, patches), jnp.float32),
            jax.ShapeDtypeStruct((heads, 3 * patches, HEAD_DIM), jnp.bfloat16),
        ),
        in_specs=[smem, smem] + in_vmem(3) + [pl.BlockSpec(memory_space=pl.ANY)],
        out_specs=tuple(in_vmem(4)),
        compiler_params=params(32),
        name="softmax_parts",
    )(lengths.reshape(1, -1), first.reshape(1, 1), own, before, after, later)


def gather_kernel(pieces_ref, _, out_ref):
    count, row_count, width = pieces_ref.shape
    total = pieces_ref[0].astype(jnp.float32)
    for p in range(1, count):
        total = total + pieces_ref[p].astype(jnp.float32)
    total = total.astype(jnp.bfloat16)
    columns = width // 4
    patch = iota((row_count, 4 * row_count), 1)
    token = iota((row_count, 4 * row_count), 0)
    result = jnp.zeros((columns, 4 * row_count), jnp.float32)
    for j in range(4):
        put = jnp.where(patch == 4 * token + j, 1.0, 0.0).astype(jnp.bfloat16)
        result = result + dot(total[:, j * columns : (j + 1) * columns], put, TN)
    out_ref[...] = result.astype(jnp.bfloat16)


def gathered(pieces, later):
    _, row_count, width = pieces.shape
    return pl.pallas_call(
        gather_kernel,
        out_shape=jax.ShapeDtypeStruct((width // 4, 4 * row_count), jnp.bfloat16),
        in_specs=in_vmem(1) + [pl.BlockSpec(memory_space=pl.ANY)],
        out_specs=pl.BlockSpec(memory_space=VMEM),
        compiler_params=params(16),
        name="gather_sum",
    )(pieces, later)


def own_kernel(grad_ref, own_ref, before_ref, after_ref, probs_ref, attended_ref, values_ref,
               query_ref, key_ref, value_ref):
    columns, patches = grad_ref.shape
    for h in range(columns // HEAD_DIM):
        cols = slice(h * HEAD_DIM, (h + 1) * HEAD_DIM)
        grad = grad_ref[cols]
        delta = jnp.sum(grad.astype(jnp.float32) * attended_ref[1, cols], 0, keepdims=True)
        total = jnp.zeros((HEAD_DIM, patches), jnp.float32)
        for b, ref in enumerate((before_ref, own_ref, after_ref)):
            rows = slice(b * patches, (b + 1) * patches)
            probs = probs_ref[h, rows]
            slope = dot(values_ref[h, rows], grad, NN)
            scores = (probs.astype(jnp.float32) * (slope - delta)).astype(jnp.bfloat16)
            key = ref[columns + h * HEAD_DIM : columns + (h + 1) * HEAD_DIM]
            total = total + dot(key, scores, NN)
            if b == 1:
                key_ref[cols] = dot(ref[cols], scores, NT)
                value_ref[cols] = dot(grad, probs, NT)
        query_ref[cols] = (total * SCALE).astype(jnp.bfloat16)


def own_terms(grad, own, before, after, probs, attended, values):
    return pl.pallas_call(
        own_kernel,
        out_shape=(
            jax.ShapeDtypeStruct(grad.shape, jnp.bfloat16),
            jax.ShapeDtypeStruct(grad.shape, jnp.float32),
            jax.ShapeDtypeStruct(grad.shape, jnp.float32),
        ),
        in_specs=in_vmem(7),
        out_specs=tuple(in_vmem(3)),
        compiler_params=params(32),
        name="own_terms",
    )(grad, own, before, after, probs, attended, values)


def side_kernel(left_ref, right_ref, before_ref, after_ref, probs_ref, attended_ref, values_ref,
                key_part_ref, value_part_ref, key_ref, value_ref):
    columns, patches = left_ref.shape
    for h in range(columns // HEAD_DIM):
        cols = slice(h * HEAD_DIM, (h + 1) * HEAD_DIM)
        key, value = key_part_ref[cols], value_part_ref[cols]
        for side, (grad_ref, ref) in enumerate(((left_ref, before_ref), (right_ref, after_ref))):
            grad = grad_ref[cols]
            delta = jnp.sum(
                grad.astype(jnp.float32) * attended_ref[2 * side, cols], 0, keepdims=True
            )
            probs = probs_ref[h, side]
            slope = dot(values_ref[h, patches : 2 * patches], grad, NN)
            scores = (probs.astype(jnp.float32) * (slope - delta)).astype(jnp.bfloat16)
            key = key + dot(ref[cols], scores, NT)
            value = value + dot(grad, probs, NT)
        key_ref[cols] = (key * SCALE).astype(jnp.bfloat16)
        value_ref[cols] = value.astype(jnp.bfloat16)


def side_terms(left, right, before, after, probs, attended, values, key_part, value_part):
    shape = jax.ShapeDtypeStruct(left.shape, jnp.bfloat16)
    return pl.pallas_call(
        side_kernel,
        out_shape=(shape, shape),
        in_specs=in_vmem(9),
        out_specs=tuple(in_vmem(2)),
        compiler_params=params(32),
        name="side_terms",
    )(left, right, before, after, probs, attended, values, key_part, value_part)


def from_both_sides(x, axis):
    size = lax.axis_size(axis)
    up = [(i, i + 1) for i in range(size - 1)]
    return (
        lax.ppermute(x, axis, up),
        lax.ppermute(x, axis, [(j, i) for i, j in up]),
    )


def on_device(
    grad_out, destination, w_down, pre_act, w_up, queries, key_states, value_states, lengths
):
    groups = lax.axis_size("grp")
    spans = lax.axis_size("span")
    heads = lax.axis_size(("sect", "span"))
    row_count = grad_out.shape[0]
    capacity, _ = padded_slots(row_count, groups)
    pieces = down_pieces(destination, grad_out, w_down, groups, spans)
    arrived = lax.all_to_all(pieces, ("grp", "span"), split_axis=0, concat_axis=0, tiled=True)
    shares = up_pieces(arrived, pre_act, w_up, heads, capacity)
    shares, queries, key_states, value_states = lax.optimization_barrier(
        (shares, queries, key_states, value_states)
    )
    own = jnp.concatenate([queries.T, key_states.T, value_states.T], 0)
    before, after = from_both_sides(own, "grp")
    first = (lax.axis_index("grp") - 1) * row_count
    own_probs, side_probs, attended, values = softmax_parts(
        lengths, first, own, before, after, shares
    )
    shares = lax.all_to_all(shares, ("sect", "span"), split_axis=0, concat_axis=0, tiled=True)
    grad = gathered(shares, values)
    left, right = from_both_sides(grad, "grp")
    grad_query, key_part, value_part = own_terms(
        grad, own, before, after, own_probs, attended, values
    )
    grad_key, grad_value = side_terms(
        left, right, before, after, side_probs, attended, values, key_part, value_part
    )
    return grad_query.T, grad_key.T, grad_value.T


def solution(mesh):
    split = P("grp", ("sect", "span"))
    placed = (
        P("grp", "span"),
        P("grp"),
        P("sect", "span"),
        split,
        P(None, ("sect", "span")),
        split,
        split,
        split,
        P(),
    )
    return jax.shard_map(
        on_device,
        mesh=mesh,
        in_specs=placed,
        out_specs=(split, split, split),
        check_vma=False,
    )
```

```python
import functools

import jax
import jax.numpy as jnp
from jax import lax
from jax.experimental import pallas as pl
from jax.experimental.pallas import tpu as pltpu
from jax.sharding import PartitionSpec as P

HEAD_DIM = 80
SCALE = HEAD_DIM**-0.5
MIB = 1024 * 1024
VMEM = pltpu.MemorySpace.VMEM
NT = (((1,), (1,)), ((), ()))
NN = (((1,), (0,)), ((), ()))
TN = (((0,), (0,)), ((), ()))


def dot(a, b, dims):
    return lax.dot_general(a, b, dims, preferred_element_type=jnp.float32)


def iota(shape, dim):
    return lax.broadcasted_iota(jnp.int32, shape, dim)


def params(mib):
    return pltpu.CompilerParams(vmem_limit_bytes=mib * MIB)


def in_vmem(count):
    return [pl.BlockSpec(memory_space=VMEM) for _ in range(count)]


def in_hbm(count):
    return [pl.BlockSpec(memory_space=pltpu.MemorySpace.HBM) for _ in range(count)]


def fetched(pairs, sems):
    copies = [pltpu.make_async_copy(a, b, sems.at[i]) for i, (a, b) in enumerate(pairs)]
    for copy in copies:
        copy.start()
    return copies


def padded_slots(row_count, groups):
    offsets = min(groups, row_count // 2)
    capacity = row_count // offsets
    return capacity, -(-(capacity + 1) // 8) * 8


DONE = jax.ShapeDtypeStruct((8, 128), jnp.float32)


def one_product(count, slots, hidden):
    return count * slots <= hidden


def down_kernel(groups, spans, capacity, slots, step, dest_hbm, rows_hbm, weight_ref, out_ref,
                dest_ref, rows_ref, held, sems):
    row_count = rows_ref.shape[0]
    hidden = weight_ref.shape[0] // spans
    pairs = [(dest_hbm, dest_ref), (rows_hbm, rows_ref)]
    for at in range(0, spans * hidden, step):
        pairs.append((weight_ref.at[pl.ds(at, step)], held.at[pl.ds(at, step)]))
    copies = fetched(pairs, sems)
    copies[0].wait()
    across = jnp.broadcast_to(dest_ref[...].astype(jnp.float32), (row_count, row_count))
    down = across.T
    group_across = jnp.floor((across + 0.5) * (1.0 / row_count))
    group_down = jnp.floor((down + 0.5) * (1.0 / row_count))
    slot_down = down - group_down * row_count
    same = group_across == group_down
    earlier = iota((row_count, row_count), 0) < iota((row_count, row_count), 1)
    later = iota((row_count, row_count), 1) < iota((row_count, row_count), 0)
    rank_across = jnp.sum(jnp.where(same & earlier, 1.0, 0.0), 0, keepdims=True)
    rank_down = jnp.sum(jnp.where(same & later, 1.0, 0.0), 1, keepdims=True)
    row_of = group_across[:1] * slots + rank_across
    places = iota((groups * slots, row_count), 0).astype(jnp.float32)
    pick = jnp.where(places == row_of, 1.0, 0.0).astype(jnp.bfloat16)
    lane = iota((row_count, hidden), 1).astype(jnp.float32)
    shift = 0.0
    if one_product(groups * spans, slots, hidden):
        device = lax.axis_index("grp") * spans + lax.axis_index("span")
        shift = (device * slots).astype(jnp.float32)
    at_rank = lane == rank_down + shift
    label_row = iota((slots, hidden), 0) == capacity
    labels = []
    for g in range(groups):
        hit = at_rank & (group_down[:, :1] == g)
        labels.append(jnp.sum(jnp.where(hit, slot_down[:, :1] + 1.0, 0.0), 0, keepdims=True) - 1.0)
    copies[1].wait()
    for s in range(spans):
        total = []
        for at in range(s * hidden, (s + 1) * hidden, step):
            copies[2 + at // step].wait()
            product = dot(held[at : at + step], rows_ref[...], NT)
            total.append(product.astype(jnp.bfloat16))
        moved = dot(pick, jnp.concatenate(total, 0), NT)
        for g in range(groups):
            piece = jnp.where(label_row, labels[g], moved[g * slots : (g + 1) * slots])
            out_ref[g * spans + s] = piece.astype(jnp.bfloat16)


def down_pieces(dest, rows, weight, groups, spans):
    row_count = rows.shape[0]
    capacity, slots = padded_slots(row_count, groups)
    hidden = weight.shape[0] // spans
    step = hidden if hidden < 320 else 320
    return pl.pallas_call(
        functools.partial(down_kernel, groups, spans, capacity, slots, step),
        out_shape=jax.ShapeDtypeStruct((groups * spans, slots, hidden), jnp.bfloat16),
        in_specs=in_hbm(3),
        out_specs=pl.BlockSpec(memory_space=VMEM),
        scratch_shapes=[
            pltpu.VMEM((1, row_count), jnp.int32),
            pltpu.VMEM(rows.shape, jnp.bfloat16),
            pltpu.VMEM(weight.shape, jnp.bfloat16),
            pltpu.SemaphoreType.DMA((2 + weight.shape[0] // step,)),
        ],
        compiler_params=params(60),
        name="down_product",
    )(dest.reshape(1, row_count), rows, weight)


def up_kernel(heads, capacity, pieces_ref, pre_ref, weight_ref, out_ref, held, sems):
    row_count, hidden = pre_ref.shape
    count, slots, _ = pieces_ref.shape
    width = weight_ref.shape[0] // (4 * heads)
    copies = []
    for h in range(heads):
        for j in range(4):
            copy = pltpu.make_async_copy(
                weight_ref.at[pl.ds((j * heads + h) * width, width)],
                held.at[h, pl.ds(j * width, width)],
                sems.at[h * 4 + j],
            )
            copy.start()
            copies.append(copy)
    label_at = slice(capacity, capacity + 1)
    if one_product(count, slots, hidden):
        pieces = [pieces_ref[p].astype(jnp.float32) for p in range(count)]
        labels = functools.reduce(jnp.maximum, [x[label_at, : count * slots] for x in pieces])
        row = iota((row_count, count * slots), 0).astype(jnp.float32)
        put = jnp.where(row == labels, 1.0, 0.0).astype(jnp.bfloat16)
        total = dot(put, jnp.concatenate(pieces, 0).astype(jnp.bfloat16), NN)
    else:
        row = iota((row_count, slots), 0).astype(jnp.float32)

        def placed(p, total):
            piece = pieces_ref[p]
            labels = piece.astype(jnp.float32)[label_at, :slots]
            put = jnp.where(row == labels, 1.0, 0.0).astype(jnp.bfloat16)
            return total + dot(put, piece, NN)

        total = lax.fori_loop(0, count, placed, jnp.zeros((row_count, hidden), jnp.float32))
    pre = pre_ref[...].astype(jnp.float32)
    cdf = 0.5 * (1.0 + lax.erf(pre * 0.7071067811865476))
    slope = cdf + pre * jnp.exp(-0.5 * pre * pre) * 0.3989422804014327
    grad_pre = (total * slope).astype(jnp.bfloat16)
    for h in range(heads):
        for j in range(4):
            copies[h * 4 + j].wait()
        out_ref[h] = dot(held[h], grad_pre, NT).T.astype(jnp.bfloat16)


def up_pieces(pieces, pre, weight, heads, capacity):
    width = weight.shape[0] // heads
    return pl.pallas_call(
        functools.partial(up_kernel, heads, capacity),
        out_shape=jax.ShapeDtypeStruct((heads, pre.shape[0], width), jnp.bfloat16),
        in_specs=in_vmem(2) + in_hbm(1),
        out_specs=pl.BlockSpec(memory_space=VMEM),
        scratch_shapes=[
            pltpu.VMEM((heads, width, weight.shape[1]), jnp.bfloat16),
            pltpu.SemaphoreType.DMA((heads * 4,)),
        ],
        compiler_params=params(60),
        cost_estimate=pl.CostEstimate(
            flops=8 * pre.shape[0] * weight.size, bytes_accessed=8 * weight.size, transcendentals=0
        ),
        name="up_product",
    )(pieces, pre, weight)


def softmax_kernel(lengths_ref, first_ref, own_ref, before_ref, after_ref, own_probs_out,
                   side_probs_out, attended_out, values_out, done_ref, own_probs_ref,
                   side_probs_ref, attended_ref, values_ref, sems):
    columns, patches = own_ref.shape[0] // 3, own_ref.shape[1]
    first = first_ref[0, 0]

    def image_of(shape, dim):
        token = iota(shape, dim) // 4 + first

        def step(i, state):
            image, bound = state
            bound = bound + lengths_ref[0, i]
            return image + jnp.where(token >= bound, 1, 0), bound

        start = (jnp.where(token < 0, -1, 0), jnp.int32(0))
        return lax.fori_loop(0, lengths_ref.shape[1], step, start)[0]

    key_image = image_of((3 * patches, 1), 0)
    query_image = image_of((1, 3 * patches), 1)
    blocks = (before_ref, own_ref, after_ref)
    heads = columns // HEAD_DIM
    for h in range(heads):
        q, k, v = [
            [b[t * columns + h * HEAD_DIM : t * columns + (h + 1) * HEAD_DIM] for b in blocks]
            for t in range(3)
        ]
        rows_of = lambda x: x.astype(jnp.float32).T.astype(jnp.bfloat16)
        k_rows = [rows_of(x) for x in k]
        for b in range(3):
            values_ref[h, b * patches : (b + 1) * patches] = rows_of(v[b])
        for qb, keys in ((0, (0, 1)), (1, (0, 1, 2)), (2, (1, 2))):
            scores = []
            image = query_image[:, qb * patches : (qb + 1) * patches]
            for kb in keys:
                same = key_image[kb * patches : (kb + 1) * patches] == image
                scores.append(jnp.where(same, dot(k_rows[kb], q[qb], NN) * SCALE, -jnp.inf))
            tops = [jnp.max(s, 0, keepdims=True) for s in scores]
            top = functools.reduce(jnp.maximum, tops)
            weights = [jnp.exp(s - top) for s in scores]
            over = 1.0 / functools.reduce(jnp.add, [jnp.sum(w, 0, keepdims=True) for w in weights])
            attended = jnp.zeros((HEAD_DIM, patches), jnp.float32)
            for kb, w in zip(keys, weights):
                probs = (w * over).astype(jnp.bfloat16)
                if qb == 1:
                    own_probs_ref[h, kb * patches : (kb + 1) * patches] = probs
                else:
                    attended = attended + dot(v[kb], probs, NN)
                    if kb == 1:
                        side_probs_ref[h, qb // 2] = probs
            if qb != 1:
                attended_ref[qb // 2, h * HEAD_DIM : (h + 1) * HEAD_DIM] = attended
    pairs = (
        (own_probs_ref, own_probs_out),
        (side_probs_ref, side_probs_out),
        (attended_ref, attended_out),
        (values_ref, values_out),
    )
    copies = [pltpu.make_async_copy(a, b, sems.at[i]) for i, (a, b) in enumerate(pairs)]
    for copy in copies:
        copy.start()
    for copy in copies:
        copy.wait()
    done_ref[...] = jnp.zeros(done_ref.shape, jnp.float32)


def softmax_parts(lengths, first, own, before, after):
    columns, patches = own.shape[0] // 3, own.shape[1]
    heads = columns // HEAD_DIM
    smem = pl.BlockSpec(memory_space=pltpu.MemorySpace.SMEM)
    shapes = (
        jax.ShapeDtypeStruct((heads, 3 * patches, patches), jnp.bfloat16),
        jax.ShapeDtypeStruct((heads, 2, patches, patches), jnp.bfloat16),
        jax.ShapeDtypeStruct((2, columns, patches), jnp.float32),
        jax.ShapeDtypeStruct((heads, 3 * patches, HEAD_DIM), jnp.bfloat16),
    )
    return pl.pallas_call(
        softmax_kernel,
        out_shape=shapes + (DONE,),
        in_specs=[smem, smem] + in_vmem(3),
        out_specs=tuple(in_hbm(4) + in_vmem(1)),
        scratch_shapes=[pltpu.VMEM(x.shape, x.dtype) for x in shapes]
        + [pltpu.SemaphoreType.DMA((4,))],
        compiler_params=params(32),
        cost_estimate=pl.CostEstimate(
            flops=200 * 9 * heads * patches * patches,
            bytes_accessed=30 * heads * patches * patches,
            transcendentals=9 * heads * patches * patches,
        ),
        name="softmax_parts",
    )(lengths.reshape(1, -1), first.reshape(1, 1), own, before, after)


def gather_kernel(pieces_ref, _, out_ref):
    count, row_count, width = pieces_ref.shape
    total = pieces_ref[0].astype(jnp.float32)
    for p in range(1, count):
        total = total + pieces_ref[p].astype(jnp.float32)
    total = total.astype(jnp.bfloat16)
    columns = width // 4
    patch = iota((row_count, 4 * row_count), 1)
    token = iota((row_count, 4 * row_count), 0)
    result = jnp.zeros((columns, 4 * row_count), jnp.float32)
    for j in range(4):
        put = jnp.where(patch == 4 * token + j, 1.0, 0.0).astype(jnp.bfloat16)
        result = result + dot(total[:, j * columns : (j + 1) * columns], put, TN)
    out_ref[...] = result.astype(jnp.bfloat16)


def gathered(pieces, later):
    _, row_count, width = pieces.shape
    return pl.pallas_call(
        gather_kernel,
        out_shape=jax.ShapeDtypeStruct((width // 4, 4 * row_count), jnp.bfloat16),
        in_specs=in_vmem(2),
        out_specs=pl.BlockSpec(memory_space=VMEM),
        compiler_params=params(16),
        name="gather_sum",
    )(pieces, later)


def own_kernel(grad_ref, own_ref, before_ref, after_ref, probs_hbm, values_hbm,
               query_ref, key_ref, value_ref, probs_ref, values_ref, sems):
    columns, patches = grad_ref.shape
    heads = columns // HEAD_DIM
    pairs = [(values_hbm, values_ref)]
    copies = fetched(pairs + [(probs_hbm.at[h], probs_ref.at[h]) for h in range(heads)], sems)
    blocks = (before_ref, own_ref, after_ref)
    copies[0].wait()
    for h in range(heads):
        cols = slice(h * HEAD_DIM, (h + 1) * HEAD_DIM)
        grad = grad_ref[cols]
        slopes = [dot(values_ref[h, b * patches : (b + 1) * patches], grad, NN) for b in range(3)]
        copies[1 + h].wait()
        probs = [probs_ref[h, b * patches : (b + 1) * patches] for b in range(3)]
        wide = [p.astype(jnp.float32) for p in probs]
        delta = sum([jnp.sum(p * s, 0, keepdims=True) for p, s in zip(wide, slopes)])
        total = jnp.zeros((HEAD_DIM, patches), jnp.float32)
        for b, ref in enumerate(blocks):
            scores = (wide[b] * (slopes[b] - delta)).astype(jnp.bfloat16)
            key = ref[columns + h * HEAD_DIM : columns + (h + 1) * HEAD_DIM]
            total = total + dot(key, scores, NN)
            if b == 1:
                key_ref[cols] = dot(ref[cols], scores, NT)
                value_ref[cols] = dot(grad, probs[b], NT)
        query_ref[cols] = (total * SCALE).astype(jnp.bfloat16)


def own_terms(grad, own, before, after, probs, values):
    heads = probs.shape[0]
    return pl.pallas_call(
        own_kernel,
        out_shape=(
            jax.ShapeDtypeStruct(grad.shape, jnp.bfloat16),
            jax.ShapeDtypeStruct(grad.shape, jnp.float32),
            jax.ShapeDtypeStruct(grad.shape, jnp.float32),
        ),
        in_specs=in_vmem(4) + in_hbm(2),
        out_specs=tuple(in_vmem(3)),
        scratch_shapes=[
            pltpu.VMEM(probs.shape, probs.dtype),
            pltpu.VMEM(values.shape, values.dtype),
            pltpu.SemaphoreType.DMA((1 + heads,)),
        ],
        compiler_params=params(32),
        name="own_terms",
    )(grad, own, before, after, probs, values)


def side_kernel(left_ref, right_ref, before_ref, after_ref, probs_hbm, attended_hbm, values_hbm,
                key_part_ref, value_part_ref, key_ref, value_ref, probs_ref, attended_ref,
                values_ref, sems):
    columns, patches = left_ref.shape
    heads = columns // HEAD_DIM
    middle = pl.ds(patches, patches)
    pairs = [(values_hbm.at[h, middle], values_ref.at[h]) for h in range(heads)]
    pairs += [(attended_hbm, attended_ref)]
    pairs += [(probs_hbm.at[h], probs_ref.at[h]) for h in range(heads)]
    copies = fetched(pairs, sems)
    for h in range(heads):
        cols = slice(h * HEAD_DIM, (h + 1) * HEAD_DIM)
        copies[h].wait()
        grads = (left_ref[cols], right_ref[cols])
        slopes = [dot(values_ref[h], grad, NN) for grad in grads]
        key, value = key_part_ref[cols], value_part_ref[cols]
        if h == 0:
            copies[heads].wait()
        copies[heads + 1 + h].wait()
        for side, ref in enumerate((before_ref, after_ref)):
            grad = grads[side]
            attended = attended_ref[side, cols]
            delta = jnp.sum(grad.astype(jnp.float32) * attended, 0, keepdims=True)
            probs = probs_ref[h, side]
            scores = (probs.astype(jnp.float32) * (slopes[side] - delta)).astype(jnp.bfloat16)
            key = key + dot(ref[cols], scores, NT)
            value = value + dot(grad, probs, NT)
        key_ref[cols] = (key * SCALE).astype(jnp.bfloat16)
        value_ref[cols] = value.astype(jnp.bfloat16)


def side_terms(left, right, before, after, probs, attended, values, key_part, value_part):
    shape = jax.ShapeDtypeStruct(left.shape, jnp.bfloat16)
    heads, _, patches, _ = probs.shape
    return pl.pallas_call(
        side_kernel,
        out_shape=(shape, shape),
        in_specs=in_vmem(4) + in_hbm(3) + in_vmem(2),
        out_specs=tuple(in_vmem(2)),
        scratch_shapes=[
            pltpu.VMEM(probs.shape, probs.dtype),
            pltpu.VMEM(attended.shape, attended.dtype),
            pltpu.VMEM((heads, patches, HEAD_DIM), values.dtype),
            pltpu.SemaphoreType.DMA((1 + 2 * heads,)),
        ],
        compiler_params=params(32),
        name="side_terms",
    )(left, right, before, after, probs, attended, values, key_part, value_part)


def from_both_sides(x, axis):
    size = lax.axis_size(axis)
    up = [(i, i + 1) for i in range(size - 1)]
    return (
        lax.ppermute(x, axis, up),
        lax.ppermute(x, axis, [(j, i) for i, j in up]),
    )


def on_device(
    grad_out, destination, w_down, pre_act, w_up, queries, key_states, value_states, lengths
):
    groups = lax.axis_size("grp")
    spans = lax.axis_size("span")
    heads = lax.axis_size(("sect", "span"))
    row_count = grad_out.shape[0]
    capacity, _ = padded_slots(row_count, groups)
    pieces = down_pieces(destination, grad_out, w_down, groups, spans)
    pieces, queries, key_states, value_states = lax.optimization_barrier(
        (pieces, queries, key_states, value_states)
    )
    arrived = lax.all_to_all(pieces, ("grp", "span"), split_axis=0, concat_axis=0, tiled=True)
    own = jnp.concatenate([queries.T, key_states.T, value_states.T], 0)
    before, after = from_both_sides(own, "grp")
    first = (lax.axis_index("grp") - 1) * row_count
    own_probs, side_probs, attended, values, softmax_done = softmax_parts(
        lengths, first, own, before, after
    )
    shares = up_pieces(arrived, pre_act, w_up, heads, capacity)
    shares = lax.all_to_all(shares, ("sect", "span"), split_axis=0, concat_axis=0, tiled=True)
    grad = gathered(shares, softmax_done)
    left, right = from_both_sides(grad, "grp")
    grad_query, key_part, value_part = own_terms(grad, own, before, after, own_probs, values)
    grad_key, grad_value = side_terms(
        left, right, before, after, side_probs, attended, values, key_part, value_part
    )
    return grad_query.T, grad_key.T, grad_value.T


def solution(mesh):
    split = P("grp", ("sect", "span"))
    placed = (
        P("grp", "span"),
        P("grp"),
        P("sect", "span"),
        split,
        P(None, ("sect", "span")),
        split,
        split,
        split,
        P(),
    )
    return jax.shard_map(
        on_device,
        mesh=mesh,
        in_specs=placed,
        out_specs=(split, split, split),
        check_vma=False,
    )
```

```python
import functools

import jax
import jax.numpy as jnp
from jax import lax
from jax.experimental import pallas as pl
from jax.experimental.pallas import tpu as pltpu
from jax.sharding import PartitionSpec as P

HEAD_DIM = 80
SCALE = HEAD_DIM**-0.5
MIB = 1024 * 1024
VMEM = pltpu.MemorySpace.VMEM
NT = (((1,), (1,)), ((), ()))
NN = (((1,), (0,)), ((), ()))
TN = (((0,), (0,)), ((), ()))


def dot(a, b, dims):
    return lax.dot_general(a, b, dims, preferred_element_type=jnp.float32)


def iota(shape, dim):
    return lax.broadcasted_iota(jnp.int32, shape, dim)


def params(mib):
    return pltpu.CompilerParams(vmem_limit_bytes=mib * MIB)


def in_vmem(count):
    return [pl.BlockSpec(memory_space=VMEM) for _ in range(count)]


def in_hbm(count):
    return [pl.BlockSpec(memory_space=pltpu.MemorySpace.HBM) for _ in range(count)]


def fetched(pairs, sems):
    copies = [pltpu.make_async_copy(a, b, sems.at[i]) for i, (a, b) in enumerate(pairs)]
    for copy in copies:
        copy.start()
    return copies


def padded_slots(row_count, groups):
    offsets = min(groups, row_count // 2)
    capacity = row_count // offsets
    return capacity, -(-(capacity + 1) // 8) * 8


DONE = jax.ShapeDtypeStruct((8, 128), jnp.float32)


def one_product(count, slots, hidden):
    return count * slots <= hidden


def down_kernel(groups, spans, capacity, slots, step, dest_hbm, rows_hbm, weight_ref, out_ref,
                dest_ref, rows_ref, held, sems):
    row_count = rows_ref.shape[0]
    hidden = weight_ref.shape[0] // spans
    pairs = [(dest_hbm, dest_ref), (rows_hbm, rows_ref)]
    for at in range(0, spans * hidden, step):
        pairs.append((weight_ref.at[pl.ds(at, step)], held.at[pl.ds(at, step)]))
    copies = fetched(pairs, sems)
    copies[0].wait()
    across = jnp.broadcast_to(dest_ref[...].astype(jnp.float32), (row_count, row_count))
    down = across.T
    group_across = jnp.floor((across + 0.5) * (1.0 / row_count))
    group_down = jnp.floor((down + 0.5) * (1.0 / row_count))
    slot_down = down - group_down * row_count
    same = group_across == group_down
    earlier = iota((row_count, row_count), 0) < iota((row_count, row_count), 1)
    later = iota((row_count, row_count), 1) < iota((row_count, row_count), 0)
    rank_across = jnp.sum(jnp.where(same & earlier, 1.0, 0.0), 0, keepdims=True)
    rank_down = jnp.sum(jnp.where(same & later, 1.0, 0.0), 1, keepdims=True)
    row_of = group_across[:1] * slots + rank_across
    places = iota((groups * slots, row_count), 0).astype(jnp.float32)
    pick = jnp.where(places == row_of, 1.0, 0.0).astype(jnp.bfloat16)
    lane = iota((row_count, hidden), 1).astype(jnp.float32)
    shift = 0.0
    if one_product(groups * spans, slots, hidden):
        device = lax.axis_index("grp") * spans + lax.axis_index("span")
        shift = (device * slots).astype(jnp.float32)
    at_rank = lane == rank_down + shift
    label_row = iota((slots, hidden), 0) == capacity
    labels = []
    for g in range(groups):
        hit = at_rank & (group_down[:, :1] == g)
        labels.append(jnp.sum(jnp.where(hit, slot_down[:, :1] + 1.0, 0.0), 0, keepdims=True) - 1.0)
    copies[1].wait()
    for s in range(spans):
        total = []
        for at in range(s * hidden, (s + 1) * hidden, step):
            copies[2 + at // step].wait()
            product = dot(held[at : at + step], rows_ref[...], NT)
            total.append(product.astype(jnp.bfloat16))
        moved = dot(pick, jnp.concatenate(total, 0), NT)
        for g in range(groups):
            piece = jnp.where(label_row, labels[g], moved[g * slots : (g + 1) * slots])
            out_ref[g * spans + s] = piece.astype(jnp.bfloat16)


def down_pieces(dest, rows, weight, groups, spans):
    row_count = rows.shape[0]
    capacity, slots = padded_slots(row_count, groups)
    hidden = weight.shape[0] // spans
    step = hidden if hidden < 320 else 320
    return pl.pallas_call(
        functools.partial(down_kernel, groups, spans, capacity, slots, step),
        out_shape=jax.ShapeDtypeStruct((groups * spans, slots, hidden), jnp.bfloat16),
        in_specs=in_hbm(3),
        out_specs=pl.BlockSpec(memory_space=VMEM),
        scratch_shapes=[
            pltpu.VMEM((1, row_count), jnp.int32),
            pltpu.VMEM(rows.shape, jnp.bfloat16),
            pltpu.VMEM(weight.shape, jnp.bfloat16),
            pltpu.SemaphoreType.DMA((2 + weight.shape[0] // step,)),
        ],
        compiler_params=params(60),
        name="down_product",
    )(dest.reshape(1, row_count), rows, weight)


def up_kernel(heads, capacity, pieces_ref, pre_ref, weight_ref, out_ref, held, sems):
    row_count, hidden = pre_ref.shape
    count, slots, _ = pieces_ref.shape
    width = weight_ref.shape[0] // (4 * heads)
    copies = []
    for h in range(heads):
        for j in range(4):
            copy = pltpu.make_async_copy(
                weight_ref.at[pl.ds((j * heads + h) * width, width)],
                held.at[h, pl.ds(j * width, width)],
                sems.at[h * 4 + j],
            )
            copy.start()
            copies.append(copy)
    label_at = slice(capacity, capacity + 1)
    if one_product(count, slots, hidden):
        pieces = [pieces_ref[p].astype(jnp.float32) for p in range(count)]
        labels = functools.reduce(jnp.maximum, [x[label_at, : count * slots] for x in pieces])
        row = iota((row_count, count * slots), 0).astype(jnp.float32)
        put = jnp.where(row == labels, 1.0, 0.0).astype(jnp.bfloat16)
        total = dot(put, jnp.concatenate(pieces, 0).astype(jnp.bfloat16), NN)
    else:
        row = iota((row_count, slots), 0).astype(jnp.float32)

        def placed(p, total):
            piece = pieces_ref[p]
            labels = piece.astype(jnp.float32)[label_at, :slots]
            put = jnp.where(row == labels, 1.0, 0.0).astype(jnp.bfloat16)
            return total + dot(put, piece, NN)

        total = lax.fori_loop(0, count, placed, jnp.zeros((row_count, hidden), jnp.float32))
    pre = pre_ref[...].astype(jnp.float32)
    cdf = 0.5 * (1.0 + lax.erf(pre * 0.7071067811865476))
    slope = cdf + pre * jnp.exp(-0.5 * pre * pre) * 0.3989422804014327
    grad_pre = (total * slope).astype(jnp.bfloat16)
    for h in range(heads):
        for j in range(4):
            copies[h * 4 + j].wait()
        out_ref[h] = dot(held[h], grad_pre, NT).T.astype(jnp.bfloat16)


def up_pieces(pieces, pre, weight, heads, capacity):
    width = weight.shape[0] // heads
    return pl.pallas_call(
        functools.partial(up_kernel, heads, capacity),
        out_shape=jax.ShapeDtypeStruct((heads, pre.shape[0], width), jnp.bfloat16),
        in_specs=in_vmem(2) + in_hbm(1),
        out_specs=pl.BlockSpec(memory_space=VMEM),
        scratch_shapes=[
            pltpu.VMEM((heads, width, weight.shape[1]), jnp.bfloat16),
            pltpu.SemaphoreType.DMA((heads * 4,)),
        ],
        compiler_params=params(60),
        cost_estimate=pl.CostEstimate(
            flops=8 * pre.shape[0] * weight.size, bytes_accessed=8 * weight.size, transcendentals=0
        ),
        name="up_product",
    )(pieces, pre, weight)


def softmax_kernel(lengths_ref, first_ref, own_ref, before_ref, after_ref, own_probs_out,
                   side_probs_out, attended_out, values_out, done_ref, own_probs_ref,
                   side_probs_ref, attended_ref, values_ref, sems):
    columns, patches = own_ref.shape[0] // 3, own_ref.shape[1]
    first = first_ref[0, 0]

    def image_of(shape, dim):
        token = iota(shape, dim) // 4 + first

        def step(i, state):
            image, bound = state
            bound = bound + lengths_ref[0, i]
            return image + jnp.where(token >= bound, 1, 0), bound

        start = (jnp.where(token < 0, -1, 0), jnp.int32(0))
        return lax.fori_loop(0, lengths_ref.shape[1], step, start)[0]

    key_image = image_of((3 * patches, 1), 0)
    query_image = image_of((1, 3 * patches), 1)
    blocks = (before_ref, own_ref, after_ref)
    heads = columns // HEAD_DIM
    for h in range(heads):
        q, k, v = [
            [b[t * columns + h * HEAD_DIM : t * columns + (h + 1) * HEAD_DIM] for b in blocks]
            for t in range(3)
        ]
        rows_of = lambda x: x.astype(jnp.float32).T.astype(jnp.bfloat16)
        k_rows = [rows_of(x) for x in k]
        for b in range(3):
            values_ref[h, b * patches : (b + 1) * patches] = rows_of(v[b])
        for qb, keys in ((0, (0, 1)), (1, (0, 1, 2)), (2, (1, 2))):
            scores = []
            image = query_image[:, qb * patches : (qb + 1) * patches]
            for kb in keys:
                same = key_image[kb * patches : (kb + 1) * patches] == image
                scores.append(jnp.where(same, dot(k_rows[kb], q[qb], NN) * SCALE, -jnp.inf))
            tops = [jnp.max(s, 0, keepdims=True) for s in scores]
            top = functools.reduce(jnp.maximum, tops)
            weights = [jnp.exp(s - top) for s in scores]
            over = 1.0 / functools.reduce(jnp.add, [jnp.sum(w, 0, keepdims=True) for w in weights])
            attended = jnp.zeros((HEAD_DIM, patches), jnp.float32)
            for kb, w in zip(keys, weights):
                probs = (w * over).astype(jnp.bfloat16)
                if qb == 1:
                    own_probs_ref[h, kb * patches : (kb + 1) * patches] = probs
                else:
                    attended = attended + dot(v[kb], probs, NN)
                    if kb == 1:
                        side_probs_ref[h, qb // 2] = probs
            if qb != 1:
                attended_ref[qb // 2, h * HEAD_DIM : (h + 1) * HEAD_DIM] = attended
    pairs = (
        (own_probs_ref, own_probs_out),
        (side_probs_ref, side_probs_out),
        (attended_ref, attended_out),
        (values_ref, values_out),
    )
    copies = [pltpu.make_async_copy(a, b, sems.at[i]) for i, (a, b) in enumerate(pairs)]
    for copy in copies:
        copy.start()
    for copy in copies:
        copy.wait()
    done_ref[...] = jnp.zeros(done_ref.shape, jnp.float32)


def softmax_parts(lengths, first, own, before, after):
    columns, patches = own.shape[0] // 3, own.shape[1]
    heads = columns // HEAD_DIM
    smem = pl.BlockSpec(memory_space=pltpu.MemorySpace.SMEM)
    shapes = (
        jax.ShapeDtypeStruct((heads, 3 * patches, patches), jnp.bfloat16),
        jax.ShapeDtypeStruct((heads, 2, patches, patches), jnp.bfloat16),
        jax.ShapeDtypeStruct((2, columns, patches), jnp.float32),
        jax.ShapeDtypeStruct((heads, 3 * patches, HEAD_DIM), jnp.bfloat16),
    )
    return pl.pallas_call(
        softmax_kernel,
        out_shape=shapes + (DONE,),
        in_specs=[smem, smem] + in_vmem(3),
        out_specs=tuple(in_hbm(4) + in_vmem(1)),
        scratch_shapes=[pltpu.VMEM(x.shape, x.dtype) for x in shapes]
        + [pltpu.SemaphoreType.DMA((4,))],
        compiler_params=params(60),
        cost_estimate=pl.CostEstimate(
            flops=100_000 * heads * patches * patches,
            bytes_accessed=500 * heads * patches * patches,
            transcendentals=9 * heads * patches * patches,
        ),
        name="softmax_parts",
    )(lengths.reshape(1, -1), first.reshape(1, 1), own, before, after)


def gather_kernel(pieces_ref, _, out_ref):
    count, row_count, width = pieces_ref.shape
    total = pieces_ref[0].astype(jnp.float32)
    for p in range(1, count):
        total = total + pieces_ref[p].astype(jnp.float32)
    total = total.astype(jnp.bfloat16)
    columns = width // 4
    patch = iota((row_count, 4 * row_count), 1)
    token = iota((row_count, 4 * row_count), 0)
    result = jnp.zeros((columns, 4 * row_count), jnp.float32)
    for j in range(4):
        put = jnp.where(patch == 4 * token + j, 1.0, 0.0).astype(jnp.bfloat16)
        result = result + dot(total[:, j * columns : (j + 1) * columns], put, TN)
    out_ref[...] = result.astype(jnp.bfloat16)


def gathered(pieces, later):
    _, row_count, width = pieces.shape
    return pl.pallas_call(
        gather_kernel,
        out_shape=jax.ShapeDtypeStruct((width // 4, 4 * row_count), jnp.bfloat16),
        in_specs=in_vmem(2),
        out_specs=pl.BlockSpec(memory_space=VMEM),
        compiler_params=params(16),
        name="gather_sum",
    )(pieces, later)


def own_kernel(grad_ref, own_ref, before_ref, after_ref, probs_ref, values_ref,
               query_ref, key_ref, value_ref):
    columns, patches = grad_ref.shape
    blocks = (before_ref, own_ref, after_ref)
    for h in range(columns // HEAD_DIM):
        cols = slice(h * HEAD_DIM, (h + 1) * HEAD_DIM)
        grad = grad_ref[cols]
        rows = [slice(b * patches, (b + 1) * patches) for b in range(3)]
        slopes = [dot(values_ref[h, r], grad, NN) for r in rows]
        probs = [probs_ref[h, r] for r in rows]
        wide = [p.astype(jnp.float32) for p in probs]
        delta = sum([jnp.sum(p * s, 0, keepdims=True) for p, s in zip(wide, slopes)])
        total = jnp.zeros((HEAD_DIM, patches), jnp.float32)
        for b, ref in enumerate(blocks):
            scores = (wide[b] * (slopes[b] - delta)).astype(jnp.bfloat16)
            key = ref[columns + h * HEAD_DIM : columns + (h + 1) * HEAD_DIM]
            total = total + dot(key, scores, NN)
            if b == 1:
                key_ref[cols] = dot(ref[cols], scores, NT)
                value_ref[cols] = dot(grad, probs[b], NT)
        query_ref[cols] = (total * SCALE).astype(jnp.bfloat16)


def own_terms(grad, own, before, after, probs, values):
    return pl.pallas_call(
        own_kernel,
        out_shape=(
            jax.ShapeDtypeStruct(grad.shape, jnp.bfloat16),
            jax.ShapeDtypeStruct(grad.shape, jnp.float32),
            jax.ShapeDtypeStruct(grad.shape, jnp.float32),
        ),
        in_specs=in_vmem(6),
        out_specs=tuple(in_vmem(3)),
        compiler_params=params(32),
        name="own_terms",
    )(grad, own, before, after, probs, values)


def side_kernel(left_ref, right_ref, before_ref, after_ref, probs_ref, attended_ref, values_ref,
                key_part_ref, value_part_ref, key_ref, value_ref):
    columns, patches = left_ref.shape
    for h in range(columns // HEAD_DIM):
        cols = slice(h * HEAD_DIM, (h + 1) * HEAD_DIM)
        key, value = key_part_ref[cols], value_part_ref[cols]
        for side, (grad_ref, ref) in enumerate(((left_ref, before_ref), (right_ref, after_ref))):
            grad = grad_ref[cols]
            attended = attended_ref[side, cols]
            delta = jnp.sum(grad.astype(jnp.float32) * attended, 0, keepdims=True)
            probs = probs_ref[h, side]
            slope = dot(values_ref[h, patches : 2 * patches], grad, NN)
            scores = (probs.astype(jnp.float32) * (slope - delta)).astype(jnp.bfloat16)
            key = key + dot(ref[cols], scores, NT)
            value = value + dot(grad, probs, NT)
        key_ref[cols] = (key * SCALE).astype(jnp.bfloat16)
        value_ref[cols] = value.astype(jnp.bfloat16)


def side_terms(left, right, before, after, probs, attended, values, key_part, value_part):
    shape = jax.ShapeDtypeStruct(left.shape, jnp.bfloat16)
    return pl.pallas_call(
        side_kernel,
        out_shape=(shape, shape),
        in_specs=in_vmem(9),
        out_specs=tuple(in_vmem(2)),
        compiler_params=params(32),
        name="side_terms",
    )(left, right, before, after, probs, attended, values, key_part, value_part)


def from_both_sides(x, axis):
    size = lax.axis_size(axis)
    up = [(i, i + 1) for i in range(size - 1)]
    return (
        lax.ppermute(x, axis, up),
        lax.ppermute(x, axis, [(j, i) for i, j in up]),
    )


def on_device(
    grad_out, destination, w_down, pre_act, w_up, queries, key_states, value_states, lengths
):
    groups = lax.axis_size("grp")
    spans = lax.axis_size("span")
    heads = lax.axis_size(("sect", "span"))
    row_count = grad_out.shape[0]
    capacity, _ = padded_slots(row_count, groups)
    pieces = down_pieces(destination, grad_out, w_down, groups, spans)
    pieces, queries, key_states, value_states = lax.optimization_barrier(
        (pieces, queries, key_states, value_states)
    )
    arrived = lax.all_to_all(pieces, ("grp", "span"), split_axis=0, concat_axis=0, tiled=True)
    own = jnp.concatenate([queries.T, key_states.T, value_states.T], 0)
    before, after = from_both_sides(own, "grp")
    first = (lax.axis_index("grp") - 1) * row_count
    own_probs, side_probs, attended, values, softmax_done = softmax_parts(
        lengths, first, own, before, after
    )
    shares = up_pieces(arrived, pre_act, w_up, heads, capacity)
    shares = lax.all_to_all(shares, ("sect", "span"), split_axis=0, concat_axis=0, tiled=True)
    grad = gathered(shares, softmax_done)
    left, right = from_both_sides(grad, "grp")
    grad_query, key_part, value_part = own_terms(grad, own, before, after, own_probs, values)
    grad_key, grad_value = side_terms(
        left, right, before, after, side_probs, attended, values, key_part, value_part
    )
    return grad_query.T, grad_key.T, grad_value.T


def solution(mesh):
    split = P("grp", ("sect", "span"))
    placed = (
        P("grp", "span"),
        P("grp"),
        P("sect", "span"),
        split,
        P(None, ("sect", "span")),
        split,
        split,
        split,
        P(),
    )
    return jax.shard_map(
        on_device,
        mesh=mesh,
        in_specs=placed,
        out_specs=(split, split, split),
        check_vma=False,
    )
```

```python
import functools

import jax
import jax.numpy as jnp
from jax import lax
from jax.experimental import pallas as pl
from jax.experimental.pallas import tpu as pltpu
from jax.sharding import PartitionSpec as P

HEAD_DIM = 80
SCALE = HEAD_DIM**-0.5
MIB = 1024 * 1024
VMEM = pltpu.MemorySpace.VMEM
NT = (((1,), (1,)), ((), ()))
NN = (((1,), (0,)), ((), ()))
TN = (((0,), (0,)), ((), ()))


def dot(a, b, dims):
    return lax.dot_general(a, b, dims, preferred_element_type=jnp.float32)


def iota(shape, dim):
    return lax.broadcasted_iota(jnp.int32, shape, dim)


def params(mib):
    return pltpu.CompilerParams(vmem_limit_bytes=mib * MIB)


def in_vmem(count):
    return [pl.BlockSpec(memory_space=VMEM) for _ in range(count)]


def in_hbm(count):
    return [pl.BlockSpec(memory_space=pltpu.MemorySpace.HBM) for _ in range(count)]


def fetched(pairs, sems):
    copies = [pltpu.make_async_copy(a, b, sems.at[i]) for i, (a, b) in enumerate(pairs)]
    for copy in copies:
        copy.start()
    return copies


def padded_slots(row_count, groups):
    offsets = min(groups, row_count // 2)
    capacity = row_count // offsets
    return capacity, -(-(capacity + 1) // 8) * 8


def one_product(count, slots, hidden):
    return count * slots <= hidden


def down_kernel(groups, spans, capacity, slots, step, dest_hbm, rows_hbm, weight_ref, out_ref,
                dest_ref, rows_ref, held, sems):
    row_count = rows_ref.shape[0]
    hidden = weight_ref.shape[0] // spans
    pairs = [(dest_hbm, dest_ref), (rows_hbm, rows_ref)]
    for at in range(0, spans * hidden, step):
        pairs.append((weight_ref.at[pl.ds(at, step)], held.at[pl.ds(at, step)]))
    copies = fetched(pairs, sems)
    copies[0].wait()
    across = jnp.broadcast_to(dest_ref[...].astype(jnp.float32), (row_count, row_count))
    down = across.T
    group_across = jnp.floor((across + 0.5) * (1.0 / row_count))
    group_down = jnp.floor((down + 0.5) * (1.0 / row_count))
    slot_down = down - group_down * row_count
    same = group_across == group_down
    earlier = iota((row_count, row_count), 0) < iota((row_count, row_count), 1)
    later = iota((row_count, row_count), 1) < iota((row_count, row_count), 0)
    rank_across = jnp.sum(jnp.where(same & earlier, 1.0, 0.0), 0, keepdims=True)
    rank_down = jnp.sum(jnp.where(same & later, 1.0, 0.0), 1, keepdims=True)
    row_of = group_across[:1] * slots + rank_across
    places = iota((groups * slots, row_count), 0).astype(jnp.float32)
    pick = jnp.where(places == row_of, 1.0, 0.0).astype(jnp.bfloat16)
    lane = iota((row_count, hidden), 1).astype(jnp.float32)
    shift = 0.0
    if one_product(groups * spans, slots, hidden):
        device = lax.axis_index("grp") * spans + lax.axis_index("span")
        shift = (device * slots).astype(jnp.float32)
    at_rank = lane == rank_down + shift
    label_row = iota((slots, hidden), 0) == capacity
    labels = []
    for g in range(groups):
        hit = at_rank & (group_down[:, :1] == g)
        labels.append(jnp.sum(jnp.where(hit, slot_down[:, :1] + 1.0, 0.0), 0, keepdims=True) - 1.0)
    copies[1].wait()
    for s in range(spans):
        total = []
        for at in range(s * hidden, (s + 1) * hidden, step):
            copies[2 + at // step].wait()
            product = dot(held[at : at + step], rows_ref[...], NT)
            total.append(product.astype(jnp.bfloat16))
        moved = dot(pick, jnp.concatenate(total, 0), NT)
        for g in range(groups):
            piece = jnp.where(label_row, labels[g], moved[g * slots : (g + 1) * slots])
            out_ref[g * spans + s] = piece.astype(jnp.bfloat16)


def down_pieces(dest, rows, weight, groups, spans):
    row_count = rows.shape[0]
    capacity, slots = padded_slots(row_count, groups)
    hidden = weight.shape[0] // spans
    step = hidden if hidden < 320 else 320
    return pl.pallas_call(
        functools.partial(down_kernel, groups, spans, capacity, slots, step),
        out_shape=jax.ShapeDtypeStruct((groups * spans, slots, hidden), jnp.bfloat16),
        in_specs=in_hbm(3),
        out_specs=pl.BlockSpec(memory_space=VMEM),
        scratch_shapes=[
            pltpu.VMEM((1, row_count), jnp.int32),
            pltpu.VMEM(rows.shape, jnp.bfloat16),
            pltpu.VMEM(weight.shape, jnp.bfloat16),
            pltpu.SemaphoreType.DMA((2 + weight.shape[0] // step,)),
        ],
        compiler_params=params(60),
        name="down_product",
    )(dest.reshape(1, row_count), rows, weight)


def up_kernel(heads, capacity, pieces_ref, pre_ref, weight_ref, out_ref, held, sems):
    row_count, hidden = pre_ref.shape
    count, slots, _ = pieces_ref.shape
    width = weight_ref.shape[0] // (4 * heads)
    copies = []
    for h in range(heads):
        for j in range(4):
            copy = pltpu.make_async_copy(
                weight_ref.at[pl.ds((j * heads + h) * width, width)],
                held.at[h, pl.ds(j * width, width)],
                sems.at[h * 4 + j],
            )
            copy.start()
            copies.append(copy)
    label_at = slice(capacity, capacity + 1)
    if one_product(count, slots, hidden):
        pieces = [pieces_ref[p].astype(jnp.float32) for p in range(count)]
        labels = functools.reduce(jnp.maximum, [x[label_at, : count * slots] for x in pieces])
        row = iota((row_count, count * slots), 0).astype(jnp.float32)
        put = jnp.where(row == labels, 1.0, 0.0).astype(jnp.bfloat16)
        total = dot(put, jnp.concatenate(pieces, 0).astype(jnp.bfloat16), NN)
    else:
        row = iota((row_count, slots), 0).astype(jnp.float32)

        def placed(p, total):
            piece = pieces_ref[p]
            labels = piece.astype(jnp.float32)[label_at, :slots]
            put = jnp.where(row == labels, 1.0, 0.0).astype(jnp.bfloat16)
            return total + dot(put, piece, NN)

        total = lax.fori_loop(0, count, placed, jnp.zeros((row_count, hidden), jnp.float32))
    pre = pre_ref[...].astype(jnp.float32)
    cdf = 0.5 * (1.0 + lax.erf(pre * 0.7071067811865476))
    slope = cdf + pre * jnp.exp(-0.5 * pre * pre) * 0.3989422804014327
    grad_pre = (total * slope).astype(jnp.bfloat16)
    for h in range(heads):
        for j in range(4):
            copies[h * 4 + j].wait()
        out_ref[h] = dot(held[h], grad_pre, NT).T.astype(jnp.bfloat16)


def up_pieces(pieces, pre, weight, heads, capacity):
    width = weight.shape[0] // heads
    return pl.pallas_call(
        functools.partial(up_kernel, heads, capacity),
        out_shape=jax.ShapeDtypeStruct((heads, pre.shape[0], width), jnp.bfloat16),
        in_specs=in_vmem(2) + in_hbm(1),
        out_specs=pl.BlockSpec(memory_space=VMEM),
        scratch_shapes=[
            pltpu.VMEM((heads, width, weight.shape[1]), jnp.bfloat16),
            pltpu.SemaphoreType.DMA((heads * 4,)),
        ],
        compiler_params=params(52),
        cost_estimate=pl.CostEstimate(
            flops=8 * pre.shape[0] * weight.size, bytes_accessed=8 * weight.size, transcendentals=0
        ),
        name="up_product",
    )(pieces, pre, weight)


class Rows:
    def __init__(self, columns, patches):
        heads = columns // HEAD_DIM
        self.columns, self.patches = columns, patches
        self.probs_at = 9 * columns
        self.side_at = self.probs_at + heads * 3 * patches
        self.attended_at = self.side_at + heads * 2 * patches
        self.total = self.attended_at + 2 * columns

    def block(self, b, kind):
        return pl.ds((3 * b + kind) * self.columns, self.columns)

    def blocks(self, b):
        return pl.ds(3 * b * self.columns, 3 * self.columns)

    def probs(self, h):
        return pl.ds(self.probs_at + h * 3 * self.patches, 3 * self.patches)

    def side_probs(self, h):
        return pl.ds(self.side_at + h * 2 * self.patches, 2 * self.patches)

    def attended(self):
        return pl.ds(self.attended_at, 2 * self.columns)


def softmax_kernel(lengths_ref, first_ref, own_hbm, before_hbm, after_hbm, out_hbm, held, sems):
    columns, patches = own_hbm.shape[0] // 3, own_hbm.shape[1]
    heads = columns // HEAD_DIM
    rows = Rows(columns, patches)
    pairs = [(x, held.at[rows.blocks(b)]) for b, x in enumerate((own_hbm, before_hbm, after_hbm))]
    copies = fetched(pairs, sems)
    first = first_ref[0, 0]

    def image_of(shape, dim):
        token = iota(shape, dim) // 4 + first

        def step(i, state):
            image, bound = state
            bound = bound + lengths_ref[0, i]
            return image + jnp.where(token >= bound, 1, 0), bound

        start = (jnp.where(token < 0, -1, 0), jnp.int32(0))
        return lax.fori_loop(0, lengths_ref.shape[1], step, start)[0]

    key_image = image_of((3 * patches, 1), 0)
    query_image = image_of((1, 3 * patches), 1)
    for copy in copies:
        copy.wait()
    at = (1, 0, 2)
    for h in range(heads):

        def part(b, kind):
            start = (3 * b + kind) * columns + h * HEAD_DIM
            return held[start : start + HEAD_DIM]

        k_rows = [part(b, 1).astype(jnp.float32).T.astype(jnp.bfloat16) for b in range(3)]
        for qb, keys in ((1, (1, 0)), (0, (1, 0, 2)), (2, (0, 2))):
            scores = []
            image = query_image[:, at[qb] * patches : (at[qb] + 1) * patches]
            for kb in keys:
                same = key_image[at[kb] * patches : (at[kb] + 1) * patches] == image
                products = dot(k_rows[kb], part(qb, 0), NN) * SCALE
                scores.append(jnp.where(same, products, -jnp.inf))
            tops = [jnp.max(s, 0, keepdims=True) for s in scores]
            top = functools.reduce(jnp.maximum, tops)
            weights = [jnp.exp(s - top) for s in scores]
            over = 1.0 / functools.reduce(jnp.add, [jnp.sum(w, 0, keepdims=True) for w in weights])
            attended = jnp.zeros((HEAD_DIM, patches), jnp.float32)
            for n, (kb, w) in enumerate(zip(keys, weights)):
                probs = (w * over).astype(jnp.bfloat16)
                if qb == 0:
                    start = rows.probs_at + (3 * h + n) * patches
                    held[start : start + patches] = probs
                else:
                    attended = attended + dot(part(kb, 2), probs, NN)
                    if kb == 0:
                        start = rows.side_at + (2 * h + qb - 1) * patches
                        held[start : start + patches] = probs
            if qb != 0:
                start = rows.attended_at + (qb - 1) * columns + h * HEAD_DIM
                held[start : start + HEAD_DIM] = attended.astype(jnp.bfloat16)
    out = pltpu.make_async_copy(held, out_hbm, sems.at[3])
    out.start()
    out.wait()


def softmax_parts(lengths, first, own, before, after):
    columns, patches = own.shape[0] // 3, own.shape[1]
    rows = Rows(columns, patches)
    smem = pl.BlockSpec(memory_space=pltpu.MemorySpace.SMEM)
    work = (columns // HEAD_DIM) * patches * patches
    return pl.pallas_call(
        softmax_kernel,
        out_shape=jax.ShapeDtypeStruct((rows.total, patches), jnp.bfloat16),
        in_specs=[smem, smem] + in_hbm(3),
        out_specs=in_hbm(1)[0],
        scratch_shapes=[
            pltpu.VMEM((rows.total, patches), jnp.bfloat16),
            pltpu.SemaphoreType.DMA((4,)),
        ],
        compiler_params=params(60),
        cost_estimate=pl.CostEstimate(
            flops=100_000 * work, bytes_accessed=500 * work, transcendentals=9 * work
        ),
        name="softmax_parts",
    )(lengths.reshape(1, -1), first.reshape(1, 1), own, before, after)


def gather_kernel(pieces_ref, _, out_ref):
    count, row_count, width = pieces_ref.shape
    total = pieces_ref[0].astype(jnp.float32)
    for p in range(1, count):
        total = total + pieces_ref[p].astype(jnp.float32)
    total = total.astype(jnp.bfloat16)
    columns = width // 4
    patch = iota((row_count, 4 * row_count), 1)
    token = iota((row_count, 4 * row_count), 0)
    result = jnp.zeros((columns, 4 * row_count), jnp.float32)
    for j in range(4):
        put = jnp.where(patch == 4 * token + j, 1.0, 0.0).astype(jnp.bfloat16)
        result = result + dot(total[:, j * columns : (j + 1) * columns], put, TN)
    out_ref[...] = result.astype(jnp.bfloat16)


def gathered(pieces, later):
    _, row_count, width = pieces.shape
    return pl.pallas_call(
        gather_kernel,
        out_shape=jax.ShapeDtypeStruct((width // 4, 4 * row_count), jnp.bfloat16),
        in_specs=in_vmem(1) + in_hbm(1),
        out_specs=pl.BlockSpec(memory_space=VMEM),
        compiler_params=params(52),
        name="gather_sum",
    )(pieces, later)


def own_kernel(grad_ref, held_hbm, query_ref, key_ref, value_ref, probs_ref, blocks_ref, own_ref,
               sems):
    columns, patches = grad_ref.shape
    heads = columns // HEAD_DIM
    rows = Rows(columns, patches)
    pairs = [(held_hbm.at[rows.block(b, 2)], blocks_ref.at[1, i]) for i, b in enumerate((1, 0, 2))]
    pairs += [(held_hbm.at[rows.probs(h)], probs_ref.at[h]) for h in range(heads)]
    pairs += [(held_hbm.at[rows.block(b, 1)], blocks_ref.at[0, i]) for i, b in enumerate((1, 0, 2))]
    pairs += [(held_hbm.at[rows.block(0, 0)], own_ref)]
    copies = fetched(pairs, sems)
    for copy in copies[:3]:
        copy.wait()
    for h in range(heads):
        cols = slice(h * HEAD_DIM, (h + 1) * HEAD_DIM)
        grad = grad_ref[cols]
        slopes = [dot(blocks_ref[1, b, cols], grad, TN) for b in range(3)]
        copies[3 + h].wait()
        probs = [probs_ref[h, b * patches : (b + 1) * patches] for b in range(3)]
        wide = [p.astype(jnp.float32) for p in probs]
        delta = sum([jnp.sum(p * s, 0, keepdims=True) for p, s in zip(wide, slopes)])
        if h == 0:
            for copy in copies[3 + heads :]:
                copy.wait()
        total = jnp.zeros((HEAD_DIM, patches), jnp.float32)
        for b in range(3):
            scores = (wide[b] * (slopes[b] - delta)).astype(jnp.bfloat16)
            total = total + dot(blocks_ref[0, b, cols], scores, NN)
            if b == 1:
                key_ref[cols] = dot(own_ref[cols], scores, NT)
                value_ref[cols] = dot(grad, probs[b], NT)
        query_ref[cols] = (total * SCALE).astype(jnp.bfloat16)


def own_terms(grad, held):
    heads = grad.shape[0] // HEAD_DIM
    columns, patches = grad.shape
    return pl.pallas_call(
        own_kernel,
        out_shape=(
            jax.ShapeDtypeStruct(grad.shape, jnp.bfloat16),
            jax.ShapeDtypeStruct(grad.shape, jnp.float32),
            jax.ShapeDtypeStruct(grad.shape, jnp.float32),
        ),
        in_specs=in_vmem(1) + in_hbm(1),
        out_specs=tuple(in_vmem(3)),
        scratch_shapes=[
            pltpu.VMEM((heads, 3 * patches, patches), jnp.bfloat16),
            pltpu.VMEM((2, 3, columns, patches), jnp.bfloat16),
            pltpu.VMEM(grad.shape, jnp.bfloat16),
            pltpu.SemaphoreType.DMA((7 + heads,)),
        ],
        compiler_params=params(52),
        name="own_terms",
    )(grad, held)


def side_kernel(left_ref, right_ref, key_part_ref, value_part_ref, held_hbm, key_ref, value_ref,
                values_ref, attended_ref, probs_ref, queries_ref, sems):
    columns, patches = left_ref.shape
    heads = columns // HEAD_DIM
    rows = Rows(columns, patches)
    pairs = [(held_hbm.at[rows.block(0, 2)], values_ref), (held_hbm.at[rows.attended()], attended_ref)]
    pairs += [(held_hbm.at[rows.side_probs(h)], probs_ref.at[h]) for h in range(heads)]
    pairs += [(held_hbm.at[rows.block(1 + i, 0)], queries_ref.at[i]) for i in range(2)]
    copies = fetched(pairs, sems)
    copies[0].wait()
    for h in range(heads):
        cols = slice(h * HEAD_DIM, (h + 1) * HEAD_DIM)
        grads = (left_ref[cols], right_ref[cols])
        slopes = [dot(values_ref[cols], grad, TN) for grad in grads]
        key, value = key_part_ref[cols], value_part_ref[cols]
        if h == 0:
            copies[1].wait()
        copies[2 + h].wait()
        scores = []
        for side, grad in enumerate(grads):
            start = side * columns + h * HEAD_DIM
            attended = attended_ref[start : start + HEAD_DIM].astype(jnp.float32)
            delta = jnp.sum(grad.astype(jnp.float32) * attended, 0, keepdims=True)
            probs = probs_ref[h, side * patches : (side + 1) * patches]
            scores.append((probs.astype(jnp.float32) * (slopes[side] - delta)).astype(jnp.bfloat16))
            value = value + dot(grad, probs, NT)
        if h == 0:
            for copy in copies[2 + heads :]:
                copy.wait()
        for side in range(2):
            key = key + dot(queries_ref[side, cols], scores[side], NT)
        key_ref[cols] = (key * SCALE).astype(jnp.bfloat16)
        value_ref[cols] = value.astype(jnp.bfloat16)


def side_terms(left, right, key_part, value_part, held):
    shape = jax.ShapeDtypeStruct(left.shape, jnp.bfloat16)
    columns, patches = left.shape
    heads = columns // HEAD_DIM
    return pl.pallas_call(
        side_kernel,
        out_shape=(shape, shape),
        in_specs=in_vmem(4) + in_hbm(1),
        out_specs=tuple(in_vmem(2)),
        scratch_shapes=[
            pltpu.VMEM(left.shape, jnp.bfloat16),
            pltpu.VMEM((2 * columns, patches), jnp.bfloat16),
            pltpu.VMEM((heads, 2 * patches, patches), jnp.bfloat16),
            pltpu.VMEM((2,) + left.shape, jnp.bfloat16),
            pltpu.SemaphoreType.DMA((4 + heads,)),
        ],
        compiler_params=params(52),
        name="side_terms",
    )(left, right, key_part, value_part, held)


def from_both_sides(x, axis):
    size = lax.axis_size(axis)
    up = [(i, i + 1) for i in range(size - 1)]
    return (
        lax.ppermute(x, axis, up),
        lax.ppermute(x, axis, [(j, i) for i, j in up]),
    )


def on_device(
    grad_out, destination, w_down, pre_act, w_up, queries, key_states, value_states, lengths
):
    groups = lax.axis_size("grp")
    spans = lax.axis_size("span")
    heads = lax.axis_size(("sect", "span"))
    row_count = grad_out.shape[0]
    capacity, _ = padded_slots(row_count, groups)
    pieces = down_pieces(destination, grad_out, w_down, groups, spans)
    pieces, queries, key_states, value_states = lax.optimization_barrier(
        (pieces, queries, key_states, value_states)
    )
    arrived = lax.all_to_all(pieces, ("grp", "span"), split_axis=0, concat_axis=0, tiled=True)
    own = jnp.concatenate([queries.T, key_states.T, value_states.T], 0)
    before, after = from_both_sides(own, "grp")
    first = (lax.axis_index("grp") - 1) * row_count
    held = softmax_parts(lengths, first, own, before, after)
    shares = up_pieces(arrived, pre_act, w_up, heads, capacity)
    shares = lax.all_to_all(shares, ("sect", "span"), split_axis=0, concat_axis=0, tiled=True)
    grad = gathered(shares, held)
    left, right = from_both_sides(grad, "grp")
    grad_query, key_part, value_part = own_terms(grad, held)
    grad_key, grad_value = side_terms(left, right, key_part, value_part, held)
    return grad_query.T, grad_key.T, grad_value.T


def solution(mesh):
    split = P("grp", ("sect", "span"))
    placed = (
        P("grp", "span"),
        P("grp"),
        P("sect", "span"),
        split,
        P(None, ("sect", "span")),
        split,
        split,
        split,
        P(),
    )
    return jax.shard_map(
        on_device,
        mesh=mesh,
        in_specs=placed,
        out_specs=(split, split, split),
        check_vma=False,
    )
```

```python
import functools

import jax
import jax.numpy as jnp
from jax import lax
from jax.experimental import pallas as pl
from jax.experimental.pallas import tpu as pltpu
from jax.sharding import PartitionSpec as P

HEAD_DIM = 80
SCALE = HEAD_DIM**-0.5
MIB = 1024 * 1024
VMEM = pltpu.MemorySpace.VMEM
NT = (((1,), (1,)), ((), ()))
NN = (((1,), (0,)), ((), ()))
TN = (((0,), (0,)), ((), ()))


def dot(a, b, dims):
    return lax.dot_general(a, b, dims, preferred_element_type=jnp.float32)


def iota(shape, dim):
    return lax.broadcasted_iota(jnp.int32, shape, dim)


def params(mib):
    return pltpu.CompilerParams(vmem_limit_bytes=mib * MIB)


def in_vmem(count):
    return [pl.BlockSpec(memory_space=VMEM) for _ in range(count)]


def in_hbm(count):
    return [pl.BlockSpec(memory_space=pltpu.MemorySpace.HBM) for _ in range(count)]


def fetched(pairs, sems):
    copies = [pltpu.make_async_copy(a, b, sems.at[i]) for i, (a, b) in enumerate(pairs)]
    for copy in copies:
        copy.start()
    return copies


def padded_slots(row_count, groups):
    offsets = min(groups, row_count // 2)
    capacity = row_count // offsets
    return capacity, -(-(capacity + 1) // 8) * 8


def one_product(count, slots, hidden):
    return count * slots <= hidden


def down_kernel(groups, spans, capacity, slots, steps, dest_hbm, rows_hbm, weight_ref, out_ref,
                dest_ref, rows_ref, held, sems):
    row_count = rows_ref.shape[0]
    hidden = weight_ref.shape[0] // spans
    pairs = [(dest_hbm, dest_ref), (rows_hbm, rows_ref)]
    at = 0
    for step in steps:
        pairs.append((weight_ref.at[pl.ds(at, step)], held.at[pl.ds(at, step)]))
        at += step
    copies = fetched(pairs, sems)
    copies[0].wait()
    across = jnp.broadcast_to(dest_ref[...].astype(jnp.float32), (row_count, row_count))
    down = across.T
    group_across = jnp.floor((across + 0.5) * (1.0 / row_count))
    group_down = jnp.floor((down + 0.5) * (1.0 / row_count))
    slot_down = down - group_down * row_count
    same = group_across == group_down
    earlier = iota((row_count, row_count), 0) < iota((row_count, row_count), 1)
    later = iota((row_count, row_count), 1) < iota((row_count, row_count), 0)
    rank_across = jnp.sum(jnp.where(same & earlier, 1.0, 0.0), 0, keepdims=True)
    rank_down = jnp.sum(jnp.where(same & later, 1.0, 0.0), 1, keepdims=True)
    row_of = group_across[:1] * slots + rank_across
    places = iota((groups * slots, row_count), 0).astype(jnp.float32)
    pick = jnp.where(places == row_of, 1.0, 0.0).astype(jnp.bfloat16)
    lane = iota((row_count, hidden), 1).astype(jnp.float32)
    shift = 0.0
    if one_product(groups * spans, slots, hidden):
        device = lax.axis_index("grp") * spans + lax.axis_index("span")
        shift = (device * slots).astype(jnp.float32)
    at_rank = lane == rank_down + shift
    label_row = iota((slots, hidden), 0) == capacity
    labels = []
    for g in range(groups):
        hit = at_rank & (group_down[:, :1] == g)
        labels.append(jnp.sum(jnp.where(hit, slot_down[:, :1] + 1.0, 0.0), 0, keepdims=True) - 1.0)
    copies[1].wait()
    at, n = 0, 0
    for s in range(spans):
        total = []
        while at < (s + 1) * hidden:
            copies[2 + n].wait()
            product = dot(held[at : at + steps[n]], rows_ref[...], NT)
            total.append(product.astype(jnp.bfloat16))
            at, n = at + steps[n], n + 1
        moved = dot(pick, jnp.concatenate(total, 0), NT)
        for g in range(groups):
            piece = jnp.where(label_row, labels[g], moved[g * slots : (g + 1) * slots])
            out_ref[g * spans + s] = piece.astype(jnp.bfloat16)


def down_pieces(dest, rows, weight, groups, spans):
    row_count = rows.shape[0]
    capacity, slots = padded_slots(row_count, groups)
    hidden = weight.shape[0] // spans
    steps = [128, hidden - 128]
    if hidden > 512:
        steps = [128, 256, hidden - 384]
    steps += [hidden // 2, hidden - hidden // 2] * (spans - 1)
    return pl.pallas_call(
        functools.partial(down_kernel, groups, spans, capacity, slots, steps),
        out_shape=jax.ShapeDtypeStruct((groups * spans, slots, hidden), jnp.bfloat16),
        in_specs=in_hbm(3),
        out_specs=pl.BlockSpec(memory_space=VMEM),
        scratch_shapes=[
            pltpu.VMEM((1, row_count), jnp.int32),
            pltpu.VMEM(rows.shape, jnp.bfloat16),
            pltpu.VMEM(weight.shape, jnp.bfloat16),
            pltpu.SemaphoreType.DMA((2 + len(steps),)),
        ],
        compiler_params=params(60),
        name="down_product",
    )(dest.reshape(1, row_count), rows, weight)


def up_kernel(heads, capacity, pieces_ref, pre_ref, weight_ref, out_ref, held, sems):
    row_count, hidden = pre_ref.shape
    count, slots, _ = pieces_ref.shape
    width = weight_ref.shape[0] // (4 * heads)
    copies = []
    for h in range(heads):
        for j in range(4):
            copy = pltpu.make_async_copy(
                weight_ref.at[pl.ds((j * heads + h) * width, width)],
                held.at[h, pl.ds(j * width, width)],
                sems.at[h * 4 + j],
            )
            copy.start()
            copies.append(copy)
    label_at = slice(capacity, capacity + 1)
    if one_product(count, slots, hidden):
        pieces = [pieces_ref[p].astype(jnp.float32) for p in range(count)]
        labels = functools.reduce(jnp.maximum, [x[label_at, : count * slots] for x in pieces])
        row = iota((row_count, count * slots), 0).astype(jnp.float32)
        put = jnp.where(row == labels, 1.0, 0.0).astype(jnp.bfloat16)
        total = dot(put, jnp.concatenate(pieces, 0).astype(jnp.bfloat16), NN)
    else:
        row = iota((row_count, slots), 0).astype(jnp.float32)

        def placed(p, total):
            piece = pieces_ref[p]
            labels = piece.astype(jnp.float32)[label_at, :slots]
            put = jnp.where(row == labels, 1.0, 0.0).astype(jnp.bfloat16)
            return total + dot(put, piece, NN)

        total = lax.fori_loop(0, count, placed, jnp.zeros((row_count, hidden), jnp.float32))
    pre = pre_ref[...].astype(jnp.float32)
    cdf = 0.5 * (1.0 + lax.erf(pre * 0.7071067811865476))
    slope = cdf + pre * jnp.exp(-0.5 * pre * pre) * 0.3989422804014327
    grad_pre = (total * slope).astype(jnp.bfloat16)
    for h in range(heads):
        for j in range(4):
            copies[h * 4 + j].wait()
        out_ref[h] = dot(held[h], grad_pre, NT).T.astype(jnp.bfloat16)


def up_pieces(pieces, pre, weight, heads, capacity):
    width = weight.shape[0] // heads
    return pl.pallas_call(
        functools.partial(up_kernel, heads, capacity),
        out_shape=jax.ShapeDtypeStruct((heads, pre.shape[0], width), jnp.bfloat16),
        in_specs=in_vmem(2) + in_hbm(1),
        out_specs=pl.BlockSpec(memory_space=VMEM),
        scratch_shapes=[
            pltpu.VMEM((heads, width, weight.shape[1]), jnp.bfloat16),
            pltpu.SemaphoreType.DMA((heads * 4,)),
        ],
        compiler_params=params(52),
        cost_estimate=pl.CostEstimate(
            flops=8 * pre.shape[0] * weight.size, bytes_accessed=8 * weight.size, transcendentals=0
        ),
        name="up_product",
    )(pieces, pre, weight)


class Rows:
    def __init__(self, columns, patches):
        heads = columns // HEAD_DIM
        self.lanes = -(-3 * patches // 128) * 128
        self.side_lanes = -(-2 * patches // 128) * 128
        self.columns, self.patches = columns, patches
        self.values = pl.ds(0, columns)
        self.keys = pl.ds(columns, columns)
        self.queries = pl.ds(2 * columns, columns)
        self.attended = pl.ds(3 * columns, columns)
        self.probs_at = 4 * columns
        self.side_at = self.probs_at + heads * patches
        self.total = self.side_at + heads * patches

    def probs(self, h):
        return pl.ds(self.probs_at + h * self.patches, self.patches)

    def side_probs(self, h):
        return pl.ds(self.side_at + h * self.patches, self.patches)


def softmax_kernel(lengths_ref, first_ref, own_ref, before_ref, after_ref, out_hbm, held, sems):
    columns, patches = own_ref.shape[0] // 3, own_ref.shape[1]
    heads = columns // HEAD_DIM
    rows = Rows(columns, patches)
    blocks = (own_ref, before_ref, after_ref)
    first = first_ref[0, 0]

    def image_of(shape, dim, block):
        token = iota(shape, dim) // 4 + (first + block * (patches // 4))

        def step(i, state):
            image, bound = state
            bound = bound + lengths_ref[0, i]
            return image + jnp.where(token >= bound, 1, 0), bound

        start = (jnp.where(token < 0, -1, 0), jnp.int32(0))
        return lax.fori_loop(0, lengths_ref.shape[1], step, start)[0]

    down = [image_of((patches, 1), 0, b) for b in (0, -1, 1)]
    across = [image_of((1, patches), 1, b) for b in (0, -1, 1)]
    all_keys = jnp.concatenate(across, 1)
    same_own = down[0] == all_keys
    copies = []

    def send(part, lanes):
        copy = pltpu.make_async_copy(
            held.at[part, pl.ds(0, lanes)], out_hbm.at[part, pl.ds(0, lanes)], sems.at[len(copies)]
        )
        copy.start()
        copies.append(copy)

    def kind(block, t, h=None):
        start = t * columns + (0 if h is None else h * HEAD_DIM)
        return blocks[block][start : start + (columns if h is None else HEAD_DIM)]

    def wide(t, which):
        return jnp.concatenate([kind(b, t).astype(jnp.float32) for b in which], 1).astype(jnp.bfloat16)

    held[rows.values, : 3 * patches] = wide(2, (0, 1, 2))
    held[rows.keys, : 3 * patches] = wide(1, (0, 1, 2))
    held[rows.queries, : 2 * patches] = wide(0, (1, 2))
    send(pl.ds(0, 2 * columns), rows.lanes)
    send(rows.queries, rows.side_lanes)
    for h in range(heads):
        cols = slice(columns + h * HEAD_DIM, columns + (h + 1) * HEAD_DIM)
        scores = dot(kind(0, 0, h), held[cols, : 3 * patches], TN) * SCALE
        scores = jnp.where(same_own, scores, -jnp.inf)
        weights = jnp.exp(scores - jnp.max(scores, 1, keepdims=True))
        over = 1.0 / jnp.sum(weights, 1, keepdims=True)
        held[rows.probs(h), : 3 * patches] = (weights * over).astype(jnp.bfloat16)
        send(rows.probs(h), rows.lanes)
    for h in range(heads):
        own_keys = kind(0, 1, h).astype(jnp.float32).T.astype(jnp.bfloat16)
        side, attended = [], []
        for b in (1, 2):
            queries = kind(b, 0, h)
            keys = kind(b, 1, h).astype(jnp.float32).T.astype(jnp.bfloat16)
            scores = []
            for n, k in ((0, own_keys), (b, keys)):
                scores.append(jnp.where(down[n] == across[b], dot(k, queries, NN) * SCALE, -jnp.inf))
            top = functools.reduce(jnp.maximum, [jnp.max(x, 0, keepdims=True) for x in scores])
            weights = [jnp.exp(x - top) for x in scores]
            over = 1.0 / sum([jnp.sum(w, 0, keepdims=True) for w in weights])
            probs = [(w * over).astype(jnp.bfloat16) for w in weights]
            attended.append(dot(kind(0, 2, h), probs[0], NN) + dot(kind(b, 2, h), probs[1], NN))
            side.append(probs[0].astype(jnp.float32))
        held[rows.side_probs(h), : 2 * patches] = jnp.concatenate(side, 1).astype(jnp.bfloat16)
        send(rows.side_probs(h), rows.side_lanes)
        cols = slice(3 * columns + h * HEAD_DIM, 3 * columns + (h + 1) * HEAD_DIM)
        held[cols, : 2 * patches] = jnp.concatenate(attended, 1).astype(jnp.bfloat16)
    send(rows.attended, rows.side_lanes)
    for copy in copies:
        copy.wait()


def softmax_parts(lengths, first, own, before, after):
    columns, patches = own.shape[0] // 3, own.shape[1]
    heads = columns // HEAD_DIM
    rows = Rows(columns, patches)
    smem = pl.BlockSpec(memory_space=pltpu.MemorySpace.SMEM)
    work = heads * patches * patches
    return pl.pallas_call(
        softmax_kernel,
        out_shape=jax.ShapeDtypeStruct((rows.total, rows.lanes), jnp.bfloat16),
        in_specs=[smem, smem] + in_vmem(3),
        out_specs=in_hbm(1)[0],
        scratch_shapes=[
            pltpu.VMEM((rows.total, rows.lanes), jnp.bfloat16),
            pltpu.SemaphoreType.DMA((3 + 2 * heads,)),
        ],
        compiler_params=params(52),
        cost_estimate=pl.CostEstimate(
            flops=100_000 * work, bytes_accessed=500 * work, transcendentals=9 * work
        ),
        name="softmax_parts",
    )(lengths.reshape(1, -1), first.reshape(1, 1), own, before, after)


def gather_kernel(pieces_ref, _, out_ref):
    count, row_count, width = pieces_ref.shape
    total = pieces_ref[0].astype(jnp.float32)
    for p in range(1, count):
        total = total + pieces_ref[p].astype(jnp.float32)
    total = total.astype(jnp.bfloat16)
    columns = width // 4
    patch = iota((row_count, 4 * row_count), 1)
    token = iota((row_count, 4 * row_count), 0)
    result = jnp.zeros((columns, 4 * row_count), jnp.float32)
    for j in range(4):
        put = jnp.where(patch == 4 * token + j, 1.0, 0.0).astype(jnp.bfloat16)
        result = result + dot(total[:, j * columns : (j + 1) * columns], put, TN)
    out_ref[...] = result.astype(jnp.bfloat16)


def gathered(pieces, later):
    _, row_count, width = pieces.shape
    return pl.pallas_call(
        gather_kernel,
        out_shape=jax.ShapeDtypeStruct((width // 4, 4 * row_count), jnp.bfloat16),
        in_specs=in_vmem(1) + in_hbm(1),
        out_specs=pl.BlockSpec(memory_space=VMEM),
        compiler_params=params(52),
        name="gather_sum",
    )(pieces, later)


def own_kernel(grad_ref, own_ref, held_hbm, query_ref, key_ref, value_ref, values_ref, keys_ref,
               probs_ref, sems):
    columns, patches = grad_ref.shape
    heads = columns // HEAD_DIM
    rows = Rows(columns, patches)
    pairs = [(held_hbm.at[rows.values], values_ref)]
    pairs += [(held_hbm.at[rows.probs(h)], probs_ref.at[h]) for h in range(heads)]
    pairs += [(held_hbm.at[rows.keys], keys_ref)]
    copies = fetched(pairs, sems)
    copies[0].wait()
    for h in range(heads):
        cols = slice(h * HEAD_DIM, (h + 1) * HEAD_DIM)
        grad = grad_ref[cols]
        slope = dot(grad, values_ref[cols, : 3 * patches], TN)
        copies[1 + h].wait()
        probs = probs_ref[h, :, : 3 * patches]
        wide = probs.astype(jnp.float32)
        delta = jnp.sum(wide * slope, 1, keepdims=True)
        scores = (wide * (slope - delta)).astype(jnp.bfloat16)
        if h == 0:
            copies[1 + heads].wait()
        query = dot(scores, keys_ref[cols, : 3 * patches], NT) * SCALE
        query_ref[cols] = query.T.astype(jnp.bfloat16)
        key_ref[cols] = dot(own_ref[cols], scores[:, :patches], NN)
        value_ref[cols] = dot(grad, probs[:, :patches], NN)


def own_terms(grad, own, held):
    columns, patches = grad.shape
    heads = columns // HEAD_DIM
    lanes = held.shape[1]
    return pl.pallas_call(
        own_kernel,
        out_shape=(
            jax.ShapeDtypeStruct(grad.shape, jnp.bfloat16),
            jax.ShapeDtypeStruct(grad.shape, jnp.float32),
            jax.ShapeDtypeStruct(grad.shape, jnp.float32),
        ),
        in_specs=in_vmem(2) + in_hbm(1),
        out_specs=tuple(in_vmem(3)),
        scratch_shapes=[
            pltpu.VMEM((columns, lanes), jnp.bfloat16),
            pltpu.VMEM((columns, lanes), jnp.bfloat16),
            pltpu.VMEM((heads, patches, lanes), jnp.bfloat16),
            pltpu.SemaphoreType.DMA((2 + heads,)),
        ],
        compiler_params=params(52),
        name="own_terms",
    )(grad, own, held)


def side_kernel(left_ref, right_ref, key_part_ref, value_part_ref, held_hbm, key_ref, value_ref,
                values_ref, attended_ref, probs_ref, queries_ref, sems):
    columns, patches = left_ref.shape
    heads = columns // HEAD_DIM
    rows = Rows(columns, patches)
    lanes = pl.ds(0, rows.side_lanes)
    pairs = [(held_hbm.at[rows.values, lanes], values_ref)]
    pairs += [(held_hbm.at[rows.attended, lanes], attended_ref)]
    pairs += [(held_hbm.at[rows.side_probs(h), lanes], probs_ref.at[h]) for h in range(heads)]
    pairs += [(held_hbm.at[rows.queries, lanes], queries_ref)]
    copies = fetched(pairs, sems)
    wide = jnp.concatenate([x[...].astype(jnp.float32) for x in (left_ref, right_ref)], 1)
    grads = wide.astype(jnp.bfloat16)
    copies[0].wait()
    for h in range(heads):
        cols = slice(h * HEAD_DIM, (h + 1) * HEAD_DIM)
        grad = grads[cols]
        slope = dot(values_ref[cols, :patches], grad, TN)
        if h == 0:
            copies[1].wait()
        attended = attended_ref[cols, : 2 * patches].astype(jnp.float32)
        delta = jnp.sum(wide[cols] * attended, 0, keepdims=True)
        copies[2 + h].wait()
        probs = probs_ref[h, :, : 2 * patches]
        value = dot(probs, grad, NT)
        scores = (probs.astype(jnp.float32) * (slope - delta)).astype(jnp.bfloat16)
        if h == 0:
            copies[2 + heads].wait()
        key = dot(scores, queries_ref[cols, : 2 * patches], NT)
        key_ref[cols] = ((key_part_ref[cols] + key.T) * SCALE).astype(jnp.bfloat16)
        value_ref[cols] = (value_part_ref[cols] + value.T).astype(jnp.bfloat16)


def side_terms(left, right, key_part, value_part, held):
    shape = jax.ShapeDtypeStruct(left.shape, jnp.bfloat16)
    columns, patches = left.shape
    heads = columns // HEAD_DIM
    lanes = Rows(columns, patches).side_lanes
    return pl.pallas_call(
        side_kernel,
        out_shape=(shape, shape),
        in_specs=in_vmem(4) + in_hbm(1),
        out_specs=tuple(in_vmem(2)),
        scratch_shapes=[
            pltpu.VMEM((columns, lanes), jnp.bfloat16),
            pltpu.VMEM((columns, lanes), jnp.bfloat16),
            pltpu.VMEM((heads, patches, lanes), jnp.bfloat16),
            pltpu.VMEM((columns, lanes), jnp.bfloat16),
            pltpu.SemaphoreType.DMA((3 + heads,)),
        ],
        compiler_params=params(52),
        name="side_terms",
    )(left, right, key_part, value_part, held)


def from_both_sides(x, axis):
    size = lax.axis_size(axis)
    up = [(i, i + 1) for i in range(size - 1)]
    return (
        lax.ppermute(x, axis, up),
        lax.ppermute(x, axis, [(j, i) for i, j in up]),
    )


def on_device(
    grad_out, destination, w_down, pre_act, w_up, queries, key_states, value_states, lengths
):
    groups = lax.axis_size("grp")
    spans = lax.axis_size("span")
    heads = lax.axis_size(("sect", "span"))
    row_count = grad_out.shape[0]
    capacity, _ = padded_slots(row_count, groups)
    pieces = down_pieces(destination, grad_out, w_down, groups, spans)
    pieces, queries, key_states, value_states = lax.optimization_barrier(
        (pieces, queries, key_states, value_states)
    )
    arrived = lax.all_to_all(pieces, ("grp", "span"), split_axis=0, concat_axis=0, tiled=True)
    own = jnp.concatenate([queries.T, key_states.T, value_states.T], 0)
    before, after = from_both_sides(own, "grp")
    first = lax.axis_index("grp") * row_count
    held = softmax_parts(lengths, first, own, before, after)
    shares = up_pieces(arrived, pre_act, w_up, heads, capacity)
    shares = lax.all_to_all(shares, ("sect", "span"), split_axis=0, concat_axis=0, tiled=True)
    grad = gathered(shares, held)
    left, right = from_both_sides(grad, "grp")
    grad_query, key_part, value_part = own_terms(grad, queries.T, held)
    grad_key, grad_value = side_terms(left, right, key_part, value_part, held)
    return grad_query.T, grad_key.T, grad_value.T


def solution(mesh):
    split = P("grp", ("sect", "span"))
    placed = (
        P("grp", "span"),
        P("grp"),
        P("sect", "span"),
        split,
        P(None, ("sect", "span")),
        split,
        split,
        split,
        P(),
    )
    return jax.shard_map(
        on_device,
        mesh=mesh,
        in_specs=placed,
        out_specs=(split, split, split),
        check_vma=False,
    )
```

```python
import functools

import jax
import jax.numpy as jnp
from jax import lax
from jax.experimental import pallas as pl
from jax.experimental.pallas import tpu as pltpu
from jax.sharding import PartitionSpec as P

HEAD_DIM = 80
SCALE = HEAD_DIM**-0.5
MIB = 1024 * 1024
VMEM = pltpu.MemorySpace.VMEM
NT = (((1,), (1,)), ((), ()))
NN = (((1,), (0,)), ((), ()))
TN = (((0,), (0,)), ((), ()))


def dot(a, b, dims):
    return lax.dot_general(a, b, dims, preferred_element_type=jnp.float32)


def iota(shape, dim):
    return lax.broadcasted_iota(jnp.int32, shape, dim)


def params(mib):
    return pltpu.CompilerParams(vmem_limit_bytes=mib * MIB)


def in_vmem(count):
    return [pl.BlockSpec(memory_space=VMEM) for _ in range(count)]


def in_hbm(count):
    return [pl.BlockSpec(memory_space=pltpu.MemorySpace.HBM) for _ in range(count)]


def fetched(pairs, sems):
    copies = [pltpu.make_async_copy(a, b, sems.at[i]) for i, (a, b) in enumerate(pairs)]
    for copy in copies:
        copy.start()
    return copies


def padded_slots(row_count, groups):
    offsets = min(groups, row_count // 2)
    capacity = row_count // offsets
    return capacity, -(-(capacity + 1) // 8) * 8


def one_product(count, slots, hidden):
    return count * slots <= hidden


def down_kernel(groups, spans, capacity, slots, steps, dest_hbm, rows_hbm, weight_ref, out_ref,
                dest_ref, rows_ref, held, sems):
    row_count = rows_ref.shape[0]
    hidden = weight_ref.shape[0] // spans
    pairs = [(dest_hbm, dest_ref), (rows_hbm, rows_ref)]
    at = 0
    for step in steps:
        pairs.append((weight_ref.at[pl.ds(at, step)], held.at[pl.ds(at, step)]))
        at += step
    copies = fetched(pairs, sems)
    copies[0].wait()
    across = jnp.broadcast_to(dest_ref[...].astype(jnp.float32), (row_count, row_count))
    down = across.T
    group_across = jnp.floor((across + 0.5) * (1.0 / row_count))
    group_down = jnp.floor((down + 0.5) * (1.0 / row_count))
    slot_down = down - group_down * row_count
    same = group_across == group_down
    earlier = iota((row_count, row_count), 0) < iota((row_count, row_count), 1)
    later = iota((row_count, row_count), 1) < iota((row_count, row_count), 0)
    rank_across = jnp.sum(jnp.where(same & earlier, 1.0, 0.0), 0, keepdims=True)
    rank_down = jnp.sum(jnp.where(same & later, 1.0, 0.0), 1, keepdims=True)
    row_of = group_across[:1] * slots + rank_across
    places = iota((groups * slots, row_count), 0).astype(jnp.float32)
    pick = jnp.where(places == row_of, 1.0, 0.0).astype(jnp.bfloat16)
    lane = iota((row_count, hidden), 1).astype(jnp.float32)
    shift = 0.0
    if one_product(groups * spans, slots, hidden):
        device = lax.axis_index("grp") * spans + lax.axis_index("span")
        shift = (device * slots).astype(jnp.float32)
    at_rank = lane == rank_down + shift
    label_row = iota((slots, hidden), 0) == capacity
    labels = []
    for g in range(groups):
        hit = at_rank & (group_down[:, :1] == g)
        labels.append(jnp.sum(jnp.where(hit, slot_down[:, :1] + 1.0, 0.0), 0, keepdims=True) - 1.0)
    copies[1].wait()
    at, n = 0, 0
    for s in range(spans):
        total = []
        while at < (s + 1) * hidden:
            copies[2 + n].wait()
            product = dot(held[at : at + steps[n]], rows_ref[...], NT)
            total.append(product.astype(jnp.bfloat16))
            at, n = at + steps[n], n + 1
        moved = dot(pick, jnp.concatenate(total, 0), NT)
        for g in range(groups):
            piece = jnp.where(label_row, labels[g], moved[g * slots : (g + 1) * slots])
            out_ref[g * spans + s] = piece.astype(jnp.bfloat16)


def down_pieces(dest, rows, weight, groups, spans):
    row_count = rows.shape[0]
    capacity, slots = padded_slots(row_count, groups)
    hidden = weight.shape[0] // spans
    steps = [128, hidden - 128]
    if hidden > 512:
        steps = [128, 256, hidden - 384]
    steps += [hidden // 2, hidden - hidden // 2] * (spans - 1)
    return pl.pallas_call(
        functools.partial(down_kernel, groups, spans, capacity, slots, steps),
        out_shape=jax.ShapeDtypeStruct((groups * spans, slots, hidden), jnp.bfloat16),
        in_specs=in_hbm(3),
        out_specs=pl.BlockSpec(memory_space=VMEM),
        scratch_shapes=[
            pltpu.VMEM((1, row_count), jnp.int32),
            pltpu.VMEM(rows.shape, jnp.bfloat16),
            pltpu.VMEM(weight.shape, jnp.bfloat16),
            pltpu.SemaphoreType.DMA((2 + len(steps),)),
        ],
        compiler_params=params(60),
        name="down_product",
    )(dest.reshape(1, row_count), rows, weight)


def up_kernel(heads, capacity, pieces_ref, pre_ref, weight_ref, out_ref, held, sems):
    row_count, hidden = pre_ref.shape
    count, slots, _ = pieces_ref.shape
    width = weight_ref.shape[0] // (4 * heads)
    copies = []
    for h in range(heads):
        for j in range(4):
            copy = pltpu.make_async_copy(
                weight_ref.at[pl.ds((j * heads + h) * width, width)],
                held.at[h, pl.ds(j * width, width)],
                sems.at[h * 4 + j],
            )
            copy.start()
            copies.append(copy)
    label_at = slice(capacity, capacity + 1)
    if one_product(count, slots, hidden):
        pieces = [pieces_ref[p].astype(jnp.float32) for p in range(count)]
        labels = functools.reduce(jnp.maximum, [x[label_at, : count * slots] for x in pieces])
        row = iota((row_count, count * slots), 0).astype(jnp.float32)
        put = jnp.where(row == labels, 1.0, 0.0).astype(jnp.bfloat16)
        total = dot(put, jnp.concatenate(pieces, 0).astype(jnp.bfloat16), NN)
    else:
        row = iota((row_count, slots), 0).astype(jnp.float32)

        def placed(p, total):
            piece = pieces_ref[p]
            labels = piece.astype(jnp.float32)[label_at, :slots]
            put = jnp.where(row == labels, 1.0, 0.0).astype(jnp.bfloat16)
            return total + dot(put, piece, NN)

        total = lax.fori_loop(0, count, placed, jnp.zeros((row_count, hidden), jnp.float32))
    pre = pre_ref[...].astype(jnp.float32)
    cdf = 0.5 * (1.0 + lax.erf(pre * 0.7071067811865476))
    slope = cdf + pre * jnp.exp(-0.5 * pre * pre) * 0.3989422804014327
    grad_pre = (total * slope).astype(jnp.bfloat16)
    for h in range(heads):
        for j in range(4):
            copies[h * 4 + j].wait()
        out_ref[h] = dot(held[h], grad_pre, NT).T.astype(jnp.bfloat16)


def up_pieces(pieces, pre, weight, heads, capacity):
    width = weight.shape[0] // heads
    return pl.pallas_call(
        functools.partial(up_kernel, heads, capacity),
        out_shape=jax.ShapeDtypeStruct((heads, pre.shape[0], width), jnp.bfloat16),
        in_specs=in_vmem(2) + in_hbm(1),
        out_specs=pl.BlockSpec(memory_space=VMEM),
        scratch_shapes=[
            pltpu.VMEM((heads, width, weight.shape[1]), jnp.bfloat16),
            pltpu.SemaphoreType.DMA((heads * 4,)),
        ],
        compiler_params=params(52),
        cost_estimate=pl.CostEstimate(
            flops=8 * pre.shape[0] * weight.size, bytes_accessed=8 * weight.size, transcendentals=0
        ),
        name="up_product",
    )(pieces, pre, weight)


class Rows:
    def __init__(self, columns, patches):
        heads = columns // HEAD_DIM
        self.lanes = -(-3 * patches // 128) * 128
        self.side_lanes = -(-2 * patches // 128) * 128
        self.columns, self.patches = columns, patches
        self.values, self.keys, self.queries, self.attended = [i * columns for i in range(4)]
        self.probs_at = 4 * columns
        self.side_at = self.probs_at + heads * patches
        self.total = self.side_at + heads * patches

    def head(self, start, h):
        return slice(start + h * HEAD_DIM, start + (h + 1) * HEAD_DIM)

    def kind(self, start, count=1):
        return slice(start, start + count * self.columns)

    def probs(self, h):
        return slice(self.probs_at + h * self.patches, self.probs_at + (h + 1) * self.patches)

    def side_probs(self, h):
        return slice(self.side_at + h * self.patches, self.side_at + (h + 1) * self.patches)


def softmax_kernel(lengths_ref, first_ref, own_ref, before_ref, after_ref, out_hbm, done_ref, held,
                   sems):
    columns, patches = own_ref.shape[0] // 3, own_ref.shape[1]
    heads = columns // HEAD_DIM
    rows = Rows(columns, patches)
    blocks = (own_ref, before_ref, after_ref)
    first = first_ref[0, 0]

    def image_of(shape, dim, block):
        token = iota(shape, dim) // 4 + (first + block * (patches // 4))

        def step(i, state):
            image, bound = state
            bound = bound + lengths_ref[0, i]
            return image + jnp.where(token >= bound, 1, 0), bound

        start = (jnp.where(token < 0, -1, 0), jnp.int32(0))
        return lax.fori_loop(0, lengths_ref.shape[1], step, start)[0]

    down = [image_of((patches, 1), 0, b) for b in (0, -1, 1)]
    across = [image_of((1, patches), 1, b) for b in (0, -1, 1)]
    all_keys = jnp.concatenate(across, 1)
    same_own = down[0] == all_keys
    copies = []

    def send(part, lanes):
        at = (pl.ds(part.start, part.stop - part.start), pl.ds(0, lanes))
        copy = pltpu.make_async_copy(held.at[at], out_hbm.at[at], sems.at[len(copies)])
        copy.start()
        copies.append(copy)

    def kind(block, t, h=None):
        start = t * columns + (0 if h is None else h * HEAD_DIM)
        return blocks[block][start : start + (columns if h is None else HEAD_DIM)]

    def wide(t, which):
        return jnp.concatenate([kind(b, t).astype(jnp.float32) for b in which], 1).astype(jnp.bfloat16)

    held[rows.kind(rows.values), : 3 * patches] = wide(2, (0, 1, 2))
    held[rows.kind(rows.keys), : 3 * patches] = wide(1, (0, 1, 2))
    held[rows.kind(rows.queries), : 2 * patches] = wide(0, (1, 2))
    send(rows.kind(rows.values, 2), rows.lanes)
    send(rows.kind(rows.queries), rows.side_lanes)
    for h in range(heads):
        keys = held[rows.head(rows.keys, h), : 3 * patches]
        scores = dot(kind(0, 0, h), keys, TN) * SCALE
        scores = jnp.where(same_own, scores, -jnp.inf)
        weights = jnp.exp(scores - jnp.max(scores, 1, keepdims=True))
        over = 1.0 / jnp.sum(weights, 1, keepdims=True)
        held[rows.probs(h), : 3 * patches] = (weights * over).astype(jnp.bfloat16)
        send(rows.probs(h), rows.lanes)
    for h in range(heads):
        own_keys = kind(0, 1, h).astype(jnp.float32).T.astype(jnp.bfloat16)
        side, attended = [], []
        for b in (1, 2):
            queries = kind(b, 0, h)
            keys = kind(b, 1, h).astype(jnp.float32).T.astype(jnp.bfloat16)
            scores = []
            for n, k in ((0, own_keys), (b, keys)):
                scores.append(jnp.where(down[n] == across[b], dot(k, queries, NN) * SCALE, -jnp.inf))
            top = functools.reduce(jnp.maximum, [jnp.max(x, 0, keepdims=True) for x in scores])
            weights = [jnp.exp(x - top) for x in scores]
            over = 1.0 / sum([jnp.sum(w, 0, keepdims=True) for w in weights])
            probs = [(w * over).astype(jnp.bfloat16) for w in weights]
            attended.append(dot(kind(0, 2, h), probs[0], NN) + dot(kind(b, 2, h), probs[1], NN))
            side.append(probs[0].astype(jnp.float32))
        held[rows.side_probs(h), : 2 * patches] = jnp.concatenate(side, 1).astype(jnp.bfloat16)
        send(rows.side_probs(h), rows.side_lanes)
        attended = jnp.concatenate(attended, 1).astype(jnp.bfloat16)
        held[rows.head(rows.attended, h), : 2 * patches] = attended
    send(rows.kind(rows.attended), rows.side_lanes)
    for copy in copies:
        copy.wait()
    done_ref[...] = jnp.zeros(done_ref.shape, jnp.float32)


def softmax_parts(lengths, first, own, before, after):
    columns, patches = own.shape[0] // 3, own.shape[1]
    heads = columns // HEAD_DIM
    rows = Rows(columns, patches)
    smem = pl.BlockSpec(memory_space=pltpu.MemorySpace.SMEM)
    work = heads * patches * patches
    return pl.pallas_call(
        softmax_kernel,
        out_shape=(
            jax.ShapeDtypeStruct((rows.total, rows.lanes), jnp.bfloat16),
            jax.ShapeDtypeStruct((8, 128), jnp.float32),
        ),
        in_specs=[smem, smem] + in_vmem(3),
        out_specs=tuple(in_hbm(1) + in_vmem(1)),
        scratch_shapes=[
            pltpu.VMEM((rows.total, rows.lanes), jnp.bfloat16),
            pltpu.SemaphoreType.DMA((3 + 2 * heads,)),
        ],
        compiler_params=params(52),
        cost_estimate=pl.CostEstimate(
            flops=100_000 * work, bytes_accessed=500 * work, transcendentals=9 * work
        ),
        name="softmax_parts",
    )(lengths.reshape(1, -1), first.reshape(1, 1), own, before, after)


def gather_kernel(pieces_ref, _, out_ref):
    count, row_count, width = pieces_ref.shape
    total = pieces_ref[0].astype(jnp.float32)
    for p in range(1, count):
        total = total + pieces_ref[p].astype(jnp.float32)
    total = total.astype(jnp.bfloat16)
    columns = width // 4
    patch = iota((row_count, 4 * row_count), 1)
    token = iota((row_count, 4 * row_count), 0)
    result = jnp.zeros((columns, 4 * row_count), jnp.float32)
    for j in range(4):
        put = jnp.where(patch == 4 * token + j, 1.0, 0.0).astype(jnp.bfloat16)
        result = result + dot(total[:, j * columns : (j + 1) * columns], put, TN)
    out_ref[...] = result.astype(jnp.bfloat16)


def gathered(pieces, later):
    _, row_count, width = pieces.shape
    return pl.pallas_call(
        gather_kernel,
        out_shape=jax.ShapeDtypeStruct((width // 4, 4 * row_count), jnp.bfloat16),
        in_specs=in_vmem(2),
        out_specs=pl.BlockSpec(memory_space=VMEM),
        compiler_params=params(16),
        cost_estimate=pl.CostEstimate(
            flops=20_000 * pieces.size, bytes_accessed=400 * pieces.size, transcendentals=0
        ),
        name="gather_sum",
    )(pieces, later)


def own_kernel(grad_ref, own_ref, held_ref, query_ref, key_ref, value_ref):
    columns, patches = grad_ref.shape
    rows = Rows(columns, patches)
    for h in range(columns // HEAD_DIM):
        cols = slice(h * HEAD_DIM, (h + 1) * HEAD_DIM)
        grad = grad_ref[cols]
        slope = dot(grad, held_ref[rows.head(rows.values, h), : 3 * patches], TN)
        probs = held_ref[rows.probs(h), : 3 * patches]
        wide = probs.astype(jnp.float32)
        delta = jnp.sum(wide * slope, 1, keepdims=True)
        scores = (wide * (slope - delta)).astype(jnp.bfloat16)
        query = dot(scores, held_ref[rows.head(rows.keys, h), : 3 * patches], NT) * SCALE
        query_ref[cols] = query.T.astype(jnp.bfloat16)
        key_ref[cols] = dot(own_ref[cols], scores[:, :patches], NN)
        value_ref[cols] = dot(grad, probs[:, :patches], NN)


def own_terms(grad, own, held):
    return pl.pallas_call(
        own_kernel,
        out_shape=(
            jax.ShapeDtypeStruct(grad.shape, jnp.bfloat16),
            jax.ShapeDtypeStruct(grad.shape, jnp.float32),
            jax.ShapeDtypeStruct(grad.shape, jnp.float32),
        ),
        in_specs=in_vmem(3),
        out_specs=tuple(in_vmem(3)),
        compiler_params=params(24),
        name="own_terms",
    )(grad, own, held)


def side_kernel(left_ref, right_ref, key_part_ref, value_part_ref, held_ref, key_ref, value_ref):
    columns, patches = left_ref.shape
    rows = Rows(columns, patches)
    lanes = slice(0, 2 * patches)
    for h in range(columns // HEAD_DIM):
        cols = slice(h * HEAD_DIM, (h + 1) * HEAD_DIM)
        wide = jnp.concatenate([x[cols].astype(jnp.float32) for x in (left_ref, right_ref)], 1)
        grad = wide.astype(jnp.bfloat16)
        slope = dot(held_ref[rows.head(rows.values, h), :patches], grad, TN)
        attended = held_ref[rows.head(rows.attended, h), lanes].astype(jnp.float32)
        delta = jnp.sum(wide * attended, 0, keepdims=True)
        probs = held_ref[rows.side_probs(h), lanes]
        value = dot(probs, grad, NT)
        scores = (probs.astype(jnp.float32) * (slope - delta)).astype(jnp.bfloat16)
        key = dot(scores, held_ref[rows.head(rows.queries, h), lanes], NT)
        key_ref[cols] = ((key_part_ref[cols] + key.T) * SCALE).astype(jnp.bfloat16)
        value_ref[cols] = (value_part_ref[cols] + value.T).astype(jnp.bfloat16)


def side_terms(left, right, key_part, value_part, held):
    shape = jax.ShapeDtypeStruct(left.shape, jnp.bfloat16)
    return pl.pallas_call(
        side_kernel,
        out_shape=(shape, shape),
        in_specs=in_vmem(5),
        out_specs=tuple(in_vmem(2)),
        compiler_params=params(24),
        name="side_terms",
    )(left, right, key_part, value_part, held)


def from_both_sides(x, axis):
    size = lax.axis_size(axis)
    up = [(i, i + 1) for i in range(size - 1)]
    return (
        lax.ppermute(x, axis, up),
        lax.ppermute(x, axis, [(j, i) for i, j in up]),
    )


def on_device(
    grad_out, destination, w_down, pre_act, w_up, queries, key_states, value_states, lengths
):
    groups = lax.axis_size("grp")
    spans = lax.axis_size("span")
    heads = lax.axis_size(("sect", "span"))
    row_count = grad_out.shape[0]
    capacity, _ = padded_slots(row_count, groups)
    pieces = down_pieces(destination, grad_out, w_down, groups, spans)
    pieces, queries, key_states, value_states = lax.optimization_barrier(
        (pieces, queries, key_states, value_states)
    )
    arrived = lax.all_to_all(pieces, ("grp", "span"), split_axis=0, concat_axis=0, tiled=True)
    own = jnp.concatenate([queries.T, key_states.T, value_states.T], 0)
    before, after = from_both_sides(own, "grp")
    first = lax.axis_index("grp") * row_count
    held, held_done = softmax_parts(lengths, first, own, before, after)
    shares = up_pieces(arrived, pre_act, w_up, heads, capacity)
    shares = lax.all_to_all(shares, ("sect", "span"), split_axis=0, concat_axis=0, tiled=True)
    grad = gathered(shares, held_done)
    left, right = from_both_sides(grad, "grp")
    grad_query, key_part, value_part = own_terms(grad, queries.T, held)
    grad_key, grad_value = side_terms(left, right, key_part, value_part, held)
    return grad_query.T, grad_key.T, grad_value.T


def solution(mesh):
    split = P("grp", ("sect", "span"))
    placed = (
        P("grp", "span"),
        P("grp"),
        P("sect", "span"),
        split,
        P(None, ("sect", "span")),
        split,
        split,
        split,
        P(),
    )
    return jax.shard_map(
        on_device,
        mesh=mesh,
        in_specs=placed,
        out_specs=(split, split, split),
        check_vma=False,
    )
```

```python
import functools

import jax
import jax.numpy as jnp
from jax import lax
from jax.experimental import pallas as pl
from jax.experimental.pallas import tpu as pltpu
from jax.sharding import PartitionSpec as P

HEAD_DIM = 80
SCALE = HEAD_DIM**-0.5
MIB = 1024 * 1024
VMEM = pltpu.MemorySpace.VMEM
NT = (((1,), (1,)), ((), ()))
NN = (((1,), (0,)), ((), ()))
TN = (((0,), (0,)), ((), ()))


def dot(a, b, dims):
    return lax.dot_general(a, b, dims, preferred_element_type=jnp.float32)


def iota(shape, dim):
    return lax.broadcasted_iota(jnp.int32, shape, dim)


def params(mib):
    return pltpu.CompilerParams(vmem_limit_bytes=mib * MIB)


def in_vmem(count):
    return [pl.BlockSpec(memory_space=VMEM) for _ in range(count)]


def in_hbm(count):
    return [pl.BlockSpec(memory_space=pltpu.MemorySpace.HBM) for _ in range(count)]


def fetched(pairs, sems):
    copies = [pltpu.make_async_copy(a, b, sems.at[i]) for i, (a, b) in enumerate(pairs)]
    for copy in copies:
        copy.start()
    return copies


def padded_slots(row_count, groups):
    offsets = min(groups, row_count // 2)
    capacity = row_count // offsets
    return capacity, -(-(capacity + 1) // 8) * 8


def one_product(count, slots, hidden):
    return count * slots <= hidden


def down_kernel(groups, spans, capacity, slots, steps, dest_hbm, rows_hbm, weight_ref, out_ref,
                dest_ref, rows_ref, turned, held, sems):
    row_count = rows_ref.shape[0]
    hidden = weight_ref.shape[0] // spans
    pairs = [(dest_hbm, dest_ref), (rows_hbm, rows_ref)]
    at = 0
    for step in steps:
        pairs.append((weight_ref.at[pl.ds(at, step)], held.at[pl.ds(at, step)]))
        at += step
    copies = fetched(pairs, sems)
    copies[0].wait()
    across = jnp.broadcast_to(dest_ref[...].astype(jnp.float32), (row_count, row_count))
    down = across.T
    group_across = jnp.floor((across + 0.5) * (1.0 / row_count))
    group_down = jnp.floor((down + 0.5) * (1.0 / row_count))
    slot_down = down - group_down * row_count
    same = group_across == group_down
    earlier = iota((row_count, row_count), 0) < iota((row_count, row_count), 1)
    later = iota((row_count, row_count), 1) < iota((row_count, row_count), 0)
    rank_across = jnp.sum(jnp.where(same & earlier, 1.0, 0.0), 0, keepdims=True)
    rank_down = jnp.sum(jnp.where(same & later, 1.0, 0.0), 1, keepdims=True)
    row_of = group_across[:1] * slots + rank_across
    places = iota((groups * slots, row_count), 0).astype(jnp.float32)
    pick = jnp.where(places == row_of, 1.0, 0.0).astype(jnp.bfloat16)
    lane = iota((row_count, hidden), 1).astype(jnp.float32)
    shift = 0.0
    if one_product(groups * spans, slots, hidden):
        device = lax.axis_index("grp") * spans + lax.axis_index("span")
        shift = (device * slots).astype(jnp.float32)
    at_rank = lane == rank_down + shift
    label_row = iota((slots, hidden), 0) == capacity
    labels = []
    for g in range(groups):
        hit = at_rank & (group_down[:, :1] == g)
        labels.append(jnp.sum(jnp.where(hit, slot_down[:, :1] + 1.0, 0.0), 0, keepdims=True) - 1.0)
    copies[1].wait()
    for c in range(0, rows_ref.shape[1], 512):
        turned[c : c + 512] = rows_ref[:, c : c + 512].astype(jnp.float32).T.astype(jnp.bfloat16)
    at, n = 0, 0
    for s in range(spans):
        total = []
        while at < (s + 1) * hidden:
            copies[2 + n].wait()
            product = dot(held[at : at + steps[n]], turned[...], NN)
            total.append(product.astype(jnp.bfloat16))
            at, n = at + steps[n], n + 1
        moved = dot(pick, jnp.concatenate(total, 0), NT)
        for g in range(groups):
            piece = jnp.where(label_row, labels[g], moved[g * slots : (g + 1) * slots])
            out_ref[g * spans + s] = piece.astype(jnp.bfloat16)


def down_pieces(dest, rows, weight, groups, spans):
    row_count = rows.shape[0]
    capacity, slots = padded_slots(row_count, groups)
    hidden = weight.shape[0] // spans
    steps = [128, hidden - 128]
    if hidden > 512:
        steps = [128, 256, hidden - 384]
    steps += [hidden // 2, hidden - hidden // 2] * (spans - 1)
    return pl.pallas_call(
        functools.partial(down_kernel, groups, spans, capacity, slots, steps),
        out_shape=jax.ShapeDtypeStruct((groups * spans, slots, hidden), jnp.bfloat16),
        in_specs=in_hbm(3),
        out_specs=pl.BlockSpec(memory_space=VMEM),
        scratch_shapes=[
            pltpu.VMEM((1, row_count), jnp.int32),
            pltpu.VMEM(rows.shape, jnp.bfloat16),
            pltpu.VMEM(rows.shape[::-1], jnp.bfloat16),
            pltpu.VMEM(weight.shape, jnp.bfloat16),
            pltpu.SemaphoreType.DMA((2 + len(steps),)),
        ],
        compiler_params=params(60),
        name="down_product",
    )(dest.reshape(1, row_count), rows, weight)


def up_kernel(heads, capacity, pieces_ref, pre_ref, weight_ref, out_ref, held, sems):
    row_count, hidden = pre_ref.shape
    count, slots, _ = pieces_ref.shape
    width = weight_ref.shape[0] // (4 * heads)
    copies = []
    for h in range(heads):
        for j in range(4):
            copy = pltpu.make_async_copy(
                weight_ref.at[pl.ds((j * heads + h) * width, width)],
                held.at[h, pl.ds(j * width, width)],
                sems.at[h * 4 + j],
            )
            copy.start()
            copies.append(copy)
    label_at = slice(capacity, capacity + 1)
    if one_product(count, slots, hidden):
        pieces = [pieces_ref[p].astype(jnp.float32) for p in range(count)]
        labels = functools.reduce(jnp.maximum, [x[label_at, : count * slots] for x in pieces])
        row = iota((row_count, count * slots), 0).astype(jnp.float32)
        put = jnp.where(row == labels, 1.0, 0.0).astype(jnp.bfloat16)
        total = dot(put, jnp.concatenate(pieces, 0).astype(jnp.bfloat16), NN)
    else:
        row = iota((row_count, slots), 0).astype(jnp.float32)

        def placed(p, total):
            piece = pieces_ref[p]
            labels = piece.astype(jnp.float32)[label_at, :slots]
            put = jnp.where(row == labels, 1.0, 0.0).astype(jnp.bfloat16)
            return total + dot(put, piece, NN)

        total = lax.fori_loop(0, count, placed, jnp.zeros((row_count, hidden), jnp.float32))
    pre = pre_ref[...].astype(jnp.float32)
    cdf = 0.5 * (1.0 + lax.erf(pre * 0.7071067811865476))
    slope = cdf + pre * jnp.exp(-0.5 * pre * pre) * 0.3989422804014327
    grad_pre = (total * slope).T.astype(jnp.bfloat16)
    for h in range(heads):
        for j in range(4):
            copies[h * 4 + j].wait()
        out_ref[h] = dot(held[h], grad_pre, NN).T.astype(jnp.bfloat16)


def up_pieces(pieces, pre, weight, heads, capacity):
    width = weight.shape[0] // heads
    return pl.pallas_call(
        functools.partial(up_kernel, heads, capacity),
        out_shape=jax.ShapeDtypeStruct((heads, pre.shape[0], width), jnp.bfloat16),
        in_specs=in_vmem(2) + in_hbm(1),
        out_specs=pl.BlockSpec(memory_space=VMEM),
        scratch_shapes=[
            pltpu.VMEM((heads, width, weight.shape[1]), jnp.bfloat16),
            pltpu.SemaphoreType.DMA((heads * 4,)),
        ],
        compiler_params=params(52),
        cost_estimate=pl.CostEstimate(
            flops=8 * pre.shape[0] * weight.size, bytes_accessed=8 * weight.size, transcendentals=0
        ),
        name="up_product",
    )(pieces, pre, weight)


class Rows:
    def __init__(self, columns, patches):
        heads = columns // HEAD_DIM
        self.lanes = -(-3 * patches // 128) * 128
        self.side_lanes = -(-2 * patches // 128) * 128
        self.columns, self.patches = columns, patches
        self.values, self.keys, self.queries, self.attended = [i * columns for i in range(4)]
        self.probs_at = 4 * columns
        self.side_at = self.probs_at + heads * patches
        self.total = self.side_at + heads * patches

    def head(self, start, h):
        return slice(start + h * HEAD_DIM, start + (h + 1) * HEAD_DIM)

    def kind(self, start, count=1):
        return slice(start, start + count * self.columns)

    def probs(self, h):
        return slice(self.probs_at + h * self.patches, self.probs_at + (h + 1) * self.patches)

    def side_probs(self, h):
        return slice(self.side_at + h * self.patches, self.side_at + (h + 1) * self.patches)


def softmax_kernel(lengths_ref, first_ref, own_ref, before_ref, after_ref, out_hbm, done_ref, held,
                   sems):
    columns, patches = own_ref.shape[0] // 3, own_ref.shape[1]
    heads = columns // HEAD_DIM
    rows = Rows(columns, patches)
    blocks = (own_ref, before_ref, after_ref)
    first = first_ref[0, 0]

    def image_of(shape, dim, block):
        token = iota(shape, dim) // 4 + (first + block * (patches // 4))

        def step(i, state):
            image, bound = state
            bound = bound + lengths_ref[0, i]
            return image + jnp.where(token >= bound, 1, 0), bound

        start = (jnp.where(token < 0, -1, 0), jnp.int32(0))
        return lax.fori_loop(0, lengths_ref.shape[1], step, start)[0]

    down = [image_of((patches, 1), 0, b) for b in (0, -1, 1)]
    across = [image_of((1, patches), 1, b) for b in (0, -1, 1)]
    all_keys = jnp.concatenate(across, 1)
    same_own = down[0] == all_keys
    copies = []

    def send(part, lanes):
        at = (pl.ds(part.start, part.stop - part.start), pl.ds(0, lanes))
        copy = pltpu.make_async_copy(held.at[at], out_hbm.at[at], sems.at[len(copies)])
        copy.start()
        copies.append(copy)

    def kind(block, t, h=None):
        start = t * columns + (0 if h is None else h * HEAD_DIM)
        return blocks[block][start : start + (columns if h is None else HEAD_DIM)]

    def wide(t, which):
        return jnp.concatenate([kind(b, t).astype(jnp.float32) for b in which], 1).astype(jnp.bfloat16)

    held[rows.kind(rows.values), : 3 * patches] = wide(2, (0, 1, 2))
    held[rows.kind(rows.keys), : 3 * patches] = wide(1, (0, 1, 2))
    held[rows.kind(rows.queries), : 2 * patches] = wide(0, (1, 2))
    send(rows.kind(rows.values, 2), rows.lanes)
    send(rows.kind(rows.queries), rows.side_lanes)
    for h in range(heads):
        keys = held[rows.head(rows.keys, h), : 3 * patches]
        scores = dot(kind(0, 0, h), keys, TN) * SCALE
        scores = jnp.where(same_own, scores, -jnp.inf)
        weights = jnp.exp(scores - jnp.max(scores, 1, keepdims=True))
        over = 1.0 / jnp.sum(weights, 1, keepdims=True)
        held[rows.probs(h), : 3 * patches] = (weights * over).astype(jnp.bfloat16)
        send(rows.probs(h), rows.lanes)
    for h in range(heads):
        own_keys = kind(0, 1, h).astype(jnp.float32).T.astype(jnp.bfloat16)
        side, attended = [], []
        for b in (1, 2):
            queries = kind(b, 0, h)
            keys = kind(b, 1, h).astype(jnp.float32).T.astype(jnp.bfloat16)
            scores = []
            for n, k in ((0, own_keys), (b, keys)):
                scores.append(jnp.where(down[n] == across[b], dot(k, queries, NN) * SCALE, -jnp.inf))
            top = functools.reduce(jnp.maximum, [jnp.max(x, 0, keepdims=True) for x in scores])
            weights = [jnp.exp(x - top) for x in scores]
            over = 1.0 / sum([jnp.sum(w, 0, keepdims=True) for w in weights])
            probs = [(w * over).astype(jnp.bfloat16) for w in weights]
            attended.append(dot(kind(0, 2, h), probs[0], NN) + dot(kind(b, 2, h), probs[1], NN))
            side.append(probs[0].astype(jnp.float32))
        held[rows.side_probs(h), : 2 * patches] = jnp.concatenate(side, 1).astype(jnp.bfloat16)
        send(rows.side_probs(h), rows.side_lanes)
        attended = jnp.concatenate(attended, 1).astype(jnp.bfloat16)
        held[rows.head(rows.attended, h), : 2 * patches] = attended
    send(rows.kind(rows.attended), rows.side_lanes)
    for copy in copies:
        copy.wait()
    done_ref[...] = jnp.zeros(done_ref.shape, jnp.float32)


def softmax_parts(lengths, first, own, before, after):
    columns, patches = own.shape[0] // 3, own.shape[1]
    heads = columns // HEAD_DIM
    rows = Rows(columns, patches)
    smem = pl.BlockSpec(memory_space=pltpu.MemorySpace.SMEM)
    work = heads * patches * patches
    return pl.pallas_call(
        softmax_kernel,
        out_shape=(
            jax.ShapeDtypeStruct((rows.total, rows.lanes), jnp.bfloat16),
            jax.ShapeDtypeStruct((8, 128), jnp.float32),
        ),
        in_specs=[smem, smem] + in_vmem(3),
        out_specs=tuple(in_hbm(1) + in_vmem(1)),
        scratch_shapes=[
            pltpu.VMEM((rows.total, rows.lanes), jnp.bfloat16),
            pltpu.SemaphoreType.DMA((3 + 2 * heads,)),
        ],
        compiler_params=params(52),
        cost_estimate=pl.CostEstimate(
            flops=100_000 * work, bytes_accessed=500 * work, transcendentals=9 * work
        ),
        name="softmax_parts",
    )(lengths.reshape(1, -1), first.reshape(1, 1), own, before, after)


def gather_kernel(pieces_ref, _, out_ref):
    count, row_count, width = pieces_ref.shape
    total = pieces_ref[0].astype(jnp.float32)
    for p in range(1, count):
        total = total + pieces_ref[p].astype(jnp.float32)
    total = total.astype(jnp.bfloat16)
    columns = width // 4
    patch = iota((row_count, 4 * row_count), 1)
    token = iota((row_count, 4 * row_count), 0)
    result = jnp.zeros((columns, 4 * row_count), jnp.float32)
    for j in range(4):
        put = jnp.where(patch == 4 * token + j, 1.0, 0.0).astype(jnp.bfloat16)
        result = result + dot(total[:, j * columns : (j + 1) * columns], put, TN)
    out_ref[...] = result.astype(jnp.bfloat16)


def gathered(pieces, later):
    _, row_count, width = pieces.shape
    return pl.pallas_call(
        gather_kernel,
        out_shape=jax.ShapeDtypeStruct((width // 4, 4 * row_count), jnp.bfloat16),
        in_specs=in_vmem(2),
        out_specs=pl.BlockSpec(memory_space=VMEM),
        compiler_params=params(16),
        cost_estimate=pl.CostEstimate(
            flops=20_000 * pieces.size, bytes_accessed=400 * pieces.size, transcendentals=0
        ),
        name="gather_sum",
    )(pieces, later)


def own_kernel(grad_ref, own_ref, held_ref, query_ref, key_ref, value_ref):
    columns, patches = grad_ref.shape
    rows = Rows(columns, patches)
    for h in range(columns // HEAD_DIM):
        cols = slice(h * HEAD_DIM, (h + 1) * HEAD_DIM)
        grad = grad_ref[cols]
        slope = dot(grad, held_ref[rows.head(rows.values, h), : 3 * patches], TN)
        probs = held_ref[rows.probs(h), : 3 * patches]
        wide = probs.astype(jnp.float32)
        delta = jnp.sum(wide * slope, 1, keepdims=True)
        scores = (wide * (slope - delta)).astype(jnp.bfloat16)
        query = dot(scores, held_ref[rows.head(rows.keys, h), : 3 * patches], NT) * SCALE
        query_ref[cols] = query.T.astype(jnp.bfloat16)
        key_ref[cols] = dot(own_ref[cols], scores[:, :patches], NN)
        value_ref[cols] = dot(grad, probs[:, :patches], NN)


def own_terms(grad, own, held):
    return pl.pallas_call(
        own_kernel,
        out_shape=(
            jax.ShapeDtypeStruct(grad.shape, jnp.bfloat16),
            jax.ShapeDtypeStruct(grad.shape, jnp.float32),
            jax.ShapeDtypeStruct(grad.shape, jnp.float32),
        ),
        in_specs=in_vmem(3),
        out_specs=tuple(in_vmem(3)),
        compiler_params=params(24),
        name="own_terms",
    )(grad, own, held)


def side_kernel(left_ref, right_ref, key_part_ref, value_part_ref, held_ref, key_ref, value_ref):
    columns, patches = left_ref.shape
    rows = Rows(columns, patches)
    lanes = slice(0, 2 * patches)
    for h in range(columns // HEAD_DIM):
        cols = slice(h * HEAD_DIM, (h + 1) * HEAD_DIM)
        wide = jnp.concatenate([x[cols].astype(jnp.float32) for x in (left_ref, right_ref)], 1)
        grad = wide.astype(jnp.bfloat16)
        slope = dot(held_ref[rows.head(rows.values, h), :patches], grad, TN)
        attended = held_ref[rows.head(rows.attended, h), lanes].astype(jnp.float32)
        delta = jnp.sum(wide * attended, 0, keepdims=True)
        probs = held_ref[rows.side_probs(h), lanes]
        value = dot(probs, grad, NT)
        scores = (probs.astype(jnp.float32) * (slope - delta)).astype(jnp.bfloat16)
        key = dot(scores, held_ref[rows.head(rows.queries, h), lanes], NT)
        key_ref[cols] = ((key_part_ref[cols] + key.T) * SCALE).astype(jnp.bfloat16)
        value_ref[cols] = (value_part_ref[cols] + value.T).astype(jnp.bfloat16)


def side_terms(left, right, key_part, value_part, held):
    shape = jax.ShapeDtypeStruct(left.shape, jnp.bfloat16)
    return pl.pallas_call(
        side_kernel,
        out_shape=(shape, shape),
        in_specs=in_vmem(5),
        out_specs=tuple(in_vmem(2)),
        compiler_params=params(24),
        name="side_terms",
    )(left, right, key_part, value_part, held)


def from_both_sides(x, axis):
    size = lax.axis_size(axis)
    up = [(i, i + 1) for i in range(size - 1)]
    return (
        lax.ppermute(x, axis, up),
        lax.ppermute(x, axis, [(j, i) for i, j in up]),
    )


def on_device(
    grad_out, destination, w_down, pre_act, w_up, queries, key_states, value_states, lengths
):
    groups = lax.axis_size("grp")
    spans = lax.axis_size("span")
    heads = lax.axis_size(("sect", "span"))
    row_count = grad_out.shape[0]
    capacity, _ = padded_slots(row_count, groups)
    pieces = down_pieces(destination, grad_out, w_down, groups, spans)
    pieces, queries, key_states, value_states = lax.optimization_barrier(
        (pieces, queries, key_states, value_states)
    )
    arrived = lax.all_to_all(pieces, ("grp", "span"), split_axis=0, concat_axis=0, tiled=True)
    own = jnp.concatenate([queries.T, key_states.T, value_states.T], 0)
    before, after = from_both_sides(own, "grp")
    first = lax.axis_index("grp") * row_count
    held, held_done = softmax_parts(lengths, first, own, before, after)
    shares = up_pieces(arrived, pre_act, w_up, heads, capacity)
    shares = lax.all_to_all(shares, ("sect", "span"), split_axis=0, concat_axis=0, tiled=True)
    grad = gathered(shares, held_done)
    left, right = from_both_sides(grad, "grp")
    grad_query, key_part, value_part = own_terms(grad, queries.T, held)
    grad_key, grad_value = side_terms(left, right, key_part, value_part, held)
    return grad_query.T, grad_key.T, grad_value.T


def solution(mesh):
    split = P("grp", ("sect", "span"))
    placed = (
        P("grp", "span"),
        P("grp"),
        P("sect", "span"),
        split,
        P(None, ("sect", "span")),
        split,
        split,
        split,
        P(),
    )
    return jax.shard_map(
        on_device,
        mesh=mesh,
        in_specs=placed,
        out_specs=(split, split, split),
        check_vma=False,
    )
```

```python
import functools

import jax
import jax.numpy as jnp
from jax import lax
from jax.experimental import pallas as pl
from jax.experimental.pallas import tpu as pltpu
from jax.sharding import PartitionSpec as P

HEAD_DIM = 80
SCALE = HEAD_DIM**-0.5
MIB = 1024 * 1024
VMEM = pltpu.MemorySpace.VMEM
NT = (((1,), (1,)), ((), ()))
NN = (((1,), (0,)), ((), ()))
TN = (((0,), (0,)), ((), ()))


def dot(a, b, dims):
    return lax.dot_general(a, b, dims, preferred_element_type=jnp.float32)


def iota(shape, dim):
    return lax.broadcasted_iota(jnp.int32, shape, dim)


def params(mib):
    return pltpu.CompilerParams(vmem_limit_bytes=mib * MIB)


def in_vmem(count):
    return [pl.BlockSpec(memory_space=VMEM) for _ in range(count)]


def in_hbm(count):
    return [pl.BlockSpec(memory_space=pltpu.MemorySpace.HBM) for _ in range(count)]


def fetched(pairs, sems):
    copies = [pltpu.make_async_copy(a, b, sems.at[i]) for i, (a, b) in enumerate(pairs)]
    for copy in copies:
        copy.start()
    return copies


def padded_slots(row_count, groups):
    offsets = min(groups, row_count // 2)
    capacity = row_count // offsets
    return capacity, -(-(capacity + 1) // 8) * 8


def one_product(count, slots, hidden):
    return count * slots <= hidden


def down_kernel(groups, spans, capacity, slots, steps, dest_hbm, rows_hbm, weight_ref, out_ref,
                dest_ref, rows_ref, held, total_ref, sems):
    row_count = rows_ref.shape[0]
    hidden = weight_ref.shape[0] // spans
    everything = pl.ds(0, weight_ref.shape[0])
    pairs = [(dest_hbm, dest_ref), (rows_hbm, rows_ref)]
    for at, step in steps:
        part = (everything, pl.ds(at, step))
        pairs.append((weight_ref.at[part], held.at[part]))
    copies = fetched(pairs, sems)
    copies[0].wait()
    across = jnp.broadcast_to(dest_ref[...].astype(jnp.float32), (row_count, row_count))
    down = across.T
    group_across = jnp.floor((across + 0.5) * (1.0 / row_count))
    group_down = jnp.floor((down + 0.5) * (1.0 / row_count))
    slot_down = down - group_down * row_count
    same = group_across == group_down
    earlier = iota((row_count, row_count), 0) < iota((row_count, row_count), 1)
    later = iota((row_count, row_count), 1) < iota((row_count, row_count), 0)
    rank_across = jnp.sum(jnp.where(same & earlier, 1.0, 0.0), 0, keepdims=True)
    rank_down = jnp.sum(jnp.where(same & later, 1.0, 0.0), 1, keepdims=True)
    row_of = group_across[:1] * slots + rank_across
    places = iota((groups * slots, row_count), 0).astype(jnp.float32)
    pick = jnp.where(places == row_of, 1.0, 0.0).astype(jnp.bfloat16)
    lane = iota((row_count, hidden), 1).astype(jnp.float32)
    shift = 0.0
    if one_product(groups * spans, slots, hidden):
        device = lax.axis_index("grp") * spans + lax.axis_index("span")
        shift = (device * slots).astype(jnp.float32)
    at_rank = lane == rank_down + shift
    label_row = iota((slots, hidden), 0) == capacity
    labels = []
    for g in range(groups):
        hit = at_rank & (group_down[:, :1] == g)
        labels.append(jnp.sum(jnp.where(hit, slot_down[:, :1] + 1.0, 0.0), 0, keepdims=True) - 1.0)
    copies[1].wait()
    for n, (at, step) in enumerate(steps):
        turned = rows_ref[:, at : at + step].astype(jnp.float32).T.astype(jnp.bfloat16)
        copies[2 + n].wait()
        product = dot(held[:, at : at + step], turned, NN)
        total_ref[...] = product if n == 0 else total_ref[...] + product
    for s in range(spans):
        part = total_ref[s * hidden : (s + 1) * hidden].astype(jnp.bfloat16)
        moved = dot(pick, part, NT)
        for g in range(groups):
            piece = jnp.where(label_row, labels[g], moved[g * slots : (g + 1) * slots])
            out_ref[g * spans + s] = piece.astype(jnp.bfloat16)


def down_pieces(dest, rows, weight, groups, spans):
    row_count = rows.shape[0]
    capacity, slots = padded_slots(row_count, groups)
    hidden = weight.shape[0] // spans
    depth = weight.shape[1]
    edges = [0, depth // 8, 3 * depth // 8, 5 * depth // 8, depth]
    steps = [(i, j - i) for i, j in zip(edges, edges[1:])]
    return pl.pallas_call(
        functools.partial(down_kernel, groups, spans, capacity, slots, steps),
        out_shape=jax.ShapeDtypeStruct((groups * spans, slots, hidden), jnp.bfloat16),
        in_specs=in_hbm(3),
        out_specs=pl.BlockSpec(memory_space=VMEM),
        scratch_shapes=[
            pltpu.VMEM((1, row_count), jnp.int32),
            pltpu.VMEM(rows.shape, jnp.bfloat16),
            pltpu.VMEM(weight.shape, jnp.bfloat16),
            pltpu.VMEM((weight.shape[0], row_count), jnp.float32),
            pltpu.SemaphoreType.DMA((2 + len(steps),)),
        ],
        compiler_params=params(60),
        name="down_product",
    )(dest.reshape(1, row_count), rows, weight)


def up_kernel(heads, capacity, pieces_ref, pre_ref, weight_ref, out_ref, held, sems):
    row_count, hidden = pre_ref.shape
    count, slots, _ = pieces_ref.shape
    width = weight_ref.shape[0] // (4 * heads)
    copies = []
    for h in range(heads):
        for j in range(4):
            copy = pltpu.make_async_copy(
                weight_ref.at[pl.ds((j * heads + h) * width, width)],
                held.at[h, pl.ds(j * width, width)],
                sems.at[h * 4 + j],
            )
            copy.start()
            copies.append(copy)
    label_at = slice(capacity, capacity + 1)
    if one_product(count, slots, hidden):
        pieces = [pieces_ref[p].astype(jnp.float32) for p in range(count)]
        labels = functools.reduce(jnp.maximum, [x[label_at, : count * slots] for x in pieces])
        row = iota((row_count, count * slots), 0).astype(jnp.float32)
        put = jnp.where(row == labels, 1.0, 0.0).astype(jnp.bfloat16)
        total = dot(put, jnp.concatenate(pieces, 0).astype(jnp.bfloat16), NN)
    else:
        row = iota((row_count, slots), 0).astype(jnp.float32)

        def placed(p, total):
            piece = pieces_ref[p]
            labels = piece.astype(jnp.float32)[label_at, :slots]
            put = jnp.where(row == labels, 1.0, 0.0).astype(jnp.bfloat16)
            return total + dot(put, piece, NN)

        total = lax.fori_loop(0, count, placed, jnp.zeros((row_count, hidden), jnp.float32))
    pre = pre_ref[...].astype(jnp.float32)
    cdf = 0.5 * (1.0 + lax.erf(pre * 0.7071067811865476))
    slope = cdf + pre * jnp.exp(-0.5 * pre * pre) * 0.3989422804014327
    grad_pre = (total * slope).T.astype(jnp.bfloat16)
    width = 4 * width
    waiting = None
    for h in range(0, heads, 2):
        for copy in copies[h * 4 : h * 4 + 8]:
            copy.wait()
        product = dot(held[h : h + 2].reshape(2 * width, hidden), grad_pre, NN)
        if waiting is not None:
            for i in range(2):
                part = waiting[i * width : (i + 1) * width]
                out_ref[h - 2 + i] = part.T.astype(jnp.bfloat16)
        waiting = product
    for i in range(2):
        out_ref[heads - 2 + i] = waiting[i * width : (i + 1) * width].T.astype(jnp.bfloat16)


def up_pieces(pieces, pre, weight, heads, capacity):
    width = weight.shape[0] // heads
    return pl.pallas_call(
        functools.partial(up_kernel, heads, capacity),
        out_shape=jax.ShapeDtypeStruct((heads, pre.shape[0], width), jnp.bfloat16),
        in_specs=in_vmem(2) + in_hbm(1),
        out_specs=pl.BlockSpec(memory_space=VMEM),
        scratch_shapes=[
            pltpu.VMEM((heads, width, weight.shape[1]), jnp.bfloat16),
            pltpu.SemaphoreType.DMA((heads * 4,)),
        ],
        compiler_params=params(52),
        cost_estimate=pl.CostEstimate(
            flops=8 * pre.shape[0] * weight.size, bytes_accessed=8 * weight.size, transcendentals=0
        ),
        name="up_product",
    )(pieces, pre, weight)


class Rows:
    def __init__(self, columns, patches):
        heads = columns // HEAD_DIM
        self.lanes = -(-3 * patches // 128) * 128
        self.side_lanes = -(-2 * patches // 128) * 128
        self.columns, self.patches = columns, patches
        self.values, self.keys, self.queries, self.attended = [i * columns for i in range(4)]
        self.probs_at = 4 * columns
        self.side_at = self.probs_at + heads * patches
        self.total = self.side_at + heads * patches

    def head(self, start, h):
        return slice(start + h * HEAD_DIM, start + (h + 1) * HEAD_DIM)

    def kind(self, start, count=1):
        return slice(start, start + count * self.columns)

    def probs(self, h):
        return slice(self.probs_at + h * self.patches, self.probs_at + (h + 1) * self.patches)

    def side_probs(self, h):
        return slice(self.side_at + h * self.patches, self.side_at + (h + 1) * self.patches)


def softmax_kernel(lengths_ref, first_ref, own_ref, before_ref, after_ref, out_hbm, done_ref, held,
                   sems):
    columns, patches = own_ref.shape[0] // 3, own_ref.shape[1]
    heads = columns // HEAD_DIM
    rows = Rows(columns, patches)
    blocks = (own_ref, before_ref, after_ref)
    first = first_ref[0, 0]

    def image_of(shape, dim, block):
        token = iota(shape, dim) // 4 + (first + block * (patches // 4))

        def step(i, state):
            image, bound = state
            bound = bound + lengths_ref[0, i]
            return image + jnp.where(token >= bound, 1, 0), bound

        start = (jnp.where(token < 0, -1, 0), jnp.int32(0))
        return lax.fori_loop(0, lengths_ref.shape[1], step, start)[0]

    down = [image_of((patches, 1), 0, b) for b in (0, -1, 1)]
    across = [image_of((1, patches), 1, b) for b in (0, -1, 1)]
    all_keys = jnp.concatenate(across, 1)
    same_own = down[0] == all_keys
    copies = []

    def send(part, lanes):
        at = (pl.ds(part.start, part.stop - part.start), pl.ds(0, lanes))
        copy = pltpu.make_async_copy(held.at[at], out_hbm.at[at], sems.at[len(copies)])
        copy.start()
        copies.append(copy)

    def kind(block, t, h=None):
        start = t * columns + (0 if h is None else h * HEAD_DIM)
        return blocks[block][start : start + (columns if h is None else HEAD_DIM)]

    def wide(t, which):
        return jnp.concatenate([kind(b, t).astype(jnp.float32) for b in which], 1).astype(jnp.bfloat16)

    held[rows.kind(rows.values), : 3 * patches] = wide(2, (0, 1, 2))
    held[rows.kind(rows.keys), : 3 * patches] = wide(1, (0, 1, 2))
    held[rows.kind(rows.queries), : 2 * patches] = wide(0, (1, 2))
    send(rows.kind(rows.values, 2), rows.lanes)
    send(rows.kind(rows.queries), rows.side_lanes)
    for h in range(heads):
        keys = held[rows.head(rows.keys, h), : 3 * patches]
        scores = dot(kind(0, 0, h), keys, TN) * SCALE
        scores = jnp.where(same_own, scores, -jnp.inf)
        weights = jnp.exp(scores - jnp.max(scores, 1, keepdims=True))
        over = 1.0 / jnp.sum(weights, 1, keepdims=True)
        held[rows.probs(h), : 3 * patches] = (weights * over).astype(jnp.bfloat16)
        send(rows.probs(h), rows.lanes)
    for h in range(heads):
        own_keys = kind(0, 1, h).astype(jnp.float32).T.astype(jnp.bfloat16)
        side, attended = [], []
        for b in (1, 2):
            queries = kind(b, 0, h)
            keys = kind(b, 1, h).astype(jnp.float32).T.astype(jnp.bfloat16)
            scores = []
            for n, k in ((0, own_keys), (b, keys)):
                scores.append(jnp.where(down[n] == across[b], dot(k, queries, NN) * SCALE, -jnp.inf))
            top = functools.reduce(jnp.maximum, [jnp.max(x, 0, keepdims=True) for x in scores])
            weights = [jnp.exp(x - top) for x in scores]
            over = 1.0 / sum([jnp.sum(w, 0, keepdims=True) for w in weights])
            probs = [(w * over).astype(jnp.bfloat16) for w in weights]
            attended.append(dot(kind(0, 2, h), probs[0], NN) + dot(kind(b, 2, h), probs[1], NN))
            side.append(probs[0].astype(jnp.float32))
        held[rows.side_probs(h), : 2 * patches] = jnp.concatenate(side, 1).astype(jnp.bfloat16)
        send(rows.side_probs(h), rows.side_lanes)
        attended = jnp.concatenate(attended, 1).astype(jnp.bfloat16)
        held[rows.head(rows.attended, h), : 2 * patches] = attended
    send(rows.kind(rows.attended), rows.side_lanes)
    for copy in copies:
        copy.wait()
    done_ref[...] = jnp.zeros(done_ref.shape, jnp.float32)


def softmax_parts(lengths, first, own, before, after):
    columns, patches = own.shape[0] // 3, own.shape[1]
    heads = columns // HEAD_DIM
    rows = Rows(columns, patches)
    smem = pl.BlockSpec(memory_space=pltpu.MemorySpace.SMEM)
    work = heads * patches * patches
    return pl.pallas_call(
        softmax_kernel,
        out_shape=(
            jax.ShapeDtypeStruct((rows.total, rows.lanes), jnp.bfloat16),
            jax.ShapeDtypeStruct((8, 128), jnp.float32),
        ),
        in_specs=[smem, smem] + in_vmem(3),
        out_specs=tuple(in_hbm(1) + in_vmem(1)),
        scratch_shapes=[
            pltpu.VMEM((rows.total, rows.lanes), jnp.bfloat16),
            pltpu.SemaphoreType.DMA((3 + 2 * heads,)),
        ],
        compiler_params=params(52),
        cost_estimate=pl.CostEstimate(
            flops=100_000 * work, bytes_accessed=500 * work, transcendentals=9 * work
        ),
        name="softmax_parts",
    )(lengths.reshape(1, -1), first.reshape(1, 1), own, before, after)


def gather_kernel(pieces_ref, _, out_ref):
    count, row_count, width = pieces_ref.shape
    total = pieces_ref[0].astype(jnp.float32)
    for p in range(1, count):
        total = total + pieces_ref[p].astype(jnp.float32)
    total = total.astype(jnp.bfloat16)
    columns = width // 4
    patch = iota((row_count, 4 * row_count), 1)
    token = iota((row_count, 4 * row_count), 0)
    result = jnp.zeros((columns, 4 * row_count), jnp.float32)
    for j in range(4):
        put = jnp.where(patch == 4 * token + j, 1.0, 0.0).astype(jnp.bfloat16)
        result = result + dot(total[:, j * columns : (j + 1) * columns], put, TN)
    out_ref[...] = result.astype(jnp.bfloat16)


def gathered(pieces, later):
    _, row_count, width = pieces.shape
    return pl.pallas_call(
        gather_kernel,
        out_shape=jax.ShapeDtypeStruct((width // 4, 4 * row_count), jnp.bfloat16),
        in_specs=in_vmem(2),
        out_specs=pl.BlockSpec(memory_space=VMEM),
        compiler_params=params(16),
        cost_estimate=pl.CostEstimate(
            flops=20_000 * pieces.size, bytes_accessed=400 * pieces.size, transcendentals=0
        ),
        name="gather_sum",
    )(pieces, later)


def own_kernel(grad_ref, own_ref, held_ref, query_ref, key_ref, value_ref):
    columns, patches = grad_ref.shape
    rows = Rows(columns, patches)
    for h in range(columns // HEAD_DIM):
        cols = slice(h * HEAD_DIM, (h + 1) * HEAD_DIM)
        grad = grad_ref[cols]
        slope = dot(grad, held_ref[rows.head(rows.values, h), : 3 * patches], TN)
        probs = held_ref[rows.probs(h), : 3 * patches]
        wide = probs.astype(jnp.float32)
        delta = jnp.sum(wide * slope, 1, keepdims=True)
        scores = (wide * (slope - delta)).astype(jnp.bfloat16)
        query = dot(scores, held_ref[rows.head(rows.keys, h), : 3 * patches], NT) * SCALE
        query_ref[cols] = query.T.astype(jnp.bfloat16)
        key_ref[cols] = dot(own_ref[cols], scores[:, :patches], NN)
        value_ref[cols] = dot(grad, probs[:, :patches], NN)


def own_terms(grad, own, held):
    return pl.pallas_call(
        own_kernel,
        out_shape=(
            jax.ShapeDtypeStruct(grad.shape, jnp.bfloat16),
            jax.ShapeDtypeStruct(grad.shape, jnp.float32),
            jax.ShapeDtypeStruct(grad.shape, jnp.float32),
        ),
        in_specs=in_vmem(3),
        out_specs=tuple(in_vmem(3)),
        compiler_params=params(24),
        name="own_terms",
    )(grad, own, held)


def side_kernel(left_ref, right_ref, key_part_ref, value_part_ref, held_ref, key_ref, value_ref):
    columns, patches = left_ref.shape
    rows = Rows(columns, patches)
    lanes = slice(0, 2 * patches)
    for h in range(columns // HEAD_DIM):
        cols = slice(h * HEAD_DIM, (h + 1) * HEAD_DIM)
        wide = jnp.concatenate([x[cols].astype(jnp.float32) for x in (left_ref, right_ref)], 1)
        grad = wide.astype(jnp.bfloat16)
        slope = dot(held_ref[rows.head(rows.values, h), :patches], grad, TN)
        attended = held_ref[rows.head(rows.attended, h), lanes].astype(jnp.float32)
        delta = jnp.sum(wide * attended, 0, keepdims=True)
        probs = held_ref[rows.side_probs(h), lanes]
        value = dot(probs, grad, NT)
        scores = (probs.astype(jnp.float32) * (slope - delta)).astype(jnp.bfloat16)
        key = dot(scores, held_ref[rows.head(rows.queries, h), lanes], NT)
        key_ref[cols] = ((key_part_ref[cols] + key.T) * SCALE).astype(jnp.bfloat16)
        value_ref[cols] = (value_part_ref[cols] + value.T).astype(jnp.bfloat16)


def side_terms(left, right, key_part, value_part, held):
    shape = jax.ShapeDtypeStruct(left.shape, jnp.bfloat16)
    return pl.pallas_call(
        side_kernel,
        out_shape=(shape, shape),
        in_specs=in_vmem(5),
        out_specs=tuple(in_vmem(2)),
        compiler_params=params(24),
        name="side_terms",
    )(left, right, key_part, value_part, held)


def from_both_sides(x, axis):
    size = lax.axis_size(axis)
    up = [(i, i + 1) for i in range(size - 1)]
    return (
        lax.ppermute(x, axis, up),
        lax.ppermute(x, axis, [(j, i) for i, j in up]),
    )


def on_device(
    grad_out, destination, w_down, pre_act, w_up, queries, key_states, value_states, lengths
):
    groups = lax.axis_size("grp")
    spans = lax.axis_size("span")
    heads = lax.axis_size(("sect", "span"))
    row_count = grad_out.shape[0]
    capacity, _ = padded_slots(row_count, groups)
    pieces = down_pieces(destination, grad_out, w_down, groups, spans)
    pieces, queries, key_states, value_states = lax.optimization_barrier(
        (pieces, queries, key_states, value_states)
    )
    arrived = lax.all_to_all(pieces, ("grp", "span"), split_axis=0, concat_axis=0, tiled=True)
    own = jnp.concatenate([queries.T, key_states.T, value_states.T], 0)
    before, after = from_both_sides(own, "grp")
    first = lax.axis_index("grp") * row_count
    held, held_done = softmax_parts(lengths, first, own, before, after)
    shares = up_pieces(arrived, pre_act, w_up, heads, capacity)
    shares = lax.all_to_all(shares, ("sect", "span"), split_axis=0, concat_axis=0, tiled=True)
    grad = gathered(shares, held_done)
    left, right = from_both_sides(grad, "grp")
    grad_query, key_part, value_part = own_terms(grad, queries.T, held)
    grad_key, grad_value = side_terms(left, right, key_part, value_part, held)
    return grad_query.T, grad_key.T, grad_value.T


def solution(mesh):
    split = P("grp", ("sect", "span"))
    placed = (
        P("grp", "span"),
        P("grp"),
        P("sect", "span"),
        split,
        P(None, ("sect", "span")),
        split,
        split,
        split,
        P(),
    )
    return jax.shard_map(
        on_device,
        mesh=mesh,
        in_specs=placed,
        out_specs=(split, split, split),
        check_vma=False,
    )
```

```python
import functools

import jax
import jax.numpy as jnp
from jax import lax
from jax.experimental import pallas as pl
from jax.experimental.pallas import tpu as pltpu
from jax.sharding import PartitionSpec as P

HEAD_DIM = 80
SCALE = HEAD_DIM**-0.5
MIB = 1024 * 1024
VMEM = pltpu.MemorySpace.VMEM
NT = (((1,), (1,)), ((), ()))
NN = (((1,), (0,)), ((), ()))
TN = (((0,), (0,)), ((), ()))


def dot(a, b, dims):
    return lax.dot_general(a, b, dims, preferred_element_type=jnp.float32)


def iota(shape, dim):
    return lax.broadcasted_iota(jnp.int32, shape, dim)


def params(mib):
    return pltpu.CompilerParams(vmem_limit_bytes=mib * MIB)


def in_vmem(count):
    return [pl.BlockSpec(memory_space=VMEM) for _ in range(count)]


def in_hbm(count):
    return [pl.BlockSpec(memory_space=pltpu.MemorySpace.HBM) for _ in range(count)]


def fetched(pairs, sems, at_first=None):
    copies = [pltpu.make_async_copy(a, b, sems.at[i]) for i, (a, b) in enumerate(pairs)]
    for copy in copies[:at_first]:
        copy.start()
    return copies


def padded_slots(row_count, groups):
    offsets = min(groups, row_count // 2)
    capacity = row_count // offsets
    return capacity, -(-(capacity + 1) // 8) * 8


def one_product(count, slots, hidden):
    return count * slots <= hidden


def down_kernel(groups, spans, capacity, slots, steps, dest_hbm, rows_hbm, weight_ref, out_ref,
                dest_ref, rows_ref, held, total_ref, sems):
    row_count = rows_ref.shape[0]
    hidden = weight_ref.shape[0] // spans
    everything = pl.ds(0, weight_ref.shape[0])
    pairs = [(dest_hbm, dest_ref), (rows_hbm, rows_ref)]
    for at, step in steps:
        part = (everything, pl.ds(at, step))
        pairs.append((weight_ref.at[part], held.at[part]))
    ahead = 3
    copies = fetched(pairs, sems, 2 + ahead)
    copies[0].wait()
    across = jnp.broadcast_to(dest_ref[...].astype(jnp.float32), (row_count, row_count))
    down = across.T
    group_across = jnp.floor((across + 0.5) * (1.0 / row_count))
    group_down = jnp.floor((down + 0.5) * (1.0 / row_count))
    slot_down = down - group_down * row_count
    same = group_across == group_down
    earlier = iota((row_count, row_count), 0) < iota((row_count, row_count), 1)
    later = iota((row_count, row_count), 1) < iota((row_count, row_count), 0)
    rank_across = jnp.sum(jnp.where(same & earlier, 1.0, 0.0), 0, keepdims=True)
    rank_down = jnp.sum(jnp.where(same & later, 1.0, 0.0), 1, keepdims=True)
    row_of = group_across[:1] * slots + rank_across
    places = iota((groups * slots, row_count), 0).astype(jnp.float32)
    pick = jnp.where(places == row_of, 1.0, 0.0).astype(jnp.bfloat16)
    lane = iota((row_count, hidden), 1).astype(jnp.float32)
    shift = 0.0
    if one_product(groups * spans, slots, hidden):
        device = lax.axis_index("grp") * spans + lax.axis_index("span")
        shift = (device * slots).astype(jnp.float32)
    at_rank = lane == rank_down + shift
    label_row = iota((slots, hidden), 0) == capacity
    labels = []
    for g in range(groups):
        hit = at_rank & (group_down[:, :1] == g)
        labels.append(jnp.sum(jnp.where(hit, slot_down[:, :1] + 1.0, 0.0), 0, keepdims=True) - 1.0)
    copies[1].wait()
    for n, (at, step) in enumerate(steps):
        turned = rows_ref[:, at : at + step].astype(jnp.float32).T.astype(jnp.bfloat16)
        copies[2 + n].wait()
        for copy in copies[2 + n + ahead : 3 + n + ahead]:
            copy.start()
        product = dot(held[:, at : at + step], turned, NN)
        total_ref[...] = product if n == 0 else total_ref[...] + product
    for s in range(spans):
        part = total_ref[s * hidden : (s + 1) * hidden].astype(jnp.bfloat16)
        moved = dot(pick, part, NT)
        for g in range(groups):
            piece = jnp.where(label_row, labels[g], moved[g * slots : (g + 1) * slots])
            out_ref[g * spans + s] = piece.astype(jnp.bfloat16)


def down_pieces(dest, rows, weight, groups, spans):
    row_count = rows.shape[0]
    capacity, slots = padded_slots(row_count, groups)
    hidden = weight.shape[0] // spans
    depth = weight.shape[1]
    edges = [depth * i // 16 for i in (0, 2, 5, 8, 11, 14, 16)]
    steps = [(i, j - i) for i, j in zip(edges, edges[1:])]
    return pl.pallas_call(
        functools.partial(down_kernel, groups, spans, capacity, slots, steps),
        out_shape=jax.ShapeDtypeStruct((groups * spans, slots, hidden), jnp.bfloat16),
        in_specs=in_hbm(3),
        out_specs=pl.BlockSpec(memory_space=VMEM),
        scratch_shapes=[
            pltpu.VMEM((1, row_count), jnp.int32),
            pltpu.VMEM(rows.shape, jnp.bfloat16),
            pltpu.VMEM(weight.shape, jnp.bfloat16),
            pltpu.VMEM((weight.shape[0], row_count), jnp.float32),
            pltpu.SemaphoreType.DMA((2 + len(steps),)),
        ],
        compiler_params=params(60),
        name="down_product",
    )(dest.reshape(1, row_count), rows, weight)


def up_kernel(heads, capacity, pieces_ref, pre_ref, weight_ref, out_ref, held, sems):
    row_count, hidden = pre_ref.shape
    count, slots, _ = pieces_ref.shape
    width = weight_ref.shape[0] // (4 * heads)
    pairs = []
    for h in range(heads):
        for j in range(4):
            source = weight_ref.at[pl.ds((j * heads + h) * width, width)]
            pairs.append((source, held.at[h, pl.ds(j * width, width)]))
    ahead = 16
    copies = fetched(pairs, sems, ahead)
    label_at = slice(capacity, capacity + 1)
    if one_product(count, slots, hidden):
        pieces = [pieces_ref[p].astype(jnp.float32) for p in range(count)]
        labels = functools.reduce(jnp.maximum, [x[label_at, : count * slots] for x in pieces])
        row = iota((row_count, count * slots), 0).astype(jnp.float32)
        put = jnp.where(row == labels, 1.0, 0.0).astype(jnp.bfloat16)
        total = dot(put, jnp.concatenate(pieces, 0).astype(jnp.bfloat16), NN)
    else:
        row = iota((row_count, slots), 0).astype(jnp.float32)

        def placed(p, total):
            piece = pieces_ref[p]
            labels = piece.astype(jnp.float32)[label_at, :slots]
            put = jnp.where(row == labels, 1.0, 0.0).astype(jnp.bfloat16)
            return total + dot(put, piece, NN)

        total = lax.fori_loop(0, count, placed, jnp.zeros((row_count, hidden), jnp.float32))
    pre = pre_ref[...].astype(jnp.float32)
    cdf = 0.5 * (1.0 + lax.erf(pre * 0.7071067811865476))
    slope = cdf + pre * jnp.exp(-0.5 * pre * pre) * 0.3989422804014327
    grad_pre = (total * slope).T.astype(jnp.bfloat16)
    width = 4 * width
    deep = hidden - hidden % 256
    if hidden - deep == 128 and row_count <= 128:
        tail = jnp.concatenate([grad_pre[deep:], jnp.zeros((128, 128 - row_count), jnp.bfloat16)], 1)
        zero = jnp.zeros_like(tail)
        twice = jnp.concatenate(
            [jnp.concatenate([tail, zero], 1), jnp.concatenate([zero, tail], 1)], 0
        )

        def products(h):
            main = dot(held[h : h + 2].reshape(2 * width, hidden)[:, :deep], grad_pre[:deep], NN)
            both = dot(jnp.concatenate([held[h, :, deep:], held[h + 1, :, deep:]], 1), twice, NN)
            return (
                main[:width] + both[:, :row_count],
                main[width:] + both[:, 128 : 128 + row_count],
            )

    else:

        def products(h):
            both = dot(held[h : h + 2].reshape(2 * width, hidden), grad_pre, NN)
            return both[:width], both[width:]

    waiting = None
    for h in range(0, heads, 2):
        for copy in copies[h * 4 : h * 4 + 8]:
            copy.wait()
        for copy in copies[h * 4 + ahead : h * 4 + 8 + ahead]:
            copy.start()
        product = products(h)
        if waiting is not None:
            for i in range(2):
                out_ref[h - 2 + i] = waiting[i].T.astype(jnp.bfloat16)
        waiting = product
    for i in range(2):
        out_ref[heads - 2 + i] = waiting[i].T.astype(jnp.bfloat16)


def up_pieces(pieces, pre, weight, heads, capacity):
    width = weight.shape[0] // heads
    return pl.pallas_call(
        functools.partial(up_kernel, heads, capacity),
        out_shape=jax.ShapeDtypeStruct((heads, pre.shape[0], width), jnp.bfloat16),
        in_specs=in_vmem(2) + in_hbm(1),
        out_specs=pl.BlockSpec(memory_space=VMEM),
        scratch_shapes=[
            pltpu.VMEM((heads, width, weight.shape[1]), jnp.bfloat16),
            pltpu.SemaphoreType.DMA((heads * 4,)),
        ],
        compiler_params=params(52),
        cost_estimate=pl.CostEstimate(
            flops=8 * pre.shape[0] * weight.size, bytes_accessed=8 * weight.size, transcendentals=0
        ),
        name="up_product",
    )(pieces, pre, weight)


class Rows:
    def __init__(self, columns, patches):
        heads = columns // HEAD_DIM
        self.lanes = -(-3 * patches // 128) * 128
        self.side_lanes = -(-2 * patches // 128) * 128
        self.columns, self.patches = columns, patches
        self.values, self.keys, self.queries, self.attended = [i * columns for i in range(4)]
        self.probs_at = 4 * columns
        self.side_at = self.probs_at + heads * patches
        self.total = self.side_at + heads * patches

    def head(self, start, h):
        return slice(start + h * HEAD_DIM, start + (h + 1) * HEAD_DIM)

    def kind(self, start, count=1):
        return slice(start, start + count * self.columns)

    def probs(self, h):
        return slice(self.probs_at + h * self.patches, self.probs_at + (h + 1) * self.patches)

    def side_probs(self, h):
        return slice(self.side_at + h * self.patches, self.side_at + (h + 1) * self.patches)


def softmax_kernel(lengths_ref, first_ref, own_ref, before_ref, after_ref, out_hbm, done_ref, held,
                   sems):
    columns, patches = own_ref.shape[0] // 3, own_ref.shape[1]
    heads = columns // HEAD_DIM
    rows = Rows(columns, patches)
    blocks = (own_ref, before_ref, after_ref)
    first = first_ref[0, 0]

    def image_of(shape, dim, block):
        token = iota(shape, dim) // 4 + (first + block * (patches // 4))

        def step(i, state):
            image, bound = state
            bound = bound + lengths_ref[0, i]
            return image + jnp.where(token >= bound, 1, 0), bound

        start = (jnp.where(token < 0, -1, 0), jnp.int32(0))
        return lax.fori_loop(0, lengths_ref.shape[1], step, start)[0]

    down = [image_of((patches, 1), 0, b) for b in (0, -1, 1)]
    across = [image_of((1, patches), 1, b) for b in (0, -1, 1)]
    all_keys = jnp.concatenate(across, 1)
    same_own = down[0] == all_keys
    copies = []

    def send(part, lanes):
        at = (pl.ds(part.start, part.stop - part.start), pl.ds(0, lanes))
        copy = pltpu.make_async_copy(held.at[at], out_hbm.at[at], sems.at[len(copies)])
        copy.start()
        copies.append(copy)

    def kind(block, t, h=None):
        start = t * columns + (0 if h is None else h * HEAD_DIM)
        return blocks[block][start : start + (columns if h is None else HEAD_DIM)]

    def wide(t, which):
        return jnp.concatenate([kind(b, t).astype(jnp.float32) for b in which], 1).astype(jnp.bfloat16)

    held[rows.kind(rows.values), : 3 * patches] = wide(2, (0, 1, 2))
    held[rows.kind(rows.keys), : 3 * patches] = wide(1, (0, 1, 2))
    held[rows.kind(rows.queries), : 2 * patches] = wide(0, (1, 2))
    send(rows.kind(rows.values, 2), rows.lanes)
    send(rows.kind(rows.queries), rows.side_lanes)
    for h in range(heads):
        keys = held[rows.head(rows.keys, h), : 3 * patches]
        scores = dot(kind(0, 0, h), keys, TN) * SCALE
        scores = jnp.where(same_own, scores, -jnp.inf)
        weights = jnp.exp(scores - jnp.max(scores, 1, keepdims=True))
        over = 1.0 / jnp.sum(weights, 1, keepdims=True)
        held[rows.probs(h), : 3 * patches] = (weights * over).astype(jnp.bfloat16)
        send(rows.probs(h), rows.lanes)
    for h in range(heads):
        own_keys = kind(0, 1, h).astype(jnp.float32).T.astype(jnp.bfloat16)
        side, attended = [], []
        for b in (1, 2):
            queries = kind(b, 0, h)
            keys = kind(b, 1, h).astype(jnp.float32).T.astype(jnp.bfloat16)
            scores = []
            for n, k in ((0, own_keys), (b, keys)):
                scores.append(jnp.where(down[n] == across[b], dot(k, queries, NN) * SCALE, -jnp.inf))
            top = functools.reduce(jnp.maximum, [jnp.max(x, 0, keepdims=True) for x in scores])
            weights = [jnp.exp(x - top) for x in scores]
            over = 1.0 / sum([jnp.sum(w, 0, keepdims=True) for w in weights])
            probs = [(w * over).astype(jnp.bfloat16) for w in weights]
            attended.append(dot(kind(0, 2, h), probs[0], NN) + dot(kind(b, 2, h), probs[1], NN))
            side.append(probs[0].astype(jnp.float32))
        held[rows.side_probs(h), : 2 * patches] = jnp.concatenate(side, 1).astype(jnp.bfloat16)
        send(rows.side_probs(h), rows.side_lanes)
        attended = jnp.concatenate(attended, 1).astype(jnp.bfloat16)
        held[rows.head(rows.attended, h), : 2 * patches] = attended
    send(rows.kind(rows.attended), rows.side_lanes)
    for copy in copies:
        copy.wait()
    done_ref[...] = jnp.zeros(done_ref.shape, jnp.float32)


def softmax_parts(lengths, first, own, before, after):
    columns, patches = own.shape[0] // 3, own.shape[1]
    heads = columns // HEAD_DIM
    rows = Rows(columns, patches)
    smem = pl.BlockSpec(memory_space=pltpu.MemorySpace.SMEM)
    work = heads * patches * patches
    return pl.pallas_call(
        softmax_kernel,
        out_shape=(
            jax.ShapeDtypeStruct((rows.total, rows.lanes), jnp.bfloat16),
            jax.ShapeDtypeStruct((8, 128), jnp.float32),
        ),
        in_specs=[smem, smem] + in_vmem(3),
        out_specs=tuple(in_hbm(1) + in_vmem(1)),
        scratch_shapes=[
            pltpu.VMEM((rows.total, rows.lanes), jnp.bfloat16),
            pltpu.SemaphoreType.DMA((3 + 2 * heads,)),
        ],
        compiler_params=params(52),
        cost_estimate=pl.CostEstimate(
            flops=100_000 * work, bytes_accessed=500 * work, transcendentals=9 * work
        ),
        name="softmax_parts",
    )(lengths.reshape(1, -1), first.reshape(1, 1), own, before, after)


def gather_kernel(pieces_ref, _, out_ref):
    count, row_count, width = pieces_ref.shape
    total = pieces_ref[0].astype(jnp.float32)
    for p in range(1, count):
        total = total + pieces_ref[p].astype(jnp.float32)
    total = total.astype(jnp.bfloat16)
    columns = width // 4
    patch = iota((row_count, 4 * row_count), 1)
    token = iota((row_count, 4 * row_count), 0)
    result = jnp.zeros((columns, 4 * row_count), jnp.float32)
    for j in range(4):
        put = jnp.where(patch == 4 * token + j, 1.0, 0.0).astype(jnp.bfloat16)
        result = result + dot(total[:, j * columns : (j + 1) * columns], put, TN)
    out_ref[...] = result.astype(jnp.bfloat16)


def gathered(pieces, later):
    _, row_count, width = pieces.shape
    return pl.pallas_call(
        gather_kernel,
        out_shape=jax.ShapeDtypeStruct((width // 4, 4 * row_count), jnp.bfloat16),
        in_specs=in_vmem(2),
        out_specs=pl.BlockSpec(memory_space=VMEM),
        compiler_params=params(16),
        cost_estimate=pl.CostEstimate(
            flops=20_000 * pieces.size, bytes_accessed=400 * pieces.size, transcendentals=0
        ),
        name="gather_sum",
    )(pieces, later)


def own_kernel(grad_ref, own_ref, held_ref, query_ref, key_ref, value_ref):
    columns, patches = grad_ref.shape
    rows = Rows(columns, patches)
    for h in range(columns // HEAD_DIM):
        cols = slice(h * HEAD_DIM, (h + 1) * HEAD_DIM)
        grad = grad_ref[cols]
        slope = dot(grad, held_ref[rows.head(rows.values, h), : 3 * patches], TN)
        probs = held_ref[rows.probs(h), : 3 * patches]
        wide = probs.astype(jnp.float32)
        delta = jnp.sum(wide * slope, 1, keepdims=True)
        scores = (wide * (slope - delta)).astype(jnp.bfloat16)
        query = dot(scores, held_ref[rows.head(rows.keys, h), : 3 * patches], NT) * SCALE
        query_ref[cols] = query.T.astype(jnp.bfloat16)
        key_ref[cols] = dot(own_ref[cols], scores[:, :patches], NN)
        value_ref[cols] = dot(grad, probs[:, :patches], NN)


def own_terms(grad, own, held):
    return pl.pallas_call(
        own_kernel,
        out_shape=(
            jax.ShapeDtypeStruct(grad.shape, jnp.bfloat16),
            jax.ShapeDtypeStruct(grad.shape, jnp.float32),
            jax.ShapeDtypeStruct(grad.shape, jnp.float32),
        ),
        in_specs=in_vmem(3),
        out_specs=tuple(in_vmem(3)),
        compiler_params=params(24),
        name="own_terms",
    )(grad, own, held)


def side_kernel(left_ref, right_ref, key_part_ref, value_part_ref, held_ref, key_ref, value_ref):
    columns, patches = left_ref.shape
    rows = Rows(columns, patches)
    lanes = slice(0, 2 * patches)
    for h in range(columns // HEAD_DIM):
        cols = slice(h * HEAD_DIM, (h + 1) * HEAD_DIM)
        wide = jnp.concatenate([x[cols].astype(jnp.float32) for x in (left_ref, right_ref)], 1)
        grad = wide.astype(jnp.bfloat16)
        slope = dot(held_ref[rows.head(rows.values, h), :patches], grad, TN)
        attended = held_ref[rows.head(rows.attended, h), lanes].astype(jnp.float32)
        delta = jnp.sum(wide * attended, 0, keepdims=True)
        probs = held_ref[rows.side_probs(h), lanes]
        value = dot(probs, grad, NT)
        scores = (probs.astype(jnp.float32) * (slope - delta)).astype(jnp.bfloat16)
        key = dot(scores, held_ref[rows.head(rows.queries, h), lanes], NT)
        key_ref[cols] = ((key_part_ref[cols] + key.T) * SCALE).astype(jnp.bfloat16)
        value_ref[cols] = (value_part_ref[cols] + value.T).astype(jnp.bfloat16)


def side_terms(left, right, key_part, value_part, held):
    shape = jax.ShapeDtypeStruct(left.shape, jnp.bfloat16)
    return pl.pallas_call(
        side_kernel,
        out_shape=(shape, shape),
        in_specs=in_vmem(5),
        out_specs=tuple(in_vmem(2)),
        compiler_params=params(24),
        name="side_terms",
    )(left, right, key_part, value_part, held)


def from_both_sides(x, axis):
    size = lax.axis_size(axis)
    up = [(i, i + 1) for i in range(size - 1)]
    return (
        lax.ppermute(x, axis, up),
        lax.ppermute(x, axis, [(j, i) for i, j in up]),
    )


def on_device(
    grad_out, destination, w_down, pre_act, w_up, queries, key_states, value_states, lengths
):
    groups = lax.axis_size("grp")
    spans = lax.axis_size("span")
    heads = lax.axis_size(("sect", "span"))
    row_count = grad_out.shape[0]
    capacity, _ = padded_slots(row_count, groups)
    pieces = down_pieces(destination, grad_out, w_down, groups, spans)
    pieces, queries, key_states, value_states = lax.optimization_barrier(
        (pieces, queries, key_states, value_states)
    )
    arrived = lax.all_to_all(pieces, ("grp", "span"), split_axis=0, concat_axis=0, tiled=True)
    own = jnp.concatenate([queries.T, key_states.T, value_states.T], 0)
    before, after = from_both_sides(own, "grp")
    first = lax.axis_index("grp") * row_count
    held, held_done = softmax_parts(lengths, first, own, before, after)
    shares = up_pieces(arrived, pre_act, w_up, heads, capacity)
    shares = lax.all_to_all(shares, ("sect", "span"), split_axis=0, concat_axis=0, tiled=True)
    grad = gathered(shares, held_done)
    left, right = from_both_sides(grad, "grp")
    grad_query, key_part, value_part = own_terms(grad, queries.T, held)
    grad_key, grad_value = side_terms(left, right, key_part, value_part, held)
    return grad_query.T, grad_key.T, grad_value.T


def solution(mesh):
    split = P("grp", ("sect", "span"))
    placed = (
        P("grp", "span"),
        P("grp"),
        P("sect", "span"),
        split,
        P(None, ("sect", "span")),
        split,
        split,
        split,
        P(),
    )
    return jax.shard_map(
        on_device,
        mesh=mesh,
        in_specs=placed,
        out_specs=(split, split, split),
        check_vma=False,
    )
```

```python
import functools

import jax
import jax.numpy as jnp
from jax import lax
from jax.experimental import pallas as pl
from jax.experimental.pallas import tpu as pltpu
from jax.sharding import PartitionSpec as P

HEAD_DIM = 80
SCALE = HEAD_DIM**-0.5
MIB = 1024 * 1024
VMEM = pltpu.MemorySpace.VMEM
NT = (((1,), (1,)), ((), ()))
NN = (((1,), (0,)), ((), ()))
TN = (((0,), (0,)), ((), ()))


def dot(a, b, dims):
    return lax.dot_general(a, b, dims, preferred_element_type=jnp.float32)


def iota(shape, dim):
    return lax.broadcasted_iota(jnp.int32, shape, dim)


def params(mib):
    return pltpu.CompilerParams(vmem_limit_bytes=mib * MIB)


def in_vmem(count):
    return [pl.BlockSpec(memory_space=VMEM) for _ in range(count)]


def in_hbm(count):
    return [pl.BlockSpec(memory_space=pltpu.MemorySpace.HBM) for _ in range(count)]


def fetched(pairs, sems):
    copies = [pltpu.make_async_copy(a, b, sems.at[i]) for i, (a, b) in enumerate(pairs)]
    for copy in copies:
        copy.start()
    return copies


def padded_slots(row_count, groups):
    offsets = min(groups, row_count // 2)
    capacity = row_count // offsets
    return capacity, -(-(capacity + 1) // 8) * 8


def one_product(count, slots, hidden):
    return count * slots <= hidden


def down_kernel(groups, spans, capacity, slots, steps, dest_hbm, rows_hbm, weight_ref, out_hbm,
                dest_ref, rows_ref, held, total_ref, pieces_ref, sems, out_sems):
    row_count = rows_ref.shape[0]
    hidden = weight_ref.shape[0] // spans
    everything = pl.ds(0, weight_ref.shape[0])
    pairs = [(dest_hbm, dest_ref), (rows_hbm, rows_ref)]
    for at, step in steps:
        part = (everything, pl.ds(at, step))
        pairs.append((weight_ref.at[part], held.at[part]))
    copies = fetched(pairs, sems)
    copies[0].wait()
    across = jnp.broadcast_to(dest_ref[...].astype(jnp.float32), (row_count, row_count))
    down = across.T
    group_across = jnp.floor((across + 0.5) * (1.0 / row_count))
    group_down = jnp.floor((down + 0.5) * (1.0 / row_count))
    slot_down = down - group_down * row_count
    same = group_across == group_down
    earlier = iota((row_count, row_count), 0) < iota((row_count, row_count), 1)
    later = iota((row_count, row_count), 1) < iota((row_count, row_count), 0)
    rank_across = jnp.sum(jnp.where(same & earlier, 1.0, 0.0), 0, keepdims=True)
    rank_down = jnp.sum(jnp.where(same & later, 1.0, 0.0), 1, keepdims=True)
    row_of = group_across[:1] * slots + rank_across
    places = iota((groups * slots, row_count), 0).astype(jnp.float32)
    pick = jnp.where(places == row_of, 1.0, 0.0).astype(jnp.bfloat16)
    lane = iota((row_count, hidden), 1).astype(jnp.float32)
    shift = 0.0
    if one_product(groups * spans, slots, hidden):
        device = lax.axis_index("grp") * spans + lax.axis_index("span")
        shift = (device * slots).astype(jnp.float32)
    at_rank = lane == rank_down + shift
    label_row = iota((slots, hidden), 0) == capacity
    labels = []
    for g in range(groups):
        hit = at_rank & (group_down[:, :1] == g)
        labels.append(jnp.sum(jnp.where(hit, slot_down[:, :1] + 1.0, 0.0), 0, keepdims=True) - 1.0)
    copies[1].wait()
    for n, (at, step) in enumerate(steps):
        turned = rows_ref[:, at : at + step].astype(jnp.float32).T.astype(jnp.bfloat16)
        copies[2 + n].wait()
        product = dot(held[:, at : at + step], turned, NN)
        total_ref[...] = product if n == 0 else total_ref[...] + product
    outgoing = []
    for s in range(spans):
        part = total_ref[s * hidden : (s + 1) * hidden].astype(jnp.bfloat16)
        moved = dot(pick, part, NT)
        for g in range(groups):
            piece = jnp.where(label_row, labels[g], moved[g * slots : (g + 1) * slots])
            pieces_ref[s, g] = piece.astype(jnp.bfloat16)
        copy = pltpu.make_async_copy(pieces_ref.at[s], out_hbm.at[:, s], out_sems.at[s])
        copy.start()
        outgoing.append(copy)
    for copy in outgoing:
        copy.wait()


def down_pieces(dest, rows, weight, groups, spans):
    row_count = rows.shape[0]
    capacity, slots = padded_slots(row_count, groups)
    hidden = weight.shape[0] // spans
    depth = weight.shape[1]
    edges = [depth * i // 8 for i in (0, 2, 5, 7, 8)]
    steps = [(i, j - i) for i, j in zip(edges, edges[1:])]
    pieces = pl.pallas_call(
        functools.partial(down_kernel, groups, spans, capacity, slots, steps),
        out_shape=jax.ShapeDtypeStruct((groups, spans, slots, hidden), jnp.bfloat16),
        in_specs=in_hbm(3),
        out_specs=in_hbm(1)[0],
        scratch_shapes=[
            pltpu.VMEM((1, row_count), jnp.int32),
            pltpu.VMEM(rows.shape, jnp.bfloat16),
            pltpu.VMEM(weight.shape, jnp.bfloat16),
            pltpu.VMEM((weight.shape[0], row_count), jnp.float32),
            pltpu.VMEM((spans, groups, slots, hidden), jnp.bfloat16),
            pltpu.SemaphoreType.DMA((2 + len(steps),)),
            pltpu.SemaphoreType.DMA((spans,)),
        ],
        compiler_params=params(60),
        name="down_product",
    )(dest.reshape(1, row_count), rows, weight)
    return pieces.reshape(groups * spans, slots, hidden)


def up_kernel(heads, capacity, pieces_ref, pre_ref, weight_ref, out_hbm, held, out_ref, sems,
              out_sems):
    row_count, hidden = pre_ref.shape
    count, slots, _ = pieces_ref.shape
    width = weight_ref.shape[0] // (4 * heads)
    copies = []
    for h in range(heads):
        for j in range(4):
            copy = pltpu.make_async_copy(
                weight_ref.at[pl.ds((j * heads + h) * width, width)],
                held.at[h, pl.ds(j * width, width)],
                sems.at[h * 4 + j],
            )
            copy.start()
            copies.append(copy)
    label_at = slice(capacity, capacity + 1)
    if one_product(count, slots, hidden):
        pieces = [pieces_ref[p].astype(jnp.float32) for p in range(count)]
        labels = functools.reduce(jnp.maximum, [x[label_at, : count * slots] for x in pieces])
        row = iota((row_count, count * slots), 0).astype(jnp.float32)
        put = jnp.where(row == labels, 1.0, 0.0).astype(jnp.bfloat16)
        total = dot(put, jnp.concatenate(pieces, 0).astype(jnp.bfloat16), NN)
    else:
        row = iota((row_count, slots), 0).astype(jnp.float32)

        def placed(p, total):
            piece = pieces_ref[p]
            labels = piece.astype(jnp.float32)[label_at, :slots]
            put = jnp.where(row == labels, 1.0, 0.0).astype(jnp.bfloat16)
            return total + dot(put, piece, NN)

        total = lax.fori_loop(0, count, placed, jnp.zeros((row_count, hidden), jnp.float32))
    pre = pre_ref[...].astype(jnp.float32)
    cdf = 0.5 * (1.0 + lax.erf(pre * 0.7071067811865476))
    slope = cdf + pre * jnp.exp(-0.5 * pre * pre) * 0.3989422804014327
    grad_pre = (total * slope).T.astype(jnp.bfloat16)
    width = 4 * width
    outgoing = []

    def send(h, products):
        for i in range(2):
            part = products[i * width : (i + 1) * width]
            out_ref[h + i] = part.T.astype(jnp.bfloat16)
        at = pl.ds(h, 2)
        outgoing.append(pltpu.make_async_copy(out_ref.at[at], out_hbm.at[at], out_sems.at[h // 2]))
        outgoing[-1].start()

    waiting = None
    for h in range(0, heads, 2):
        for copy in copies[h * 4 : h * 4 + 8]:
            copy.wait()
        product = dot(held[h : h + 2].reshape(2 * width, hidden), grad_pre, NN)
        if waiting is not None:
            send(h - 2, waiting)
        waiting = product
    send(heads - 2, waiting)
    for copy in outgoing:
        copy.wait()


def up_pieces(pieces, pre, weight, heads, capacity):
    width = weight.shape[0] // heads
    return pl.pallas_call(
        functools.partial(up_kernel, heads, capacity),
        out_shape=jax.ShapeDtypeStruct((heads, pre.shape[0], width), jnp.bfloat16),
        in_specs=in_vmem(2) + in_hbm(1),
        out_specs=in_hbm(1)[0],
        scratch_shapes=[
            pltpu.VMEM((heads, width, weight.shape[1]), jnp.bfloat16),
            pltpu.VMEM((heads, pre.shape[0], width), jnp.bfloat16),
            pltpu.SemaphoreType.DMA((heads * 4,)),
            pltpu.SemaphoreType.DMA((heads // 2,)),
        ],
        compiler_params=params(52),
        cost_estimate=pl.CostEstimate(
            flops=8 * pre.shape[0] * weight.size, bytes_accessed=8 * weight.size, transcendentals=0
        ),
        name="up_product",
    )(pieces, pre, weight)


class Rows:
    def __init__(self, columns, patches):
        heads = columns // HEAD_DIM
        self.lanes = -(-3 * patches // 128) * 128
        self.side_lanes = -(-2 * patches // 128) * 128
        self.columns, self.patches = columns, patches
        self.values, self.keys, self.queries, self.attended = [i * columns for i in range(4)]
        self.probs_at = 4 * columns
        self.side_at = self.probs_at + heads * patches
        self.total = self.side_at + heads * patches

    def head(self, start, h):
        return slice(start + h * HEAD_DIM, start + (h + 1) * HEAD_DIM)

    def kind(self, start, count=1):
        return slice(start, start + count * self.columns)

    def probs(self, h):
        return slice(self.probs_at + h * self.patches, self.probs_at + (h + 1) * self.patches)

    def side_probs(self, h):
        return slice(self.side_at + h * self.patches, self.side_at + (h + 1) * self.patches)


def softmax_kernel(lengths_ref, first_ref, own_ref, before_ref, after_ref, out_hbm, done_ref, held,
                   sems):
    columns, patches = own_ref.shape[0] // 3, own_ref.shape[1]
    heads = columns // HEAD_DIM
    rows = Rows(columns, patches)
    blocks = (own_ref, before_ref, after_ref)
    first = first_ref[0, 0]

    def image_of(shape, dim, block):
        token = iota(shape, dim) // 4 + (first + block * (patches // 4))

        def step(i, state):
            image, bound = state
            bound = bound + lengths_ref[0, i]
            return image + jnp.where(token >= bound, 1, 0), bound

        start = (jnp.where(token < 0, -1, 0), jnp.int32(0))
        return lax.fori_loop(0, lengths_ref.shape[1], step, start)[0]

    down = [image_of((patches, 1), 0, b) for b in (0, -1, 1)]
    across = [image_of((1, patches), 1, b) for b in (0, -1, 1)]
    all_keys = jnp.concatenate(across, 1)
    same_own = down[0] == all_keys
    copies = []

    def send(part, lanes):
        at = (pl.ds(part.start, part.stop - part.start), pl.ds(0, lanes))
        copy = pltpu.make_async_copy(held.at[at], out_hbm.at[at], sems.at[len(copies)])
        copy.start()
        copies.append(copy)

    def kind(block, t, h=None):
        start = t * columns + (0 if h is None else h * HEAD_DIM)
        return blocks[block][start : start + (columns if h is None else HEAD_DIM)]

    def wide(t, which):
        return jnp.concatenate([kind(b, t).astype(jnp.float32) for b in which], 1).astype(jnp.bfloat16)

    held[rows.kind(rows.values), : 3 * patches] = wide(2, (0, 1, 2))
    held[rows.kind(rows.keys), : 3 * patches] = wide(1, (0, 1, 2))
    held[rows.kind(rows.queries), : 2 * patches] = wide(0, (1, 2))
    send(rows.kind(rows.values, 2), rows.lanes)
    send(rows.kind(rows.queries), rows.side_lanes)
    for h in range(heads):
        keys = held[rows.head(rows.keys, h), : 3 * patches]
        scores = dot(kind(0, 0, h), keys, TN) * SCALE
        scores = jnp.where(same_own, scores, -jnp.inf)
        weights = jnp.exp(scores - jnp.max(scores, 1, keepdims=True))
        over = 1.0 / jnp.sum(weights, 1, keepdims=True)
        held[rows.probs(h), : 3 * patches] = (weights * over).astype(jnp.bfloat16)
        send(rows.probs(h), rows.lanes)
    for h in range(heads):
        own_keys = kind(0, 1, h).astype(jnp.float32).T.astype(jnp.bfloat16)
        side, attended = [], []
        for b in (1, 2):
            queries = kind(b, 0, h)
            keys = kind(b, 1, h).astype(jnp.float32).T.astype(jnp.bfloat16)
            scores = []
            for n, k in ((0, own_keys), (b, keys)):
                scores.append(jnp.where(down[n] == across[b], dot(k, queries, NN) * SCALE, -jnp.inf))
            top = functools.reduce(jnp.maximum, [jnp.max(x, 0, keepdims=True) for x in scores])
            weights = [jnp.exp(x - top) for x in scores]
            over = 1.0 / sum([jnp.sum(w, 0, keepdims=True) for w in weights])
            probs = [(w * over).astype(jnp.bfloat16) for w in weights]
            attended.append(dot(kind(0, 2, h), probs[0], NN) + dot(kind(b, 2, h), probs[1], NN))
            side.append(probs[0].astype(jnp.float32))
        held[rows.side_probs(h), : 2 * patches] = jnp.concatenate(side, 1).astype(jnp.bfloat16)
        send(rows.side_probs(h), rows.side_lanes)
        attended = jnp.concatenate(attended, 1).astype(jnp.bfloat16)
        held[rows.head(rows.attended, h), : 2 * patches] = attended
    send(rows.kind(rows.attended), rows.side_lanes)
    for copy in copies:
        copy.wait()
    done_ref[...] = jnp.zeros(done_ref.shape, jnp.float32)


def softmax_parts(lengths, first, own, before, after):
    columns, patches = own.shape[0] // 3, own.shape[1]
    heads = columns // HEAD_DIM
    rows = Rows(columns, patches)
    smem = pl.BlockSpec(memory_space=pltpu.MemorySpace.SMEM)
    work = heads * patches * patches
    return pl.pallas_call(
        softmax_kernel,
        out_shape=(
            jax.ShapeDtypeStruct((rows.total, rows.lanes), jnp.bfloat16),
            jax.ShapeDtypeStruct((8, 128), jnp.float32),
        ),
        in_specs=[smem, smem] + in_vmem(3),
        out_specs=tuple(in_hbm(1) + in_vmem(1)),
        scratch_shapes=[
            pltpu.VMEM((rows.total, rows.lanes), jnp.bfloat16),
            pltpu.SemaphoreType.DMA((3 + 2 * heads,)),
        ],
        compiler_params=params(52),
        cost_estimate=pl.CostEstimate(
            flops=100_000 * work, bytes_accessed=500 * work, transcendentals=9 * work
        ),
        name="softmax_parts",
    )(lengths.reshape(1, -1), first.reshape(1, 1), own, before, after)


def gather_kernel(pieces_ref, _, out_ref):
    count, row_count, width = pieces_ref.shape
    total = pieces_ref[0].astype(jnp.float32)
    for p in range(1, count):
        total = total + pieces_ref[p].astype(jnp.float32)
    total = total.astype(jnp.bfloat16)
    columns = width // 4
    patch = iota((row_count, 4 * row_count), 1)
    token = iota((row_count, 4 * row_count), 0)
    result = jnp.zeros((columns, 4 * row_count), jnp.float32)
    for j in range(4):
        put = jnp.where(patch == 4 * token + j, 1.0, 0.0).astype(jnp.bfloat16)
        result = result + dot(total[:, j * columns : (j + 1) * columns], put, TN)
    out_ref[...] = result.astype(jnp.bfloat16)


def gathered(pieces, later):
    _, row_count, width = pieces.shape
    return pl.pallas_call(
        gather_kernel,
        out_shape=jax.ShapeDtypeStruct((width // 4, 4 * row_count), jnp.bfloat16),
        in_specs=in_vmem(2),
        out_specs=pl.BlockSpec(memory_space=VMEM),
        compiler_params=params(16),
        cost_estimate=pl.CostEstimate(
            flops=20_000 * pieces.size, bytes_accessed=400 * pieces.size, transcendentals=0
        ),
        name="gather_sum",
    )(pieces, later)


def own_kernel(grad_ref, own_ref, held_ref, query_ref, key_ref, value_ref):
    columns, patches = grad_ref.shape
    rows = Rows(columns, patches)
    for h in range(columns // HEAD_DIM):
        cols = slice(h * HEAD_DIM, (h + 1) * HEAD_DIM)
        grad = grad_ref[cols]
        slope = dot(grad, held_ref[rows.head(rows.values, h), : 3 * patches], TN)
        probs = held_ref[rows.probs(h), : 3 * patches]
        wide = probs.astype(jnp.float32)
        delta = jnp.sum(wide * slope, 1, keepdims=True)
        scores = (wide * (slope - delta)).astype(jnp.bfloat16)
        query = dot(scores, held_ref[rows.head(rows.keys, h), : 3 * patches], NT) * SCALE
        query_ref[cols] = query.T.astype(jnp.bfloat16)
        key_ref[cols] = dot(own_ref[cols], scores[:, :patches], NN)
        value_ref[cols] = dot(grad, probs[:, :patches], NN)


def own_terms(grad, own, held):
    return pl.pallas_call(
        own_kernel,
        out_shape=(
            jax.ShapeDtypeStruct(grad.shape, jnp.bfloat16),
            jax.ShapeDtypeStruct(grad.shape, jnp.float32),
            jax.ShapeDtypeStruct(grad.shape, jnp.float32),
        ),
        in_specs=in_vmem(3),
        out_specs=tuple(in_vmem(3)),
        compiler_params=params(24),
        name="own_terms",
    )(grad, own, held)


def side_kernel(even_ref, odd_ref, key_part_ref, value_part_ref, held_ref, key_ref, value_ref):
    columns, patches = even_ref.shape
    is_even = lax.rem(lax.axis_index("grp"), 2) == 0
    rows = Rows(columns, patches)
    lanes = slice(0, 2 * patches)
    for h in range(columns // HEAD_DIM):
        cols = slice(h * HEAD_DIM, (h + 1) * HEAD_DIM)
        even, odd = even_ref[cols].astype(jnp.float32), odd_ref[cols].astype(jnp.float32)
        left, right = jnp.where(is_even, odd, even), jnp.where(is_even, even, odd)
        wide = jnp.concatenate([left, right], 1)
        grad = wide.astype(jnp.bfloat16)
        slope = dot(held_ref[rows.head(rows.values, h), :patches], grad, TN)
        attended = held_ref[rows.head(rows.attended, h), lanes].astype(jnp.float32)
        delta = jnp.sum(wide * attended, 0, keepdims=True)
        probs = held_ref[rows.side_probs(h), lanes]
        value = dot(probs, grad, NT)
        scores = (probs.astype(jnp.float32) * (slope - delta)).astype(jnp.bfloat16)
        key = dot(scores, held_ref[rows.head(rows.queries, h), lanes], NT)
        key_ref[cols] = ((key_part_ref[cols] + key.T) * SCALE).astype(jnp.bfloat16)
        value_ref[cols] = (value_part_ref[cols] + value.T).astype(jnp.bfloat16)


def side_terms(even, odd, key_part, value_part, held):
    shape = jax.ShapeDtypeStruct(even.shape, jnp.bfloat16)
    return pl.pallas_call(
        side_kernel,
        out_shape=(shape, shape),
        in_specs=in_vmem(5),
        out_specs=tuple(in_vmem(2)),
        compiler_params=params(24),
        name="side_terms",
    )(even, odd, key_part, value_part, held)


def from_both_sides(x, axis):
    size = lax.axis_size(axis)
    up = [(i, i + 1) for i in range(size - 1)]
    return (
        lax.ppermute(x, axis, up),
        lax.ppermute(x, axis, [(j, i) for i, j in up]),
    )


def from_pairs(x, axis):
    size = lax.axis_size(axis)

    def swapped(first):
        low = range(first, size - 1, 2)
        return lax.ppermute(x, axis, [(i, i + 1) for i in low] + [(i + 1, i) for i in low])

    return swapped(0), swapped(1)


def on_device(
    grad_out, destination, w_down, pre_act, w_up, queries, key_states, value_states, lengths
):
    groups = lax.axis_size("grp")
    spans = lax.axis_size("span")
    heads = lax.axis_size(("sect", "span"))
    row_count = grad_out.shape[0]
    capacity, _ = padded_slots(row_count, groups)
    pieces = down_pieces(destination, grad_out, w_down, groups, spans)
    pieces, queries, key_states, value_states = lax.optimization_barrier(
        (pieces, queries, key_states, value_states)
    )
    arrived = lax.all_to_all(pieces, ("grp", "span"), split_axis=0, concat_axis=0, tiled=True)
    own = jnp.concatenate([queries.T, key_states.T, value_states.T], 0)
    before, after = from_both_sides(own, "grp")
    first = lax.axis_index("grp") * row_count
    held, held_done = softmax_parts(lengths, first, own, before, after)
    shares = up_pieces(arrived, pre_act, w_up, heads, capacity)
    shares = lax.all_to_all(shares, ("sect", "span"), split_axis=0, concat_axis=0, tiled=True)
    grad = gathered(shares, held_done)
    even, odd = from_pairs(grad, "grp")
    grad_query, key_part, value_part = own_terms(grad, queries.T, held)
    grad_key, grad_value = side_terms(even, odd, key_part, value_part, held)
    return grad_query.T, grad_key.T, grad_value.T


def solution(mesh):
    split = P("grp", ("sect", "span"))
    placed = (
        P("grp", "span"),
        P("grp"),
        P("sect", "span"),
        split,
        P(None, ("sect", "span")),
        split,
        split,
        split,
        P(),
    )
    return jax.shard_map(
        on_device,
        mesh=mesh,
        in_specs=placed,
        out_specs=(split, split, split),
        check_vma=False,
    )
```

```python
import functools

import jax
import jax.numpy as jnp
from jax import lax
from jax.experimental import pallas as pl
from jax.experimental.pallas import tpu as pltpu
from jax.sharding import PartitionSpec as P

HEAD_DIM = 80
SCALE = HEAD_DIM**-0.5
MIB = 1024 * 1024
VMEM = pltpu.MemorySpace.VMEM
NT = (((1,), (1,)), ((), ()))
NN = (((1,), (0,)), ((), ()))
TN = (((0,), (0,)), ((), ()))


def dot(a, b, dims):
    return lax.dot_general(a, b, dims, preferred_element_type=jnp.float32)


def iota(shape, dim):
    return lax.broadcasted_iota(jnp.int32, shape, dim)


def params(mib):
    return pltpu.CompilerParams(vmem_limit_bytes=mib * MIB)


def in_vmem(count):
    return [pl.BlockSpec(memory_space=VMEM) for _ in range(count)]


def in_hbm(count):
    return [pl.BlockSpec(memory_space=pltpu.MemorySpace.HBM) for _ in range(count)]


def fetched(pairs, sems):
    copies = [pltpu.make_async_copy(a, b, sems.at[i]) for i, (a, b) in enumerate(pairs)]
    for copy in copies:
        copy.start()
    return copies


def padded_slots(row_count, groups):
    offsets = min(groups, row_count // 2)
    capacity = row_count // offsets
    return capacity, -(-(capacity + 1) // 8) * 8


def one_product(count, slots, hidden):
    return count * slots <= hidden


def down_kernel(groups, spans, capacity, slots, steps, dest_hbm, rows_hbm, weight_ref, out_hbm,
                dest_ref, rows_ref, held, total_ref, pieces_ref, sems, out_sems):
    row_count = rows_ref.shape[0]
    hidden = weight_ref.shape[0] // spans
    everything = pl.ds(0, weight_ref.shape[0])
    pairs = [(dest_hbm, dest_ref), (rows_hbm, rows_ref)]
    for at, step in steps:
        part = (everything, pl.ds(at, step))
        pairs.append((weight_ref.at[part], held.at[part]))
    copies = fetched(pairs, sems)
    copies[0].wait()
    across = jnp.broadcast_to(dest_ref[...].astype(jnp.float32), (row_count, row_count))
    down = across.T
    group_across = jnp.floor((across + 0.5) * (1.0 / row_count))
    group_down = jnp.floor((down + 0.5) * (1.0 / row_count))
    slot_down = down - group_down * row_count
    same = group_across == group_down
    earlier = iota((row_count, row_count), 0) < iota((row_count, row_count), 1)
    later = iota((row_count, row_count), 1) < iota((row_count, row_count), 0)
    rank_across = jnp.sum(jnp.where(same & earlier, 1.0, 0.0), 0, keepdims=True)
    rank_down = jnp.sum(jnp.where(same & later, 1.0, 0.0), 1, keepdims=True)
    row_of = group_across[:1] * slots + rank_across
    places = iota((groups * slots, row_count), 0).astype(jnp.float32)
    pick = jnp.where(places == row_of, 1.0, 0.0).astype(jnp.bfloat16)
    lane = iota((row_count, hidden), 1).astype(jnp.float32)
    shift = 0.0
    if one_product(groups * spans, slots, hidden):
        device = lax.axis_index("grp") * spans + lax.axis_index("span")
        shift = (device * slots).astype(jnp.float32)
    at_rank = lane == rank_down + shift
    label_row = iota((slots, hidden), 0) == capacity
    labels = []
    for g in range(groups):
        hit = at_rank & (group_down[:, :1] == g)
        labels.append(jnp.sum(jnp.where(hit, slot_down[:, :1] + 1.0, 0.0), 0, keepdims=True) - 1.0)
    copies[1].wait()
    for n, (at, step) in enumerate(steps):
        turned = rows_ref[:, at : at + step].astype(jnp.float32).T.astype(jnp.bfloat16)
        copies[2 + n].wait()
        product = dot(held[:, at : at + step], turned, NN)
        total_ref[...] = product if n == 0 else total_ref[...] + product
    outgoing = []
    for s in range(spans):
        part = total_ref[s * hidden : (s + 1) * hidden].astype(jnp.bfloat16)
        moved = dot(pick, part, NT)
        for g in range(groups):
            piece = jnp.where(label_row, labels[g], moved[g * slots : (g + 1) * slots])
            pieces_ref[s, g] = piece.astype(jnp.bfloat16)
        copy = pltpu.make_async_copy(pieces_ref.at[s], out_hbm.at[:, s], out_sems.at[s])
        copy.start()
        outgoing.append(copy)
    for copy in outgoing:
        copy.wait()


def down_pieces(dest, rows, weight, groups, spans):
    row_count = rows.shape[0]
    capacity, slots = padded_slots(row_count, groups)
    hidden = weight.shape[0] // spans
    depth = weight.shape[1]
    edges = [depth * i // 8 for i in (0, 1, 3, 5, 8)]
    steps = [(i, j - i) for i, j in zip(edges, edges[1:])]
    pieces = pl.pallas_call(
        functools.partial(down_kernel, groups, spans, capacity, slots, steps),
        out_shape=jax.ShapeDtypeStruct((groups, spans, slots, hidden), jnp.bfloat16),
        in_specs=in_hbm(3),
        out_specs=in_hbm(1)[0],
        scratch_shapes=[
            pltpu.VMEM((1, row_count), jnp.int32),
            pltpu.VMEM(rows.shape, jnp.bfloat16),
            pltpu.VMEM(weight.shape, jnp.bfloat16),
            pltpu.VMEM((weight.shape[0], row_count), jnp.float32),
            pltpu.VMEM((spans, groups, slots, hidden), jnp.bfloat16),
            pltpu.SemaphoreType.DMA((2 + len(steps),)),
            pltpu.SemaphoreType.DMA((spans,)),
        ],
        compiler_params=params(60),
        name="down_product",
    )(dest.reshape(1, row_count), rows, weight)
    return pieces.reshape(groups * spans, slots, hidden)


def up_kernel(heads, capacity, pieces_ref, pre_ref, weight_ref, send_hbm, keep_hbm, held, out_ref,
              sems, out_sems):
    row_count, hidden = pre_ref.shape
    count, slots, _ = pieces_ref.shape
    width = weight_ref.shape[0] // (4 * heads)
    spans = lax.axis_size("span")
    core = lax.axis_index("core")
    half = heads // 2

    def head_of(n):
        chip, span = (n % half) // spans, n % spans
        return (chip * 2 + (1 - core if n < half else core)) * spans + span

    copies = []
    for h in range(heads):
        for j in range(4):
            start = pl.multiple_of((j * heads + head_of(h)) * width, width)
            copy = pltpu.make_async_copy(
                weight_ref.at[pl.ds(start, width)],
                held.at[h, pl.ds(j * width, width)],
                sems.at[h * 4 + j],
            )
            copy.start()
            copies.append(copy)
    label_at = slice(capacity, capacity + 1)
    if one_product(count, slots, hidden):
        pieces = [pieces_ref[p].astype(jnp.float32) for p in range(count)]
        labels = functools.reduce(jnp.maximum, [x[label_at, : count * slots] for x in pieces])
        row = iota((row_count, count * slots), 0).astype(jnp.float32)
        put = jnp.where(row == labels, 1.0, 0.0).astype(jnp.bfloat16)
        total = dot(put, jnp.concatenate(pieces, 0).astype(jnp.bfloat16), NN)
    else:
        row = iota((row_count, slots), 0).astype(jnp.float32)

        def placed(p, total):
            piece = pieces_ref[p]
            labels = piece.astype(jnp.float32)[label_at, :slots]
            put = jnp.where(row == labels, 1.0, 0.0).astype(jnp.bfloat16)
            return total + dot(put, piece, NN)

        total = lax.fori_loop(0, count, placed, jnp.zeros((row_count, hidden), jnp.float32))
    pre = pre_ref[...].astype(jnp.float32)
    cdf = 0.5 * (1.0 + lax.erf(pre * 0.7071067811865476))
    slope = cdf + pre * jnp.exp(-0.5 * pre * pre) * 0.3989422804014327
    grad_pre = (total * slope).T.astype(jnp.bfloat16)
    width = 4 * width
    outgoing = []

    def send(h, products):
        for i in range(2):
            part = products[i * width : (i + 1) * width]
            out_ref[h + i] = part.T.astype(jnp.bfloat16)
        out_hbm = send_hbm if h < half else keep_hbm
        copy = pltpu.make_async_copy(
            out_ref.at[pl.ds(h, 2)], out_hbm.at[pl.ds(h % half, 2)], out_sems.at[h // 2]
        )
        outgoing.append(copy)
        outgoing[-1].start()

    waiting = None
    for h in range(0, heads, 2):
        for copy in copies[h * 4 : h * 4 + 8]:
            copy.wait()
        product = dot(held[h : h + 2].reshape(2 * width, hidden), grad_pre, NN)
        if waiting is not None:
            send(h - 2, waiting)
        waiting = product
    send(heads - 2, waiting)
    for copy in outgoing:
        copy.wait()


def up_pieces(pieces, pre, weight, heads, capacity):
    width = weight.shape[0] // heads
    return pl.pallas_call(
        functools.partial(up_kernel, heads, capacity),
        out_shape=[jax.ShapeDtypeStruct((heads // 2, pre.shape[0], width), jnp.bfloat16)] * 2,
        in_specs=in_vmem(2) + in_hbm(1),
        out_specs=in_hbm(2),
        scratch_shapes=[
            pltpu.VMEM((heads, width, weight.shape[1]), jnp.bfloat16),
            pltpu.VMEM((heads, pre.shape[0], width), jnp.bfloat16),
            pltpu.SemaphoreType.DMA((heads * 4,)),
            pltpu.SemaphoreType.DMA((heads // 2,)),
        ],
        compiler_params=params(52),
        cost_estimate=pl.CostEstimate(
            flops=8 * pre.shape[0] * weight.size, bytes_accessed=8 * weight.size, transcendentals=0
        ),
        name="up_product",
    )(pieces, pre, weight)


class Rows:
    def __init__(self, columns, patches):
        heads = columns // HEAD_DIM
        self.lanes = -(-3 * patches // 128) * 128
        self.side_lanes = -(-2 * patches // 128) * 128
        self.columns, self.patches = columns, patches
        self.values, self.keys, self.queries, self.attended = [i * columns for i in range(4)]
        self.probs_at = 4 * columns
        self.side_at = self.probs_at + heads * patches
        self.total = self.side_at + heads * patches

    def head(self, start, h):
        return slice(start + h * HEAD_DIM, start + (h + 1) * HEAD_DIM)

    def kind(self, start, count=1):
        return slice(start, start + count * self.columns)

    def probs(self, h):
        return slice(self.probs_at + h * self.patches, self.probs_at + (h + 1) * self.patches)

    def side_probs(self, h):
        return slice(self.side_at + h * self.patches, self.side_at + (h + 1) * self.patches)


def softmax_kernel(lengths_ref, first_ref, own_ref, before_ref, after_ref, out_hbm, done_ref, held,
                   sems):
    columns, patches = own_ref.shape[0] // 3, own_ref.shape[1]
    heads = columns // HEAD_DIM
    rows = Rows(columns, patches)
    blocks = (own_ref, before_ref, after_ref)
    first = first_ref[0, 0]

    def image_of(shape, dim, block):
        token = iota(shape, dim) // 4 + (first + block * (patches // 4))

        def step(i, state):
            image, bound = state
            bound = bound + lengths_ref[0, i]
            return image + jnp.where(token >= bound, 1, 0), bound

        start = (jnp.where(token < 0, -1, 0), jnp.int32(0))
        return lax.fori_loop(0, lengths_ref.shape[1], step, start)[0]

    down = [image_of((patches, 1), 0, b) for b in (0, -1, 1)]
    across = [image_of((1, patches), 1, b) for b in (0, -1, 1)]
    all_keys = jnp.concatenate(across, 1)
    same_own = down[0] == all_keys
    copies = []

    def send(part, lanes):
        at = (pl.ds(part.start, part.stop - part.start), pl.ds(0, lanes))
        copy = pltpu.make_async_copy(held.at[at], out_hbm.at[at], sems.at[len(copies)])
        copy.start()
        copies.append(copy)

    def kind(block, t, h=None):
        start = t * columns + (0 if h is None else h * HEAD_DIM)
        return blocks[block][start : start + (columns if h is None else HEAD_DIM)]

    def wide(t, which):
        return jnp.concatenate([kind(b, t).astype(jnp.float32) for b in which], 1).astype(jnp.bfloat16)

    held[rows.kind(rows.values), : 3 * patches] = wide(2, (0, 1, 2))
    held[rows.kind(rows.keys), : 3 * patches] = wide(1, (0, 1, 2))
    held[rows.kind(rows.queries), : 2 * patches] = wide(0, (1, 2))
    send(rows.kind(rows.values, 2), rows.lanes)
    send(rows.kind(rows.queries), rows.side_lanes)
    for h in range(heads):
        keys = held[rows.head(rows.keys, h), : 3 * patches]
        scores = dot(kind(0, 0, h), keys, TN) * SCALE
        scores = jnp.where(same_own, scores, -jnp.inf)
        weights = jnp.exp(scores - jnp.max(scores, 1, keepdims=True))
        over = 1.0 / jnp.sum(weights, 1, keepdims=True)
        held[rows.probs(h), : 3 * patches] = (weights * over).astype(jnp.bfloat16)
        send(rows.probs(h), rows.lanes)
    for h in range(heads):
        own_keys = kind(0, 1, h).astype(jnp.float32).T.astype(jnp.bfloat16)
        side, attended = [], []
        for b in (1, 2):
            queries = kind(b, 0, h)
            keys = kind(b, 1, h).astype(jnp.float32).T.astype(jnp.bfloat16)
            scores = []
            for n, k in ((0, own_keys), (b, keys)):
                scores.append(jnp.where(down[n] == across[b], dot(k, queries, NN) * SCALE, -jnp.inf))
            top = functools.reduce(jnp.maximum, [jnp.max(x, 0, keepdims=True) for x in scores])
            weights = [jnp.exp(x - top) for x in scores]
            over = 1.0 / sum([jnp.sum(w, 0, keepdims=True) for w in weights])
            probs = [(w * over).astype(jnp.bfloat16) for w in weights]
            attended.append(dot(kind(0, 2, h), probs[0], NN) + dot(kind(b, 2, h), probs[1], NN))
            side.append(probs[0].astype(jnp.float32))
        held[rows.side_probs(h), : 2 * patches] = jnp.concatenate(side, 1).astype(jnp.bfloat16)
        send(rows.side_probs(h), rows.side_lanes)
        attended = jnp.concatenate(attended, 1).astype(jnp.bfloat16)
        held[rows.head(rows.attended, h), : 2 * patches] = attended
    send(rows.kind(rows.attended), rows.side_lanes)
    for copy in copies:
        copy.wait()
    done_ref[...] = jnp.zeros(done_ref.shape, jnp.float32)


def softmax_parts(lengths, first, own, before, after):
    columns, patches = own.shape[0] // 3, own.shape[1]
    heads = columns // HEAD_DIM
    rows = Rows(columns, patches)
    smem = pl.BlockSpec(memory_space=pltpu.MemorySpace.SMEM)
    work = heads * patches * patches
    return pl.pallas_call(
        softmax_kernel,
        out_shape=(
            jax.ShapeDtypeStruct((rows.total, rows.lanes), jnp.bfloat16),
            jax.ShapeDtypeStruct((8, 128), jnp.float32),
        ),
        in_specs=[smem, smem] + in_vmem(3),
        out_specs=tuple(in_hbm(1) + in_vmem(1)),
        scratch_shapes=[
            pltpu.VMEM((rows.total, rows.lanes), jnp.bfloat16),
            pltpu.SemaphoreType.DMA((3 + 2 * heads,)),
        ],
        compiler_params=params(52),
        cost_estimate=pl.CostEstimate(
            flops=100_000 * work, bytes_accessed=500 * work, transcendentals=9 * work
        ),
        name="softmax_parts",
    )(lengths.reshape(1, -1), first.reshape(1, 1), own, before, after)


def gather_kernel(pieces_ref, _, out_ref):
    count, row_count, width = pieces_ref.shape
    total = pieces_ref[0].astype(jnp.float32)
    for p in range(1, count):
        total = total + pieces_ref[p].astype(jnp.float32)
    total = total.astype(jnp.bfloat16)
    columns = width // 4
    patch = iota((row_count, 4 * row_count), 1)
    token = iota((row_count, 4 * row_count), 0)
    result = jnp.zeros((columns, 4 * row_count), jnp.float32)
    for j in range(4):
        put = jnp.where(patch == 4 * token + j, 1.0, 0.0).astype(jnp.bfloat16)
        result = result + dot(total[:, j * columns : (j + 1) * columns], put, TN)
    out_ref[...] = result.astype(jnp.bfloat16)


def gathered(pieces, later):
    _, row_count, width = pieces.shape
    return pl.pallas_call(
        gather_kernel,
        out_shape=jax.ShapeDtypeStruct((width // 4, 4 * row_count), jnp.bfloat16),
        in_specs=in_vmem(2),
        out_specs=pl.BlockSpec(memory_space=VMEM),
        compiler_params=params(16),
        cost_estimate=pl.CostEstimate(
            flops=20_000 * pieces.size, bytes_accessed=400 * pieces.size, transcendentals=0
        ),
        name="gather_sum",
    )(pieces, later)


def own_kernel(grad_ref, own_ref, held_ref, query_ref, key_ref, value_ref):
    columns, patches = grad_ref.shape
    rows = Rows(columns, patches)
    for h in range(columns // HEAD_DIM):
        cols = slice(h * HEAD_DIM, (h + 1) * HEAD_DIM)
        grad = grad_ref[cols]
        slope = dot(grad, held_ref[rows.head(rows.values, h), : 3 * patches], TN)
        probs = held_ref[rows.probs(h), : 3 * patches]
        wide = probs.astype(jnp.float32)
        delta = jnp.sum(wide * slope, 1, keepdims=True)
        scores = (wide * (slope - delta)).astype(jnp.bfloat16)
        query = dot(scores, held_ref[rows.head(rows.keys, h), : 3 * patches], NT) * SCALE
        query_ref[cols] = query.T.astype(jnp.bfloat16)
        key_ref[cols] = dot(own_ref[cols], scores[:, :patches], NN)
        value_ref[cols] = dot(grad, probs[:, :patches], NN)


def own_terms(grad, own, held):
    return pl.pallas_call(
        own_kernel,
        out_shape=(
            jax.ShapeDtypeStruct(grad.shape, jnp.bfloat16),
            jax.ShapeDtypeStruct(grad.shape, jnp.float32),
            jax.ShapeDtypeStruct(grad.shape, jnp.float32),
        ),
        in_specs=in_vmem(3),
        out_specs=tuple(in_vmem(3)),
        compiler_params=params(24),
        name="own_terms",
    )(grad, own, held)


def side_kernel(even_ref, odd_ref, key_part_ref, value_part_ref, held_ref, key_ref, value_ref):
    columns, patches = even_ref.shape
    is_even = lax.rem(lax.axis_index("grp"), 2) == 0
    rows = Rows(columns, patches)
    lanes = slice(0, 2 * patches)
    for h in range(columns // HEAD_DIM):
        cols = slice(h * HEAD_DIM, (h + 1) * HEAD_DIM)
        even, odd = even_ref[cols].astype(jnp.float32), odd_ref[cols].astype(jnp.float32)
        left, right = jnp.where(is_even, odd, even), jnp.where(is_even, even, odd)
        wide = jnp.concatenate([left, right], 1)
        grad = wide.astype(jnp.bfloat16)
        slope = dot(held_ref[rows.head(rows.values, h), :patches], grad, TN)
        attended = held_ref[rows.head(rows.attended, h), lanes].astype(jnp.float32)
        delta = jnp.sum(wide * attended, 0, keepdims=True)
        probs = held_ref[rows.side_probs(h), lanes]
        value = dot(probs, grad, NT)
        scores = (probs.astype(jnp.float32) * (slope - delta)).astype(jnp.bfloat16)
        key = dot(scores, held_ref[rows.head(rows.queries, h), lanes], NT)
        key_ref[cols] = ((key_part_ref[cols] + key.T) * SCALE).astype(jnp.bfloat16)
        value_ref[cols] = (value_part_ref[cols] + value.T).astype(jnp.bfloat16)


def side_terms(even, odd, key_part, value_part, held):
    shape = jax.ShapeDtypeStruct(even.shape, jnp.bfloat16)
    return pl.pallas_call(
        side_kernel,
        out_shape=(shape, shape),
        in_specs=in_vmem(5),
        out_specs=tuple(in_vmem(2)),
        compiler_params=params(24),
        name="side_terms",
    )(even, odd, key_part, value_part, held)


def from_both_sides(x, axis):
    size = lax.axis_size(axis)
    up = [(i, i + 1) for i in range(size - 1)]
    return (
        lax.ppermute(x, axis, up),
        lax.ppermute(x, axis, [(j, i) for i, j in up]),
    )


def from_pairs(x, axis):
    size = lax.axis_size(axis)

    def swapped(first):
        low = range(first, size - 1, 2)
        pairs = [(i, i + 1) for i in low] + [(i + 1, i) for i in low]
        alone = set(range(size)) - {i for i, _ in pairs}
        return lax.ppermute(x, axis, pairs + [(i, i) for i in sorted(alone)])

    return swapped(0), swapped(1)


def on_device(
    grad_out, destination, w_down, pre_act, w_up, queries, key_states, value_states, lengths
):
    groups = lax.axis_size("grp")
    spans = lax.axis_size("span")
    heads = lax.axis_size(("chip", "core", "span"))
    row_count = grad_out.shape[0]
    capacity, _ = padded_slots(row_count, groups)
    pieces = down_pieces(destination, grad_out, w_down, groups, spans)
    pieces, queries, key_states, value_states = lax.optimization_barrier(
        (pieces, queries, key_states, value_states)
    )
    arrived = lax.all_to_all(pieces, ("grp", "span"), split_axis=0, concat_axis=0, tiled=True)
    own = jnp.concatenate([queries.T, key_states.T, value_states.T], 0)
    before, after = from_both_sides(own, "grp")
    first = lax.axis_index("grp") * row_count
    other, shares = up_pieces(arrived, pre_act, w_up, heads, capacity)
    other = lax.ppermute(other, "core", [(0, 1), (1, 0)])
    shares = (other.astype(jnp.float32) + shares.astype(jnp.float32)).astype(jnp.bfloat16)
    shares, own = lax.optimization_barrier((shares, own))
    held, held_done = softmax_parts(lengths, first, own, before, after)
    shares = lax.all_to_all(shares, ("chip", "span"), split_axis=0, concat_axis=0, tiled=True)
    grad = gathered(shares, held_done)
    even, odd = from_pairs(grad, "grp")
    grad_query, key_part, value_part = own_terms(grad, queries.T, held)
    grad_key, grad_value = side_terms(even, odd, key_part, value_part, held)
    return grad_query.T, grad_key.T, grad_value.T


def solution(mesh):
    sect, grp, span = (mesh.shape[name] for name in ("sect", "grp", "span"))
    finer = jax.sharding.Mesh(
        mesh.devices.reshape(sect // 2, 2, grp, span), ("chip", "core", "grp", "span")
    )
    split = P("grp", ("chip", "core", "span"))
    placed = (
        P("grp", "span"),
        P("grp"),
        P(("chip", "core"), "span"),
        split,
        P(None, ("chip", "core", "span")),
        split,
        split,
        split,
        P(),
    )
    return jax.shard_map(
        on_device,
        mesh=finer,
        in_specs=placed,
        out_specs=(split, split, split),
        check_vma=False,
    )
```

```python
import functools

import jax
import jax.numpy as jnp
from jax import lax
from jax.experimental import pallas as pl
from jax.experimental.pallas import tpu as pltpu
from jax.sharding import PartitionSpec as P

HEAD_DIM = 80
SCALE = HEAD_DIM**-0.5
MIB = 1024 * 1024
VMEM = pltpu.MemorySpace.VMEM
NT = (((1,), (1,)), ((), ()))
NN = (((1,), (0,)), ((), ()))
TN = (((0,), (0,)), ((), ()))


def dot(a, b, dims):
    return lax.dot_general(a, b, dims, preferred_element_type=jnp.float32)


def iota(shape, dim):
    return lax.broadcasted_iota(jnp.int32, shape, dim)


def params(mib):
    return pltpu.CompilerParams(vmem_limit_bytes=mib * MIB)


def in_vmem(count):
    return [pl.BlockSpec(memory_space=VMEM) for _ in range(count)]


def in_hbm(count):
    return [pl.BlockSpec(memory_space=pltpu.MemorySpace.HBM) for _ in range(count)]


def fetched(pairs, sems):
    copies = [pltpu.make_async_copy(a, b, sems.at[i]) for i, (a, b) in enumerate(pairs)]
    for copy in copies:
        copy.start()
    return copies


def padded_slots(row_count, groups):
    offsets = min(groups, row_count // 2)
    capacity = row_count // offsets
    return capacity, -(-(capacity + 1) // 8) * 8


def one_product(count, slots, hidden):
    return count * slots <= hidden


def down_kernel(groups, spans, capacity, slots, steps, dest_hbm, rows_hbm, weight_ref, out_hbm,
                dest_ref, rows_ref, held, total_ref, pieces_ref, sems, out_sems):
    row_count = rows_ref.shape[0]
    hidden = weight_ref.shape[0] // spans
    everything = pl.ds(0, weight_ref.shape[0])
    pairs = [(dest_hbm, dest_ref), (rows_hbm, rows_ref)]
    for at, step in steps:
        part = (everything, pl.ds(at, step))
        pairs.append((weight_ref.at[part], held.at[part]))
    copies = fetched(pairs, sems)
    copies[0].wait()
    across = jnp.broadcast_to(dest_ref[...].astype(jnp.float32), (row_count, row_count))
    down = across.T
    group_across = jnp.floor((across + 0.5) * (1.0 / row_count))
    group_down = jnp.floor((down + 0.5) * (1.0 / row_count))
    slot_down = down - group_down * row_count
    same = group_across == group_down
    earlier = iota((row_count, row_count), 0) < iota((row_count, row_count), 1)
    later = iota((row_count, row_count), 1) < iota((row_count, row_count), 0)
    rank_across = jnp.sum(jnp.where(same & earlier, 1.0, 0.0), 0, keepdims=True)
    rank_down = jnp.sum(jnp.where(same & later, 1.0, 0.0), 1, keepdims=True)
    row_of = group_across[:1] * slots + rank_across
    places = iota((groups * slots, row_count), 0).astype(jnp.float32)
    pick = jnp.where(places == row_of, 1.0, 0.0).astype(jnp.bfloat16)
    lane = iota((row_count, hidden), 1).astype(jnp.float32)
    shift = 0.0
    if one_product(groups * spans, slots, hidden):
        device = lax.axis_index("grp") * spans + lax.axis_index("span")
        shift = (device * slots).astype(jnp.float32)
    at_rank = lane == rank_down + shift
    label_row = iota((slots, hidden), 0) == capacity
    labels = []
    for g in range(groups):
        hit = at_rank & (group_down[:, :1] == g)
        labels.append(jnp.sum(jnp.where(hit, slot_down[:, :1] + 1.0, 0.0), 0, keepdims=True) - 1.0)
    copies[1].wait()
    for n, (at, step) in enumerate(steps):
        turned = rows_ref[:, at : at + step].astype(jnp.float32).T.astype(jnp.bfloat16)
        copies[2 + n].wait()
        product = dot(held[:, at : at + step], turned, NN)
        total_ref[...] = product if n == 0 else total_ref[...] + product
    outgoing = []
    for s in range(spans):
        part = total_ref[s * hidden : (s + 1) * hidden].astype(jnp.bfloat16)
        moved = dot(pick, part, NT)
        for g in range(groups):
            piece = jnp.where(label_row, labels[g], moved[g * slots : (g + 1) * slots])
            pieces_ref[s, g] = piece.astype(jnp.bfloat16)
        copy = pltpu.make_async_copy(pieces_ref.at[s], out_hbm.at[:, s], out_sems.at[s])
        copy.start()
        outgoing.append(copy)
    for copy in outgoing:
        copy.wait()


def down_pieces(dest, rows, weight, groups, spans):
    row_count = rows.shape[0]
    capacity, slots = padded_slots(row_count, groups)
    hidden = weight.shape[0] // spans
    depth = weight.shape[1]
    edges = [depth * i // 8 for i in (0, 1, 3, 5, 8)]
    steps = [(i, j - i) for i, j in zip(edges, edges[1:])]
    pieces = pl.pallas_call(
        functools.partial(down_kernel, groups, spans, capacity, slots, steps),
        out_shape=jax.ShapeDtypeStruct((groups, spans, slots, hidden), jnp.bfloat16),
        in_specs=in_hbm(3),
        out_specs=in_hbm(1)[0],
        scratch_shapes=[
            pltpu.VMEM((1, row_count), jnp.int32),
            pltpu.VMEM(rows.shape, jnp.bfloat16),
            pltpu.VMEM(weight.shape, jnp.bfloat16),
            pltpu.VMEM((weight.shape[0], row_count), jnp.float32),
            pltpu.VMEM((spans, groups, slots, hidden), jnp.bfloat16),
            pltpu.SemaphoreType.DMA((2 + len(steps),)),
            pltpu.SemaphoreType.DMA((spans,)),
        ],
        compiler_params=params(60),
        name="down_product",
    )(dest.reshape(1, row_count), rows, weight)
    return pieces.reshape(groups * spans, slots, hidden)


def up_kernel(heads, capacity, pieces_ref, pre_ref, weight_ref, send_hbm, keep_hbm, held, out_ref,
              sems, out_sems):
    row_count, hidden = pre_ref.shape
    count, slots, _ = pieces_ref.shape
    width = weight_ref.shape[0] // (4 * heads)
    spans = lax.axis_size("span")
    core = lax.axis_index("core")
    half = heads // 2

    me = lax.axis_index("chip") * spans + lax.axis_index("span")

    def head_of(n):
        place = lax.bitwise_xor(me, n % half)
        chip, span = lax.div(place, spans), lax.rem(place, spans)
        return (chip * 2 + (1 - core if n < half else core)) * spans + span

    copies = []
    for h in range(heads):
        for j in range(4):
            start = pl.multiple_of((j * heads + head_of(h)) * width, width)
            copy = pltpu.make_async_copy(
                weight_ref.at[pl.ds(start, width)],
                held.at[h, pl.ds(j * width, width)],
                sems.at[h * 4 + j],
            )
            copy.start()
            copies.append(copy)
    label_at = slice(capacity, capacity + 1)
    if one_product(count, slots, hidden):
        pieces = [pieces_ref[p].astype(jnp.float32) for p in range(count)]
        labels = functools.reduce(jnp.maximum, [x[label_at, : count * slots] for x in pieces])
        row = iota((row_count, count * slots), 0).astype(jnp.float32)
        put = jnp.where(row == labels, 1.0, 0.0).astype(jnp.bfloat16)
        total = dot(put, jnp.concatenate(pieces, 0).astype(jnp.bfloat16), NN)
    else:
        row = iota((row_count, slots), 0).astype(jnp.float32)

        def placed(p, total):
            piece = pieces_ref[p]
            labels = piece.astype(jnp.float32)[label_at, :slots]
            put = jnp.where(row == labels, 1.0, 0.0).astype(jnp.bfloat16)
            return total + dot(put, piece, NN)

        total = lax.fori_loop(0, count, placed, jnp.zeros((row_count, hidden), jnp.float32))
    pre = pre_ref[...].astype(jnp.float32)
    cdf = 0.5 * (1.0 + lax.erf(pre * 0.7071067811865476))
    slope = cdf + pre * jnp.exp(-0.5 * pre * pre) * 0.3989422804014327
    grad_pre = (total * slope).T.astype(jnp.bfloat16)
    width = 4 * width
    outgoing = []

    def send(h, products):
        for i in range(2):
            part = products[i * width : (i + 1) * width]
            out_ref[h + i] = part.T.astype(jnp.bfloat16)
        out_hbm = send_hbm if h < half else keep_hbm
        copy = pltpu.make_async_copy(
            out_ref.at[pl.ds(h, 2)], out_hbm.at[pl.ds(h % half, 2)], out_sems.at[h // 2]
        )
        outgoing.append(copy)
        outgoing[-1].start()

    waiting = None
    for h in range(0, heads, 2):
        for copy in copies[h * 4 : h * 4 + 8]:
            copy.wait()
        product = dot(held[h : h + 2].reshape(2 * width, hidden), grad_pre, NN)
        if waiting is not None:
            send(h - 2, waiting)
        waiting = product
    send(heads - 2, waiting)
    for copy in outgoing:
        copy.wait()


def up_pieces(pieces, pre, weight, heads, capacity):
    width = weight.shape[0] // heads
    return pl.pallas_call(
        functools.partial(up_kernel, heads, capacity),
        out_shape=[jax.ShapeDtypeStruct((heads // 2, pre.shape[0], width), jnp.bfloat16)] * 2,
        in_specs=in_vmem(2) + in_hbm(1),
        out_specs=in_hbm(2),
        scratch_shapes=[
            pltpu.VMEM((heads, width, weight.shape[1]), jnp.bfloat16),
            pltpu.VMEM((heads, pre.shape[0], width), jnp.bfloat16),
            pltpu.SemaphoreType.DMA((heads * 4,)),
            pltpu.SemaphoreType.DMA((heads // 2,)),
        ],
        compiler_params=params(52),
        cost_estimate=pl.CostEstimate(
            flops=8 * pre.shape[0] * weight.size, bytes_accessed=8 * weight.size, transcendentals=0
        ),
        name="up_product",
    )(pieces, pre, weight)


class Rows:
    def __init__(self, columns, patches):
        heads = columns // HEAD_DIM
        self.lanes = -(-3 * patches // 128) * 128
        self.side_lanes = -(-2 * patches // 128) * 128
        self.columns, self.patches = columns, patches
        self.values, self.keys, self.queries, self.attended = [i * columns for i in range(4)]
        self.probs_at = 4 * columns
        self.side_at = self.probs_at + heads * patches
        self.total = self.side_at + heads * patches

    def head(self, start, h):
        return slice(start + h * HEAD_DIM, start + (h + 1) * HEAD_DIM)

    def kind(self, start, count=1):
        return slice(start, start + count * self.columns)

    def probs(self, h):
        return slice(self.probs_at + h * self.patches, self.probs_at + (h + 1) * self.patches)

    def side_probs(self, h):
        return slice(self.side_at + h * self.patches, self.side_at + (h + 1) * self.patches)


def softmax_kernel(lengths_ref, first_ref, own_ref, even_ref, odd_ref, out_hbm, done_ref, held,
                   sems):
    columns, patches = own_ref.shape[0] // 3, own_ref.shape[1]
    heads = columns // HEAD_DIM
    rows = Rows(columns, patches)
    is_even = lax.rem(lax.axis_index("grp"), 2) == 0
    first = first_ref[0, 0]

    def image_of(shape, dim, block):
        token = iota(shape, dim) // 4 + (first + block * (patches // 4))

        def step(i, state):
            image, bound = state
            bound = bound + lengths_ref[0, i]
            return image + jnp.where(token >= bound, 1, 0), bound

        start = (jnp.where(token < 0, -1, 0), jnp.int32(0))
        return lax.fori_loop(0, lengths_ref.shape[1], step, start)[0]

    down = [image_of((patches, 1), 0, b) for b in (0, -1, 1)]
    across = [image_of((1, patches), 1, b) for b in (0, -1, 1)]
    all_keys = jnp.concatenate(across, 1)
    same_own = down[0] == all_keys
    copies = []

    def send(part, lanes):
        at = (pl.ds(part.start, part.stop - part.start), pl.ds(0, lanes))
        copy = pltpu.make_async_copy(held.at[at], out_hbm.at[at], sems.at[len(copies)])
        copy.start()
        copies.append(copy)

    def kind(block, t, h=None):
        start = t * columns + (0 if h is None else h * HEAD_DIM)
        at = slice(start, start + (columns if h is None else HEAD_DIM))
        if block == 0:
            return own_ref[at]
        before, after = (odd_ref, even_ref) if block == 1 else (even_ref, odd_ref)
        return jnp.where(is_even, before[at], after[at])

    def wide(t, which):
        return jnp.concatenate([kind(b, t).astype(jnp.float32) for b in which], 1).astype(jnp.bfloat16)

    held[rows.kind(rows.values), : 3 * patches] = wide(2, (0, 1, 2))
    held[rows.kind(rows.keys), : 3 * patches] = wide(1, (0, 1, 2))
    held[rows.kind(rows.queries), : 2 * patches] = wide(0, (1, 2))
    send(rows.kind(rows.values, 2), rows.lanes)
    send(rows.kind(rows.queries), rows.side_lanes)
    for h in range(heads):
        keys = held[rows.head(rows.keys, h), : 3 * patches]
        scores = dot(kind(0, 0, h), keys, TN) * SCALE
        scores = jnp.where(same_own, scores, -jnp.inf)
        weights = jnp.exp(scores - jnp.max(scores, 1, keepdims=True))
        over = 1.0 / jnp.sum(weights, 1, keepdims=True)
        held[rows.probs(h), : 3 * patches] = (weights * over).astype(jnp.bfloat16)
        send(rows.probs(h), rows.lanes)
    for h in range(heads):
        own_keys = kind(0, 1, h).astype(jnp.float32).T.astype(jnp.bfloat16)
        side, attended = [], []
        for b in (1, 2):
            queries = kind(b, 0, h)
            keys = kind(b, 1, h).astype(jnp.float32).T.astype(jnp.bfloat16)
            scores = []
            for n, k in ((0, own_keys), (b, keys)):
                scores.append(jnp.where(down[n] == across[b], dot(k, queries, NN) * SCALE, -jnp.inf))
            top = functools.reduce(jnp.maximum, [jnp.max(x, 0, keepdims=True) for x in scores])
            weights = [jnp.exp(x - top) for x in scores]
            over = 1.0 / sum([jnp.sum(w, 0, keepdims=True) for w in weights])
            probs = [(w * over).astype(jnp.bfloat16) for w in weights]
            attended.append(dot(kind(0, 2, h), probs[0], NN) + dot(kind(b, 2, h), probs[1], NN))
            side.append(probs[0].astype(jnp.float32))
        held[rows.side_probs(h), : 2 * patches] = jnp.concatenate(side, 1).astype(jnp.bfloat16)
        send(rows.side_probs(h), rows.side_lanes)
        attended = jnp.concatenate(attended, 1).astype(jnp.bfloat16)
        held[rows.head(rows.attended, h), : 2 * patches] = attended
    send(rows.kind(rows.attended), rows.side_lanes)
    for copy in copies:
        copy.wait()
    done_ref[...] = jnp.zeros(done_ref.shape, jnp.float32)


def softmax_parts(lengths, first, own, even, odd):
    columns, patches = own.shape[0] // 3, own.shape[1]
    heads = columns // HEAD_DIM
    rows = Rows(columns, patches)
    smem = pl.BlockSpec(memory_space=pltpu.MemorySpace.SMEM)
    work = heads * patches * patches
    return pl.pallas_call(
        softmax_kernel,
        out_shape=(
            jax.ShapeDtypeStruct((rows.total, rows.lanes), jnp.bfloat16),
            jax.ShapeDtypeStruct((8, 128), jnp.float32),
        ),
        in_specs=[smem, smem] + in_vmem(3),
        out_specs=tuple(in_hbm(1) + in_vmem(1)),
        scratch_shapes=[
            pltpu.VMEM((rows.total, rows.lanes), jnp.bfloat16),
            pltpu.SemaphoreType.DMA((3 + 2 * heads,)),
        ],
        compiler_params=params(52),
        cost_estimate=pl.CostEstimate(
            flops=100_000 * work, bytes_accessed=500 * work, transcendentals=9 * work
        ),
        name="softmax_parts",
    )(lengths.reshape(1, -1), first.reshape(1, 1), own, even, odd)


def gather_kernel(count, *refs):
    _, row_count, width = refs[0].shape
    total = refs[0][0].astype(jnp.float32)
    for p in range(1, count):
        total = total + refs[p][0].astype(jnp.float32)
    out_ref = refs[-1]
    total = total.astype(jnp.bfloat16)
    columns = width // 4
    patch = iota((row_count, 4 * row_count), 1)
    token = iota((row_count, 4 * row_count), 0)
    result = jnp.zeros((columns, 4 * row_count), jnp.float32)
    for j in range(4):
        put = jnp.where(patch == 4 * token + j, 1.0, 0.0).astype(jnp.bfloat16)
        result = result + dot(total[:, j * columns : (j + 1) * columns], put, TN)
    out_ref[...] = result.astype(jnp.bfloat16)


def gathered(pieces, later):
    _, row_count, width = pieces[0].shape
    size = len(pieces) * row_count * width
    return pl.pallas_call(
        functools.partial(gather_kernel, len(pieces)),
        out_shape=jax.ShapeDtypeStruct((width // 4, 4 * row_count), jnp.bfloat16),
        in_specs=in_vmem(len(pieces) + 1),
        out_specs=pl.BlockSpec(memory_space=VMEM),
        compiler_params=params(16),
        cost_estimate=pl.CostEstimate(
            flops=20_000 * size, bytes_accessed=400 * size, transcendentals=0
        ),
        name="gather_sum",
    )(*pieces, later)


def own_kernel(grad_ref, own_ref, held_ref, query_ref, key_ref, value_ref):
    columns, patches = grad_ref.shape
    rows = Rows(columns, patches)
    for h in range(columns // HEAD_DIM):
        cols = slice(h * HEAD_DIM, (h + 1) * HEAD_DIM)
        grad = grad_ref[cols]
        slope = dot(grad, held_ref[rows.head(rows.values, h), : 3 * patches], TN)
        probs = held_ref[rows.probs(h), : 3 * patches]
        wide = probs.astype(jnp.float32)
        delta = jnp.sum(wide * slope, 1, keepdims=True)
        scores = (wide * (slope - delta)).astype(jnp.bfloat16)
        query = dot(scores, held_ref[rows.head(rows.keys, h), : 3 * patches], NT) * SCALE
        query_ref[cols] = query.T.astype(jnp.bfloat16)
        key_ref[cols] = dot(own_ref[cols], scores[:, :patches], NN)
        value_ref[cols] = dot(grad, probs[:, :patches], NN)


def own_terms(grad, own, held):
    return pl.pallas_call(
        own_kernel,
        out_shape=(
            jax.ShapeDtypeStruct(grad.shape, jnp.bfloat16),
            jax.ShapeDtypeStruct(grad.shape, jnp.float32),
            jax.ShapeDtypeStruct(grad.shape, jnp.float32),
        ),
        in_specs=in_vmem(3),
        out_specs=tuple(in_vmem(3)),
        compiler_params=params(24),
        name="own_terms",
    )(grad, own, held)


def side_kernel(even_ref, odd_ref, key_part_ref, value_part_ref, held_ref, key_ref, value_ref):
    columns, patches = even_ref.shape
    is_even = lax.rem(lax.axis_index("grp"), 2) == 0
    rows = Rows(columns, patches)
    lanes = slice(0, 2 * patches)
    for h in range(columns // HEAD_DIM):
        cols = slice(h * HEAD_DIM, (h + 1) * HEAD_DIM)
        even, odd = even_ref[cols].astype(jnp.float32), odd_ref[cols].astype(jnp.float32)
        left, right = jnp.where(is_even, odd, even), jnp.where(is_even, even, odd)
        wide = jnp.concatenate([left, right], 1)
        grad = wide.astype(jnp.bfloat16)
        slope = dot(held_ref[rows.head(rows.values, h), :patches], grad, TN)
        attended = held_ref[rows.head(rows.attended, h), lanes].astype(jnp.float32)
        delta = jnp.sum(wide * attended, 0, keepdims=True)
        probs = held_ref[rows.side_probs(h), lanes]
        value = dot(probs, grad, NT)
        scores = (probs.astype(jnp.float32) * (slope - delta)).astype(jnp.bfloat16)
        key = dot(scores, held_ref[rows.head(rows.queries, h), lanes], NT)
        key_ref[cols] = ((key_part_ref[cols] + key.T) * SCALE).astype(jnp.bfloat16)
        value_ref[cols] = (value_part_ref[cols] + value.T).astype(jnp.bfloat16)


def side_terms(even, odd, key_part, value_part, held):
    shape = jax.ShapeDtypeStruct(even.shape, jnp.bfloat16)
    return pl.pallas_call(
        side_kernel,
        out_shape=(shape, shape),
        in_specs=in_vmem(5),
        out_specs=tuple(in_vmem(2)),
        compiler_params=params(24),
        name="side_terms",
    )(even, odd, key_part, value_part, held)


def from_pairs(x):
    size = lax.axis_size("grp")

    def swapped(first):
        partner = {}
        for core in range(2):
            for i in range(size):
                j = i + 1 if (i - first) % 2 == 0 else i - 1
                pair = (core, j) if 0 <= j < size else (1 - core, i)
                partner[core * size + i] = pair[0] * size + pair[1]
        return lax.ppermute(x, ("core", "grp"), sorted(partner.items()))

    return swapped(0), swapped(1)


def exchanged(pieces, axes):
    count = pieces.shape[0]
    parts = [pieces[d : d + 1] for d in range(count)]
    return parts[:1] + [
        lax.ppermute(parts[d], axes, [(i, i ^ d) for i in range(count)]) for d in range(1, count)
    ]


def on_device(
    grad_out, destination, w_down, pre_act, w_up, queries, key_states, value_states, lengths
):
    groups = lax.axis_size("grp")
    spans = lax.axis_size("span")
    heads = lax.axis_size(("chip", "core", "span"))
    row_count = grad_out.shape[0]
    capacity, _ = padded_slots(row_count, groups)
    pieces = down_pieces(destination, grad_out, w_down, groups, spans)
    pieces, queries, key_states, value_states = lax.optimization_barrier(
        (pieces, queries, key_states, value_states)
    )
    arrived = lax.all_to_all(pieces, ("grp", "span"), split_axis=0, concat_axis=0, tiled=True)
    own = jnp.concatenate([queries.T, key_states.T, value_states.T], 0)
    sides = from_pairs(own)
    first = lax.axis_index("grp") * row_count
    other, shares = up_pieces(arrived, pre_act, w_up, heads, capacity)
    other, *sides = lax.optimization_barrier((other, *sides))
    other = lax.ppermute(other, "core", [(0, 1), (1, 0)])
    shares = (other.astype(jnp.float32) + shares.astype(jnp.float32)).astype(jnp.bfloat16)
    shares, own = lax.optimization_barrier((shares, own))
    held, held_done = softmax_parts(lengths, first, own, *sides)
    grad = gathered(exchanged(shares, ("chip", "span")), held_done)
    even, odd = from_pairs(grad)
    grad_query, key_part, value_part = own_terms(grad, queries.T, held)
    grad_key, grad_value = side_terms(even, odd, key_part, value_part, held)
    return grad_query.T, grad_key.T, grad_value.T


def solution(mesh):
    sect, grp, span = (mesh.shape[name] for name in ("sect", "grp", "span"))
    finer = jax.sharding.Mesh(
        mesh.devices.reshape(sect // 2, 2, grp, span), ("chip", "core", "grp", "span")
    )
    split = P("grp", ("chip", "core", "span"))
    placed = (
        P("grp", "span"),
        P("grp"),
        P(("chip", "core"), "span"),
        split,
        P(None, ("chip", "core", "span")),
        split,
        split,
        split,
        P(),
    )
    return jax.shard_map(
        on_device,
        mesh=finer,
        in_specs=placed,
        out_specs=(split, split, split),
        check_vma=False,
    )
```

```python
import functools

import jax
import jax.numpy as jnp
from jax import lax
from jax.experimental import pallas as pl
from jax.experimental.pallas import tpu as pltpu
from jax.sharding import PartitionSpec as P

HEAD_DIM = 80
SCALE = HEAD_DIM**-0.5
MIB = 1024 * 1024
VMEM = pltpu.MemorySpace.VMEM
NT = (((1,), (1,)), ((), ()))
NN = (((1,), (0,)), ((), ()))
TN = (((0,), (0,)), ((), ()))


def dot(a, b, dims):
    return lax.dot_general(a, b, dims, preferred_element_type=jnp.float32)


def iota(shape, dim):
    return lax.broadcasted_iota(jnp.int32, shape, dim)


def params(mib):
    return pltpu.CompilerParams(vmem_limit_bytes=mib * MIB)


def in_vmem(count):
    return [pl.BlockSpec(memory_space=VMEM) for _ in range(count)]


def in_hbm(count):
    return [pl.BlockSpec(memory_space=pltpu.MemorySpace.HBM) for _ in range(count)]


def fetched(pairs, sems):
    copies = [pltpu.make_async_copy(a, b, sems.at[i]) for i, (a, b) in enumerate(pairs)]
    for copy in copies:
        copy.start()
    return copies


def padded_slots(row_count, groups):
    offsets = min(groups, row_count // 2)
    capacity = row_count // offsets
    return capacity, -(-(capacity + 1) // 8) * 8


def by_swaps(count, slots, hidden):
    return count in (2, 4, 8, 16) and count * slots <= hidden


def down_kernel(groups, spans, capacity, slots, steps, dest_hbm, rows_hbm, weight_ref, *refs):
    *outs, dest_ref, rows_ref, held, total_ref, pieces_ref, sems, out_sems = refs
    count = groups * spans
    me = lax.axis_index("grp") * spans + lax.axis_index("span")
    row_count = rows_ref.shape[0]
    hidden = weight_ref.shape[0] // spans
    everything = pl.ds(0, weight_ref.shape[0])
    pairs = [(dest_hbm, dest_ref), (rows_hbm, rows_ref)]
    for at, step in steps:
        part = (everything, pl.ds(at, step))
        pairs.append((weight_ref.at[part], held.at[part]))
    copies = fetched(pairs, sems)
    copies[0].wait()
    across = jnp.broadcast_to(dest_ref[...].astype(jnp.float32), (row_count, row_count))
    down = across.T
    group_across = jnp.floor((across + 0.5) * (1.0 / row_count))
    group_down = jnp.floor((down + 0.5) * (1.0 / row_count))
    slot_down = down - group_down * row_count
    same = group_across == group_down
    earlier = iota((row_count, row_count), 0) < iota((row_count, row_count), 1)
    later = iota((row_count, row_count), 1) < iota((row_count, row_count), 0)
    rank_across = jnp.sum(jnp.where(same & earlier, 1.0, 0.0), 0, keepdims=True)
    rank_down = jnp.sum(jnp.where(same & later, 1.0, 0.0), 1, keepdims=True)
    row_of = group_across[:1] * slots + rank_across
    places = iota((groups * slots, row_count), 0).astype(jnp.float32)
    pick = jnp.where(places == row_of, 1.0, 0.0).astype(jnp.bfloat16)
    width = hidden
    if by_swaps(count, slots, hidden):
        width = min(hidden, -(-count * slots // 128) * 128)
    lane = iota((row_count, width), 1).astype(jnp.float32)
    rank_in = [jnp.where(group_down[:, :1] == g, rank_down, -1e6) for g in range(groups)]

    def labels(g, s):
        shift = 0.0
        if by_swaps(count, slots, hidden):
            shift = (lax.bitwise_xor(me, g * spans + s) * slots).astype(jnp.float32)
        hit = lane == rank_in[g] + shift
        row = jnp.sum(jnp.where(hit, slot_down[:, :1] + 1.0, 0.0), 0, keepdims=True) - 1.0
        if width < hidden:
            row = jnp.concatenate([row, jnp.full((1, hidden - width), -1.0, jnp.float32)], 1)
        return row

    label_row = iota((slots, hidden), 0) == capacity
    copies[1].wait()
    for n, (at, step) in enumerate(steps):
        turned = rows_ref[:, at : at + step].astype(jnp.float32).T.astype(jnp.bfloat16)
        copies[2 + n].wait()
        product = dot(held[:, at : at + step], turned, NN)
        total_ref[...] = product if n == 0 else total_ref[...] + product
    for s in range(spans):
        part = total_ref[s * hidden : (s + 1) * hidden].astype(jnp.bfloat16)
        moved = dot(pick, part, NT)
        for g in range(groups):
            piece = jnp.where(label_row, labels(g, s), moved[g * slots : (g + 1) * slots])
            pieces_ref[g * spans + s] = piece.astype(jnp.bfloat16)
    if by_swaps(count, slots, hidden):
        pairs = [(pieces_ref.at[pl.ds(lax.bitwise_xor(me, d), 1)], outs[d]) for d in range(count)]
    else:
        pairs = [(pieces_ref, outs[0])]
    for copy in fetched(pairs, out_sems):
        copy.wait()


def down_pieces(dest, rows, weight, groups, spans):
    row_count = rows.shape[0]
    capacity, slots = padded_slots(row_count, groups)
    hidden = weight.shape[0] // spans
    depth = weight.shape[1]
    edges = [depth * i // 8 for i in (0, 1, 3, 5, 8)]
    steps = [(i, j - i) for i, j in zip(edges, edges[1:])]
    count = groups * spans
    parts = count if by_swaps(count, slots, hidden) else 1
    pieces = pl.pallas_call(
        functools.partial(down_kernel, groups, spans, capacity, slots, steps),
        out_shape=[jax.ShapeDtypeStruct((count // parts, slots, hidden), jnp.bfloat16)] * parts,
        in_specs=in_hbm(3),
        out_specs=in_hbm(parts),
        scratch_shapes=[
            pltpu.VMEM((1, row_count), jnp.int32),
            pltpu.VMEM(rows.shape, jnp.bfloat16),
            pltpu.VMEM(weight.shape, jnp.bfloat16),
            pltpu.VMEM((weight.shape[0], row_count), jnp.float32),
            pltpu.VMEM((count, slots, hidden), jnp.bfloat16),
            pltpu.SemaphoreType.DMA((2 + len(steps),)),
            pltpu.SemaphoreType.DMA((parts,)),
        ],
        compiler_params=params(60),
        cost_estimate=pl.CostEstimate(
            flops=200 * row_count * weight.size, bytes_accessed=8 * weight.size, transcendentals=0
        ),
        name="down_product",
    )(dest.reshape(1, row_count), rows, weight)
    if parts == 1:
        axes = ("grp", "span")
        return [lax.all_to_all(pieces[0], axes, split_axis=0, concat_axis=0, tiled=True)]
    return exchanged(pieces, ("grp", "span"))


def up_kernel(heads, capacity, *refs):
    *pieces_refs, pre_ref, weight_ref, _, send_hbm, keep_hbm, held, out_ref, sems, out_sems = refs
    pieces_ref = pieces_refs[0]
    row_count, hidden = pre_ref.shape
    slots = pieces_ref.shape[1]
    count = sum(ref.shape[0] for ref in pieces_refs)
    width = weight_ref.shape[0] // (4 * heads)
    spans = lax.axis_size("span")
    core = lax.axis_index("core")
    half = heads // 2

    me = lax.axis_index("chip") * spans + lax.axis_index("span")

    def head_of(n):
        place = lax.bitwise_xor(me, n % half)
        chip, span = lax.div(place, spans), lax.rem(place, spans)
        return (chip * 2 + (1 - core if n < half else core)) * spans + span

    copies = []
    for h in range(heads):
        for j in range(4):
            start = pl.multiple_of((j * heads + head_of(h)) * width, width)
            copy = pltpu.make_async_copy(
                weight_ref.at[pl.ds(start, width)],
                held.at[h, pl.ds(j * width, width)],
                sems.at[h * 4 + j],
            )
            copy.start()
            copies.append(copy)
    label_at = slice(capacity, capacity + 1)
    if by_swaps(count, slots, hidden):
        pieces = [ref[p].astype(jnp.float32) for ref in pieces_refs for p in range(ref.shape[0])]
        labels = functools.reduce(jnp.maximum, [x[label_at, : count * slots] for x in pieces])
        row = iota((row_count, count * slots), 0).astype(jnp.float32)
        put = jnp.where(row == labels, 1.0, 0.0).astype(jnp.bfloat16)
        total = dot(put, jnp.concatenate(pieces, 0).astype(jnp.bfloat16), NN)
    else:
        row = iota((row_count, slots), 0).astype(jnp.float32)

        def placed(p, total):
            piece = pieces_ref[p]
            labels = piece.astype(jnp.float32)[label_at, :slots]
            put = jnp.where(row == labels, 1.0, 0.0).astype(jnp.bfloat16)
            return total + dot(put, piece, NN)

        total = lax.fori_loop(0, count, placed, jnp.zeros((row_count, hidden), jnp.float32))
    pre = pre_ref[...].astype(jnp.float32)
    cdf = 0.5 * (1.0 + lax.erf(pre * 0.7071067811865476))
    slope = cdf + pre * jnp.exp(-0.5 * pre * pre) * 0.3989422804014327
    grad_pre = (total * slope).T.astype(jnp.bfloat16)
    width = 4 * width
    outgoing = []

    def send(h, products):
        for i in range(2):
            part = products[i * width : (i + 1) * width]
            out_ref[h + i] = part.T.astype(jnp.bfloat16)
        out_hbm = send_hbm if h < half else keep_hbm
        copy = pltpu.make_async_copy(
            out_ref.at[pl.ds(h, 2)], out_hbm.at[pl.ds(h % half, 2)], out_sems.at[h // 2]
        )
        outgoing.append(copy)
        outgoing[-1].start()

    waiting = None
    for h in range(0, heads, 2):
        for copy in copies[h * 4 : h * 4 + 8]:
            copy.wait()
        product = dot(held[h : h + 2].reshape(2 * width, hidden), grad_pre, NN)
        if waiting is not None:
            send(h - 2, waiting)
        waiting = product
    send(heads - 2, waiting)
    for copy in outgoing:
        copy.wait()


def up_pieces(pieces, pre, weight, heads, capacity, later):
    width = weight.shape[0] // heads
    return pl.pallas_call(
        functools.partial(up_kernel, heads, capacity),
        out_shape=[jax.ShapeDtypeStruct((heads // 2, pre.shape[0], width), jnp.bfloat16)] * 2,
        in_specs=in_vmem(len(pieces) + 1) + in_hbm(1) + in_vmem(1),
        out_specs=in_hbm(2),
        scratch_shapes=[
            pltpu.VMEM((heads, width, weight.shape[1]), jnp.bfloat16),
            pltpu.VMEM((heads, pre.shape[0], width), jnp.bfloat16),
            pltpu.SemaphoreType.DMA((heads * 4,)),
            pltpu.SemaphoreType.DMA((heads // 2,)),
        ],
        compiler_params=params(52),
        cost_estimate=pl.CostEstimate(
            flops=8 * pre.shape[0] * weight.size, bytes_accessed=8 * weight.size, transcendentals=0
        ),
        name="up_product",
    )(*pieces, pre, weight, later)


class Rows:
    def __init__(self, columns, patches):
        heads = columns // HEAD_DIM
        self.lanes = -(-3 * patches // 128) * 128
        self.side_lanes = -(-2 * patches // 128) * 128
        self.columns, self.patches = columns, patches
        self.values, self.keys, self.queries, self.attended = [i * columns for i in range(4)]
        self.probs_at = 4 * columns
        self.side_at = self.probs_at + heads * patches
        self.total = self.side_at + heads * patches

    def head(self, start, h):
        return slice(start + h * HEAD_DIM, start + (h + 1) * HEAD_DIM)

    def kind(self, start, count=1):
        return slice(start, start + count * self.columns)

    def probs(self, h):
        return slice(self.probs_at + h * self.patches, self.probs_at + (h + 1) * self.patches)

    def side_probs(self, h):
        return slice(self.side_at + h * self.patches, self.side_at + (h + 1) * self.patches)


def softmax_kernel(lengths_ref, first_ref, own_ref, even_ref, odd_ref, out_hbm, done_ref, held,
                   sems):
    columns, patches = own_ref.shape[0] // 3, own_ref.shape[1]
    heads = columns // HEAD_DIM
    rows = Rows(columns, patches)
    is_even = lax.rem(lax.axis_index("grp"), 2) == 0
    first = first_ref[0, 0]

    def image_of(shape, dim, block):
        token = iota(shape, dim) // 4 + (first + block * (patches // 4))

        def step(i, state):
            image, bound = state
            bound = bound + lengths_ref[0, i]
            return image + jnp.where(token >= bound, 1, 0), bound

        start = (jnp.where(token < 0, -1, 0), jnp.int32(0))
        return lax.fori_loop(0, lengths_ref.shape[1], step, start)[0]

    down = [image_of((patches, 1), 0, b) for b in (0, -1, 1)]
    across = [image_of((1, patches), 1, b) for b in (0, -1, 1)]
    all_keys = jnp.concatenate(across, 1)
    same_own = down[0] == all_keys
    copies = []

    def send(part, lanes):
        at = (pl.ds(part.start, part.stop - part.start), pl.ds(0, lanes))
        copy = pltpu.make_async_copy(held.at[at], out_hbm.at[at], sems.at[len(copies)])
        copy.start()
        copies.append(copy)

    def kind(block, t, h=None):
        start = t * columns + (0 if h is None else h * HEAD_DIM)
        at = slice(start, start + (columns if h is None else HEAD_DIM))
        if block == 0:
            return own_ref[at]
        before, after = (odd_ref, even_ref) if block == 1 else (even_ref, odd_ref)
        return jnp.where(is_even, before[at], after[at])

    def wide(t, which):
        return jnp.concatenate([kind(b, t).astype(jnp.float32) for b in which], 1).astype(jnp.bfloat16)

    held[rows.kind(rows.values), : 3 * patches] = wide(2, (0, 1, 2))
    held[rows.kind(rows.keys), : 3 * patches] = wide(1, (0, 1, 2))
    held[rows.kind(rows.queries), : 2 * patches] = wide(0, (1, 2))
    send(rows.kind(rows.values, 2), rows.lanes)
    send(rows.kind(rows.queries), rows.side_lanes)
    for h in range(heads):
        keys = held[rows.head(rows.keys, h), : 3 * patches]
        scores = dot(kind(0, 0, h), keys, TN) * SCALE
        scores = jnp.where(same_own, scores, -jnp.inf)
        weights = jnp.exp(scores - jnp.max(scores, 1, keepdims=True))
        over = 1.0 / jnp.sum(weights, 1, keepdims=True)
        held[rows.probs(h), : 3 * patches] = (weights * over).astype(jnp.bfloat16)
        send(rows.probs(h), rows.lanes)
    for h in range(heads):
        own_keys = kind(0, 1, h).astype(jnp.float32).T.astype(jnp.bfloat16)
        side, attended = [], []
        for b in (1, 2):
            queries = kind(b, 0, h)
            keys = kind(b, 1, h).astype(jnp.float32).T.astype(jnp.bfloat16)
            scores = []
            for n, k in ((0, own_keys), (b, keys)):
                scores.append(jnp.where(down[n] == across[b], dot(k, queries, NN) * SCALE, -jnp.inf))
            top = functools.reduce(jnp.maximum, [jnp.max(x, 0, keepdims=True) for x in scores])
            weights = [jnp.exp(x - top) for x in scores]
            over = 1.0 / sum([jnp.sum(w, 0, keepdims=True) for w in weights])
            probs = [(w * over).astype(jnp.bfloat16) for w in weights]
            attended.append(dot(kind(0, 2, h), probs[0], NN) + dot(kind(b, 2, h), probs[1], NN))
            side.append(probs[0].astype(jnp.float32))
        held[rows.side_probs(h), : 2 * patches] = jnp.concatenate(side, 1).astype(jnp.bfloat16)
        send(rows.side_probs(h), rows.side_lanes)
        attended = jnp.concatenate(attended, 1).astype(jnp.bfloat16)
        held[rows.head(rows.attended, h), : 2 * patches] = attended
    send(rows.kind(rows.attended), rows.side_lanes)
    for copy in copies:
        copy.wait()
    done_ref[...] = jnp.zeros(done_ref.shape, jnp.float32)


def softmax_parts(lengths, first, own, even, odd):
    columns, patches = own.shape[0] // 3, own.shape[1]
    heads = columns // HEAD_DIM
    rows = Rows(columns, patches)
    smem = pl.BlockSpec(memory_space=pltpu.MemorySpace.SMEM)
    work = heads * patches * patches
    return pl.pallas_call(
        softmax_kernel,
        out_shape=(
            jax.ShapeDtypeStruct((rows.total, rows.lanes), jnp.bfloat16),
            jax.ShapeDtypeStruct((8, 128), jnp.float32),
        ),
        in_specs=[smem, smem] + in_vmem(3),
        out_specs=tuple(in_hbm(1) + in_vmem(1)),
        scratch_shapes=[
            pltpu.VMEM((rows.total, rows.lanes), jnp.bfloat16),
            pltpu.SemaphoreType.DMA((3 + 2 * heads,)),
        ],
        compiler_params=params(52),
        cost_estimate=pl.CostEstimate(
            flops=100_000 * work, bytes_accessed=500 * work, transcendentals=9 * work
        ),
        name="softmax_parts",
    )(lengths.reshape(1, -1), first.reshape(1, 1), own, even, odd)


def gather_kernel(count, *refs):
    _, row_count, width = refs[0].shape
    total = refs[0][0].astype(jnp.float32)
    for p in range(1, count):
        total = total + refs[p][0].astype(jnp.float32)
    out_ref = refs[-1]
    total = total.astype(jnp.bfloat16)
    columns = width // 4
    patch = iota((row_count, 4 * row_count), 1)
    token = iota((row_count, 4 * row_count), 0)
    result = jnp.zeros((columns, 4 * row_count), jnp.float32)
    for j in range(4):
        put = jnp.where(patch == 4 * token + j, 1.0, 0.0).astype(jnp.bfloat16)
        result = result + dot(total[:, j * columns : (j + 1) * columns], put, TN)
    out_ref[...] = result.astype(jnp.bfloat16)


def gathered(pieces, later):
    _, row_count, width = pieces[0].shape
    size = len(pieces) * row_count * width
    return pl.pallas_call(
        functools.partial(gather_kernel, len(pieces)),
        out_shape=jax.ShapeDtypeStruct((width // 4, 4 * row_count), jnp.bfloat16),
        in_specs=in_vmem(len(pieces) + 1),
        out_specs=pl.BlockSpec(memory_space=VMEM),
        compiler_params=params(16),
        cost_estimate=pl.CostEstimate(
            flops=20_000 * size, bytes_accessed=400 * size, transcendentals=0
        ),
        name="gather_sum",
    )(*pieces, later)


def own_kernel(grad_ref, own_ref, held_ref, query_ref, key_ref, value_ref):
    columns, patches = grad_ref.shape
    rows = Rows(columns, patches)
    for h in range(columns // HEAD_DIM):
        cols = slice(h * HEAD_DIM, (h + 1) * HEAD_DIM)
        grad = grad_ref[cols]
        slope = dot(grad, held_ref[rows.head(rows.values, h), : 3 * patches], TN)
        probs = held_ref[rows.probs(h), : 3 * patches]
        wide = probs.astype(jnp.float32)
        delta = jnp.sum(wide * slope, 1, keepdims=True)
        scores = (wide * (slope - delta)).astype(jnp.bfloat16)
        query = dot(scores, held_ref[rows.head(rows.keys, h), : 3 * patches], NT) * SCALE
        query_ref[cols] = query.T.astype(jnp.bfloat16)
        key_ref[cols] = dot(own_ref[cols], scores[:, :patches], NN)
        value_ref[cols] = dot(grad, probs[:, :patches], NN)


def own_terms(grad, own, held):
    return pl.pallas_call(
        own_kernel,
        out_shape=(
            jax.ShapeDtypeStruct(grad.shape, jnp.bfloat16),
            jax.ShapeDtypeStruct(grad.shape, jnp.float32),
            jax.ShapeDtypeStruct(grad.shape, jnp.float32),
        ),
        in_specs=in_vmem(3),
        out_specs=tuple(in_vmem(3)),
        compiler_params=params(24),
        name="own_terms",
    )(grad, own, held)


def side_kernel(even_ref, odd_ref, key_part_ref, value_part_ref, held_ref, key_ref, value_ref):
    columns, patches = even_ref.shape
    is_even = lax.rem(lax.axis_index("grp"), 2) == 0
    rows = Rows(columns, patches)
    lanes = slice(0, 2 * patches)
    for h in range(columns // HEAD_DIM):
        cols = slice(h * HEAD_DIM, (h + 1) * HEAD_DIM)
        even, odd = even_ref[cols].astype(jnp.float32), odd_ref[cols].astype(jnp.float32)
        left, right = jnp.where(is_even, odd, even), jnp.where(is_even, even, odd)
        wide = jnp.concatenate([left, right], 1)
        grad = wide.astype(jnp.bfloat16)
        slope = dot(held_ref[rows.head(rows.values, h), :patches], grad, TN)
        attended = held_ref[rows.head(rows.attended, h), lanes].astype(jnp.float32)
        delta = jnp.sum(wide * attended, 0, keepdims=True)
        probs = held_ref[rows.side_probs(h), lanes]
        value = dot(probs, grad, NT)
        scores = (probs.astype(jnp.float32) * (slope - delta)).astype(jnp.bfloat16)
        key = dot(scores, held_ref[rows.head(rows.queries, h), lanes], NT)
        key_ref[cols] = ((key_part_ref[cols] + key.T) * SCALE).astype(jnp.bfloat16)
        value_ref[cols] = (value_part_ref[cols] + value.T).astype(jnp.bfloat16)


def side_terms(even, odd, key_part, value_part, held):
    shape = jax.ShapeDtypeStruct(even.shape, jnp.bfloat16)
    return pl.pallas_call(
        side_kernel,
        out_shape=(shape, shape),
        in_specs=in_vmem(5),
        out_specs=tuple(in_vmem(2)),
        compiler_params=params(24),
        name="side_terms",
    )(even, odd, key_part, value_part, held)


def from_pairs(x):
    size = lax.axis_size("grp")

    def swapped(first):
        partner = {}
        for core in range(2):
            for i in range(size):
                j = i + 1 if (i - first) % 2 == 0 else i - 1
                pair = (core, j) if 0 <= j < size else (1 - core, i)
                partner[core * size + i] = pair[0] * size + pair[1]
        return lax.ppermute(x, ("core", "grp"), sorted(partner.items()))

    return swapped(0), swapped(1)


def exchanged(pieces, axes):
    count = len(pieces)
    return [pieces[0]] + [
        lax.ppermute(pieces[d], axes, [(i, i ^ d) for i in range(count)]) for d in range(1, count)
    ]


def on_device(
    grad_out, destination, w_down, pre_act, w_up, queries, key_states, value_states, lengths
):
    groups = lax.axis_size("grp")
    spans = lax.axis_size("span")
    heads = lax.axis_size(("chip", "core", "span"))
    row_count = grad_out.shape[0]
    capacity, _ = padded_slots(row_count, groups)
    own = jnp.concatenate([queries.T, key_states.T, value_states.T], 0)
    sides = from_pairs(own)
    pieces = down_pieces(destination, grad_out, w_down, groups, spans)
    first = lax.axis_index("grp") * row_count
    held, held_done = softmax_parts(lengths, first, own, *sides)
    other, shares = up_pieces(pieces, pre_act, w_up, heads, capacity, held_done)
    other = lax.ppermute(other, "core", [(0, 1), (1, 0)])
    shares = (other.astype(jnp.float32) + shares.astype(jnp.float32)).astype(jnp.bfloat16)
    shares = [shares[d : d + 1] for d in range(shares.shape[0])]
    grad = gathered(exchanged(shares, ("chip", "span")), held_done)
    even, odd = from_pairs(grad)
    grad_query, key_part, value_part = own_terms(grad, queries.T, held)
    grad_key, grad_value = side_terms(even, odd, key_part, value_part, held)
    return grad_query.T, grad_key.T, grad_value.T


def solution(mesh):
    sect, grp, span = (mesh.shape[name] for name in ("sect", "grp", "span"))
    finer = jax.sharding.Mesh(
        mesh.devices.reshape(sect // 2, 2, grp, span), ("chip", "core", "grp", "span")
    )
    split = P("grp", ("chip", "core", "span"))
    placed = (
        P("grp", "span"),
        P("grp"),
        P(("chip", "core"), "span"),
        split,
        P(None, ("chip", "core", "span")),
        split,
        split,
        split,
        P(),
    )
    return jax.shard_map(
        on_device,
        mesh=finer,
        in_specs=placed,
        out_specs=(split, split, split),
        check_vma=False,
    )
```

```python
import functools

import jax
import jax.numpy as jnp
from jax import lax
from jax.experimental import pallas as pl
from jax.experimental.pallas import tpu as pltpu
from jax.sharding import PartitionSpec as P

HEAD_DIM = 80
SCALE = HEAD_DIM**-0.5
MIB = 1024 * 1024
VMEM = pltpu.MemorySpace.VMEM
NT = (((1,), (1,)), ((), ()))
NN = (((1,), (0,)), ((), ()))
TN = (((0,), (0,)), ((), ()))


def dot(a, b, dims):
    return lax.dot_general(a, b, dims, preferred_element_type=jnp.float32)


def iota(shape, dim):
    return lax.broadcasted_iota(jnp.int32, shape, dim)


def params(mib):
    return pltpu.CompilerParams(vmem_limit_bytes=mib * MIB)


def in_vmem(count):
    return [pl.BlockSpec(memory_space=VMEM) for _ in range(count)]


def in_hbm(count):
    return [pl.BlockSpec(memory_space=pltpu.MemorySpace.HBM) for _ in range(count)]


def fetched(pairs, sems):
    copies = [pltpu.make_async_copy(a, b, sems.at[i]) for i, (a, b) in enumerate(pairs)]
    for copy in copies:
        copy.start()
    return copies


def padded_slots(row_count, groups):
    offsets = min(groups, row_count // 2)
    capacity = row_count // offsets
    return capacity, -(-(capacity + 1) // 8) * 8


def one_product(count, slots, hidden):
    return count * slots <= hidden


def down_kernel(groups, spans, capacity, slots, steps, dest_hbm, rows_hbm, weight_ref, out_hbm,
                dest_ref, rows_ref, held, total_ref, pieces_ref, sems, out_sems):
    row_count = rows_ref.shape[0]
    hidden = weight_ref.shape[0] // spans
    everything = pl.ds(0, weight_ref.shape[0])
    pairs = [(dest_hbm, dest_ref), (rows_hbm, rows_ref)]
    for at, step in steps:
        part = (everything, pl.ds(at, step))
        pairs.append((weight_ref.at[part], held.at[part]))
    copies = fetched(pairs, sems)
    copies[0].wait()
    across = jnp.broadcast_to(dest_ref[...].astype(jnp.float32), (row_count, row_count))
    down = across.T
    group_across = jnp.floor((across + 0.5) * (1.0 / row_count))
    group_down = jnp.floor((down + 0.5) * (1.0 / row_count))
    slot_down = down - group_down * row_count
    same = group_across == group_down
    earlier = iota((row_count, row_count), 0) < iota((row_count, row_count), 1)
    later = iota((row_count, row_count), 1) < iota((row_count, row_count), 0)
    rank_across = jnp.sum(jnp.where(same & earlier, 1.0, 0.0), 0, keepdims=True)
    rank_down = jnp.sum(jnp.where(same & later, 1.0, 0.0), 1, keepdims=True)
    row_of = group_across[:1] * slots + rank_across
    places = iota((groups * slots, row_count), 0).astype(jnp.float32)
    pick = jnp.where(places == row_of, 1.0, 0.0).astype(jnp.bfloat16)
    lane = iota((row_count, hidden), 1).astype(jnp.float32)
    shift = 0.0
    if one_product(groups * spans, slots, hidden):
        device = lax.axis_index("grp") * spans + lax.axis_index("span")
        shift = (device * slots).astype(jnp.float32)
    at_rank = lane == rank_down + shift
    label_row = iota((slots, hidden), 0) == capacity
    labels = []
    for g in range(groups):
        hit = at_rank & (group_down[:, :1] == g)
        labels.append(jnp.sum(jnp.where(hit, slot_down[:, :1] + 1.0, 0.0), 0, keepdims=True) - 1.0)
    copies[1].wait()
    for n, (at, step) in enumerate(steps):
        turned = rows_ref[:, at : at + step].astype(jnp.float32).T.astype(jnp.bfloat16)
        copies[2 + n].wait()
        product = dot(held[:, at : at + step], turned, NN)
        total_ref[...] = product if n == 0 else total_ref[...] + product
    outgoing = []
    for s in range(spans):
        part = total_ref[s * hidden : (s + 1) * hidden].astype(jnp.bfloat16)
        moved = dot(pick, part, NT)
        for g in range(groups):
            piece = jnp.where(label_row, labels[g], moved[g * slots : (g + 1) * slots])
            pieces_ref[s, g] = piece.astype(jnp.bfloat16)
        copy = pltpu.make_async_copy(pieces_ref.at[s], out_hbm.at[:, s], out_sems.at[s])
        copy.start()
        outgoing.append(copy)
    for copy in outgoing:
        copy.wait()


def down_pieces(dest, rows, weight, groups, spans):
    row_count = rows.shape[0]
    capacity, slots = padded_slots(row_count, groups)
    hidden = weight.shape[0] // spans
    depth = weight.shape[1]
    edges = [depth * i // 8 for i in (0, 1, 3, 5, 8)]
    steps = [(i, j - i) for i, j in zip(edges, edges[1:])]
    pieces = pl.pallas_call(
        functools.partial(down_kernel, groups, spans, capacity, slots, steps),
        out_shape=jax.ShapeDtypeStruct((groups, spans, slots, hidden), jnp.bfloat16),
        in_specs=in_hbm(3),
        out_specs=in_hbm(1)[0],
        scratch_shapes=[
            pltpu.VMEM((1, row_count), jnp.int32),
            pltpu.VMEM(rows.shape, jnp.bfloat16),
            pltpu.VMEM(weight.shape, jnp.bfloat16),
            pltpu.VMEM((weight.shape[0], row_count), jnp.float32),
            pltpu.VMEM((spans, groups, slots, hidden), jnp.bfloat16),
            pltpu.SemaphoreType.DMA((2 + len(steps),)),
            pltpu.SemaphoreType.DMA((spans,)),
        ],
        compiler_params=params(60),
        name="down_product",
    )(dest.reshape(1, row_count), rows, weight)
    return pieces.reshape(groups * spans, slots, hidden)


def up_kernel(heads, capacity, pieces_ref, pre_ref, weight_ref, send_hbm, keep_hbm, held, out_ref,
              sems, out_sems):
    row_count, hidden = pre_ref.shape
    count, slots, _ = pieces_ref.shape
    width = weight_ref.shape[0] // (4 * heads)
    spans = lax.axis_size("span")
    core = lax.axis_index("core")
    half = heads // 2

    me = lax.axis_index("chip") * spans + lax.axis_index("span")

    def head_of(n):
        place = lax.bitwise_xor(me, n % half)
        chip, span = lax.div(place, spans), lax.rem(place, spans)
        return (chip * 2 + (1 - core if n < half else core)) * spans + span

    copies = []
    for h in range(heads):
        for j in range(4):
            start = pl.multiple_of((j * heads + head_of(h)) * width, width)
            copy = pltpu.make_async_copy(
                weight_ref.at[pl.ds(start, width)],
                held.at[h, pl.ds(j * width, width)],
                sems.at[h * 4 + j],
            )
            copy.start()
            copies.append(copy)
    label_at = slice(capacity, capacity + 1)
    if one_product(count, slots, hidden):
        pieces = [pieces_ref[p].astype(jnp.float32) for p in range(count)]
        labels = functools.reduce(jnp.maximum, [x[label_at, : count * slots] for x in pieces])
        row = iota((row_count, count * slots), 0).astype(jnp.float32)
        put = jnp.where(row == labels, 1.0, 0.0).astype(jnp.bfloat16)
        total = dot(put, jnp.concatenate(pieces, 0).astype(jnp.bfloat16), NN)
    else:
        row = iota((row_count, slots), 0).astype(jnp.float32)

        def placed(p, total):
            piece = pieces_ref[p]
            labels = piece.astype(jnp.float32)[label_at, :slots]
            put = jnp.where(row == labels, 1.0, 0.0).astype(jnp.bfloat16)
            return total + dot(put, piece, NN)

        total = lax.fori_loop(0, count, placed, jnp.zeros((row_count, hidden), jnp.float32))
    pre = pre_ref[...].astype(jnp.float32)
    cdf = 0.5 * (1.0 + lax.erf(pre * 0.7071067811865476))
    slope = cdf + pre * jnp.exp(-0.5 * pre * pre) * 0.3989422804014327
    grad_pre = (total * slope).T.astype(jnp.bfloat16)
    width = 4 * width
    outgoing = []

    def send(h, products):
        for i in range(2):
            part = products[i * width : (i + 1) * width]
            out_ref[h + i] = part.astype(jnp.bfloat16).T
        out_hbm = send_hbm if h < half else keep_hbm
        copy = pltpu.make_async_copy(
            out_ref.at[pl.ds(h, 2)], out_hbm.at[pl.ds(h % half, 2)], out_sems.at[h // 2]
        )
        outgoing.append(copy)
        outgoing[-1].start()

    waiting = None
    for h in range(0, heads, 2):
        for copy in copies[h * 4 : h * 4 + 8]:
            copy.wait()
        product = dot(held[h : h + 2].reshape(2 * width, hidden), grad_pre, NN)
        if waiting is not None:
            send(h - 2, waiting)
        waiting = product
    send(heads - 2, waiting)
    for copy in outgoing:
        copy.wait()


def up_pieces(pieces, pre, weight, heads, capacity):
    width = weight.shape[0] // heads
    return pl.pallas_call(
        functools.partial(up_kernel, heads, capacity),
        out_shape=[jax.ShapeDtypeStruct((heads // 2, pre.shape[0], width), jnp.bfloat16)] * 2,
        in_specs=in_vmem(2) + in_hbm(1),
        out_specs=in_hbm(2),
        scratch_shapes=[
            pltpu.VMEM((heads, width, weight.shape[1]), jnp.bfloat16),
            pltpu.VMEM((heads, pre.shape[0], width), jnp.bfloat16),
            pltpu.SemaphoreType.DMA((heads * 4,)),
            pltpu.SemaphoreType.DMA((heads // 2,)),
        ],
        compiler_params=params(52),
        cost_estimate=pl.CostEstimate(
            flops=8 * pre.shape[0] * weight.size, bytes_accessed=8 * weight.size, transcendentals=0
        ),
        name="up_product",
    )(pieces, pre, weight)


class Rows:
    def __init__(self, columns, patches):
        heads = columns // HEAD_DIM
        self.lanes = -(-3 * patches // 128) * 128
        self.side_lanes = -(-2 * patches // 128) * 128
        self.columns, self.patches = columns, patches
        self.values, self.keys, self.queries, self.attended = [i * columns for i in range(4)]
        self.probs_at = 4 * columns
        self.side_at = self.probs_at + heads * patches
        self.total = self.side_at + heads * patches

    def head(self, start, h):
        return slice(start + h * HEAD_DIM, start + (h + 1) * HEAD_DIM)

    def kind(self, start, count=1):
        return slice(start, start + count * self.columns)

    def probs(self, h):
        return slice(self.probs_at + h * self.patches, self.probs_at + (h + 1) * self.patches)

    def side_probs(self, h):
        return slice(self.side_at + h * self.patches, self.side_at + (h + 1) * self.patches)


def softmax_kernel(lengths_ref, first_ref, own_ref, even_ref, odd_ref, held, done_ref):
    columns, patches = own_ref.shape[0] // 3, own_ref.shape[1]
    rows = Rows(columns, patches)
    is_even = lax.rem(lax.axis_index("grp"), 2) == 0
    first = first_ref[0, 0]

    def image_of(shape, dim, block):
        token = iota(shape, dim) // 4 + (first + block * (patches // 4))

        def step(i, state):
            image, bound = state
            bound = bound + lengths_ref[0, i]
            return image + jnp.where(token >= bound, 1, 0), bound

        start = (jnp.where(token < 0, -1, 0), jnp.int32(0))
        return lax.fori_loop(0, lengths_ref.shape[1], step, start)[0]

    down = [image_of((patches, 1), 0, b) for b in (0, -1, 1)]
    across = [image_of((1, patches), 1, b) for b in (0, -1, 1)]

    def kind(block, t, h=None):
        start = t * columns + (0 if h is None else h * HEAD_DIM)
        at = slice(start, start + (columns if h is None else HEAD_DIM))
        if block == 0:
            return own_ref[at]
        before, after = (odd_ref, even_ref) if block == 1 else (even_ref, odd_ref)
        return jnp.where(is_even, before[at], after[at])

    def wide(t, which, h=None):
        parts = [kind(b, t, h).astype(jnp.float32) for b in which]
        return jnp.concatenate(parts, 1).astype(jnp.bfloat16)

    def softmax(queries, keys, same):
        scores = jnp.where(same, dot(queries, keys, TN) * SCALE, -jnp.inf)
        weights = jnp.exp(scores - jnp.max(scores, 1, keepdims=True))
        return weights * (1.0 / jnp.sum(weights, 1, keepdims=True))

    held[rows.kind(rows.values), : 3 * patches] = wide(2, (0, 1, 2))
    held[rows.kind(rows.keys), : 3 * patches] = wide(1, (0, 1, 2))
    held[rows.kind(rows.queries), : 2 * patches] = wide(0, (1, 2))
    same_own = down[0] == jnp.concatenate(across, 1)
    same_side = [down[b] == jnp.concatenate([across[0], across[b]], 1) for b in (1, 2)]
    for h in range(columns // HEAD_DIM):
        keys = held[rows.head(rows.keys, h), : 3 * patches]
        probs = softmax(kind(0, 0, h), keys, same_own)
        held[rows.probs(h), : 3 * patches] = probs.astype(jnp.bfloat16)
        side, attended = [], []
        for b in (1, 2):
            probs = softmax(kind(b, 0, h), wide(1, (0, b), h), same_side[b - 1])
            seen = dot(probs.astype(jnp.bfloat16), wide(2, (0, b), h), NT)
            attended.append(seen.T)
            side.append(probs[:, :patches].T)
        held[rows.side_probs(h), : 2 * patches] = jnp.concatenate(side, 1).astype(jnp.bfloat16)
        attended = jnp.concatenate(attended, 1).astype(jnp.bfloat16)
        held[rows.head(rows.attended, h), : 2 * patches] = attended
    done_ref[...] = jnp.zeros(done_ref.shape, jnp.float32)


def softmax_parts(lengths, first, own, even, odd):
    columns, patches = own.shape[0] // 3, own.shape[1]
    rows = Rows(columns, patches)
    smem = pl.BlockSpec(memory_space=pltpu.MemorySpace.SMEM)
    work = (columns // HEAD_DIM) * patches * patches
    return pl.pallas_call(
        softmax_kernel,
        out_shape=(
            jax.ShapeDtypeStruct((rows.total, rows.lanes), jnp.bfloat16),
            jax.ShapeDtypeStruct((8, 128), jnp.float32),
        ),
        in_specs=[smem, smem] + in_vmem(3),
        out_specs=tuple(in_vmem(2)),
        compiler_params=params(32),
        cost_estimate=pl.CostEstimate(
            flops=100_000 * work, bytes_accessed=500 * work, transcendentals=9 * work
        ),
        name="softmax_parts",
    )(lengths.reshape(1, -1), first.reshape(1, 1), own, even, odd)


def gather_kernel(count, *refs):
    _, row_count, width = refs[0].shape
    total = refs[0][0].astype(jnp.float32)
    for p in range(1, count):
        total = total + refs[p][0].astype(jnp.float32)
    out_ref = refs[-1]
    total = total.astype(jnp.bfloat16)
    columns = width // 4
    patch = iota((row_count, 4 * row_count), 1)
    token = iota((row_count, 4 * row_count), 0)
    result = jnp.zeros((columns, 4 * row_count), jnp.float32)
    for j in range(4):
        put = jnp.where(patch == 4 * token + j, 1.0, 0.0).astype(jnp.bfloat16)
        result = result + dot(total[:, j * columns : (j + 1) * columns], put, TN)
    out_ref[...] = result.astype(jnp.bfloat16)


def gathered(pieces, later):
    _, row_count, width = pieces[0].shape
    size = len(pieces) * row_count * width
    return pl.pallas_call(
        functools.partial(gather_kernel, len(pieces)),
        out_shape=jax.ShapeDtypeStruct((width // 4, 4 * row_count), jnp.bfloat16),
        in_specs=in_vmem(len(pieces) + 1),
        out_specs=pl.BlockSpec(memory_space=VMEM),
        compiler_params=params(16),
        cost_estimate=pl.CostEstimate(
            flops=20_000 * size, bytes_accessed=400 * size, transcendentals=0
        ),
        name="gather_sum",
    )(*pieces, later)


def own_kernel(grad_ref, own_ref, held_ref, query_ref, key_ref, value_ref):
    columns, patches = grad_ref.shape
    rows = Rows(columns, patches)
    for h in range(columns // HEAD_DIM):
        cols = slice(h * HEAD_DIM, (h + 1) * HEAD_DIM)
        grad = grad_ref[cols]
        slope = dot(grad, held_ref[rows.head(rows.values, h), : 3 * patches], TN)
        probs = held_ref[rows.probs(h), : 3 * patches]
        wide = probs.astype(jnp.float32)
        delta = jnp.sum(wide * slope, 1, keepdims=True)
        scores = (wide * (slope - delta)).astype(jnp.bfloat16)
        query = dot(scores, held_ref[rows.head(rows.keys, h), : 3 * patches], NT) * SCALE
        query_ref[cols] = query.T.astype(jnp.bfloat16)
        key_ref[cols] = dot(own_ref[cols], scores[:, :patches], NN)
        value_ref[cols] = dot(grad, probs[:, :patches], NN)


def own_terms(grad, own, held):
    return pl.pallas_call(
        own_kernel,
        out_shape=(
            jax.ShapeDtypeStruct(grad.shape, jnp.bfloat16),
            jax.ShapeDtypeStruct(grad.shape, jnp.float32),
            jax.ShapeDtypeStruct(grad.shape, jnp.float32),
        ),
        in_specs=in_vmem(3),
        out_specs=tuple(in_vmem(3)),
        compiler_params=params(24),
        name="own_terms",
    )(grad, own, held)


def side_kernel(even_ref, odd_ref, key_part_ref, value_part_ref, held_ref, key_ref, value_ref):
    columns, patches = even_ref.shape
    is_even = lax.rem(lax.axis_index("grp"), 2) == 0
    rows = Rows(columns, patches)
    lanes = slice(0, 2 * patches)
    for h in range(columns // HEAD_DIM):
        cols = slice(h * HEAD_DIM, (h + 1) * HEAD_DIM)
        even, odd = even_ref[cols].astype(jnp.float32), odd_ref[cols].astype(jnp.float32)
        left, right = jnp.where(is_even, odd, even), jnp.where(is_even, even, odd)
        wide = jnp.concatenate([left, right], 1)
        grad = wide.astype(jnp.bfloat16)
        slope = dot(held_ref[rows.head(rows.values, h), :patches], grad, TN)
        attended = held_ref[rows.head(rows.attended, h), lanes].astype(jnp.float32)
        delta = jnp.sum(wide * attended, 0, keepdims=True)
        probs = held_ref[rows.side_probs(h), lanes]
        value = dot(probs, grad, NT)
        scores = (probs.astype(jnp.float32) * (slope - delta)).astype(jnp.bfloat16)
        key = dot(scores, held_ref[rows.head(rows.queries, h), lanes], NT)
        key_ref[cols] = ((key_part_ref[cols] + key.T) * SCALE).astype(jnp.bfloat16)
        value_ref[cols] = (value_part_ref[cols] + value.T).astype(jnp.bfloat16)


def side_terms(even, odd, key_part, value_part, held):
    shape = jax.ShapeDtypeStruct(even.shape, jnp.bfloat16)
    return pl.pallas_call(
        side_kernel,
        out_shape=(shape, shape),
        in_specs=in_vmem(5),
        out_specs=tuple(in_vmem(2)),
        compiler_params=params(24),
        name="side_terms",
    )(even, odd, key_part, value_part, held)


def from_pairs(x):
    size = lax.axis_size("grp")

    def swapped(first):
        partner = {}
        for core in range(2):
            for i in range(size):
                j = i + 1 if (i - first) % 2 == 0 else i - 1
                pair = (core, j) if 0 <= j < size else (1 - core, i)
                partner[core * size + i] = pair[0] * size + pair[1]
        return lax.ppermute(x, ("core", "grp"), sorted(partner.items()))

    return swapped(0), swapped(1)


def exchanged(pieces, axes):
    count = pieces.shape[0]
    parts = [pieces[d : d + 1] for d in range(count)]
    return parts[:1] + [
        lax.ppermute(parts[d], axes, [(i, i ^ d) for i in range(count)]) for d in range(1, count)
    ]


def on_device(
    grad_out, destination, w_down, pre_act, w_up, queries, key_states, value_states, lengths
):
    groups = lax.axis_size("grp")
    spans = lax.axis_size("span")
    heads = lax.axis_size(("chip", "core", "span"))
    row_count = grad_out.shape[0]
    capacity, _ = padded_slots(row_count, groups)
    pieces = down_pieces(destination, grad_out, w_down, groups, spans)
    pieces, queries, key_states, value_states = lax.optimization_barrier(
        (pieces, queries, key_states, value_states)
    )
    arrived = lax.all_to_all(pieces, ("grp", "span"), split_axis=0, concat_axis=0, tiled=True)
    own = jnp.concatenate([queries.T, key_states.T, value_states.T], 0)
    sides = from_pairs(own)
    first = lax.axis_index("grp") * row_count
    other, shares = up_pieces(arrived, pre_act, w_up, heads, capacity)
    other, *sides = lax.optimization_barrier((other, *sides))
    other = lax.ppermute(other, "core", [(0, 1), (1, 0)])
    shares = (other.astype(jnp.float32) + shares.astype(jnp.float32)).astype(jnp.bfloat16)
    shares, own = lax.optimization_barrier((shares, own))
    held, held_done = softmax_parts(lengths, first, own, *sides)
    grad = gathered(exchanged(shares, ("chip", "span")), held_done)
    even, odd = from_pairs(grad)
    grad_query, key_part, value_part = own_terms(grad, queries.T, held)
    grad_key, grad_value = side_terms(even, odd, key_part, value_part, held)
    return grad_query.T, grad_key.T, grad_value.T


def solution(mesh):
    sect, grp, span = (mesh.shape[name] for name in ("sect", "grp", "span"))
    finer = jax.sharding.Mesh(
        mesh.devices.reshape(sect // 2, 2, grp, span), ("chip", "core", "grp", "span")
    )
    split = P("grp", ("chip", "core", "span"))
    placed = (
        P("grp", "span"),
        P("grp"),
        P(("chip", "core"), "span"),
        split,
        P(None, ("chip", "core", "span")),
        split,
        split,
        split,
        P(),
    )
    return jax.shard_map(
        on_device,
        mesh=finer,
        in_specs=placed,
        out_specs=(split, split, split),
        check_vma=False,
    )
```

```python
import functools

import jax
import jax.numpy as jnp
from jax import lax
from jax.experimental import pallas as pl
from jax.experimental.pallas import tpu as pltpu
from jax.sharding import PartitionSpec as P

HEAD_DIM = 80
SCALE = HEAD_DIM**-0.5
MIB = 1024 * 1024
VMEM = pltpu.MemorySpace.VMEM
NT = (((1,), (1,)), ((), ()))
NN = (((1,), (0,)), ((), ()))
TN = (((0,), (0,)), ((), ()))


def dot(a, b, dims):
    return lax.dot_general(a, b, dims, preferred_element_type=jnp.float32)


def iota(shape, dim):
    return lax.broadcasted_iota(jnp.int32, shape, dim)


def params(mib):
    return pltpu.CompilerParams(vmem_limit_bytes=mib * MIB)


def in_vmem(count):
    return [pl.BlockSpec(memory_space=VMEM) for _ in range(count)]


def in_hbm(count):
    return [pl.BlockSpec(memory_space=pltpu.MemorySpace.HBM) for _ in range(count)]


def fetched(pairs, sems):
    copies = [pltpu.make_async_copy(a, b, sems.at[i]) for i, (a, b) in enumerate(pairs)]
    for copy in copies:
        copy.start()
    return copies


def padded_slots(row_count, groups):
    offsets = min(groups, row_count // 2)
    capacity = row_count // offsets
    return capacity, -(-(capacity + 1) // 8) * 8


def one_product(count, slots, hidden):
    return count * slots <= hidden


def down_kernel(groups, spans, capacity, slots, steps, dest_hbm, rows_hbm, weight_ref, out_hbm,
                dest_ref, rows_ref, held, total_ref, pieces_ref, sems, out_sems):
    row_count = rows_ref.shape[0]
    hidden = weight_ref.shape[0] // spans
    everything = pl.ds(0, weight_ref.shape[0])
    pairs = [(dest_hbm, dest_ref), (rows_hbm, rows_ref)]
    for at, step in steps:
        part = (everything, pl.ds(at, step))
        pairs.append((weight_ref.at[part], held.at[part]))
    copies = fetched(pairs, sems)
    copies[0].wait()
    across = jnp.broadcast_to(dest_ref[...].astype(jnp.float32), (row_count, row_count))
    down = across.T
    group_across = jnp.floor((across + 0.5) * (1.0 / row_count))
    group_down = jnp.floor((down + 0.5) * (1.0 / row_count))
    slot_down = down - group_down * row_count
    same = group_across == group_down
    earlier = iota((row_count, row_count), 0) < iota((row_count, row_count), 1)
    later = iota((row_count, row_count), 1) < iota((row_count, row_count), 0)
    rank_across = jnp.sum(jnp.where(same & earlier, 1.0, 0.0), 0, keepdims=True)
    rank_down = jnp.sum(jnp.where(same & later, 1.0, 0.0), 1, keepdims=True)
    row_of = group_across[:1] * slots + rank_across
    places = iota((groups * slots, row_count), 0).astype(jnp.float32)
    pick = jnp.where(places == row_of, 1.0, 0.0).astype(jnp.bfloat16)
    lane = iota((row_count, hidden), 1).astype(jnp.float32)
    shift = 0.0
    if one_product(groups * spans, slots, hidden):
        device = lax.axis_index("grp") * spans + lax.axis_index("span")
        shift = (device * slots).astype(jnp.float32)
    at_rank = lane == rank_down + shift
    label_row = iota((slots, hidden), 0) == capacity
    labels = []
    for g in range(groups):
        hit = at_rank & (group_down[:, :1] == g)
        labels.append(jnp.sum(jnp.where(hit, slot_down[:, :1] + 1.0, 0.0), 0, keepdims=True) - 1.0)
    copies[1].wait()
    for n, (at, step) in enumerate(steps):
        turned = rows_ref[:, at : at + step].astype(jnp.float32).T.astype(jnp.bfloat16)
        copies[2 + n].wait()
        product = dot(held[:, at : at + step], turned, NN)
        total_ref[...] = product if n == 0 else total_ref[...] + product
    outgoing = []
    for s in range(spans):
        part = total_ref[s * hidden : (s + 1) * hidden].astype(jnp.bfloat16)
        moved = dot(pick, part, NT)
        for g in range(groups):
            piece = jnp.where(label_row, labels[g], moved[g * slots : (g + 1) * slots])
            pieces_ref[s, g] = piece.astype(jnp.bfloat16)
        copy = pltpu.make_async_copy(pieces_ref.at[s], out_hbm.at[:, s], out_sems.at[s])
        copy.start()
        outgoing.append(copy)
    for copy in outgoing:
        copy.wait()


def down_pieces(dest, rows, weight, groups, spans):
    row_count = rows.shape[0]
    capacity, slots = padded_slots(row_count, groups)
    hidden = weight.shape[0] // spans
    depth = weight.shape[1]
    edges = [depth * i // 8 for i in (0, 1, 3, 5, 8)]
    steps = [(i, j - i) for i, j in zip(edges, edges[1:])]
    pieces = pl.pallas_call(
        functools.partial(down_kernel, groups, spans, capacity, slots, steps),
        out_shape=jax.ShapeDtypeStruct((groups, spans, slots, hidden), jnp.bfloat16),
        in_specs=in_hbm(3),
        out_specs=in_hbm(1)[0],
        scratch_shapes=[
            pltpu.VMEM((1, row_count), jnp.int32),
            pltpu.VMEM(rows.shape, jnp.bfloat16),
            pltpu.VMEM(weight.shape, jnp.bfloat16),
            pltpu.VMEM((weight.shape[0], row_count), jnp.float32),
            pltpu.VMEM((spans, groups, slots, hidden), jnp.bfloat16),
            pltpu.SemaphoreType.DMA((2 + len(steps),)),
            pltpu.SemaphoreType.DMA((spans,)),
        ],
        compiler_params=params(60),
        name="down_product",
    )(dest.reshape(1, row_count), rows, weight)
    return pieces.reshape(groups * spans, slots, hidden)


def up_kernel(heads, capacity, pieces_ref, pre_ref, weight_ref, send_hbm, keep_hbm, held, out_ref,
              sems, out_sems):
    row_count, hidden = pre_ref.shape
    count, slots, _ = pieces_ref.shape
    width = weight_ref.shape[0] // (4 * heads)
    spans = lax.axis_size("span")
    core = lax.axis_index("core")
    chip = lax.axis_index("chip")
    chips = heads // (2 * spans)
    block = spans * width

    def first_row(n, j):
        place = lax.bitwise_xor(chip, n % chips) * 2 + (1 - core if n < chips else core)
        return pl.multiple_of((j * (heads // spans) + place) * block, block)

    pairs = []
    for n in range(2 * chips):
        for j in range(4):
            source = weight_ref.at[pl.ds(first_row(n, j), block)]
            pairs.append((source, held.at[n, pl.ds(j * block, block)]))
    copies = fetched(pairs, sems)
    label_at = slice(capacity, capacity + 1)
    if one_product(count, slots, hidden):
        pieces = [pieces_ref[p].astype(jnp.float32) for p in range(count)]
        labels = functools.reduce(jnp.maximum, [x[label_at, : count * slots] for x in pieces])
        row = iota((row_count, count * slots), 0).astype(jnp.float32)
        put = jnp.where(row == labels, 1.0, 0.0).astype(jnp.bfloat16)
        total = dot(put, jnp.concatenate(pieces, 0).astype(jnp.bfloat16), NN)
    else:
        row = iota((row_count, slots), 0).astype(jnp.float32)

        def placed(p, total):
            piece = pieces_ref[p]
            labels = piece.astype(jnp.float32)[label_at, :slots]
            put = jnp.where(row == labels, 1.0, 0.0).astype(jnp.bfloat16)
            return total + dot(put, piece, NN)

        total = lax.fori_loop(0, count, placed, jnp.zeros((row_count, hidden), jnp.float32))
    pre = pre_ref[...].astype(jnp.float32)
    cdf = 0.5 * (1.0 + lax.erf(pre * 0.7071067811865476))
    slope = cdf + pre * jnp.exp(-0.5 * pre * pre) * 0.3989422804014327
    grad_pre = (total * slope).T.astype(jnp.bfloat16)
    outgoing = []
    span = lax.axis_index("span")

    def send(n, product):
        for i in range(spans):
            parts = [product[j * block + i * width : j * block + (i + 1) * width] for j in range(4)]
            part = jnp.concatenate(parts, 0).astype(jnp.bfloat16).T
            out_ref[n * spans + lax.bitwise_xor(span, i)] = part
        out_hbm = send_hbm if n < chips else keep_hbm
        source, target = pl.ds(n * spans, spans), pl.ds(n % chips * spans, spans)
        copy = pltpu.make_async_copy(out_ref.at[source], out_hbm.at[target], out_sems.at[n])
        outgoing.append(copy)
        copy.start()

    waiting = None
    for n in range(2 * chips):
        for copy in copies[n * 4 : n * 4 + 4]:
            copy.wait()
        product = dot(held[n], grad_pre, NN)
        if waiting is not None:
            send(n - 1, waiting)
        waiting = product
    send(2 * chips - 1, waiting)
    for copy in outgoing:
        copy.wait()


def up_pieces(pieces, pre, weight, heads, capacity):
    width = weight.shape[0] // heads
    spans = lax.axis_size("span")
    blocks = heads // spans
    return pl.pallas_call(
        functools.partial(up_kernel, heads, capacity),
        out_shape=[jax.ShapeDtypeStruct((heads // 2, pre.shape[0], width), jnp.bfloat16)] * 2,
        in_specs=in_vmem(2) + in_hbm(1),
        out_specs=in_hbm(2),
        scratch_shapes=[
            pltpu.VMEM((blocks, spans * width, weight.shape[1]), jnp.bfloat16),
            pltpu.VMEM((heads, pre.shape[0], width), jnp.bfloat16),
            pltpu.SemaphoreType.DMA((blocks * 4,)),
            pltpu.SemaphoreType.DMA((blocks,)),
        ],
        compiler_params=params(52),
        cost_estimate=pl.CostEstimate(
            flops=8 * pre.shape[0] * weight.size, bytes_accessed=8 * weight.size, transcendentals=0
        ),
        name="up_product",
    )(pieces, pre, weight)


class Rows:
    def __init__(self, columns, patches):
        heads = columns // HEAD_DIM
        self.lanes = -(-3 * patches // 128) * 128
        self.side_lanes = -(-2 * patches // 128) * 128
        self.columns, self.patches = columns, patches
        self.values, self.keys, self.queries, self.attended = [i * columns for i in range(4)]
        self.probs_at = 4 * columns
        self.side_at = self.probs_at + heads * patches
        self.total = self.side_at + heads * patches

    def head(self, start, h):
        return slice(start + h * HEAD_DIM, start + (h + 1) * HEAD_DIM)

    def kind(self, start, count=1):
        return slice(start, start + count * self.columns)

    def probs(self, h):
        return slice(self.probs_at + h * self.patches, self.probs_at + (h + 1) * self.patches)

    def side_probs(self, h):
        return slice(self.side_at + h * self.patches, self.side_at + (h + 1) * self.patches)


def softmax_kernel(lengths_ref, first_ref, own_ref, even_ref, odd_ref, held, done_ref):
    columns, patches = own_ref.shape[0] // 3, own_ref.shape[1]
    rows = Rows(columns, patches)
    is_even = lax.rem(lax.axis_index("grp"), 2) == 0
    first = first_ref[0, 0]

    def image_of(shape, dim, block):
        token = iota(shape, dim) // 4 + (first + block * (patches // 4))

        def step(i, state):
            image, bound = state
            bound = bound + lengths_ref[0, i]
            return image + jnp.where(token >= bound, 1, 0), bound

        start = (jnp.where(token < 0, -1, 0), jnp.int32(0))
        return lax.fori_loop(0, lengths_ref.shape[1], step, start)[0]

    down = [image_of((patches, 1), 0, b) for b in (0, -1, 1)]
    across = [image_of((1, patches), 1, b) for b in (0, -1, 1)]

    def kind(block, t, h=None):
        start = t * columns + (0 if h is None else h * HEAD_DIM)
        at = slice(start, start + (columns if h is None else HEAD_DIM))
        if block == 0:
            return own_ref[at]
        before, after = (odd_ref, even_ref) if block == 1 else (even_ref, odd_ref)
        return jnp.where(is_even, before[at], after[at])

    def wide(t, which, h=None):
        parts = [kind(b, t, h).astype(jnp.float32) for b in which]
        return jnp.concatenate(parts, 1).astype(jnp.bfloat16)

    def softmax(queries, keys, same):
        scores = jnp.where(same, dot(queries, keys, TN) * SCALE, -jnp.inf)
        weights = jnp.exp(scores - jnp.max(scores, 1, keepdims=True))
        return weights * (1.0 / jnp.sum(weights, 1, keepdims=True))

    held[rows.kind(rows.values), : 3 * patches] = wide(2, (0, 1, 2))
    held[rows.kind(rows.keys), : 3 * patches] = wide(1, (0, 1, 2))
    held[rows.kind(rows.queries), : 2 * patches] = wide(0, (1, 2))
    same_own = down[0] == jnp.concatenate(across, 1)
    same_side = [down[b] == jnp.concatenate([across[0], across[b]], 1) for b in (1, 2)]
    for h in range(columns // HEAD_DIM):
        keys = held[rows.head(rows.keys, h), : 3 * patches]
        probs = softmax(kind(0, 0, h), keys, same_own)
        held[rows.probs(h), : 3 * patches] = probs.astype(jnp.bfloat16)
        side, attended = [], []
        for b in (1, 2):
            probs = softmax(kind(b, 0, h), wide(1, (0, b), h), same_side[b - 1])
            seen = dot(probs.astype(jnp.bfloat16), wide(2, (0, b), h), NT)
            attended.append(seen.T)
            side.append(probs[:, :patches].T)
        held[rows.side_probs(h), : 2 * patches] = jnp.concatenate(side, 1).astype(jnp.bfloat16)
        attended = jnp.concatenate(attended, 1).astype(jnp.bfloat16)
        held[rows.head(rows.attended, h), : 2 * patches] = attended
    done_ref[...] = jnp.zeros(done_ref.shape, jnp.float32)


def softmax_parts(lengths, first, own, even, odd):
    columns, patches = own.shape[0] // 3, own.shape[1]
    rows = Rows(columns, patches)
    smem = pl.BlockSpec(memory_space=pltpu.MemorySpace.SMEM)
    work = (columns // HEAD_DIM) * patches * patches
    return pl.pallas_call(
        softmax_kernel,
        out_shape=(
            jax.ShapeDtypeStruct((rows.total, rows.lanes), jnp.bfloat16),
            jax.ShapeDtypeStruct((8, 128), jnp.float32),
        ),
        in_specs=[smem, smem] + in_vmem(3),
        out_specs=tuple(in_vmem(2)),
        compiler_params=params(32),
        cost_estimate=pl.CostEstimate(
            flops=100_000 * work, bytes_accessed=500 * work, transcendentals=9 * work
        ),
        name="softmax_parts",
    )(lengths.reshape(1, -1), first.reshape(1, 1), own, even, odd)


def packed_rows(columns, patches):
    heads = columns // HEAD_DIM
    return patches // 128 * columns + (heads + 1) // 2 * HEAD_DIM


def packed(x):
    columns, patches = x.shape
    whole = patches // 128 * 128
    parts = [x[:, at : at + 128] for at in range(0, whole, 128)]
    tails = [x[at : at + HEAD_DIM, whole:] for at in range(0, columns, HEAD_DIM)]
    tails += [jnp.zeros_like(tails[0])] * (len(tails) % 2)
    parts += [jnp.concatenate(tails[i : i + 2], 1) for i in range(0, len(tails), 2)]
    return jnp.concatenate(parts, 0)


def unpacked(ref, h, columns, patches):
    tiles = patches // 128
    starts = [t * columns + h * HEAD_DIM for t in range(tiles)]
    parts = [ref[at : at + HEAD_DIM].astype(jnp.float32) for at in starts]
    at = tiles * columns + h // 2 * HEAD_DIM
    tail = ref[at : at + HEAD_DIM].astype(jnp.float32)
    return jnp.concatenate(parts + [tail[:, h % 2 * 64 : h % 2 * 64 + 64]], 1)


def gather_kernel(count, *refs):
    _, row_count, width = refs[0].shape
    total = refs[0][0].astype(jnp.float32)
    for p in range(1, count):
        total = total + refs[p][0].astype(jnp.float32)
    out_ref, packed_ref = refs[-2:]
    total = total.astype(jnp.bfloat16)
    columns = width // 4
    patch = iota((row_count, 4 * row_count), 1)
    token = iota((row_count, 4 * row_count), 0)
    result = jnp.zeros((columns, 4 * row_count), jnp.float32)
    for j in range(4):
        put = jnp.where(patch == 4 * token + j, 1.0, 0.0).astype(jnp.bfloat16)
        result = result + dot(total[:, j * columns : (j + 1) * columns], put, TN)
    out_ref[...] = result.astype(jnp.bfloat16)
    packed_ref[...] = packed(result).astype(jnp.bfloat16)


def gathered(pieces, later):
    _, row_count, width = pieces[0].shape
    size = len(pieces) * row_count * width
    return pl.pallas_call(
        functools.partial(gather_kernel, len(pieces)),
        out_shape=(
            jax.ShapeDtypeStruct((width // 4, 4 * row_count), jnp.bfloat16),
            jax.ShapeDtypeStruct((packed_rows(width // 4, 4 * row_count), 128), jnp.bfloat16),
        ),
        in_specs=in_vmem(len(pieces) + 1),
        out_specs=tuple(in_vmem(2)),
        compiler_params=params(16),
        cost_estimate=pl.CostEstimate(
            flops=20_000 * size, bytes_accessed=400 * size, transcendentals=0
        ),
        name="gather_sum",
    )(*pieces, later)


def own_kernel(grad_ref, own_ref, held_ref, query_ref, key_ref, value_ref):
    columns, patches = grad_ref.shape
    rows = Rows(columns, patches)
    for h in range(columns // HEAD_DIM):
        cols = slice(h * HEAD_DIM, (h + 1) * HEAD_DIM)
        grad = grad_ref[cols]
        slope = dot(grad, held_ref[rows.head(rows.values, h), : 3 * patches], TN)
        probs = held_ref[rows.probs(h), : 3 * patches]
        wide = probs.astype(jnp.float32)
        delta = jnp.sum(wide * slope, 1, keepdims=True)
        scores = (wide * (slope - delta)).astype(jnp.bfloat16)
        query = dot(scores, held_ref[rows.head(rows.keys, h), : 3 * patches], NT) * SCALE
        query_ref[cols] = query.T.astype(jnp.bfloat16)
        key_ref[cols] = dot(own_ref[cols], scores[:, :patches], NN)
        value_ref[cols] = dot(grad, probs[:, :patches], NN)


def own_terms(grad, own, held):
    return pl.pallas_call(
        own_kernel,
        out_shape=(
            jax.ShapeDtypeStruct(grad.shape, jnp.bfloat16),
            jax.ShapeDtypeStruct(grad.shape, jnp.float32),
            jax.ShapeDtypeStruct(grad.shape, jnp.float32),
        ),
        in_specs=in_vmem(3),
        out_specs=tuple(in_vmem(3)),
        compiler_params=params(24),
        name="own_terms",
    )(grad, own, held)


def side_kernel(even_ref, odd_ref, key_part_ref, value_part_ref, held_ref, key_ref, value_ref):
    columns, patches = key_part_ref.shape
    is_even = lax.rem(lax.axis_index("grp"), 2) == 0
    rows = Rows(columns, patches)
    lanes = slice(0, 2 * patches)
    for h in range(columns // HEAD_DIM):
        cols = slice(h * HEAD_DIM, (h + 1) * HEAD_DIM)
        even, odd = [unpacked(x, h, columns, patches) for x in (even_ref, odd_ref)]
        left, right = jnp.where(is_even, odd, even), jnp.where(is_even, even, odd)
        wide = jnp.concatenate([left, right], 1)
        grad = wide.astype(jnp.bfloat16)
        slope = dot(held_ref[rows.head(rows.values, h), :patches], grad, TN)
        attended = held_ref[rows.head(rows.attended, h), lanes].astype(jnp.float32)
        delta = jnp.sum(wide * attended, 0, keepdims=True)
        probs = held_ref[rows.side_probs(h), lanes]
        value = dot(probs, grad, NT)
        scores = (probs.astype(jnp.float32) * (slope - delta)).astype(jnp.bfloat16)
        key = dot(scores, held_ref[rows.head(rows.queries, h), lanes], NT)
        key_ref[cols] = ((key_part_ref[cols] + key.T) * SCALE).astype(jnp.bfloat16)
        value_ref[cols] = (value_part_ref[cols] + value.T).astype(jnp.bfloat16)


def side_terms(even, odd, key_part, value_part, held):
    shape = jax.ShapeDtypeStruct(key_part.shape, jnp.bfloat16)
    return pl.pallas_call(
        side_kernel,
        out_shape=(shape, shape),
        in_specs=in_vmem(5),
        out_specs=tuple(in_vmem(2)),
        compiler_params=params(24),
        name="side_terms",
    )(even, odd, key_part, value_part, held)


def from_pairs(x):
    size = lax.axis_size("grp")

    def swapped(first):
        partner = {}
        for core in range(2):
            for i in range(size):
                j = i + 1 if (i - first) % 2 == 0 else i - 1
                pair = (core, j) if 0 <= j < size else (1 - core, i)
                partner[core * size + i] = pair[0] * size + pair[1]
        return lax.ppermute(x, ("core", "grp"), sorted(partner.items()))

    return swapped(0), swapped(1)


def exchanged(pieces, axes):
    count = pieces.shape[0]
    parts = [pieces[d : d + 1] for d in range(count)]
    return parts[:1] + [
        lax.ppermute(parts[d], axes, [(i, i ^ d) for i in range(count)]) for d in range(1, count)
    ]


def on_device(
    grad_out, destination, w_down, pre_act, w_up, queries, key_states, value_states, lengths
):
    groups = lax.axis_size("grp")
    spans = lax.axis_size("span")
    heads = lax.axis_size(("chip", "core", "span"))
    row_count = grad_out.shape[0]
    capacity, _ = padded_slots(row_count, groups)
    pieces = down_pieces(destination, grad_out, w_down, groups, spans)
    pieces, queries, key_states, value_states = lax.optimization_barrier(
        (pieces, queries, key_states, value_states)
    )
    arrived = lax.all_to_all(pieces, ("grp", "span"), split_axis=0, concat_axis=0, tiled=True)
    own = jnp.concatenate([queries.T, key_states.T, value_states.T], 0)
    sides = from_pairs(own)
    first = lax.axis_index("grp") * row_count
    other, shares = up_pieces(arrived, pre_act, w_up, heads, capacity)
    other, *sides = lax.optimization_barrier((other, *sides))
    other = lax.ppermute(other, "core", [(0, 1), (1, 0)])
    shares = (other.astype(jnp.float32) + shares.astype(jnp.float32)).astype(jnp.bfloat16)
    shares, own = lax.optimization_barrier((shares, own))
    held, held_done = softmax_parts(lengths, first, own, *sides)
    grad, grad_packed = gathered(exchanged(shares, ("chip", "span")), held_done)
    even, odd = from_pairs(grad_packed)
    grad_query, key_part, value_part = own_terms(grad, queries.T, held)
    grad_key, grad_value = side_terms(even, odd, key_part, value_part, held)
    return grad_query.T, grad_key.T, grad_value.T


def solution(mesh):
    sect, grp, span = (mesh.shape[name] for name in ("sect", "grp", "span"))
    finer = jax.sharding.Mesh(
        mesh.devices.reshape(sect // 2, 2, grp, span), ("chip", "core", "grp", "span")
    )
    split = P("grp", ("chip", "core", "span"))
    placed = (
        P("grp", "span"),
        P("grp"),
        P(("chip", "core"), "span"),
        split,
        P(None, ("chip", "core", "span")),
        split,
        split,
        split,
        P(),
    )
    return jax.shard_map(
        on_device,
        mesh=finer,
        in_specs=placed,
        out_specs=(split, split, split),
        check_vma=False,
    )
```

```python
import functools

import jax
import jax.numpy as jnp
from jax import lax
from jax.experimental import pallas as pl
from jax.experimental.pallas import tpu as pltpu
from jax.sharding import PartitionSpec as P

HEAD_DIM = 80
SCALE = HEAD_DIM**-0.5
MIB = 1024 * 1024
VMEM = pltpu.MemorySpace.VMEM
NT = (((1,), (1,)), ((), ()))
NN = (((1,), (0,)), ((), ()))
TN = (((0,), (0,)), ((), ()))


def dot(a, b, dims):
    return lax.dot_general(a, b, dims, preferred_element_type=jnp.float32)


def iota(shape, dim):
    return lax.broadcasted_iota(jnp.int32, shape, dim)


def params(mib):
    return pltpu.CompilerParams(vmem_limit_bytes=mib * MIB)


def in_vmem(count):
    return [pl.BlockSpec(memory_space=VMEM) for _ in range(count)]


def in_hbm(count):
    return [pl.BlockSpec(memory_space=pltpu.MemorySpace.HBM) for _ in range(count)]


def fetched(pairs, sems):
    copies = [pltpu.make_async_copy(a, b, sems.at[i]) for i, (a, b) in enumerate(pairs)]
    for copy in copies:
        copy.start()
    return copies


def padded_slots(row_count, groups):
    offsets = min(groups, row_count // 2)
    capacity = row_count // offsets
    return capacity, -(-(capacity + 1) // 8) * 8


def one_product(count, slots, hidden):
    return count * slots <= hidden


def down_kernel(groups, spans, capacity, slots, steps, dest_hbm, rows_hbm, weight_ref, out_hbm,
                dest_ref, rows_ref, held, total_ref, pieces_ref, sems, out_sems):
    row_count = rows_ref.shape[0]
    hidden = weight_ref.shape[0] // spans
    everything = pl.ds(0, weight_ref.shape[0])
    pairs = [(dest_hbm, dest_ref), (rows_hbm, rows_ref)]
    for at, step in steps:
        part = (everything, pl.ds(at, step))
        pairs.append((weight_ref.at[part], held.at[part]))
    copies = fetched(pairs, sems)
    copies[0].wait()
    across = jnp.broadcast_to(dest_ref[...].astype(jnp.float32), (row_count, row_count))
    down = across.T
    group_across = jnp.floor((across + 0.5) * (1.0 / row_count))
    group_down = jnp.floor((down + 0.5) * (1.0 / row_count))
    slot_down = down - group_down * row_count
    same = group_across == group_down
    earlier = iota((row_count, row_count), 0) < iota((row_count, row_count), 1)
    later = iota((row_count, row_count), 1) < iota((row_count, row_count), 0)
    rank_across = jnp.sum(jnp.where(same & earlier, 1.0, 0.0), 0, keepdims=True)
    rank_down = jnp.sum(jnp.where(same & later, 1.0, 0.0), 1, keepdims=True)
    row_of = group_across[:1] * slots + rank_across
    places = iota((groups * slots, row_count), 0).astype(jnp.float32)
    pick = jnp.where(places == row_of, 1.0, 0.0).astype(jnp.bfloat16)
    lane = iota((row_count, hidden), 1).astype(jnp.float32)
    shift = 0.0
    if one_product(groups * spans, slots, hidden):
        device = lax.axis_index("grp") * spans + lax.axis_index("span")
        shift = (device * slots).astype(jnp.float32)
    at_rank = lane == rank_down + shift
    label_row = iota((slots, hidden), 0) == capacity
    labels = []
    for g in range(groups):
        hit = at_rank & (group_down[:, :1] == g)
        labels.append(jnp.sum(jnp.where(hit, slot_down[:, :1] + 1.0, 0.0), 0, keepdims=True) - 1.0)
    copies[1].wait()
    for n, (at, step) in enumerate(steps):
        turned = rows_ref[:, at : at + step].astype(jnp.float32).T.astype(jnp.bfloat16)
        copies[2 + n].wait()
        product = dot(held[:, at : at + step], turned, NN)
        total_ref[...] = product if n == 0 else total_ref[...] + product
    outgoing = []
    for s in range(spans):
        part = total_ref[s * hidden : (s + 1) * hidden].astype(jnp.bfloat16)
        moved = dot(pick, part, NT)
        for g in range(groups):
            piece = jnp.where(label_row, labels[g], moved[g * slots : (g + 1) * slots])
            pieces_ref[s, g] = piece.astype(jnp.bfloat16)
        copy = pltpu.make_async_copy(pieces_ref.at[s], out_hbm.at[:, s], out_sems.at[s])
        copy.start()
        outgoing.append(copy)
    for copy in outgoing:
        copy.wait()


def down_pieces(dest, rows, weight, groups, spans):
    row_count = rows.shape[0]
    capacity, slots = padded_slots(row_count, groups)
    hidden = weight.shape[0] // spans
    depth = weight.shape[1]
    edges = [depth * i // 8 for i in (0, 1, 3, 5, 8)]
    steps = [(i, j - i) for i, j in zip(edges, edges[1:])]
    pieces = pl.pallas_call(
        functools.partial(down_kernel, groups, spans, capacity, slots, steps),
        out_shape=jax.ShapeDtypeStruct((groups, spans, slots, hidden), jnp.bfloat16),
        in_specs=in_hbm(3),
        out_specs=in_hbm(1)[0],
        scratch_shapes=[
            pltpu.VMEM((1, row_count), jnp.int32),
            pltpu.VMEM(rows.shape, jnp.bfloat16),
            pltpu.VMEM(weight.shape, jnp.bfloat16),
            pltpu.VMEM((weight.shape[0], row_count), jnp.float32),
            pltpu.VMEM((spans, groups, slots, hidden), jnp.bfloat16),
            pltpu.SemaphoreType.DMA((2 + len(steps),)),
            pltpu.SemaphoreType.DMA((spans,)),
        ],
        compiler_params=params(60),
        name="down_product",
    )(dest.reshape(1, row_count), rows, weight)
    return pieces.reshape(groups * spans, slots, hidden)


def up_kernel(heads, capacity, pieces_ref, pre_ref, weight_ref, send_hbm, keep_hbm, held, out_ref,
              sems, out_sems):
    row_count, hidden = pre_ref.shape
    count, slots, _ = pieces_ref.shape
    width = weight_ref.shape[2] // lax.axis_size("span")
    spans = lax.axis_size("span")
    core = lax.axis_index("core")
    chip = lax.axis_index("chip")
    chips = heads // (2 * spans)
    block = spans * width

    pairs = []
    for n in range(2 * chips):
        place = lax.bitwise_xor(chip, n % chips) * 2 + (1 - core if n < chips else core)
        pairs.append((weight_ref.at[:, place], held.at[n]))
    copies = fetched(pairs, sems)
    label_at = slice(capacity, capacity + 1)
    if one_product(count, slots, hidden):
        pieces = [pieces_ref[p].astype(jnp.float32) for p in range(count)]
        labels = functools.reduce(jnp.maximum, [x[label_at, : count * slots] for x in pieces])
        row = iota((row_count, count * slots), 0).astype(jnp.float32)
        put = jnp.where(row == labels, 1.0, 0.0).astype(jnp.bfloat16)
        total = dot(put, jnp.concatenate(pieces, 0).astype(jnp.bfloat16), NN)
    else:
        row = iota((row_count, slots), 0).astype(jnp.float32)

        def placed(p, total):
            piece = pieces_ref[p]
            labels = piece.astype(jnp.float32)[label_at, :slots]
            put = jnp.where(row == labels, 1.0, 0.0).astype(jnp.bfloat16)
            return total + dot(put, piece, NN)

        total = lax.fori_loop(0, count, placed, jnp.zeros((row_count, hidden), jnp.float32))
    pre = pre_ref[...].astype(jnp.float32)
    cdf = 0.5 * (1.0 + lax.erf(pre * 0.7071067811865476))
    slope = cdf + pre * jnp.exp(-0.5 * pre * pre) * 0.3989422804014327
    grad_pre = (total * slope).T.astype(jnp.bfloat16)
    outgoing = []
    span = lax.axis_index("span")

    def send(n, product):
        for i in range(spans):
            parts = [product[j * block + i * width : j * block + (i + 1) * width] for j in range(4)]
            part = jnp.concatenate(parts, 0).astype(jnp.bfloat16).T
            out_ref[n * spans + lax.bitwise_xor(span, i)] = part
        out_hbm = send_hbm if n < chips else keep_hbm
        source, target = pl.ds(n * spans, spans), pl.ds(n % chips * spans, spans)
        copy = pltpu.make_async_copy(out_ref.at[source], out_hbm.at[target], out_sems.at[n])
        outgoing.append(copy)
        copy.start()

    waiting = None
    for n in range(2 * chips):
        copies[n].wait()
        product = dot(held[n].reshape(4 * block, hidden), grad_pre, NN)
        if waiting is not None:
            send(n - 1, waiting)
        waiting = product
    send(2 * chips - 1, waiting)
    for copy in outgoing:
        copy.wait()


def up_pieces(pieces, pre, weight, heads, capacity):
    width = weight.shape[0] // heads
    spans = lax.axis_size("span")
    blocks = heads // spans
    return pl.pallas_call(
        functools.partial(up_kernel, heads, capacity),
        out_shape=[jax.ShapeDtypeStruct((heads // 2, pre.shape[0], width), jnp.bfloat16)] * 2,
        in_specs=in_vmem(2) + in_hbm(1),
        out_specs=in_hbm(2),
        scratch_shapes=[
            pltpu.VMEM((blocks, 4, spans * width // 4, weight.shape[1]), jnp.bfloat16),
            pltpu.VMEM((heads, pre.shape[0], width), jnp.bfloat16),
            pltpu.SemaphoreType.DMA((blocks,)),
            pltpu.SemaphoreType.DMA((blocks,)),
        ],
        compiler_params=params(52),
        cost_estimate=pl.CostEstimate(
            flops=8 * pre.shape[0] * weight.size, bytes_accessed=8 * weight.size, transcendentals=0
        ),
        name="up_product",
    )(pieces, pre, weight.reshape(4, blocks, -1, weight.shape[1]))


class Rows:
    def __init__(self, columns, patches):
        heads = columns // HEAD_DIM
        self.lanes = -(-3 * patches // 128) * 128
        self.columns, self.patches = columns, patches
        self.values, self.keys, self.probs_at = 0, columns, 2 * columns
        self.total = 2 * columns + heads * patches

    def head(self, start, h):
        return slice(start + h * HEAD_DIM, start + (h + 1) * HEAD_DIM)

    def kind(self, start):
        return slice(start, start + self.columns)

    def probs(self, h):
        return slice(self.probs_at + h * self.patches, self.probs_at + (h + 1) * self.patches)

    def side(self, i):
        start = i * self.total
        return start, start + self.columns

    def side_probs(self, i, h):
        start = i * self.total + self.probs_at + h * self.patches
        return slice(start, start + self.patches)


def softmax_kernel(lengths_ref, first_ref, own_ref, odd_ref, even_ref, held, side_ref, done_ref):
    columns, patches = own_ref.shape[0] // 3, own_ref.shape[1]
    rows = Rows(columns, patches)
    heads = columns // HEAD_DIM
    step_even = 1 - 2 * lax.rem(lax.axis_index("grp"), 2)
    offsets = (0, -step_even, step_even)
    first = first_ref[0, 0]

    def image_of(shape, dim, block):
        token = iota(shape, dim) // 4 + (first + block * (patches // 4))

        def step(i, state):
            image, bound = state
            bound = bound + lengths_ref[0, i]
            return image + jnp.where(token >= bound, 1, 0), bound

        start = (jnp.where(token < 0, -1, 0), jnp.int32(0))
        return lax.fori_loop(0, lengths_ref.shape[1], step, start)[0]

    down = [image_of((patches, 1), 0, b) for b in offsets]
    across = [image_of((1, patches), 1, b) for b in offsets]

    def kind(block, t, h):
        if block == 0:
            start = t * columns + h * HEAD_DIM
            return own_ref[start : start + HEAD_DIM].astype(jnp.float32)
        return unpacked((odd_ref, even_ref)[block - 1], t * heads + h, 3 * columns, patches)

    def wide(t, which, h):
        return jnp.concatenate([kind(b, t, h) for b in which], 1).astype(jnp.bfloat16)

    def softmax(queries, keys, same):
        scores = jnp.where(same, dot(queries, keys, TN) * SCALE, -jnp.inf)
        weights = jnp.exp(scores - jnp.max(scores, 1, keepdims=True))
        return weights * (1.0 / jnp.sum(weights, 1, keepdims=True))

    for h in range(heads):
        held[rows.head(rows.values, h), : 3 * patches] = wide(2, (0, 1, 2), h)
        held[rows.head(rows.keys, h), : 3 * patches] = wide(1, (0, 1, 2), h)
    same_own = down[0] == jnp.concatenate(across, 1)
    same_side = [down[b] == jnp.concatenate([across[0], across[b]], 1) for b in (1, 2)]
    for h in range(heads):
        keys = held[rows.head(rows.keys, h), : 3 * patches]
        probs = softmax(kind(0, 0, h).astype(jnp.bfloat16), keys, same_own)
        held[rows.probs(h), : 3 * patches] = probs.astype(jnp.bfloat16)
        for i, b in enumerate((1, 2)):
            queries_at, attended_at = rows.side(i)
            queries = kind(b, 0, h).astype(jnp.bfloat16)
            probs = softmax(queries, wide(1, (0, b), h), same_side[i])
            seen = dot(probs.astype(jnp.bfloat16), wide(2, (0, b), h), NT)
            side_ref[rows.head(queries_at, h)] = queries
            side_ref[rows.head(attended_at, h)] = seen.T.astype(jnp.bfloat16)
            side_ref[rows.side_probs(i, h)] = probs[:, :patches].T.astype(jnp.bfloat16)
    done_ref[...] = jnp.zeros(done_ref.shape, jnp.float32)


def softmax_parts(lengths, first, own, odd, even):
    columns, patches = own.shape[0] // 3, own.shape[1]
    rows = Rows(columns, patches)
    smem = pl.BlockSpec(memory_space=pltpu.MemorySpace.SMEM)
    work = (columns // HEAD_DIM) * patches * patches
    return pl.pallas_call(
        softmax_kernel,
        out_shape=(
            jax.ShapeDtypeStruct((rows.total, rows.lanes), jnp.bfloat16),
            jax.ShapeDtypeStruct((2 * rows.total, patches), jnp.bfloat16),
            jax.ShapeDtypeStruct((8, 128), jnp.float32),
        ),
        in_specs=[smem, smem] + in_vmem(3),
        out_specs=tuple(in_vmem(3)),
        compiler_params=params(32),
        cost_estimate=pl.CostEstimate(
            flops=100_000 * work, bytes_accessed=500 * work, transcendentals=9 * work
        ),
        name="softmax_parts",
    )(lengths.reshape(1, -1), first.reshape(1, 1), own, odd, even)


def packed_rows(columns, patches):
    heads = columns // HEAD_DIM
    return patches // 128 * columns + (heads + 1) // 2 * HEAD_DIM


def packed(x):
    columns, patches = x.shape
    whole = patches // 128 * 128
    parts = [x[:, at : at + 128] for at in range(0, whole, 128)]
    tails = [x[at : at + HEAD_DIM, whole:] for at in range(0, columns, HEAD_DIM)]
    tails += [jnp.zeros_like(tails[0])] * (len(tails) % 2)
    parts += [jnp.concatenate(tails[i : i + 2], 1) for i in range(0, len(tails), 2)]
    return jnp.concatenate(parts, 0)


def unpacked(ref, h, columns, patches):
    tiles = patches // 128
    starts = [t * columns + h * HEAD_DIM for t in range(tiles)]
    parts = [ref[at : at + HEAD_DIM].astype(jnp.float32) for at in starts]
    at = tiles * columns + h // 2 * HEAD_DIM
    tail = ref[at : at + HEAD_DIM].astype(jnp.float32)
    return jnp.concatenate(parts + [tail[:, h % 2 * 64 : h % 2 * 64 + 64]], 1)


def gather_kernel(count, *refs):
    _, row_count, width = refs[0].shape
    total = refs[0][0].astype(jnp.float32)
    for p in range(1, count):
        total = total + refs[p][0].astype(jnp.float32)
    out_ref, packed_ref = refs[-2:]
    total = total.astype(jnp.bfloat16)
    columns = width // 4
    patch = iota((row_count, 4 * row_count), 1)
    token = iota((row_count, 4 * row_count), 0)
    result = jnp.zeros((columns, 4 * row_count), jnp.float32)
    for j in range(4):
        put = jnp.where(patch == 4 * token + j, 1.0, 0.0).astype(jnp.bfloat16)
        result = result + dot(total[:, j * columns : (j + 1) * columns], put, TN)
    out_ref[...] = result.astype(jnp.bfloat16)
    packed_ref[...] = packed(result).astype(jnp.bfloat16)


def gathered(pieces, later):
    _, row_count, width = pieces[0].shape
    size = len(pieces) * row_count * width
    return pl.pallas_call(
        functools.partial(gather_kernel, len(pieces)),
        out_shape=(
            jax.ShapeDtypeStruct((width // 4, 4 * row_count), jnp.bfloat16),
            jax.ShapeDtypeStruct((packed_rows(width // 4, 4 * row_count), 128), jnp.bfloat16),
        ),
        in_specs=in_vmem(len(pieces) + 1),
        out_specs=tuple(in_vmem(2)),
        compiler_params=params(16),
        cost_estimate=pl.CostEstimate(
            flops=20_000 * size, bytes_accessed=400 * size, transcendentals=0
        ),
        name="gather_sum",
    )(*pieces, later)


def own_kernel(grad_ref, own_ref, held_ref, query_ref, key_ref, value_ref):
    columns, patches = grad_ref.shape
    rows = Rows(columns, patches)
    for h in range(columns // HEAD_DIM):
        cols = slice(h * HEAD_DIM, (h + 1) * HEAD_DIM)
        grad = grad_ref[cols]
        slope = dot(grad, held_ref[rows.head(rows.values, h), : 3 * patches], TN)
        probs = held_ref[rows.probs(h), : 3 * patches]
        wide = probs.astype(jnp.float32)
        delta = jnp.sum(wide * slope, 1, keepdims=True)
        scores = (wide * (slope - delta)).astype(jnp.bfloat16)
        query = dot(scores, held_ref[rows.head(rows.keys, h), : 3 * patches], NT) * SCALE
        query_ref[cols] = query.T.astype(jnp.bfloat16)
        key_ref[cols] = dot(own_ref[cols], scores[:, :patches], NN)
        value_ref[cols] = dot(grad, probs[:, :patches], NN)


def own_terms(grad, own, held):
    return pl.pallas_call(
        own_kernel,
        out_shape=(
            jax.ShapeDtypeStruct(grad.shape, jnp.bfloat16),
            jax.ShapeDtypeStruct(grad.shape, jnp.float32),
            jax.ShapeDtypeStruct(grad.shape, jnp.float32),
        ),
        in_specs=in_vmem(3),
        out_specs=tuple(in_vmem(3)),
        compiler_params=params(24),
        name="own_terms",
    )(grad, own, held)


def side_kernel(i, grad_ref, key_part_ref, value_part_ref, held_ref, side_ref, key_ref, value_ref):
    columns, patches = key_part_ref.shape
    rows = Rows(columns, patches)
    queries_at, attended_at = rows.side(i)
    for h in range(columns // HEAD_DIM):
        cols = slice(h * HEAD_DIM, (h + 1) * HEAD_DIM)
        wide = unpacked(grad_ref, h, columns, patches)
        grad = wide.astype(jnp.bfloat16)
        slope = dot(held_ref[rows.head(rows.values, h), :patches], grad, TN)
        attended = side_ref[rows.head(attended_at, h)].astype(jnp.float32)
        delta = jnp.sum(wide * attended, 0, keepdims=True)
        probs = side_ref[rows.side_probs(i, h)]
        value = dot(probs, grad, NT)
        scores = (probs.astype(jnp.float32) * (slope - delta)).astype(jnp.bfloat16)
        key = dot(scores, side_ref[rows.head(queries_at, h)], NT)
        key = key_part_ref[cols] + key.T
        key_ref[cols] = (key * SCALE if i == 1 else key).astype(key_ref.dtype)
        value_ref[cols] = (value_part_ref[cols] + value.T).astype(value_ref.dtype)


def side_terms(i, grad, key_part, value_part, held, side):
    kind = jnp.bfloat16 if i == 1 else jnp.float32
    shape = jax.ShapeDtypeStruct(key_part.shape, kind)
    return pl.pallas_call(
        functools.partial(side_kernel, i),
        out_shape=(shape, shape),
        in_specs=in_vmem(5),
        out_specs=tuple(in_vmem(2)),
        compiler_params=params(24),
        name="side_terms",
    )(grad, key_part, value_part, held, side)


def from_pairs(x):
    size = lax.axis_size("grp")

    def swapped(first):
        partner = {}
        for core in range(2):
            for i in range(size):
                j = i + 1 if (i - first) % 2 == 0 else i - 1
                pair = (core, j) if 0 <= j < size else (1 - core, i)
                partner[core * size + i] = pair[0] * size + pair[1]
        return lax.ppermute(x, ("core", "grp"), sorted(partner.items()))

    return swapped(0), swapped(1)


def exchanged(pieces, axes):
    count = len(pieces)
    return pieces[:1] + [
        lax.ppermute(pieces[d], axes, [(i, i ^ d) for i in range(count)]) for d in range(1, count)
    ]


def on_device(
    grad_out, destination, w_down, pre_act, w_up, queries, key_states, value_states, lengths
):
    groups = lax.axis_size("grp")
    spans = lax.axis_size("span")
    heads = lax.axis_size(("chip", "core", "span"))
    row_count = grad_out.shape[0]
    capacity, _ = padded_slots(row_count, groups)
    pieces = down_pieces(destination, grad_out, w_down, groups, spans)
    pieces, queries, key_states, value_states = lax.optimization_barrier(
        (pieces, queries, key_states, value_states)
    )
    arrived = lax.all_to_all(pieces, ("grp", "span"), split_axis=0, concat_axis=0, tiled=True)
    own = jnp.concatenate([queries.T, key_states.T, value_states.T], 0)
    even, odd = from_pairs(packed(own))
    first = lax.axis_index("grp") * row_count
    other, shares = up_pieces(arrived, pre_act, w_up, heads, capacity)
    other, odd, even = lax.optimization_barrier((other, odd, even))
    other = lax.ppermute(other, "core", [(0, 1), (1, 0)])
    shares = (other.astype(jnp.float32) + shares.astype(jnp.float32)).astype(jnp.bfloat16)
    shares, own = lax.optimization_barrier((shares, own))
    held, side, held_done = softmax_parts(lengths, first, own, odd, even)
    shares = [shares[d : d + 1] for d in range(shares.shape[0])]
    grad, grad_packed = gathered(exchanged(shares, ("chip", "span")), held_done)
    even, odd = from_pairs(grad_packed)
    grad_query, key_part, value_part = own_terms(grad, queries.T, held)
    parts = side_terms(0, odd, key_part, value_part, held, side)
    grad_key, grad_value = side_terms(1, even, *parts, held, side)
    return grad_query.T, grad_key.T, grad_value.T


def solution(mesh):
    sect, grp, span = (mesh.shape[name] for name in ("sect", "grp", "span"))
    finer = jax.sharding.Mesh(
        mesh.devices.reshape(sect // 2, 2, grp, span), ("chip", "core", "grp", "span")
    )
    split = P("grp", ("chip", "core", "span"))
    placed = (
        P("grp", "span"),
        P("grp"),
        P(("chip", "core"), "span"),
        split,
        P(None, ("chip", "core", "span")),
        split,
        split,
        split,
        P(),
    )
    return jax.shard_map(
        on_device,
        mesh=finer,
        in_specs=placed,
        out_specs=(split, split, split),
        check_vma=False,
    )
```

```python
import functools

import jax
import jax.numpy as jnp
from jax import lax
from jax.experimental import pallas as pl
from jax.experimental.pallas import tpu as pltpu
from jax.sharding import PartitionSpec as P

HEAD_DIM = 80
SCALE = HEAD_DIM**-0.5
MIB = 1024 * 1024
VMEM = pltpu.MemorySpace.VMEM
NT = (((1,), (1,)), ((), ()))
NN = (((1,), (0,)), ((), ()))
TN = (((0,), (0,)), ((), ()))


def dot(a, b, dims):
    return lax.dot_general(a, b, dims, preferred_element_type=jnp.float32)


def iota(shape, dim):
    return lax.broadcasted_iota(jnp.int32, shape, dim)


def params(mib):
    return pltpu.CompilerParams(vmem_limit_bytes=mib * MIB)


def in_vmem(count):
    return [pl.BlockSpec(memory_space=VMEM) for _ in range(count)]


def in_hbm(count):
    return [pl.BlockSpec(memory_space=pltpu.MemorySpace.HBM) for _ in range(count)]


def fetched(pairs, sems):
    copies = [pltpu.make_async_copy(a, b, sems.at[i]) for i, (a, b) in enumerate(pairs)]
    for copy in copies:
        copy.start()
    return copies


def padded_slots(row_count, groups):
    offsets = min(groups, row_count // 2)
    capacity = row_count // offsets
    return capacity, -(-(capacity + 1) // 8) * 8


def by_swaps(groups, spans, slots, hidden):
    return spans == 2 and groups in (2, 4, 8) and groups * slots <= hidden


def down_kernel(groups, spans, capacity, slots, steps, dest_hbm, rows_hbm, weight_ref, *refs):
    *outs, dest_ref, rows_ref, held, total_ref, pieces_ref, sems, out_sems = refs
    me, span = lax.axis_index("grp"), lax.axis_index("span")
    row_count = rows_ref.shape[0]
    hidden = weight_ref.shape[0] // spans
    everything = pl.ds(0, weight_ref.shape[0])
    pairs = [(dest_hbm, dest_ref), (rows_hbm, rows_ref)]
    for at, step in steps:
        part = (everything, pl.ds(at, step))
        pairs.append((weight_ref.at[part], held.at[part]))
    copies = fetched(pairs, sems)
    copies[0].wait()
    across = jnp.broadcast_to(dest_ref[...].astype(jnp.float32), (row_count, row_count))
    down = across.T
    group_across = jnp.floor((across + 0.5) * (1.0 / row_count))
    group_down = jnp.floor((down + 0.5) * (1.0 / row_count))
    slot_down = down - group_down * row_count
    same = group_across == group_down
    earlier = iota((row_count, row_count), 0) < iota((row_count, row_count), 1)
    later = iota((row_count, row_count), 1) < iota((row_count, row_count), 0)
    rank_across = jnp.sum(jnp.where(same & earlier, 1.0, 0.0), 0, keepdims=True)
    rank_down = jnp.sum(jnp.where(same & later, 1.0, 0.0), 1, keepdims=True)
    row_of = group_across[:1] * slots + rank_across
    places = iota((groups * slots, row_count), 0).astype(jnp.float32)
    pick = jnp.where(places == row_of, 1.0, 0.0).astype(jnp.bfloat16)
    swaps = by_swaps(groups, spans, slots, hidden)
    lane = iota((row_count, hidden), 1).astype(jnp.float32)
    labels = []
    for g in range(groups):
        shift = (lax.bitwise_xor(me, g) * slots).astype(jnp.float32) if swaps else 0.0
        hit = (lane == rank_down + shift) & (group_down[:, :1] == g)
        labels.append(jnp.sum(jnp.where(hit, slot_down[:, :1] + 1.0, 0.0), 0, keepdims=True) - 1.0)
    label_row = iota((slots, hidden), 0) == capacity
    copies[1].wait()
    for n, (at, step) in enumerate(steps):
        turned = rows_ref[:, at : at + step].astype(jnp.float32).T.astype(jnp.bfloat16)
        copies[2 + n].wait()
        product = dot(held[:, at : at + step], turned, NN)
        total_ref[...] = product if n == 0 else total_ref[...] + product
    for s in range(spans):
        part = total_ref[s * hidden : (s + 1) * hidden].astype(jnp.bfloat16)
        moved = dot(pick, part, NT)
        said = jnp.where(span == s, 1.0, 0.0) if swaps else 1.0
        for g in range(groups):
            piece = jnp.where(label_row, labels[g] * said, moved[g * slots : (g + 1) * slots])
            pieces_ref[s, g] = piece.astype(jnp.bfloat16)
    if swaps:
        pairs = [
            (pieces_ref.at[s, lax.bitwise_xor(me, d)], out.at[d])
            for out, s in zip(outs, (1 - span, span))
            for d in range(groups)
        ]
    else:
        pairs = [(pieces_ref.at[s], outs[0].at[:, s]) for s in range(spans)]
    for copy in fetched(pairs, out_sems):
        copy.wait()


def down_pieces(dest, rows, weight, groups, spans):
    row_count = rows.shape[0]
    capacity, slots = padded_slots(row_count, groups)
    hidden = weight.shape[0] // spans
    depth = weight.shape[1]
    edges = [depth * i // 8 for i in (0, 1, 3, 5, 8)]
    steps = [(i, j - i) for i, j in zip(edges, edges[1:])]
    swaps = by_swaps(groups, spans, slots, hidden)
    shape = (groups, spans, slots, hidden)
    shapes = [shape[:1] + shape[2:]] * 2 if swaps else [shape]
    pieces = pl.pallas_call(
        functools.partial(down_kernel, groups, spans, capacity, slots, steps),
        out_shape=[jax.ShapeDtypeStruct(x, jnp.bfloat16) for x in shapes],
        in_specs=in_hbm(3),
        out_specs=in_hbm(len(shapes)),
        scratch_shapes=[
            pltpu.VMEM((1, row_count), jnp.int32),
            pltpu.VMEM(rows.shape, jnp.bfloat16),
            pltpu.VMEM(weight.shape, jnp.bfloat16),
            pltpu.VMEM((weight.shape[0], row_count), jnp.float32),
            pltpu.VMEM((spans, groups, slots, hidden), jnp.bfloat16),
            pltpu.SemaphoreType.DMA((2 + len(steps),)),
            pltpu.SemaphoreType.DMA((2 * groups if swaps else spans,)),
        ],
        compiler_params=params(60),
        name="down_product",
    )(dest.reshape(1, row_count), rows, weight)
    if swaps:
        return pieces
    return [pieces[0].reshape(groups * spans, slots, hidden)]


def up_kernel(heads, capacity, swaps, *refs):
    *pieces_refs, pre_ref, weight_ref, send_hbm, keep_hbm, held, out_ref, sems, out_sems = refs
    pieces_ref = pieces_refs[0]
    row_count, hidden = pre_ref.shape
    count, slots, _ = pieces_ref.shape
    width = weight_ref.shape[2] // lax.axis_size("span")
    spans = lax.axis_size("span")
    core = lax.axis_index("core")
    chip = lax.axis_index("chip")
    chips = heads // (2 * spans)
    block = spans * width

    pairs = []
    for n in range(2 * chips):
        place = lax.bitwise_xor(chip, n % chips) * 2 + (1 - core if n < chips else core)
        pairs.append((weight_ref.at[:, place], held.at[n]))
    copies = fetched(pairs, sems)
    label_at = slice(capacity, capacity + 1)
    if swaps:
        count = len(pieces_refs)
        pieces = [ref[0].astype(jnp.float32) for ref in pieces_refs]
        labels = functools.reduce(jnp.maximum, [x[label_at, : count * slots] for x in pieces])
        row = iota((row_count, count * slots), 0).astype(jnp.float32)
        put = jnp.where(row == labels, 1.0, 0.0).astype(jnp.bfloat16)
        total = dot(put, jnp.concatenate(pieces, 0).astype(jnp.bfloat16), NN)
    else:
        row = iota((row_count, slots), 0).astype(jnp.float32)

        def placed(p, total):
            piece = pieces_ref[p]
            labels = piece.astype(jnp.float32)[label_at, :slots]
            put = jnp.where(row == labels, 1.0, 0.0).astype(jnp.bfloat16)
            return total + dot(put, piece, NN)

        total = lax.fori_loop(0, count, placed, jnp.zeros((row_count, hidden), jnp.float32))
    pre = pre_ref[...].astype(jnp.float32)
    cdf = 0.5 * (1.0 + lax.erf(pre * 0.7071067811865476))
    slope = cdf + pre * jnp.exp(-0.5 * pre * pre) * 0.3989422804014327
    grad_pre = (total * slope).T.astype(jnp.bfloat16)
    outgoing = []
    span = lax.axis_index("span")

    def send(n, product):
        for i in range(spans):
            parts = [product[j * block + i * width : j * block + (i + 1) * width] for j in range(4)]
            part = jnp.concatenate(parts, 0).astype(jnp.bfloat16).T
            out_ref[n * spans + lax.bitwise_xor(span, i)] = part
        out_hbm = send_hbm if n < chips else keep_hbm
        source, target = pl.ds(n * spans, spans), pl.ds(n % chips * spans, spans)
        copy = pltpu.make_async_copy(out_ref.at[source], out_hbm.at[target], out_sems.at[n])
        outgoing.append(copy)
        copy.start()

    waiting = None
    for n in range(2 * chips):
        copies[n].wait()
        product = dot(held[n].reshape(4 * block, hidden), grad_pre, NN)
        if waiting is not None:
            send(n - 1, waiting)
        waiting = product
    send(2 * chips - 1, waiting)
    for copy in outgoing:
        copy.wait()


def up_pieces(pieces, pre, weight, heads, capacity):
    width = weight.shape[0] // heads
    spans = lax.axis_size("span")
    blocks = heads // spans
    return pl.pallas_call(
        functools.partial(up_kernel, heads, capacity, len(pieces) > 1),
        out_shape=[jax.ShapeDtypeStruct((heads // 2, pre.shape[0], width), jnp.bfloat16)] * 2,
        in_specs=in_vmem(len(pieces) + 1) + in_hbm(1),
        out_specs=in_hbm(2),
        scratch_shapes=[
            pltpu.VMEM((blocks, 4, spans * width // 4, weight.shape[1]), jnp.bfloat16),
            pltpu.VMEM((heads, pre.shape[0], width), jnp.bfloat16),
            pltpu.SemaphoreType.DMA((blocks,)),
            pltpu.SemaphoreType.DMA((blocks,)),
        ],
        compiler_params=params(52),
        cost_estimate=pl.CostEstimate(
            flops=8 * pre.shape[0] * weight.size, bytes_accessed=8 * weight.size, transcendentals=0
        ),
        name="up_product",
    )(*pieces, pre, weight.reshape(4, blocks, -1, weight.shape[1]))


class Rows:
    def __init__(self, columns, patches):
        heads = columns // HEAD_DIM
        self.lanes = -(-3 * patches // 128) * 128
        self.columns, self.patches = columns, patches
        self.values, self.keys, self.probs_at = 0, columns, 2 * columns
        self.total = 2 * columns + heads * patches

    def head(self, start, h):
        return slice(start + h * HEAD_DIM, start + (h + 1) * HEAD_DIM)

    def kind(self, start):
        return slice(start, start + self.columns)

    def probs(self, h):
        return slice(self.probs_at + h * self.patches, self.probs_at + (h + 1) * self.patches)

    def side(self, i):
        start = i * self.total
        return start, start + self.columns

    def side_probs(self, i, h):
        start = i * self.total + self.probs_at + h * self.patches
        return slice(start, start + self.patches)


def softmax_kernel(lengths_ref, first_ref, own_ref, odd_ref, even_ref, held, side_ref, done_ref):
    columns, patches = own_ref.shape[0] // 3, own_ref.shape[1]
    rows = Rows(columns, patches)
    heads = columns // HEAD_DIM
    step_even = 1 - 2 * lax.rem(lax.axis_index("grp"), 2)
    offsets = (0, -step_even, step_even)
    first = first_ref[0, 0]

    def image_of(shape, dim, block):
        token = iota(shape, dim) // 4 + (first + block * (patches // 4))

        def step(i, state):
            image, bound = state
            bound = bound + lengths_ref[0, i]
            return image + jnp.where(token >= bound, 1, 0), bound

        start = (jnp.where(token < 0, -1, 0), jnp.int32(0))
        return lax.fori_loop(0, lengths_ref.shape[1], step, start)[0]

    down = [image_of((patches, 1), 0, b) for b in offsets]
    across = [image_of((1, patches), 1, b) for b in offsets]

    def kind(block, t, h):
        if block == 0:
            start = t * columns + h * HEAD_DIM
            return own_ref[start : start + HEAD_DIM].astype(jnp.float32)
        return unpacked((odd_ref, even_ref)[block - 1], t * heads + h, 3 * columns, patches)

    def wide(t, which, h):
        return jnp.concatenate([kind(b, t, h) for b in which], 1).astype(jnp.bfloat16)

    def softmax(queries, keys, same):
        scores = jnp.where(same, dot(queries, keys, TN) * SCALE, -jnp.inf)
        weights = jnp.exp(scores - jnp.max(scores, 1, keepdims=True))
        return weights * (1.0 / jnp.sum(weights, 1, keepdims=True))

    for h in range(heads):
        held[rows.head(rows.values, h), : 3 * patches] = wide(2, (0, 1, 2), h)
        held[rows.head(rows.keys, h), : 3 * patches] = wide(1, (0, 1, 2), h)
    same_own = down[0] == jnp.concatenate(across, 1)
    same_side = [down[b] == jnp.concatenate([across[0], across[b]], 1) for b in (1, 2)]
    for h in range(heads):
        keys = held[rows.head(rows.keys, h), : 3 * patches]
        probs = softmax(kind(0, 0, h).astype(jnp.bfloat16), keys, same_own)
        held[rows.probs(h), : 3 * patches] = probs.astype(jnp.bfloat16)
        for i, b in enumerate((1, 2)):
            queries_at, attended_at = rows.side(i)
            queries = kind(b, 0, h).astype(jnp.bfloat16)
            probs = softmax(queries, wide(1, (0, b), h), same_side[i])
            seen = dot(probs.astype(jnp.bfloat16), wide(2, (0, b), h), NT)
            side_ref[rows.head(queries_at, h)] = queries
            side_ref[rows.head(attended_at, h)] = seen.T.astype(jnp.bfloat16)
            side_ref[rows.side_probs(i, h)] = probs[:, :patches].T.astype(jnp.bfloat16)
    done_ref[...] = jnp.zeros(done_ref.shape, jnp.float32)


def softmax_parts(lengths, first, own, odd, even):
    columns, patches = own.shape[0] // 3, own.shape[1]
    rows = Rows(columns, patches)
    smem = pl.BlockSpec(memory_space=pltpu.MemorySpace.SMEM)
    work = (columns // HEAD_DIM) * patches * patches
    return pl.pallas_call(
        softmax_kernel,
        out_shape=(
            jax.ShapeDtypeStruct((rows.total, rows.lanes), jnp.bfloat16),
            jax.ShapeDtypeStruct((2 * rows.total, patches), jnp.bfloat16),
            jax.ShapeDtypeStruct((8, 128), jnp.float32),
        ),
        in_specs=[smem, smem] + in_vmem(3),
        out_specs=tuple(in_vmem(3)),
        compiler_params=params(32),
        cost_estimate=pl.CostEstimate(
            flops=100_000 * work, bytes_accessed=500 * work, transcendentals=9 * work
        ),
        name="softmax_parts",
    )(lengths.reshape(1, -1), first.reshape(1, 1), own, odd, even)


def packed_rows(columns, patches):
    heads = columns // HEAD_DIM
    return patches // 128 * columns + (heads + 1) // 2 * HEAD_DIM


def packed(x):
    columns, patches = x.shape
    whole = patches // 128 * 128
    parts = [x[:, at : at + 128] for at in range(0, whole, 128)]
    tails = [x[at : at + HEAD_DIM, whole:] for at in range(0, columns, HEAD_DIM)]
    tails += [jnp.zeros_like(tails[0])] * (len(tails) % 2)
    parts += [jnp.concatenate(tails[i : i + 2], 1) for i in range(0, len(tails), 2)]
    return jnp.concatenate(parts, 0)


def unpacked(ref, h, columns, patches):
    tiles = patches // 128
    starts = [t * columns + h * HEAD_DIM for t in range(tiles)]
    parts = [ref[at : at + HEAD_DIM].astype(jnp.float32) for at in starts]
    at = tiles * columns + h // 2 * HEAD_DIM
    tail = ref[at : at + HEAD_DIM].astype(jnp.float32)
    return jnp.concatenate(parts + [tail[:, h % 2 * 64 : h % 2 * 64 + 64]], 1)


def gather_kernel(count, *refs):
    _, row_count, width = refs[0].shape
    total = refs[0][0].astype(jnp.float32)
    for p in range(1, count):
        total = total + refs[p][0].astype(jnp.float32)
    out_ref, packed_ref = refs[-2:]
    total = total.astype(jnp.bfloat16)
    columns = width // 4
    patch = iota((row_count, 4 * row_count), 1)
    token = iota((row_count, 4 * row_count), 0)
    result = jnp.zeros((columns, 4 * row_count), jnp.float32)
    for j in range(4):
        put = jnp.where(patch == 4 * token + j, 1.0, 0.0).astype(jnp.bfloat16)
        result = result + dot(total[:, j * columns : (j + 1) * columns], put, TN)
    out_ref[...] = result.astype(jnp.bfloat16)
    packed_ref[...] = packed(result).astype(jnp.bfloat16)


def gathered(pieces, later):
    _, row_count, width = pieces[0].shape
    size = len(pieces) * row_count * width
    return pl.pallas_call(
        functools.partial(gather_kernel, len(pieces)),
        out_shape=(
            jax.ShapeDtypeStruct((width // 4, 4 * row_count), jnp.bfloat16),
            jax.ShapeDtypeStruct((packed_rows(width // 4, 4 * row_count), 128), jnp.bfloat16),
        ),
        in_specs=in_vmem(len(pieces) + 1),
        out_specs=tuple(in_vmem(2)),
        compiler_params=params(16),
        cost_estimate=pl.CostEstimate(
            flops=20_000 * size, bytes_accessed=400 * size, transcendentals=0
        ),
        name="gather_sum",
    )(*pieces, later)


def own_kernel(grad_ref, own_ref, held_ref, query_ref, key_ref, value_ref):
    columns, patches = grad_ref.shape
    rows = Rows(columns, patches)
    for h in range(columns // HEAD_DIM):
        cols = slice(h * HEAD_DIM, (h + 1) * HEAD_DIM)
        grad = grad_ref[cols]
        slope = dot(grad, held_ref[rows.head(rows.values, h), : 3 * patches], TN)
        probs = held_ref[rows.probs(h), : 3 * patches]
        wide = probs.astype(jnp.float32)
        delta = jnp.sum(wide * slope, 1, keepdims=True)
        scores = (wide * (slope - delta)).astype(jnp.bfloat16)
        query = dot(scores, held_ref[rows.head(rows.keys, h), : 3 * patches], NT) * SCALE
        query_ref[cols] = query.T.astype(jnp.bfloat16)
        key_ref[cols] = dot(own_ref[cols], scores[:, :patches], NN)
        value_ref[cols] = dot(grad, probs[:, :patches], NN)


def own_terms(grad, own, held):
    return pl.pallas_call(
        own_kernel,
        out_shape=(
            jax.ShapeDtypeStruct(grad.shape, jnp.bfloat16),
            jax.ShapeDtypeStruct(grad.shape, jnp.float32),
            jax.ShapeDtypeStruct(grad.shape, jnp.float32),
        ),
        in_specs=in_vmem(3),
        out_specs=tuple(in_vmem(3)),
        compiler_params=params(24),
        name="own_terms",
    )(grad, own, held)


def side_kernel(i, grad_ref, key_part_ref, value_part_ref, held_ref, side_ref, key_ref, value_ref):
    columns, patches = key_part_ref.shape
    rows = Rows(columns, patches)
    queries_at, attended_at = rows.side(i)
    for h in range(columns // HEAD_DIM):
        cols = slice(h * HEAD_DIM, (h + 1) * HEAD_DIM)
        wide = unpacked(grad_ref, h, columns, patches)
        grad = wide.astype(jnp.bfloat16)
        slope = dot(held_ref[rows.head(rows.values, h), :patches], grad, TN)
        attended = side_ref[rows.head(attended_at, h)].astype(jnp.float32)
        delta = jnp.sum(wide * attended, 0, keepdims=True)
        probs = side_ref[rows.side_probs(i, h)]
        value = dot(probs, grad, NT)
        scores = (probs.astype(jnp.float32) * (slope - delta)).astype(jnp.bfloat16)
        key = dot(scores, side_ref[rows.head(queries_at, h)], NT)
        key = key_part_ref[cols] + key.T
        key_ref[cols] = (key * SCALE if i == 1 else key).astype(key_ref.dtype)
        value_ref[cols] = (value_part_ref[cols] + value.T).astype(value_ref.dtype)


def side_terms(i, grad, key_part, value_part, held, side):
    kind = jnp.bfloat16 if i == 1 else jnp.float32
    shape = jax.ShapeDtypeStruct(key_part.shape, kind)
    return pl.pallas_call(
        functools.partial(side_kernel, i),
        out_shape=(shape, shape),
        in_specs=in_vmem(5),
        out_specs=tuple(in_vmem(2)),
        compiler_params=params(24),
        name="side_terms",
    )(grad, key_part, value_part, held, side)


def from_pairs(x):
    size = lax.axis_size("grp")

    def swapped(first):
        partner = {}
        for core in range(2):
            for i in range(size):
                j = i + 1 if (i - first) % 2 == 0 else i - 1
                pair = (core, j) if 0 <= j < size else (1 - core, i)
                partner[core * size + i] = pair[0] * size + pair[1]
        return lax.ppermute(x, ("core", "grp"), sorted(partner.items()))

    return swapped(0), swapped(1)


def summed(other, mine, axis):
    other = lax.ppermute(other, axis, [(0, 1), (1, 0)])
    total = (other.astype(jnp.float32) + mine.astype(jnp.float32)).astype(jnp.bfloat16)
    return [total[d : d + 1] for d in range(total.shape[0])]


def exchanged(pieces, axes):
    count = len(pieces)
    return pieces[:1] + [
        lax.ppermute(pieces[d], axes, [(i, i ^ d) for i in range(count)]) for d in range(1, count)
    ]


def on_device(
    grad_out, destination, w_down, pre_act, w_up, queries, key_states, value_states, lengths
):
    groups = lax.axis_size("grp")
    spans = lax.axis_size("span")
    heads = lax.axis_size(("chip", "core", "span"))
    row_count = grad_out.shape[0]
    capacity, _ = padded_slots(row_count, groups)
    pieces = down_pieces(destination, grad_out, w_down, groups, spans)
    pieces, queries, key_states, value_states = lax.optimization_barrier(
        (pieces, queries, key_states, value_states)
    )
    if len(pieces) > 1:
        arrived = exchanged(summed(*pieces, "span"), "grp")
    else:
        axes = ("grp", "span")
        arrived = [lax.all_to_all(pieces[0], axes, split_axis=0, concat_axis=0, tiled=True)]
    own = jnp.concatenate([queries.T, key_states.T, value_states.T], 0)
    even, odd = from_pairs(packed(own))
    first = lax.axis_index("grp") * row_count
    other, shares = up_pieces(arrived, pre_act, w_up, heads, capacity)
    other, odd, even = lax.optimization_barrier((other, odd, even))
    other = lax.ppermute(other, "core", [(0, 1), (1, 0)])
    shares = (other.astype(jnp.float32) + shares.astype(jnp.float32)).astype(jnp.bfloat16)
    shares, own = lax.optimization_barrier((shares, own))
    held, side, held_done = softmax_parts(lengths, first, own, odd, even)
    shares = [shares[d : d + 1] for d in range(shares.shape[0])]
    grad, grad_packed = gathered(exchanged(shares, ("chip", "span")), held_done)
    even, odd = from_pairs(grad_packed)
    grad_query, key_part, value_part = own_terms(grad, queries.T, held)
    parts = side_terms(0, odd, key_part, value_part, held, side)
    grad_key, grad_value = side_terms(1, even, *parts, held, side)
    return grad_query.T, grad_key.T, grad_value.T


def solution(mesh):
    sect, grp, span = (mesh.shape[name] for name in ("sect", "grp", "span"))
    finer = jax.sharding.Mesh(
        mesh.devices.reshape(sect // 2, 2, grp, span), ("chip", "core", "grp", "span")
    )
    split = P("grp", ("chip", "core", "span"))
    placed = (
        P("grp", "span"),
        P("grp"),
        P(("chip", "core"), "span"),
        split,
        P(None, ("chip", "core", "span")),
        split,
        split,
        split,
        P(),
    )
    return jax.shard_map(
        on_device,
        mesh=finer,
        in_specs=placed,
        out_specs=(split, split, split),
        check_vma=False,
    )
```

```python
import functools

import jax
import jax.numpy as jnp
from jax import lax
from jax.experimental import pallas as pl
from jax.experimental.pallas import tpu as pltpu
from jax.sharding import PartitionSpec as P

HEAD_DIM = 80
SCALE = HEAD_DIM**-0.5
MIB = 1024 * 1024
VMEM = pltpu.MemorySpace.VMEM
NT = (((1,), (1,)), ((), ()))
NN = (((1,), (0,)), ((), ()))
TN = (((0,), (0,)), ((), ()))


def dot(a, b, dims):
    return lax.dot_general(a, b, dims, preferred_element_type=jnp.float32)


def iota(shape, dim):
    return lax.broadcasted_iota(jnp.int32, shape, dim)


def params(mib):
    return pltpu.CompilerParams(vmem_limit_bytes=mib * MIB)


def in_vmem(count):
    return [pl.BlockSpec(memory_space=VMEM) for _ in range(count)]


def in_hbm(count):
    return [pl.BlockSpec(memory_space=pltpu.MemorySpace.HBM) for _ in range(count)]


def fetched(pairs, sems):
    copies = [pltpu.make_async_copy(a, b, sems.at[i]) for i, (a, b) in enumerate(pairs)]
    for copy in copies:
        copy.start()
    return copies


def padded_slots(row_count, groups):
    offsets = min(groups, row_count // 2)
    capacity = row_count // offsets
    return capacity, -(-(capacity + 1) // 8) * 8


def by_swaps(groups, spans, slots, hidden):
    return spans == 2 and groups in (2, 4, 8) and groups * slots <= hidden


def down_kernel(groups, spans, capacity, slots, steps, dest_hbm, rows_hbm, weight_ref, *refs):
    *outs, dest_ref, rows_ref, held, total_ref, pieces_ref, sems, out_sems = refs
    me, span = lax.axis_index("grp"), lax.axis_index("span")
    row_count = rows_ref.shape[0]
    hidden = weight_ref.shape[0] // spans
    everything = pl.ds(0, weight_ref.shape[0])
    pairs = [(dest_hbm, dest_ref), (rows_hbm, rows_ref)]
    for at, step in steps:
        part = (everything, pl.ds(at, step))
        pairs.append((weight_ref.at[part], held.at[part]))
    copies = fetched(pairs, sems)
    copies[0].wait()
    across = jnp.broadcast_to(dest_ref[...].astype(jnp.float32), (row_count, row_count))
    down = across.T
    group_across = jnp.floor((across + 0.5) * (1.0 / row_count))
    group_down = jnp.floor((down + 0.5) * (1.0 / row_count))
    slot_down = down - group_down * row_count
    same = group_across == group_down
    earlier = iota((row_count, row_count), 0) < iota((row_count, row_count), 1)
    later = iota((row_count, row_count), 1) < iota((row_count, row_count), 0)
    rank_across = jnp.sum(jnp.where(same & earlier, 1.0, 0.0), 0, keepdims=True)
    rank_down = jnp.sum(jnp.where(same & later, 1.0, 0.0), 1, keepdims=True)
    row_of = group_across[:1] * slots + rank_across
    places = iota((groups * slots, row_count), 0).astype(jnp.float32)
    pick = jnp.where(places == row_of, 1.0, 0.0).astype(jnp.bfloat16)
    swaps = by_swaps(groups, spans, slots, hidden)
    lane = iota((row_count, hidden), 1).astype(jnp.float32)
    labels = []
    for g in range(groups):
        shift = (lax.bitwise_xor(me, g) * slots).astype(jnp.float32) if swaps else 0.0
        hit = (lane == rank_down + shift) & (group_down[:, :1] == g)
        labels.append(jnp.sum(jnp.where(hit, slot_down[:, :1] + 1.0, 0.0), 0, keepdims=True) - 1.0)
    label_row = iota((slots, hidden), 0) == capacity
    copies[1].wait()
    for n, (at, step) in enumerate(steps):
        turned = rows_ref[:, at : at + step].astype(jnp.float32).T.astype(jnp.bfloat16)
        copies[2 + n].wait()
        product = dot(held[:, at : at + step], turned, NN)
        total_ref[...] = product if n == 0 else total_ref[...] + product
    for s in range(spans):
        part = total_ref[s * hidden : (s + 1) * hidden].astype(jnp.bfloat16)
        moved = dot(pick, part, NT)
        said = jnp.where(span == s, 1.0, 0.0) if swaps else 1.0
        for g in range(groups):
            piece = jnp.where(label_row, labels[g] * said, moved[g * slots : (g + 1) * slots])
            pieces_ref[s, g] = piece.astype(jnp.bfloat16)
    if swaps:
        pairs = [
            (pieces_ref.at[s, lax.bitwise_xor(me, d)], out.at[d])
            for out, s in zip(outs, (1 - span, span))
            for d in range(groups)
        ]
    else:
        pairs = [(pieces_ref.at[s], outs[0].at[:, s]) for s in range(spans)]
    for copy in fetched(pairs, out_sems):
        copy.wait()


def down_pieces(dest, rows, weight, groups, spans):
    row_count = rows.shape[0]
    capacity, slots = padded_slots(row_count, groups)
    hidden = weight.shape[0] // spans
    depth = weight.shape[1]
    edges = [depth * i // 8 for i in (0, 1, 3, 5, 8)]
    steps = [(i, j - i) for i, j in zip(edges, edges[1:])]
    swaps = by_swaps(groups, spans, slots, hidden)
    shape = (groups, spans, slots, hidden)
    shapes = [shape[:1] + shape[2:]] * 2 if swaps else [shape]
    pieces = pl.pallas_call(
        functools.partial(down_kernel, groups, spans, capacity, slots, steps),
        out_shape=[jax.ShapeDtypeStruct(x, jnp.bfloat16) for x in shapes],
        in_specs=in_hbm(3),
        out_specs=in_hbm(len(shapes)),
        scratch_shapes=[
            pltpu.VMEM((1, row_count), jnp.int32),
            pltpu.VMEM(rows.shape, jnp.bfloat16),
            pltpu.VMEM(weight.shape, jnp.bfloat16),
            pltpu.VMEM((weight.shape[0], row_count), jnp.float32),
            pltpu.VMEM((spans, groups, slots, hidden), jnp.bfloat16),
            pltpu.SemaphoreType.DMA((2 + len(steps),)),
            pltpu.SemaphoreType.DMA((2 * groups if swaps else spans,)),
        ],
        compiler_params=params(60),
        name="down_product",
    )(dest.reshape(1, row_count), rows, weight)
    if swaps:
        return pieces
    return [pieces[0].reshape(groups * spans, slots, hidden)]


def up_kernel(heads, capacity, swaps, *refs):
    *pieces_refs, pre_ref, weight_ref, send_hbm, keep_hbm, held, out_ref, sems, out_sems = refs
    pieces_ref = pieces_refs[0]
    row_count, hidden = pre_ref.shape
    count, slots, _ = pieces_ref.shape
    width = weight_ref.shape[2] // lax.axis_size("span")
    spans = lax.axis_size("span")
    core = lax.axis_index("core")
    chip = lax.axis_index("chip")
    chips = heads // (2 * spans)
    block = spans * width

    pairs = []
    for n in range(2 * chips):
        place = lax.bitwise_xor(chip, n % chips) * 2 + (1 - core if n < chips else core)
        pairs.append((weight_ref.at[:, place], held.at[n]))
    copies = fetched(pairs, sems)
    label_at = slice(capacity, capacity + 1)
    if swaps:
        count = len(pieces_refs)
        pieces = [ref[0].astype(jnp.float32) for ref in pieces_refs]
        labels = functools.reduce(jnp.maximum, [x[label_at, : count * slots] for x in pieces])
        row = iota((row_count, count * slots), 0).astype(jnp.float32)
        put = jnp.where(row == labels, 1.0, 0.0).astype(jnp.bfloat16)
        total = dot(put, jnp.concatenate(pieces, 0).astype(jnp.bfloat16), NN)
    else:
        row = iota((row_count, slots), 0).astype(jnp.float32)

        def placed(p, total):
            piece = pieces_ref[p]
            labels = piece.astype(jnp.float32)[label_at, :slots]
            put = jnp.where(row == labels, 1.0, 0.0).astype(jnp.bfloat16)
            return total + dot(put, piece, NN)

        total = lax.fori_loop(0, count, placed, jnp.zeros((row_count, hidden), jnp.float32))
    pre = pre_ref[...].astype(jnp.float32)
    cdf = 0.5 * (1.0 + lax.erf(pre * 0.7071067811865476))
    slope = cdf + pre * jnp.exp(-0.5 * pre * pre) * 0.3989422804014327
    grad_pre = (total * slope).T.astype(jnp.bfloat16)
    outgoing = []
    span = lax.axis_index("span")

    def send(n, product):
        for i in range(spans):
            parts = [product[j * block + i * width : j * block + (i + 1) * width] for j in range(4)]
            part = jnp.concatenate(parts, 0).astype(jnp.bfloat16).T
            out_ref[n * spans + lax.bitwise_xor(span, i)] = part
        out_hbm = send_hbm if n < chips else keep_hbm
        source, target = pl.ds(n * spans, spans), pl.ds(n % chips * spans, spans)
        copy = pltpu.make_async_copy(out_ref.at[source], out_hbm.at[target], out_sems.at[n])
        outgoing.append(copy)
        copy.start()

    waiting = None
    for n in range(2 * chips):
        copies[n].wait()
        product = dot(held[n].reshape(4 * block, hidden), grad_pre, NN)
        if waiting is not None:
            send(n - 1, waiting)
        waiting = product
    send(2 * chips - 1, waiting)
    for copy in outgoing:
        copy.wait()


def up_pieces(pieces, pre, weight, heads, capacity):
    width = weight.shape[0] // heads
    spans = lax.axis_size("span")
    blocks = heads // spans
    return pl.pallas_call(
        functools.partial(up_kernel, heads, capacity, len(pieces) > 1),
        out_shape=[jax.ShapeDtypeStruct((heads // 2, pre.shape[0], width), jnp.bfloat16)] * 2,
        in_specs=in_vmem(len(pieces) + 1) + in_hbm(1),
        out_specs=in_hbm(2),
        scratch_shapes=[
            pltpu.VMEM((blocks, 4, spans * width // 4, weight.shape[1]), jnp.bfloat16),
            pltpu.VMEM((heads, pre.shape[0], width), jnp.bfloat16),
            pltpu.SemaphoreType.DMA((blocks,)),
            pltpu.SemaphoreType.DMA((blocks,)),
        ],
        compiler_params=params(52),
        cost_estimate=pl.CostEstimate(
            flops=8 * pre.shape[0] * weight.size, bytes_accessed=8 * weight.size, transcendentals=0
        ),
        name="up_product",
    )(*pieces, pre, weight.reshape(4, blocks, -1, weight.shape[1]))


class Rows:
    def __init__(self, columns, patches):
        heads = columns // HEAD_DIM
        self.lanes = -(-3 * patches // 128) * 128
        self.columns, self.patches = columns, patches
        self.values, self.keys, self.probs_at = 0, columns, 2 * columns
        self.total = 2 * columns + heads * patches

    def head(self, start, h):
        return slice(start + h * HEAD_DIM, start + (h + 1) * HEAD_DIM)

    def kind(self, start):
        return slice(start, start + self.columns)

    def probs(self, h):
        return slice(self.probs_at + h * self.patches, self.probs_at + (h + 1) * self.patches)

    def side(self, i):
        start = i * self.total
        return start, start + self.columns

    def side_probs(self, i, h):
        start = i * self.total + self.probs_at + h * self.patches
        return slice(start, start + self.patches)


def softmax_kernel(lengths_ref, first_ref, own_ref, odd_ref, even_ref, held, side_ref, done_ref):
    columns, patches = own_ref.shape[0] // 3, own_ref.shape[1]
    rows = Rows(columns, patches)
    heads = columns // HEAD_DIM
    step_even = 1 - 2 * lax.rem(lax.axis_index("grp"), 2)
    offsets = (0, -step_even, step_even)
    first = first_ref[0, 0]

    def image_of(shape, dim, block):
        token = iota(shape, dim) // 4 + (first + block * (patches // 4))

        def step(i, state):
            image, bound = state
            bound = bound + lengths_ref[0, i]
            return image + jnp.where(token >= bound, 1, 0), bound

        start = (jnp.where(token < 0, -1, 0), jnp.int32(0))
        return lax.fori_loop(0, lengths_ref.shape[1], step, start)[0]

    down = [image_of((patches, 1), 0, b) for b in offsets]
    across = [image_of((1, patches), 1, b) for b in offsets]

    def kind(block, t, h):
        if block == 0:
            start = t * columns + h * HEAD_DIM
            return own_ref[start : start + HEAD_DIM].astype(jnp.float32)
        return unpacked((odd_ref, even_ref)[block - 1], t * heads + h, 3 * columns, patches)

    def wide(t, which, h):
        return jnp.concatenate([kind(b, t, h) for b in which], 1).astype(jnp.bfloat16)

    def softmax(queries, keys, same):
        scores = jnp.where(same, dot(queries, keys, TN) * SCALE, -jnp.inf)
        weights = jnp.exp(scores - jnp.max(scores, 1, keepdims=True))
        return weights * (1.0 / jnp.sum(weights, 1, keepdims=True))

    for h in range(heads):
        held[rows.head(rows.values, h), : 3 * patches] = wide(2, (0, 1, 2), h)
        held[rows.head(rows.keys, h), : 3 * patches] = wide(1, (0, 1, 2), h)
    same_own = down[0] == jnp.concatenate(across, 1)
    same_side = [down[b] == jnp.concatenate([across[0], across[b]], 1) for b in (1, 2)]
    for h in range(heads):
        keys = held[rows.head(rows.keys, h), : 3 * patches]
        probs = softmax(kind(0, 0, h).astype(jnp.bfloat16), keys, same_own)
        held[rows.probs(h), : 3 * patches] = probs.astype(jnp.bfloat16)
        for i, b in enumerate((1, 2)):
            queries_at, attended_at = rows.side(i)
            queries = kind(b, 0, h).astype(jnp.bfloat16)
            probs = softmax(queries, wide(1, (0, b), h), same_side[i])
            seen = dot(probs.astype(jnp.bfloat16), wide(2, (0, b), h), NT)
            side_ref[rows.head(queries_at, h)] = queries
            side_ref[rows.head(attended_at, h)] = seen.T.astype(jnp.bfloat16)
            side_ref[rows.side_probs(i, h)] = probs[:, :patches].T.astype(jnp.bfloat16)
    done_ref[...] = jnp.zeros(done_ref.shape, jnp.float32)


def softmax_parts(lengths, first, own, odd, even):
    columns, patches = own.shape[0] // 3, own.shape[1]
    rows = Rows(columns, patches)
    smem = pl.BlockSpec(memory_space=pltpu.MemorySpace.SMEM)
    work = (columns // HEAD_DIM) * patches * patches
    return pl.pallas_call(
        softmax_kernel,
        out_shape=(
            jax.ShapeDtypeStruct((rows.total, rows.lanes), jnp.bfloat16),
            jax.ShapeDtypeStruct((2 * rows.total, patches), jnp.bfloat16),
            jax.ShapeDtypeStruct((8, 128), jnp.float32),
        ),
        in_specs=[smem, smem] + in_vmem(3),
        out_specs=tuple(in_vmem(3)),
        compiler_params=params(32),
        cost_estimate=pl.CostEstimate(
            flops=100_000 * work, bytes_accessed=500 * work, transcendentals=9 * work
        ),
        name="softmax_parts",
    )(lengths.reshape(1, -1), first.reshape(1, 1), own, odd, even)


def packed_rows(columns, patches):
    heads = columns // HEAD_DIM
    return patches // 128 * columns + (heads + 1) // 2 * HEAD_DIM


def packed(x):
    columns, patches = x.shape
    whole = patches // 128 * 128
    parts = [x[:, at : at + 128] for at in range(0, whole, 128)]
    tails = [x[at : at + HEAD_DIM, whole:] for at in range(0, columns, HEAD_DIM)]
    tails += [jnp.zeros_like(tails[0])] * (len(tails) % 2)
    parts += [jnp.concatenate(tails[i : i + 2], 1) for i in range(0, len(tails), 2)]
    return jnp.concatenate(parts, 0)


def unpacked(ref, h, columns, patches):
    tiles = patches // 128
    starts = [t * columns + h * HEAD_DIM for t in range(tiles)]
    parts = [ref[at : at + HEAD_DIM].astype(jnp.float32) for at in starts]
    at = tiles * columns + h // 2 * HEAD_DIM
    tail = ref[at : at + HEAD_DIM].astype(jnp.float32)
    return jnp.concatenate(parts + [tail[:, h % 2 * 64 : h % 2 * 64 + 64]], 1)


def gather_kernel(count, *refs):
    _, row_count, width = refs[0].shape
    total = refs[0][0].astype(jnp.float32)
    for p in range(1, count):
        total = total + refs[p][0].astype(jnp.float32)
    out_ref, packed_ref = refs[-2:]
    total = total.astype(jnp.bfloat16)
    columns = width // 4
    patch = iota((row_count, 4 * row_count), 1)
    token = iota((row_count, 4 * row_count), 0)
    result = jnp.zeros((columns, 4 * row_count), jnp.float32)
    for j in range(4):
        put = jnp.where(patch == 4 * token + j, 1.0, 0.0).astype(jnp.bfloat16)
        result = result + dot(total[:, j * columns : (j + 1) * columns], put, TN)
    out_ref[...] = result.astype(jnp.bfloat16)
    packed_ref[...] = packed(result).astype(jnp.bfloat16)


def gathered(pieces, later):
    _, row_count, width = pieces[0].shape
    size = len(pieces) * row_count * width
    return pl.pallas_call(
        functools.partial(gather_kernel, len(pieces)),
        out_shape=(
            jax.ShapeDtypeStruct((width // 4, 4 * row_count), jnp.bfloat16),
            jax.ShapeDtypeStruct((packed_rows(width // 4, 4 * row_count), 128), jnp.bfloat16),
        ),
        in_specs=in_vmem(len(pieces) + 1),
        out_specs=tuple(in_vmem(2)),
        compiler_params=params(16),
        cost_estimate=pl.CostEstimate(
            flops=20_000 * size, bytes_accessed=400 * size, transcendentals=0
        ),
        name="gather_sum",
    )(*pieces, later)


def own_kernel(grad_ref, own_ref, held_ref, query_ref, key_ref, value_ref):
    columns, patches = grad_ref.shape
    rows = Rows(columns, patches)
    for h in range(columns // HEAD_DIM):
        cols = slice(h * HEAD_DIM, (h + 1) * HEAD_DIM)
        grad = grad_ref[cols]
        slope = dot(grad, held_ref[rows.head(rows.values, h), : 3 * patches], TN)
        probs = held_ref[rows.probs(h), : 3 * patches]
        wide = probs.astype(jnp.float32)
        delta = jnp.sum(wide * slope, 1, keepdims=True)
        scores = (wide * (slope - delta)).astype(jnp.bfloat16)
        query = dot(scores, held_ref[rows.head(rows.keys, h), : 3 * patches], NT) * SCALE
        query_ref[cols] = query.T.astype(jnp.bfloat16)
        key_ref[cols] = dot(own_ref[cols], scores[:, :patches], NN)
        value_ref[cols] = dot(grad, probs[:, :patches], NN)


def own_terms(grad, own, held):
    return pl.pallas_call(
        own_kernel,
        out_shape=(
            jax.ShapeDtypeStruct(grad.shape, jnp.bfloat16),
            jax.ShapeDtypeStruct(grad.shape, jnp.float32),
            jax.ShapeDtypeStruct(grad.shape, jnp.float32),
        ),
        in_specs=in_vmem(3),
        out_specs=tuple(in_vmem(3)),
        compiler_params=params(24),
        name="own_terms",
    )(grad, own, held)


def side_kernel(i, grad_ref, key_part_ref, value_part_ref, held_ref, side_ref, key_ref, value_ref):
    columns, patches = key_part_ref.shape
    rows = Rows(columns, patches)
    queries_at, attended_at = rows.side(i)
    for h in range(columns // HEAD_DIM):
        cols = slice(h * HEAD_DIM, (h + 1) * HEAD_DIM)
        wide = unpacked(grad_ref, h, columns, patches)
        grad = wide.astype(jnp.bfloat16)
        slope = dot(held_ref[rows.head(rows.values, h), :patches], grad, TN)
        attended = side_ref[rows.head(attended_at, h)].astype(jnp.float32)
        delta = jnp.sum(wide * attended, 0, keepdims=True)
        probs = side_ref[rows.side_probs(i, h)]
        value = dot(probs, grad, NT)
        scores = (probs.astype(jnp.float32) * (slope - delta)).astype(jnp.bfloat16)
        key = dot(scores, side_ref[rows.head(queries_at, h)], NT)
        key = key_part_ref[cols] + key.T
        key_ref[cols] = (key * SCALE if i == 1 else key).astype(key_ref.dtype)
        value_ref[cols] = (value_part_ref[cols] + value.T).astype(value_ref.dtype)


def side_terms(i, grad, key_part, value_part, held, side):
    kind = jnp.bfloat16 if i == 1 else jnp.float32
    shape = jax.ShapeDtypeStruct(key_part.shape, kind)
    return pl.pallas_call(
        functools.partial(side_kernel, i),
        out_shape=(shape, shape),
        in_specs=in_vmem(5),
        out_specs=tuple(in_vmem(2)),
        compiler_params=params(24),
        name="side_terms",
    )(grad, key_part, value_part, held, side)


def from_pairs(x):
    size = lax.axis_size("grp")

    def swapped(first):
        partner = {}
        for core in range(2):
            for i in range(size):
                j = i + 1 if (i - first) % 2 == 0 else i - 1
                pair = (core, j) if 0 <= j < size else (1 - core, i)
                partner[core * size + i] = pair[0] * size + pair[1]
        return lax.ppermute(x, ("core", "grp"), sorted(partner.items()))

    return swapped(0), swapped(1)


def summed(other, mine, axis):
    other = lax.ppermute(other, axis, [(0, 1), (1, 0)])
    total = (other.astype(jnp.float32) + mine.astype(jnp.float32)).astype(jnp.bfloat16)
    return [total[d : d + 1] for d in range(total.shape[0])]


def exchanged(pieces, axes):
    count = len(pieces)
    return pieces[:1] + [
        lax.ppermute(pieces[d], axes, [(i, i ^ d) for i in range(count)]) for d in range(1, count)
    ]


def on_device(
    grad_out, destination, w_down, pre_act, w_up, queries, key_states, value_states, lengths
):
    groups = lax.axis_size("grp")
    spans = lax.axis_size("span")
    heads = lax.axis_size(("chip", "core", "span"))
    row_count = grad_out.shape[0]
    capacity, _ = padded_slots(row_count, groups)
    pieces = down_pieces(destination, grad_out, w_down, groups, spans)
    if len(pieces) > 1:
        pieces = summed(*pieces, "span")
    pieces, queries, key_states, value_states = lax.optimization_barrier(
        (pieces, queries, key_states, value_states)
    )
    if len(pieces) > 1:
        arrived = exchanged(pieces, "grp")
    else:
        axes = ("grp", "span")
        arrived = [lax.all_to_all(pieces[0], axes, split_axis=0, concat_axis=0, tiled=True)]
    own = jnp.concatenate([queries.T, key_states.T, value_states.T], 0)
    even, odd = from_pairs(packed(own))
    first = lax.axis_index("grp") * row_count
    other, shares = up_pieces(arrived, pre_act, w_up, heads, capacity)
    other, odd, even = lax.optimization_barrier((other, odd, even))
    other = lax.ppermute(other, "core", [(0, 1), (1, 0)])
    shares = (other.astype(jnp.float32) + shares.astype(jnp.float32)).astype(jnp.bfloat16)
    shares, own = lax.optimization_barrier((shares, own))
    held, side, held_done = softmax_parts(lengths, first, own, odd, even)
    shares = [shares[d : d + 1] for d in range(shares.shape[0])]
    grad, grad_packed = gathered(exchanged(shares, ("chip", "span")), held_done)
    even, odd = from_pairs(grad_packed)
    grad_query, key_part, value_part = own_terms(grad, queries.T, held)
    parts = side_terms(0, odd, key_part, value_part, held, side)
    grad_key, grad_value = side_terms(1, even, *parts, held, side)
    return grad_query.T, grad_key.T, grad_value.T


def solution(mesh):
    sect, grp, span = (mesh.shape[name] for name in ("sect", "grp", "span"))
    finer = jax.sharding.Mesh(
        mesh.devices.reshape(sect // 2, 2, grp, span), ("chip", "core", "grp", "span")
    )
    split = P("grp", ("chip", "core", "span"))
    placed = (
        P("grp", "span"),
        P("grp"),
        P(("chip", "core"), "span"),
        split,
        P(None, ("chip", "core", "span")),
        split,
        split,
        split,
        P(),
    )
    return jax.shard_map(
        on_device,
        mesh=finer,
        in_specs=placed,
        out_specs=(split, split, split),
        check_vma=False,
    )
```

```python
import functools

import jax
import jax.numpy as jnp
from jax import lax
from jax.experimental import pallas as pl
from jax.experimental.pallas import tpu as pltpu
from jax.sharding import PartitionSpec as P

HEAD_DIM = 80
SCALE = HEAD_DIM**-0.5
MIB = 1024 * 1024
VMEM = pltpu.MemorySpace.VMEM
NT = (((1,), (1,)), ((), ()))
NN = (((1,), (0,)), ((), ()))
TN = (((0,), (0,)), ((), ()))


def dot(a, b, dims):
    return lax.dot_general(a, b, dims, preferred_element_type=jnp.float32)


def iota(shape, dim):
    return lax.broadcasted_iota(jnp.int32, shape, dim)


def params(mib):
    return pltpu.CompilerParams(vmem_limit_bytes=mib * MIB)


def in_vmem(count):
    return [pl.BlockSpec(memory_space=VMEM) for _ in range(count)]


def in_hbm(count):
    return [pl.BlockSpec(memory_space=pltpu.MemorySpace.HBM) for _ in range(count)]


def fetched(pairs, sems):
    copies = [pltpu.make_async_copy(a, b, sems.at[i]) for i, (a, b) in enumerate(pairs)]
    for copy in copies:
        copy.start()
    return copies


def padded_slots(row_count, groups):
    offsets = min(groups, row_count // 2)
    capacity = row_count // offsets
    return capacity, -(-(capacity + 1) // 8) * 8


def one_product(count, slots, hidden):
    return count * slots <= hidden


def down_kernel(groups, spans, capacity, slots, steps, dest_hbm, rows_hbm, weight_ref, out_hbm,
                dest_ref, rows_ref, held, total_ref, pieces_ref, sems, out_sems):
    row_count = rows_ref.shape[0]
    hidden = weight_ref.shape[0] // spans
    everything = pl.ds(0, weight_ref.shape[0])
    pairs = [(dest_hbm, dest_ref), (rows_hbm, rows_ref)]
    for at, step in steps:
        part = (everything, pl.ds(at, step))
        pairs.append((weight_ref.at[part], held.at[part]))
    copies = fetched(pairs, sems)
    copies[0].wait()
    across = jnp.broadcast_to(dest_ref[...].astype(jnp.float32), (row_count, row_count))
    down = across.T
    group_across = jnp.floor((across + 0.5) * (1.0 / row_count))
    group_down = jnp.floor((down + 0.5) * (1.0 / row_count))
    slot_down = down - group_down * row_count
    same = group_across == group_down
    earlier = iota((row_count, row_count), 0) < iota((row_count, row_count), 1)
    later = iota((row_count, row_count), 1) < iota((row_count, row_count), 0)
    rank_across = jnp.sum(jnp.where(same & earlier, 1.0, 0.0), 0, keepdims=True)
    rank_down = jnp.sum(jnp.where(same & later, 1.0, 0.0), 1, keepdims=True)
    row_of = group_across[:1] * slots + rank_across
    places = iota((groups * slots, row_count), 0).astype(jnp.float32)
    pick = jnp.where(places == row_of, 1.0, 0.0).astype(jnp.bfloat16)
    lane = iota((row_count, hidden), 1).astype(jnp.float32)
    shift = 0.0
    if one_product(groups * spans, slots, hidden):
        device = lax.axis_index("grp") * spans + lax.axis_index("span")
        shift = (device * slots).astype(jnp.float32)
    at_rank = lane == rank_down + shift
    label_row = iota((slots, hidden), 0) == capacity
    labels = []
    for g in range(groups):
        hit = at_rank & (group_down[:, :1] == g)
        labels.append(jnp.sum(jnp.where(hit, slot_down[:, :1] + 1.0, 0.0), 0, keepdims=True) - 1.0)
    copies[1].wait()
    for n, (at, step) in enumerate(steps):
        turned = rows_ref[:, at : at + step].astype(jnp.float32).T.astype(jnp.bfloat16)
        copies[2 + n].wait()
        product = dot(held[:, at : at + step], turned, NN)
        total_ref[...] = product if n == 0 else total_ref[...] + product
    outgoing = []
    for s in range(spans):
        part = total_ref[s * hidden : (s + 1) * hidden].astype(jnp.bfloat16)
        moved = dot(pick, part, NT)
        for g in range(groups):
            piece = jnp.where(label_row, labels[g], moved[g * slots : (g + 1) * slots])
            pieces_ref[s, g] = piece.astype(jnp.bfloat16)
        copy = pltpu.make_async_copy(pieces_ref.at[s], out_hbm.at[:, s], out_sems.at[s])
        copy.start()
        outgoing.append(copy)
    for copy in outgoing:
        copy.wait()


def down_pieces(dest, rows, weight, groups, spans):
    row_count = rows.shape[0]
    capacity, slots = padded_slots(row_count, groups)
    hidden = weight.shape[0] // spans
    depth = weight.shape[1]
    edges = [depth * i // 8 for i in (0, 1, 3, 5, 8)]
    steps = [(i, j - i) for i, j in zip(edges, edges[1:])]
    pieces = pl.pallas_call(
        functools.partial(down_kernel, groups, spans, capacity, slots, steps),
        out_shape=jax.ShapeDtypeStruct((groups, spans, slots, hidden), jnp.bfloat16),
        in_specs=in_hbm(3),
        out_specs=in_hbm(1)[0],
        scratch_shapes=[
            pltpu.VMEM((1, row_count), jnp.int32),
            pltpu.VMEM(rows.shape, jnp.bfloat16),
            pltpu.VMEM(weight.shape, jnp.bfloat16),
            pltpu.VMEM((weight.shape[0], row_count), jnp.float32),
            pltpu.VMEM((spans, groups, slots, hidden), jnp.bfloat16),
            pltpu.SemaphoreType.DMA((2 + len(steps),)),
            pltpu.SemaphoreType.DMA((spans,)),
        ],
        compiler_params=params(60),
        name="down_product",
    )(dest.reshape(1, row_count), rows, weight)
    return pieces.reshape(groups * spans, slots, hidden)


def up_kernel(heads, capacity, pieces_ref, pre_ref, weight_ref, send_hbm, keep_hbm, held, out_ref,
              sems, out_sems):
    row_count, hidden = pre_ref.shape
    count, slots, _ = pieces_ref.shape
    width = weight_ref.shape[2] // lax.axis_size("span")
    spans = lax.axis_size("span")
    core = lax.axis_index("core")
    chip = lax.axis_index("chip")
    chips = heads // (2 * spans)
    block = spans * width

    pairs = []
    for n in range(2 * chips):
        place = lax.bitwise_xor(chip, n % chips) * 2 + (1 - core if n < chips else core)
        pairs.append((weight_ref.at[:, place], held.at[n]))
    copies = fetched(pairs, sems)
    label_at = slice(capacity, capacity + 1)
    if one_product(count, slots, hidden):
        pieces = [pieces_ref[p].astype(jnp.float32) for p in range(count)]
        labels = functools.reduce(jnp.maximum, [x[label_at, : count * slots] for x in pieces])
        row = iota((row_count, count * slots), 0).astype(jnp.float32)
        put = jnp.where(row == labels, 1.0, 0.0).astype(jnp.bfloat16)
        total = dot(put, jnp.concatenate(pieces, 0).astype(jnp.bfloat16), NN)
    else:
        row = iota((row_count, slots), 0).astype(jnp.float32)

        def placed(p, total):
            piece = pieces_ref[p]
            labels = piece.astype(jnp.float32)[label_at, :slots]
            put = jnp.where(row == labels, 1.0, 0.0).astype(jnp.bfloat16)
            return total + dot(put, piece, NN)

        total = lax.fori_loop(0, count, placed, jnp.zeros((row_count, hidden), jnp.float32))
    pre = pre_ref[...].astype(jnp.float32)
    cdf = 0.5 * (1.0 + lax.erf(pre * 0.7071067811865476))
    slope = cdf + pre * jnp.exp(-0.5 * pre * pre) * 0.3989422804014327
    grad_pre = (total * slope).T.astype(jnp.bfloat16)
    outgoing = []
    span = lax.axis_index("span")

    def send(n, product):
        for i in range(spans):
            parts = [product[j * block + i * width : j * block + (i + 1) * width] for j in range(4)]
            part = jnp.concatenate(parts, 0).astype(jnp.bfloat16).T
            out_ref[n * spans + lax.bitwise_xor(span, i)] = part
        out_hbm = send_hbm if n < chips else keep_hbm
        source, target = pl.ds(n * spans, spans), pl.ds(n % chips * spans, spans)
        copy = pltpu.make_async_copy(out_ref.at[source], out_hbm.at[target], out_sems.at[n])
        outgoing.append(copy)
        copy.start()

    waiting = None
    for n in range(2 * chips):
        copies[n].wait()
        product = dot(held[n].reshape(4 * block, hidden), grad_pre, NN)
        if waiting is not None:
            send(n - 1, waiting)
        waiting = product
    send(2 * chips - 1, waiting)
    for copy in outgoing:
        copy.wait()


def up_pieces(pieces, pre, weight, heads, capacity):
    width = weight.shape[0] // heads
    spans = lax.axis_size("span")
    blocks = heads // spans
    return pl.pallas_call(
        functools.partial(up_kernel, heads, capacity),
        out_shape=[jax.ShapeDtypeStruct((heads // 2, pre.shape[0], width), jnp.bfloat16)] * 2,
        in_specs=in_vmem(2) + in_hbm(1),
        out_specs=in_hbm(2),
        scratch_shapes=[
            pltpu.VMEM((blocks, 4, spans * width // 4, weight.shape[1]), jnp.bfloat16),
            pltpu.VMEM((heads, pre.shape[0], width), jnp.bfloat16),
            pltpu.SemaphoreType.DMA((blocks,)),
            pltpu.SemaphoreType.DMA((blocks,)),
        ],
        compiler_params=params(52),
        cost_estimate=pl.CostEstimate(
            flops=8 * pre.shape[0] * weight.size, bytes_accessed=8 * weight.size, transcendentals=0
        ),
        name="up_product",
    )(pieces, pre, weight.reshape(4, blocks, -1, weight.shape[1]))


class Rows:
    def __init__(self, columns, patches):
        heads = columns // HEAD_DIM
        self.lanes = -(-3 * patches // 128) * 128
        self.columns, self.patches = columns, patches
        self.values, self.keys, self.probs_at = 0, columns, 2 * columns
        self.total = 2 * columns + heads * patches

    def head(self, start, h):
        return slice(start + h * HEAD_DIM, start + (h + 1) * HEAD_DIM)

    def kind(self, start):
        return slice(start, start + self.columns)

    def probs(self, h):
        return slice(self.probs_at + h * self.patches, self.probs_at + (h + 1) * self.patches)

    def side(self, i):
        start = i * self.total
        return start, start + self.columns

    def side_probs(self, i, h):
        start = i * self.total + self.probs_at + h * self.patches
        return slice(start, start + self.patches)


def softmax_kernel(lengths_ref, first_ref, own_ref, odd_ref, even_ref, held, side_ref, done_ref):
    columns, patches = own_ref.shape[0] // 3, own_ref.shape[1]
    rows = Rows(columns, patches)
    heads = columns // HEAD_DIM
    step_even = 1 - 2 * lax.rem(lax.axis_index("grp"), 2)
    offsets = (0, -step_even, step_even)
    first = first_ref[0, 0]

    def image_of(shape, dim, block):
        token = iota(shape, dim) // 4 + (first + block * (patches // 4))

        def step(i, state):
            image, bound = state
            bound = bound + lengths_ref[0, i]
            return image + jnp.where(token >= bound, 1, 0), bound

        start = (jnp.where(token < 0, -1, 0), jnp.int32(0))
        return lax.fori_loop(0, lengths_ref.shape[1], step, start)[0]

    def near(start, i, h):
        part = held[rows.head(start, h), :]
        if i == 0:
            return part[:, : 2 * patches]
        parts = [part[:, :patches], part[:, 2 * patches : 3 * patches]]
        return jnp.concatenate([x.astype(jnp.float32) for x in parts], 1).astype(jnp.bfloat16)

    down = [image_of((patches, 1), 0, b) for b in offsets]
    across = [image_of((1, patches), 1, b) for b in offsets]

    def kind(block, t, h):
        if block == 0:
            start = t * columns + h * HEAD_DIM
            return own_ref[start : start + HEAD_DIM].astype(jnp.float32)
        return unpacked((odd_ref, even_ref)[block - 1], t * heads + h, 3 * columns, patches)

    def wide(t, which, h):
        return jnp.concatenate([kind(b, t, h) for b in which], 1).astype(jnp.bfloat16)

    def softmax(queries, keys, same):
        scores = jnp.where(same, dot(queries, keys, TN) * SCALE, -jnp.inf)
        weights = jnp.exp(scores - jnp.max(scores, 1, keepdims=True))
        return weights * (1.0 / jnp.sum(weights, 1, keepdims=True))

    for h in range(heads):
        held[rows.head(rows.values, h), : 3 * patches] = wide(2, (0, 1, 2), h)
        held[rows.head(rows.keys, h), : 3 * patches] = wide(1, (0, 1, 2), h)
    same_own = down[0] == jnp.concatenate(across, 1)
    same_side = [down[b] == jnp.concatenate([across[0], across[b]], 1) for b in (1, 2)]
    for h in range(heads):
        keys = held[rows.head(rows.keys, h), : 3 * patches]
        probs = softmax(kind(0, 0, h).astype(jnp.bfloat16), keys, same_own)
        held[rows.probs(h), : 3 * patches] = probs.astype(jnp.bfloat16)
        for i, b in enumerate((1, 2)):
            queries_at, attended_at = rows.side(i)
            queries = kind(b, 0, h).astype(jnp.bfloat16)
            probs = softmax(queries, near(rows.keys, i, h), same_side[i])
            seen = dot(probs.astype(jnp.bfloat16), near(rows.values, i, h), NT)
            side_ref[rows.head(queries_at, h)] = queries
            side_ref[rows.head(attended_at, h)] = seen.T.astype(jnp.bfloat16)
            side_ref[rows.side_probs(i, h)] = probs[:, :patches].T.astype(jnp.bfloat16)
    done_ref[...] = jnp.zeros(done_ref.shape, jnp.float32)


def softmax_parts(lengths, first, own, odd, even):
    columns, patches = own.shape[0] // 3, own.shape[1]
    rows = Rows(columns, patches)
    smem = pl.BlockSpec(memory_space=pltpu.MemorySpace.SMEM)
    work = (columns // HEAD_DIM) * patches * patches
    return pl.pallas_call(
        softmax_kernel,
        out_shape=(
            jax.ShapeDtypeStruct((rows.total, rows.lanes), jnp.bfloat16),
            jax.ShapeDtypeStruct((2 * rows.total, patches), jnp.bfloat16),
            jax.ShapeDtypeStruct((8, 128), jnp.float32),
        ),
        in_specs=[smem, smem] + in_vmem(3),
        out_specs=tuple(in_vmem(3)),
        compiler_params=params(32),
        cost_estimate=pl.CostEstimate(
            flops=100_000 * work, bytes_accessed=500 * work, transcendentals=9 * work
        ),
        name="softmax_parts",
    )(lengths.reshape(1, -1), first.reshape(1, 1), own, odd, even)


def packed_rows(columns, patches):
    heads = columns // HEAD_DIM
    return patches // 128 * columns + (heads + 1) // 2 * HEAD_DIM


def packed(x):
    columns, patches = x.shape
    whole = patches // 128 * 128
    parts = [x[:, at : at + 128] for at in range(0, whole, 128)]
    tails = [x[at : at + HEAD_DIM, whole:] for at in range(0, columns, HEAD_DIM)]
    tails += [jnp.zeros_like(tails[0])] * (len(tails) % 2)
    parts += [jnp.concatenate(tails[i : i + 2], 1) for i in range(0, len(tails), 2)]
    return jnp.concatenate(parts, 0)


def unpacked(ref, h, columns, patches):
    tiles = patches // 128
    starts = [t * columns + h * HEAD_DIM for t in range(tiles)]
    parts = [ref[at : at + HEAD_DIM].astype(jnp.float32) for at in starts]
    at = tiles * columns + h // 2 * HEAD_DIM
    tail = ref[at : at + HEAD_DIM].astype(jnp.float32)
    return jnp.concatenate(parts + [tail[:, h % 2 * 64 : h % 2 * 64 + 64]], 1)


def gather_kernel(count, *refs):
    _, row_count, width = refs[0].shape
    total = refs[0][0].astype(jnp.float32)
    for p in range(1, count):
        total = total + refs[p][0].astype(jnp.float32)
    out_ref, packed_ref = refs[-2:]
    total = total.astype(jnp.bfloat16)
    columns = width // 4
    patch = iota((row_count, 4 * row_count), 1)
    token = iota((row_count, 4 * row_count), 0)
    result = jnp.zeros((columns, 4 * row_count), jnp.float32)
    for j in range(4):
        put = jnp.where(patch == 4 * token + j, 1.0, 0.0).astype(jnp.bfloat16)
        result = result + dot(total[:, j * columns : (j + 1) * columns], put, TN)
    out_ref[...] = result.astype(jnp.bfloat16)
    packed_ref[...] = packed(result).astype(jnp.bfloat16)


def gathered(pieces, later):
    _, row_count, width = pieces[0].shape
    size = len(pieces) * row_count * width
    return pl.pallas_call(
        functools.partial(gather_kernel, len(pieces)),
        out_shape=(
            jax.ShapeDtypeStruct((width // 4, 4 * row_count), jnp.bfloat16),
            jax.ShapeDtypeStruct((packed_rows(width // 4, 4 * row_count), 128), jnp.bfloat16),
        ),
        in_specs=in_vmem(len(pieces) + 1),
        out_specs=tuple(in_vmem(2)),
        compiler_params=params(16),
        cost_estimate=pl.CostEstimate(
            flops=20_000 * size, bytes_accessed=400 * size, transcendentals=0
        ),
        name="gather_sum",
    )(*pieces, later)


def own_kernel(grad_ref, own_ref, held_ref, query_ref, key_ref, value_ref):
    columns, patches = grad_ref.shape
    rows = Rows(columns, patches)
    for h in range(columns // HEAD_DIM):
        cols = slice(h * HEAD_DIM, (h + 1) * HEAD_DIM)
        grad = grad_ref[cols]
        slope = dot(grad, held_ref[rows.head(rows.values, h), : 3 * patches], TN)
        probs = held_ref[rows.probs(h), : 3 * patches]
        wide = probs.astype(jnp.float32)
        delta = jnp.sum(wide * slope, 1, keepdims=True)
        scores = (wide * (slope - delta)).astype(jnp.bfloat16)
        query = dot(scores, held_ref[rows.head(rows.keys, h), : 3 * patches], NT) * SCALE
        query_ref[cols] = query.T.astype(jnp.bfloat16)
        key_ref[cols] = dot(own_ref[cols], scores[:, :patches], NN)
        value_ref[cols] = dot(grad, probs[:, :patches], NN)


def own_terms(grad, own, held):
    return pl.pallas_call(
        own_kernel,
        out_shape=(
            jax.ShapeDtypeStruct(grad.shape, jnp.bfloat16),
            jax.ShapeDtypeStruct(grad.shape, jnp.float32),
            jax.ShapeDtypeStruct(grad.shape, jnp.float32),
        ),
        in_specs=in_vmem(3),
        out_specs=tuple(in_vmem(3)),
        compiler_params=params(24),
        name="own_terms",
    )(grad, own, held)


def side_kernel(i, grad_ref, key_part_ref, value_part_ref, held_ref, side_ref, key_ref, value_ref):
    columns, patches = key_part_ref.shape
    rows = Rows(columns, patches)
    queries_at, attended_at = rows.side(i)
    for h in range(columns // HEAD_DIM):
        cols = slice(h * HEAD_DIM, (h + 1) * HEAD_DIM)
        wide = unpacked(grad_ref, h, columns, patches)
        grad = wide.astype(jnp.bfloat16)
        slope = dot(held_ref[rows.head(rows.values, h), :patches], grad, TN)
        attended = side_ref[rows.head(attended_at, h)].astype(jnp.float32)
        delta = jnp.sum(wide * attended, 0, keepdims=True)
        probs = side_ref[rows.side_probs(i, h)]
        value = dot(probs, grad, NT)
        scores = (probs.astype(jnp.float32) * (slope - delta)).astype(jnp.bfloat16)
        key = dot(scores, side_ref[rows.head(queries_at, h)], NT)
        key = key_part_ref[cols] + key.T
        key_ref[cols] = (key * SCALE if i == 1 else key).astype(key_ref.dtype)
        value_ref[cols] = (value_part_ref[cols] + value.T).astype(value_ref.dtype)


def side_terms(i, grad, key_part, value_part, held, side):
    kind = jnp.bfloat16 if i == 1 else jnp.float32
    shape = jax.ShapeDtypeStruct(key_part.shape, kind)
    return pl.pallas_call(
        functools.partial(side_kernel, i),
        out_shape=(shape, shape),
        in_specs=in_vmem(5),
        out_specs=tuple(in_vmem(2)),
        compiler_params=params(24),
        name="side_terms",
    )(grad, key_part, value_part, held, side)


def from_pairs(x):
    size = lax.axis_size("grp")

    def swapped(first):
        partner = {}
        for core in range(2):
            for i in range(size):
                j = i + 1 if (i - first) % 2 == 0 else i - 1
                pair = (core, j) if 0 <= j < size else (1 - core, i)
                partner[core * size + i] = pair[0] * size + pair[1]
        return lax.ppermute(x, ("core", "grp"), sorted(partner.items()))

    return swapped(0), swapped(1)


def exchanged(pieces, axes):
    count = len(pieces)
    return pieces[:1] + [
        lax.ppermute(pieces[d], axes, [(i, i ^ d) for i in range(count)]) for d in range(1, count)
    ]


def on_device(
    grad_out, destination, w_down, pre_act, w_up, queries, key_states, value_states, lengths
):
    groups = lax.axis_size("grp")
    spans = lax.axis_size("span")
    heads = lax.axis_size(("chip", "core", "span"))
    row_count = grad_out.shape[0]
    capacity, _ = padded_slots(row_count, groups)
    pieces = down_pieces(destination, grad_out, w_down, groups, spans)
    pieces, queries, key_states, value_states = lax.optimization_barrier(
        (pieces, queries, key_states, value_states)
    )
    arrived = lax.all_to_all(pieces, ("grp", "span"), split_axis=0, concat_axis=0, tiled=True)
    own = jnp.concatenate([queries.T, key_states.T, value_states.T], 0)
    even, odd = from_pairs(packed(own))
    first = lax.axis_index("grp") * row_count
    other, shares = up_pieces(arrived, pre_act, w_up, heads, capacity)
    other, odd, even = lax.optimization_barrier((other, odd, even))
    other = lax.ppermute(other, "core", [(0, 1), (1, 0)])
    shares = (other.astype(jnp.float32) + shares.astype(jnp.float32)).astype(jnp.bfloat16)
    shares, own = lax.optimization_barrier((shares, own))
    held, side, held_done = softmax_parts(lengths, first, own, odd, even)
    shares = [shares[d : d + 1] for d in range(shares.shape[0])]
    grad, grad_packed = gathered(exchanged(shares, ("chip", "span")), held_done)
    even, odd = from_pairs(grad_packed)
    grad_query, key_part, value_part = own_terms(grad, queries.T, held)
    parts = side_terms(0, odd, key_part, value_part, held, side)
    grad_key, grad_value = side_terms(1, even, *parts, held, side)
    return grad_query.T, grad_key.T, grad_value.T


def solution(mesh):
    sect, grp, span = (mesh.shape[name] for name in ("sect", "grp", "span"))
    finer = jax.sharding.Mesh(
        mesh.devices.reshape(sect // 2, 2, grp, span), ("chip", "core", "grp", "span")
    )
    split = P("grp", ("chip", "core", "span"))
    placed = (
        P("grp", "span"),
        P("grp"),
        P(("chip", "core"), "span"),
        split,
        P(None, ("chip", "core", "span")),
        split,
        split,
        split,
        P(),
    )
    return jax.shard_map(
        on_device,
        mesh=finer,
        in_specs=placed,
        out_specs=(split, split, split),
        check_vma=False,
    )
```

```python
import functools

import jax
import jax.numpy as jnp
from jax import lax
from jax.experimental import pallas as pl
from jax.experimental.pallas import tpu as pltpu
from jax.sharding import PartitionSpec as P

HEAD_DIM = 80
SCALE = HEAD_DIM**-0.5
MIB = 1024 * 1024
VMEM = pltpu.MemorySpace.VMEM
NT = (((1,), (1,)), ((), ()))
NN = (((1,), (0,)), ((), ()))
TN = (((0,), (0,)), ((), ()))


def dot(a, b, dims):
    return lax.dot_general(a, b, dims, preferred_element_type=jnp.float32)


def iota(shape, dim):
    return lax.broadcasted_iota(jnp.int32, shape, dim)


def params(mib):
    return pltpu.CompilerParams(vmem_limit_bytes=mib * MIB)


def in_vmem(count):
    return [pl.BlockSpec(memory_space=VMEM) for _ in range(count)]


def in_hbm(count):
    return [pl.BlockSpec(memory_space=pltpu.MemorySpace.HBM) for _ in range(count)]


def fetched(pairs, sems):
    copies = [pltpu.make_async_copy(a, b, sems.at[i]) for i, (a, b) in enumerate(pairs)]
    for copy in copies:
        copy.start()
    return copies


def padded_slots(row_count, groups):
    offsets = min(groups, row_count // 2)
    capacity = row_count // offsets
    return capacity, -(-(capacity + 1) // 8) * 8


def one_product(count, slots, hidden):
    return count * slots <= hidden


def down_kernel(groups, spans, capacity, slots, steps, dest_hbm, rows_hbm, weight_ref, out_hbm,
                dest_ref, rows_ref, held, total_ref, pieces_ref, sems, out_sems):
    row_count = rows_ref.shape[0]
    hidden = weight_ref.shape[0] // spans
    everything = pl.ds(0, weight_ref.shape[0])
    pairs = [(dest_hbm, dest_ref), (rows_hbm, rows_ref)]
    for at, step in steps:
        part = (everything, pl.ds(at, step))
        pairs.append((weight_ref.at[part], held.at[part]))
    copies = fetched(pairs, sems)
    copies[0].wait()
    across = jnp.broadcast_to(dest_ref[...].astype(jnp.float32), (row_count, row_count))
    down = across.T
    group_across = jnp.floor((across + 0.5) * (1.0 / row_count))
    group_down = jnp.floor((down + 0.5) * (1.0 / row_count))
    slot_down = down - group_down * row_count
    same = group_across == group_down
    earlier = iota((row_count, row_count), 0) < iota((row_count, row_count), 1)
    later = iota((row_count, row_count), 1) < iota((row_count, row_count), 0)
    rank_across = jnp.sum(jnp.where(same & earlier, 1.0, 0.0), 0, keepdims=True)
    rank_down = jnp.sum(jnp.where(same & later, 1.0, 0.0), 1, keepdims=True)
    row_of = group_across[:1] * slots + rank_across
    places = iota((groups * slots, row_count), 0).astype(jnp.float32)
    pick = jnp.where(places == row_of, 1.0, 0.0).astype(jnp.bfloat16)
    lane = iota((row_count, hidden), 1).astype(jnp.float32)
    shift = 0.0
    if one_product(groups * spans, slots, hidden):
        device = lax.axis_index("grp") * spans + lax.axis_index("span")
        shift = (device * slots).astype(jnp.float32)
    at_rank = lane == rank_down + shift
    label_row = iota((slots, hidden), 0) == capacity
    labels = []
    for g in range(groups):
        hit = at_rank & (group_down[:, :1] == g)
        labels.append(jnp.sum(jnp.where(hit, slot_down[:, :1] + 1.0, 0.0), 0, keepdims=True) - 1.0)
    copies[1].wait()
    for n, (at, step) in enumerate(steps):
        turned = rows_ref[:, at : at + step].astype(jnp.float32).T.astype(jnp.bfloat16)
        copies[2 + n].wait()
        product = dot(held[:, at : at + step], turned, NN)
        total_ref[...] = product if n == 0 else total_ref[...] + product
    outgoing = []
    for s in range(spans):
        part = total_ref[s * hidden : (s + 1) * hidden].astype(jnp.bfloat16)
        moved = dot(pick, part, NT)
        for g in range(groups):
            piece = jnp.where(label_row, labels[g], moved[g * slots : (g + 1) * slots])
            pieces_ref[s, g] = piece.astype(jnp.bfloat16)
        copy = pltpu.make_async_copy(pieces_ref.at[s], out_hbm.at[:, s], out_sems.at[s])
        copy.start()
        outgoing.append(copy)
    for copy in outgoing:
        copy.wait()


def down_pieces(dest, rows, weight, groups, spans):
    row_count = rows.shape[0]
    capacity, slots = padded_slots(row_count, groups)
    hidden = weight.shape[0] // spans
    depth = weight.shape[1]
    edges = [depth * i // 8 for i in (0, 1, 3, 5, 8)]
    steps = [(i, j - i) for i, j in zip(edges, edges[1:])]
    pieces = pl.pallas_call(
        functools.partial(down_kernel, groups, spans, capacity, slots, steps),
        out_shape=jax.ShapeDtypeStruct((groups, spans, slots, hidden), jnp.bfloat16),
        in_specs=in_hbm(3),
        out_specs=in_hbm(1)[0],
        scratch_shapes=[
            pltpu.VMEM((1, row_count), jnp.int32),
            pltpu.VMEM(rows.shape, jnp.bfloat16),
            pltpu.VMEM(weight.shape, jnp.bfloat16),
            pltpu.VMEM((weight.shape[0], row_count), jnp.float32),
            pltpu.VMEM((spans, groups, slots, hidden), jnp.bfloat16),
            pltpu.SemaphoreType.DMA((2 + len(steps),)),
            pltpu.SemaphoreType.DMA((spans,)),
        ],
        compiler_params=params(60),
        name="down_product",
    )(dest.reshape(1, row_count), rows, weight)
    return pieces.reshape(groups * spans, slots, hidden)


def up_kernel(heads, capacity, pieces_ref, pre_ref, weight_ref, send_hbm, keep_hbm, held, out_ref,
              sems, out_sems):
    row_count, hidden = pre_ref.shape
    count, slots, _ = pieces_ref.shape
    width = weight_ref.shape[2] // lax.axis_size("span")
    spans = lax.axis_size("span")
    core = lax.axis_index("core")
    chip = lax.axis_index("chip")
    chips = heads // (2 * spans)
    block = spans * width

    pairs = []
    for n in range(2 * chips):
        place = lax.bitwise_xor(chip, n % chips) * 2 + (1 - core if n < chips else core)
        pairs.append((weight_ref.at[:, place], held.at[n]))
    copies = fetched(pairs, sems)
    label_at = slice(capacity, capacity + 1)
    if one_product(count, slots, hidden):
        pieces = [pieces_ref[p].astype(jnp.float32) for p in range(count)]
        labels = functools.reduce(jnp.maximum, [x[label_at, : count * slots] for x in pieces])
        row = iota((row_count, count * slots), 0).astype(jnp.float32)
        put = jnp.where(row == labels, 1.0, 0.0).astype(jnp.bfloat16)
        total = dot(put, jnp.concatenate(pieces, 0).astype(jnp.bfloat16), NN)
    else:
        row = iota((row_count, slots), 0).astype(jnp.float32)

        def placed(p, total):
            piece = pieces_ref[p]
            labels = piece.astype(jnp.float32)[label_at, :slots]
            put = jnp.where(row == labels, 1.0, 0.0).astype(jnp.bfloat16)
            return total + dot(put, piece, NN)

        total = lax.fori_loop(0, count, placed, jnp.zeros((row_count, hidden), jnp.float32))
    pre = pre_ref[...].astype(jnp.float32)
    cdf = 0.5 * (1.0 + lax.erf(pre * 0.7071067811865476))
    slope = cdf + pre * jnp.exp(-0.5 * pre * pre) * 0.3989422804014327
    grad_pre = (total * slope).T.astype(jnp.bfloat16)
    outgoing = []
    span = lax.axis_index("span")

    def send(n, product):
        for i in range(spans):
            parts = [product[j * block + i * width : j * block + (i + 1) * width] for j in range(4)]
            part = jnp.concatenate(parts, 0).astype(jnp.bfloat16).T
            out_ref[n * spans + lax.bitwise_xor(span, i)] = part
        out_hbm = send_hbm if n < chips else keep_hbm
        source, target = pl.ds(n * spans, spans), pl.ds(n % chips * spans, spans)
        copy = pltpu.make_async_copy(out_ref.at[source], out_hbm.at[target], out_sems.at[n])
        outgoing.append(copy)
        copy.start()

    waiting = None
    for n in range(2 * chips):
        copies[n].wait()
        product = dot(held[n].reshape(4 * block, hidden), grad_pre, NN)
        if waiting is not None:
            send(n - 1, waiting)
        waiting = product
    send(2 * chips - 1, waiting)
    for copy in outgoing:
        copy.wait()


def up_pieces(pieces, pre, weight, heads, capacity):
    width = weight.shape[0] // heads
    spans = lax.axis_size("span")
    blocks = heads // spans
    return pl.pallas_call(
        functools.partial(up_kernel, heads, capacity),
        out_shape=[jax.ShapeDtypeStruct((heads // 2, pre.shape[0], width), jnp.bfloat16)] * 2,
        in_specs=in_vmem(2) + in_hbm(1),
        out_specs=in_hbm(2),
        scratch_shapes=[
            pltpu.VMEM((blocks, 4, spans * width // 4, weight.shape[1]), jnp.bfloat16),
            pltpu.VMEM((heads, pre.shape[0], width), jnp.bfloat16),
            pltpu.SemaphoreType.DMA((blocks,)),
            pltpu.SemaphoreType.DMA((blocks,)),
        ],
        compiler_params=params(52),
        cost_estimate=pl.CostEstimate(
            flops=8 * pre.shape[0] * weight.size, bytes_accessed=8 * weight.size, transcendentals=0
        ),
        name="up_product",
    )(pieces, pre, weight.reshape(4, blocks, -1, weight.shape[1]))


class Rows:
    def __init__(self, columns, patches):
        heads = columns // HEAD_DIM
        self.lanes = -(-3 * patches // 128) * 128
        self.columns, self.patches = columns, patches
        self.values, self.keys, self.probs_at = 0, columns, 2 * columns
        self.total = 2 * columns + heads * patches

    def head(self, start, h):
        return slice(start + h * HEAD_DIM, start + (h + 1) * HEAD_DIM)

    def kind(self, start):
        return slice(start, start + self.columns)

    def probs(self, h):
        return slice(self.probs_at + h * self.patches, self.probs_at + (h + 1) * self.patches)

    def side(self, i):
        start = i * self.total
        return start, start + self.columns

    def side_probs(self, i, h):
        start = i * self.total + self.probs_at + h * self.patches
        return slice(start, start + self.patches)


def softmax_kernel(lengths_ref, first_ref, own_ref, odd_ref, even_ref, held, side_ref, done_ref):
    columns, patches = own_ref.shape[0] // 3, own_ref.shape[1]
    rows = Rows(columns, patches)
    heads = columns // HEAD_DIM
    step_even = 1 - 2 * lax.rem(lax.axis_index("grp"), 2)
    offsets = (0, -step_even, step_even)
    first = first_ref[0, 0]

    def image_of(shape, dim, block):
        token = iota(shape, dim) // 4 + (first + block * (patches // 4))

        def step(i, state):
            image, bound = state
            bound = bound + lengths_ref[0, i]
            return image + jnp.where(token >= bound, 1, 0), bound

        start = (jnp.where(token < 0, -1, 0), jnp.int32(0))
        return lax.fori_loop(0, lengths_ref.shape[1], step, start)[0]

    def near(start, i, h):
        part = held[rows.head(start, h), :]
        if i == 0:
            return part[:, : 2 * patches]
        parts = [part[:, :patches], part[:, 2 * patches : 3 * patches]]
        return jnp.concatenate([x.astype(jnp.float32) for x in parts], 1).astype(jnp.bfloat16)

    across = [image_of((1, patches), 1, b).astype(jnp.float32) for b in offsets]
    down = [jnp.broadcast_to(x, (128, patches)).T[:, :1] for x in across]

    def kind(block, t, h):
        if block == 0:
            start = t * columns + h * HEAD_DIM
            return own_ref[start : start + HEAD_DIM].astype(jnp.float32)
        return unpacked((odd_ref, even_ref)[block - 1], t * heads + h, 3 * columns, patches)

    def wide(t, which, h):
        return jnp.concatenate([kind(b, t, h) for b in which], 1).astype(jnp.bfloat16)

    def softmax(queries, keys, same):
        scores = jnp.where(same, dot(queries, keys, TN) * SCALE, -jnp.inf)
        weights = jnp.exp(scores - jnp.max(scores, 1, keepdims=True))
        return weights * (1.0 / jnp.sum(weights, 1, keepdims=True))

    for h in range(heads):
        held[rows.head(rows.values, h), : 3 * patches] = wide(2, (0, 1, 2), h)
        held[rows.head(rows.keys, h), : 3 * patches] = wide(1, (0, 1, 2), h)
    same_own = down[0] == jnp.concatenate(across, 1)
    same_side = [down[b] == jnp.concatenate([across[0], across[b]], 1) for b in (1, 2)]
    for h in range(heads):
        keys = held[rows.head(rows.keys, h), : 3 * patches]
        probs = softmax(kind(0, 0, h).astype(jnp.bfloat16), keys, same_own)
        held[rows.probs(h), : 3 * patches] = probs.astype(jnp.bfloat16)
        for i, b in enumerate((1, 2)):
            queries_at, attended_at = rows.side(i)
            queries = kind(b, 0, h).astype(jnp.bfloat16)
            probs = softmax(queries, near(rows.keys, i, h), same_side[i])
            seen = dot(probs.astype(jnp.bfloat16), near(rows.values, i, h), NT)
            side_ref[rows.head(queries_at, h)] = queries
            side_ref[rows.head(attended_at, h)] = seen.T.astype(jnp.bfloat16)
            side_ref[rows.side_probs(i, h)] = probs[:, :patches].T.astype(jnp.bfloat16)
    done_ref[...] = jnp.zeros(done_ref.shape, jnp.float32)


def softmax_parts(lengths, first, own, odd, even):
    columns, patches = own.shape[0] // 3, own.shape[1]
    rows = Rows(columns, patches)
    smem = pl.BlockSpec(memory_space=pltpu.MemorySpace.SMEM)
    work = (columns // HEAD_DIM) * patches * patches
    return pl.pallas_call(
        softmax_kernel,
        out_shape=(
            jax.ShapeDtypeStruct((rows.total, rows.lanes), jnp.bfloat16),
            jax.ShapeDtypeStruct((2 * rows.total, patches), jnp.bfloat16),
            jax.ShapeDtypeStruct((8, 128), jnp.float32),
        ),
        in_specs=[smem, smem] + in_vmem(3),
        out_specs=tuple(in_vmem(3)),
        compiler_params=params(32),
        cost_estimate=pl.CostEstimate(
            flops=100_000 * work, bytes_accessed=500 * work, transcendentals=9 * work
        ),
        name="softmax_parts",
    )(lengths.reshape(1, -1), first.reshape(1, 1), own, odd, even)


def packed_rows(columns, patches):
    heads = columns // HEAD_DIM
    return patches // 128 * columns + (heads + 1) // 2 * HEAD_DIM


def packed(x):
    columns, patches = x.shape
    whole = patches // 128 * 128
    parts = [x[:, at : at + 128] for at in range(0, whole, 128)]
    tails = [x[at : at + HEAD_DIM, whole:] for at in range(0, columns, HEAD_DIM)]
    tails += [jnp.zeros_like(tails[0])] * (len(tails) % 2)
    parts += [jnp.concatenate(tails[i : i + 2], 1) for i in range(0, len(tails), 2)]
    return jnp.concatenate(parts, 0)


def unpacked(ref, h, columns, patches):
    tiles = patches // 128
    starts = [t * columns + h * HEAD_DIM for t in range(tiles)]
    parts = [ref[at : at + HEAD_DIM].astype(jnp.float32) for at in starts]
    at = tiles * columns + h // 2 * HEAD_DIM
    tail = ref[at : at + HEAD_DIM].astype(jnp.float32)
    return jnp.concatenate(parts + [tail[:, h % 2 * 64 : h % 2 * 64 + 64]], 1)


def gather_kernel(count, *refs):
    _, row_count, width = refs[0].shape
    total = refs[0][0].astype(jnp.float32)
    for p in range(1, count):
        total = total + refs[p][0].astype(jnp.float32)
    out_ref, packed_ref = refs[-2:]
    total = total.astype(jnp.bfloat16)
    columns = width // 4
    patch = iota((row_count, 4 * row_count), 1)
    token = iota((row_count, 4 * row_count), 0)
    result = jnp.zeros((columns, 4 * row_count), jnp.float32)
    for j in range(4):
        put = jnp.where(patch == 4 * token + j, 1.0, 0.0).astype(jnp.bfloat16)
        result = result + dot(total[:, j * columns : (j + 1) * columns], put, TN)
    out_ref[...] = result.astype(jnp.bfloat16)
    packed_ref[...] = packed(result).astype(jnp.bfloat16)


def gathered(pieces, later):
    _, row_count, width = pieces[0].shape
    size = len(pieces) * row_count * width
    return pl.pallas_call(
        functools.partial(gather_kernel, len(pieces)),
        out_shape=(
            jax.ShapeDtypeStruct((width // 4, 4 * row_count), jnp.bfloat16),
            jax.ShapeDtypeStruct((packed_rows(width // 4, 4 * row_count), 128), jnp.bfloat16),
        ),
        in_specs=in_vmem(len(pieces) + 1),
        out_specs=tuple(in_vmem(2)),
        compiler_params=params(16),
        cost_estimate=pl.CostEstimate(
            flops=20_000 * size, bytes_accessed=400 * size, transcendentals=0
        ),
        name="gather_sum",
    )(*pieces, later)


def own_kernel(grad_ref, own_ref, held_ref, query_ref, key_ref, value_ref):
    columns, patches = grad_ref.shape
    rows = Rows(columns, patches)
    for h in range(columns // HEAD_DIM):
        cols = slice(h * HEAD_DIM, (h + 1) * HEAD_DIM)
        grad = grad_ref[cols]
        slope = dot(grad, held_ref[rows.head(rows.values, h), : 3 * patches], TN)
        probs = held_ref[rows.probs(h), : 3 * patches]
        wide = probs.astype(jnp.float32)
        delta = jnp.sum(wide * slope, 1, keepdims=True)
        scores = (wide * (slope - delta)).astype(jnp.bfloat16)
        query = dot(scores, held_ref[rows.head(rows.keys, h), : 3 * patches], NT) * SCALE
        query_ref[cols] = query.T.astype(jnp.bfloat16)
        key_ref[cols] = dot(own_ref[cols], scores[:, :patches], NN)
        value_ref[cols] = dot(grad, probs[:, :patches], NN)


def own_terms(grad, own, held):
    return pl.pallas_call(
        own_kernel,
        out_shape=(
            jax.ShapeDtypeStruct(grad.shape, jnp.bfloat16),
            jax.ShapeDtypeStruct(grad.shape, jnp.float32),
            jax.ShapeDtypeStruct(grad.shape, jnp.float32),
        ),
        in_specs=in_vmem(3),
        out_specs=tuple(in_vmem(3)),
        compiler_params=params(24),
        name="own_terms",
    )(grad, own, held)


def side_kernel(i, grad_ref, key_part_ref, value_part_ref, held_ref, side_ref, key_ref, value_ref):
    columns, patches = key_part_ref.shape
    rows = Rows(columns, patches)
    queries_at, attended_at = rows.side(i)
    for h in range(columns // HEAD_DIM):
        cols = slice(h * HEAD_DIM, (h + 1) * HEAD_DIM)
        wide = unpacked(grad_ref, h, columns, patches)
        grad = wide.astype(jnp.bfloat16)
        slope = dot(held_ref[rows.head(rows.values, h), :patches], grad, TN)
        attended = side_ref[rows.head(attended_at, h)].astype(jnp.float32)
        delta = jnp.sum(wide * attended, 0, keepdims=True)
        probs = side_ref[rows.side_probs(i, h)]
        value = dot(probs, grad, NT)
        scores = (probs.astype(jnp.float32) * (slope - delta)).astype(jnp.bfloat16)
        key = dot(scores, side_ref[rows.head(queries_at, h)], NT)
        key = key_part_ref[cols] + key.T
        key_ref[cols] = (key * SCALE if i == 1 else key).astype(key_ref.dtype)
        value_ref[cols] = (value_part_ref[cols] + value.T).astype(value_ref.dtype)


def side_terms(i, grad, key_part, value_part, held, side):
    kind = jnp.bfloat16 if i == 1 else jnp.float32
    shape = jax.ShapeDtypeStruct(key_part.shape, kind)
    return pl.pallas_call(
        functools.partial(side_kernel, i),
        out_shape=(shape, shape),
        in_specs=in_vmem(5),
        out_specs=tuple(in_vmem(2)),
        compiler_params=params(24),
        name="side_terms",
    )(grad, key_part, value_part, held, side)


def from_pairs(x):
    size = lax.axis_size("grp")

    def swapped(first):
        partner = {}
        for core in range(2):
            for i in range(size):
                j = i + 1 if (i - first) % 2 == 0 else i - 1
                pair = (core, j) if 0 <= j < size else (1 - core, i)
                partner[core * size + i] = pair[0] * size + pair[1]
        return lax.ppermute(x, ("core", "grp"), sorted(partner.items()))

    return swapped(0), swapped(1)


def exchanged(pieces, axes):
    count = len(pieces)
    return pieces[:1] + [
        lax.ppermute(pieces[d], axes, [(i, i ^ d) for i in range(count)]) for d in range(1, count)
    ]


def on_device(
    grad_out, destination, w_down, pre_act, w_up, queries, key_states, value_states, lengths
):
    groups = lax.axis_size("grp")
    spans = lax.axis_size("span")
    heads = lax.axis_size(("chip", "core", "span"))
    row_count = grad_out.shape[0]
    capacity, _ = padded_slots(row_count, groups)
    pieces = down_pieces(destination, grad_out, w_down, groups, spans)
    pieces, queries, key_states, value_states = lax.optimization_barrier(
        (pieces, queries, key_states, value_states)
    )
    arrived = lax.all_to_all(pieces, ("grp", "span"), split_axis=0, concat_axis=0, tiled=True)
    own = jnp.concatenate([queries.T, key_states.T, value_states.T], 0)
    even, odd = from_pairs(packed(own))
    first = lax.axis_index("grp") * row_count
    other, shares = up_pieces(arrived, pre_act, w_up, heads, capacity)
    other, odd, even = lax.optimization_barrier((other, odd, even))
    other = lax.ppermute(other, "core", [(0, 1), (1, 0)])
    shares = (other.astype(jnp.float32) + shares.astype(jnp.float32)).astype(jnp.bfloat16)
    shares, own = lax.optimization_barrier((shares, own))
    held, side, held_done = softmax_parts(lengths, first, own, odd, even)
    shares = [shares[d : d + 1] for d in range(shares.shape[0])]
    grad, grad_packed = gathered(exchanged(shares, ("chip", "span")), held_done)
    even, odd = from_pairs(grad_packed)
    grad_query, key_part, value_part = own_terms(grad, queries.T, held)
    parts = side_terms(0, odd, key_part, value_part, held, side)
    grad_key, grad_value = side_terms(1, even, *parts, held, side)
    return grad_query.T, grad_key.T, grad_value.T


def solution(mesh):
    sect, grp, span = (mesh.shape[name] for name in ("sect", "grp", "span"))
    finer = jax.sharding.Mesh(
        mesh.devices.reshape(sect // 2, 2, grp, span), ("chip", "core", "grp", "span")
    )
    split = P("grp", ("chip", "core", "span"))
    placed = (
        P("grp", "span"),
        P("grp"),
        P(("chip", "core"), "span"),
        split,
        P(None, ("chip", "core", "span")),
        split,
        split,
        split,
        P(),
    )
    return jax.shard_map(
        on_device,
        mesh=finer,
        in_specs=placed,
        out_specs=(split, split, split),
        check_vma=False,
    )
```

```python
import functools

import jax
import jax.numpy as jnp
from jax import lax
from jax.experimental import pallas as pl
from jax.experimental.pallas import tpu as pltpu
from jax.sharding import PartitionSpec as P

HEAD_DIM = 80
SCALE = HEAD_DIM**-0.5
MIB = 1024 * 1024
VMEM = pltpu.MemorySpace.VMEM
NT = (((1,), (1,)), ((), ()))
NN = (((1,), (0,)), ((), ()))
TN = (((0,), (0,)), ((), ()))


def dot(a, b, dims):
    return lax.dot_general(a, b, dims, preferred_element_type=jnp.float32)


def iota(shape, dim):
    return lax.broadcasted_iota(jnp.int32, shape, dim)


def params(mib):
    return pltpu.CompilerParams(vmem_limit_bytes=mib * MIB)


def in_vmem(count):
    return [pl.BlockSpec(memory_space=VMEM) for _ in range(count)]


def in_hbm(count):
    return [pl.BlockSpec(memory_space=pltpu.MemorySpace.HBM) for _ in range(count)]


def fetched(pairs, sems):
    copies = [pltpu.make_async_copy(a, b, sems.at[i]) for i, (a, b) in enumerate(pairs)]
    for copy in copies:
        copy.start()
    return copies


def padded_slots(row_count, groups):
    offsets = min(groups, row_count // 2)
    capacity = row_count // offsets
    return capacity, -(-(capacity + 1) // 8) * 8


def one_product(count, slots, hidden):
    return count * slots <= hidden


def down_kernel(groups, spans, capacity, slots, steps, dest_hbm, rows_hbm, weight_ref, out_hbm,
                dest_ref, rows_ref, held, total_ref, pieces_ref, sems, out_sems):
    row_count = rows_ref.shape[0]
    hidden = weight_ref.shape[0] // spans
    everything = pl.ds(0, weight_ref.shape[0])
    pairs = [(dest_hbm, dest_ref), (rows_hbm, rows_ref)]
    for at, step in steps:
        part = (everything, pl.ds(at, step))
        pairs.append((weight_ref.at[part], held.at[part]))
    copies = fetched(pairs, sems)
    copies[0].wait()
    across = jnp.broadcast_to(dest_ref[...].astype(jnp.float32), (row_count, row_count))
    down = across.T
    group_across = jnp.floor((across + 0.5) * (1.0 / row_count))
    group_down = jnp.floor((down + 0.5) * (1.0 / row_count))
    slot_down = down - group_down * row_count
    same = group_across == group_down
    earlier = iota((row_count, row_count), 0) < iota((row_count, row_count), 1)
    later = iota((row_count, row_count), 1) < iota((row_count, row_count), 0)
    rank_across = jnp.sum(jnp.where(same & earlier, 1.0, 0.0), 0, keepdims=True)
    rank_down = jnp.sum(jnp.where(same & later, 1.0, 0.0), 1, keepdims=True)
    row_of = group_across[:1] * slots + rank_across
    places = iota((groups * slots, row_count), 0).astype(jnp.float32)
    pick = jnp.where(places == row_of, 1.0, 0.0).astype(jnp.bfloat16)
    lane = iota((row_count, hidden), 1).astype(jnp.float32)
    shift = 0.0
    if one_product(groups * spans, slots, hidden):
        device = lax.axis_index("grp") * spans + lax.axis_index("span")
        shift = (device * slots).astype(jnp.float32)
    at_rank = lane == rank_down + shift
    label_row = iota((slots, hidden), 0) == capacity
    labels = []
    for g in range(groups):
        hit = at_rank & (group_down[:, :1] == g)
        labels.append(jnp.sum(jnp.where(hit, slot_down[:, :1] + 1.0, 0.0), 0, keepdims=True) - 1.0)
    copies[1].wait()
    for n, (at, step) in enumerate(steps):
        turned = rows_ref[:, at : at + step].astype(jnp.float32).T.astype(jnp.bfloat16)
        copies[2 + n].wait()
        product = dot(held[:, at : at + step], turned, NN)
        total_ref[...] = product if n == 0 else total_ref[...] + product
    outgoing = []
    for s in range(spans):
        part = total_ref[s * hidden : (s + 1) * hidden].astype(jnp.bfloat16)
        moved = dot(pick, part, NT)
        for g in range(groups):
            piece = jnp.where(label_row, labels[g], moved[g * slots : (g + 1) * slots])
            pieces_ref[s, g] = piece.astype(jnp.bfloat16)
        copy = pltpu.make_async_copy(pieces_ref.at[s], out_hbm.at[:, s], out_sems.at[s])
        copy.start()
        outgoing.append(copy)
    for copy in outgoing:
        copy.wait()


def down_pieces(dest, rows, weight, groups, spans):
    row_count = rows.shape[0]
    capacity, slots = padded_slots(row_count, groups)
    hidden = weight.shape[0] // spans
    depth = weight.shape[1]
    edges = [depth * i // 8 for i in (0, 1, 3, 5, 8)]
    steps = [(i, j - i) for i, j in zip(edges, edges[1:])]
    pieces = pl.pallas_call(
        functools.partial(down_kernel, groups, spans, capacity, slots, steps),
        out_shape=jax.ShapeDtypeStruct((groups, spans, slots, hidden), jnp.bfloat16),
        in_specs=in_hbm(3),
        out_specs=in_hbm(1)[0],
        scratch_shapes=[
            pltpu.VMEM((1, row_count), jnp.int32),
            pltpu.VMEM(rows.shape, jnp.bfloat16),
            pltpu.VMEM(weight.shape, jnp.bfloat16),
            pltpu.VMEM((weight.shape[0], row_count), jnp.float32),
            pltpu.VMEM((spans, groups, slots, hidden), jnp.bfloat16),
            pltpu.SemaphoreType.DMA((2 + len(steps),)),
            pltpu.SemaphoreType.DMA((spans,)),
        ],
        compiler_params=params(60),
        name="down_product",
    )(dest.reshape(1, row_count), rows, weight)
    return pieces.reshape(groups * spans, slots, hidden)


def up_kernel(heads, capacity, pieces_ref, pre_ref, weight_ref, send_hbm, keep_hbm, held, out_ref,
              sems, out_sems):
    row_count, hidden = pre_ref.shape
    count, slots, _ = pieces_ref.shape
    width = weight_ref.shape[2] // lax.axis_size("span")
    spans = lax.axis_size("span")
    core = lax.axis_index("core")
    chip = lax.axis_index("chip")
    chips = heads // (2 * spans)
    block = spans * width

    pairs = []
    for n in range(2 * chips):
        place = lax.bitwise_xor(chip, n % chips) * 2 + (1 - core if n < chips else core)
        pairs.append((weight_ref.at[:, place], held.at[n]))
    copies = fetched(pairs, sems)
    label_at = slice(capacity, capacity + 1)
    if one_product(count, slots, hidden):
        pieces = [pieces_ref[p].astype(jnp.float32) for p in range(count)]
        labels = functools.reduce(jnp.maximum, [x[label_at, : count * slots] for x in pieces])
        row = iota((row_count, count * slots), 0).astype(jnp.float32)
        put = jnp.where(row == labels, 1.0, 0.0).astype(jnp.bfloat16)
        total = dot(put, jnp.concatenate(pieces, 0).astype(jnp.bfloat16), NN)
    else:
        row = iota((row_count, slots), 0).astype(jnp.float32)

        def placed(p, total):
            piece = pieces_ref[p]
            labels = piece.astype(jnp.float32)[label_at, :slots]
            put = jnp.where(row == labels, 1.0, 0.0).astype(jnp.bfloat16)
            return total + dot(put, piece, NN)

        total = lax.fori_loop(0, count, placed, jnp.zeros((row_count, hidden), jnp.float32))
    pre = pre_ref[...].astype(jnp.float32)
    cdf = 0.5 * (1.0 + lax.erf(pre * 0.7071067811865476))
    slope = cdf + pre * jnp.exp(-0.5 * pre * pre) * 0.3989422804014327
    grad_pre = (total * slope).T.astype(jnp.bfloat16)
    outgoing = []
    span = lax.axis_index("span")

    def send(n, product):
        for i in range(spans):
            parts = [product[j * block + i * width : j * block + (i + 1) * width] for j in range(4)]
            part = jnp.concatenate(parts, 0).astype(jnp.bfloat16).T
            out_ref[n * spans + lax.bitwise_xor(span, i)] = part
        out_hbm = send_hbm if n < chips else keep_hbm
        source, target = pl.ds(n * spans, spans), pl.ds(n % chips * spans, spans)
        copy = pltpu.make_async_copy(out_ref.at[source], out_hbm.at[target], out_sems.at[n])
        outgoing.append(copy)
        copy.start()

    waiting = None
    for n in range(2 * chips):
        copies[n].wait()
        product = dot(held[n].reshape(4 * block, hidden), grad_pre, NN)
        if waiting is not None:
            send(n - 1, waiting)
        waiting = product
    send(2 * chips - 1, waiting)
    for copy in outgoing:
        copy.wait()


def up_pieces(pieces, pre, weight, heads, capacity):
    width = weight.shape[0] // heads
    spans = lax.axis_size("span")
    blocks = heads // spans
    return pl.pallas_call(
        functools.partial(up_kernel, heads, capacity),
        out_shape=[jax.ShapeDtypeStruct((heads // 2, pre.shape[0], width), jnp.bfloat16)] * 2,
        in_specs=in_vmem(2) + in_hbm(1),
        out_specs=in_hbm(2),
        scratch_shapes=[
            pltpu.VMEM((blocks, 4, spans * width // 4, weight.shape[1]), jnp.bfloat16),
            pltpu.VMEM((heads, pre.shape[0], width), jnp.bfloat16),
            pltpu.SemaphoreType.DMA((blocks,)),
            pltpu.SemaphoreType.DMA((blocks,)),
        ],
        compiler_params=params(52),
        cost_estimate=pl.CostEstimate(
            flops=8 * pre.shape[0] * weight.size, bytes_accessed=8 * weight.size, transcendentals=0
        ),
        name="up_product",
    )(pieces, pre, weight.reshape(4, blocks, -1, weight.shape[1]))


class Rows:
    def __init__(self, columns, patches):
        heads = columns // HEAD_DIM
        self.lanes = -(-3 * patches // 128) * 128
        self.columns, self.patches = columns, patches
        self.values, self.keys, self.probs_at = 0, columns, 2 * columns
        self.total = 2 * columns + heads * patches

    def head(self, start, h):
        return slice(start + h * HEAD_DIM, start + (h + 1) * HEAD_DIM)

    def kind(self, start):
        return slice(start, start + self.columns)

    def probs(self, h):
        return slice(self.probs_at + h * self.patches, self.probs_at + (h + 1) * self.patches)

    def side(self, i):
        start = i * self.total
        return start, start + self.columns

    def side_probs(self, i, h):
        start = i * self.total + self.probs_at + h * self.patches
        return slice(start, start + self.patches)


def softmax_kernel(lengths_ref, first_ref, own_ref, odd_ref, even_ref, held, side_ref, done_ref):
    columns, patches = own_ref.shape[0] // 3, own_ref.shape[1]
    rows = Rows(columns, patches)
    heads = columns // HEAD_DIM
    step_even = 1 - 2 * lax.rem(lax.axis_index("grp"), 2)
    offsets = (0, -step_even, step_even)
    first = first_ref[0, 0]

    def image_of(shape, dim, block):
        token = iota(shape, dim) // 4 + (first + block * (patches // 4))

        def step(i, state):
            image, bound = state
            bound = bound + lengths_ref[0, i]
            return image + jnp.where(token >= bound, 1, 0), bound

        start = (jnp.where(token < 0, -1, 0), jnp.int32(0))
        return lax.fori_loop(0, lengths_ref.shape[1], step, start)[0]

    def near(start, i, h):
        part = held[rows.head(start, h), :]
        if i == 0:
            return part[:, : 2 * patches]
        parts = [part[:, :patches], part[:, 2 * patches : 3 * patches]]
        return jnp.concatenate([x.astype(jnp.float32) for x in parts], 1).astype(jnp.bfloat16)

    across = [image_of((1, patches), 1, b).astype(jnp.float32) for b in offsets]
    down = [jnp.broadcast_to(x, (128, patches)).T[:, :1] for x in across]

    def kind(block, t, h):
        if block == 0:
            start = t * columns + h * HEAD_DIM
            return own_ref[start : start + HEAD_DIM].astype(jnp.float32)
        return unpacked((odd_ref, even_ref)[block - 1], t * heads + h, 3 * columns, patches)

    def wide(t, which, h):
        return jnp.concatenate([kind(b, t, h) for b in which], 1).astype(jnp.bfloat16)

    def softmax(queries, keys, same):
        scores = jnp.where(same, dot(queries, keys, TN) * SCALE, -jnp.inf)
        weights = jnp.exp(scores - jnp.max(scores, 1, keepdims=True))
        return weights * (1.0 / jnp.sum(weights, 1, keepdims=True))

    for h in range(heads):
        held[rows.head(rows.values, h), : 3 * patches] = wide(2, (0, 1, 2), h)
        held[rows.head(rows.keys, h), : 3 * patches] = wide(1, (0, 1, 2), h)
    same_own = down[0] == jnp.concatenate(across, 1)
    same_side = [down[b] == jnp.concatenate([across[0], across[b]], 1) for b in (1, 2)]
    for h in range(heads):
        keys = held[rows.head(rows.keys, h), : 3 * patches]
        probs = softmax(kind(0, 0, h).astype(jnp.bfloat16), keys, same_own)
        held[rows.probs(h), : 3 * patches] = probs.astype(jnp.bfloat16)
        for i, b in enumerate((1, 2)):
            queries_at, attended_at = rows.side(i)
            queries = kind(b, 0, h).astype(jnp.bfloat16)
            probs = softmax(queries, near(rows.keys, i, h), same_side[i])
            seen = dot(probs.astype(jnp.bfloat16), near(rows.values, i, h), NT)
            side_ref[rows.head(queries_at, h)] = queries
            side_ref[rows.head(attended_at, h)] = seen.T.astype(jnp.bfloat16)
            side_ref[rows.side_probs(i, h)] = probs[:, :patches].T.astype(jnp.bfloat16)
    done_ref[...] = jnp.zeros(done_ref.shape, jnp.float32)


def softmax_parts(lengths, first, own, odd, even):
    columns, patches = own.shape[0] // 3, own.shape[1]
    rows = Rows(columns, patches)
    smem = pl.BlockSpec(memory_space=pltpu.MemorySpace.SMEM)
    work = (columns // HEAD_DIM) * patches * patches
    return pl.pallas_call(
        softmax_kernel,
        out_shape=(
            jax.ShapeDtypeStruct((rows.total, rows.lanes), jnp.bfloat16),
            jax.ShapeDtypeStruct((2 * rows.total, patches), jnp.bfloat16),
            jax.ShapeDtypeStruct((8, 128), jnp.float32),
        ),
        in_specs=[smem, smem] + in_vmem(3),
        out_specs=tuple(in_vmem(3)),
        compiler_params=params(32),
        cost_estimate=pl.CostEstimate(
            flops=100_000 * work, bytes_accessed=500 * work, transcendentals=9 * work
        ),
        name="softmax_parts",
    )(lengths.reshape(1, -1), first.reshape(1, 1), own, odd, even)


def packed_rows(columns, patches):
    heads = columns // HEAD_DIM
    return patches // 128 * columns + (heads + 1) // 2 * HEAD_DIM


def packed(x):
    columns, patches = x.shape
    whole = patches // 128 * 128
    parts = [x[:, at : at + 128] for at in range(0, whole, 128)]
    tails = [x[at : at + HEAD_DIM, whole:] for at in range(0, columns, HEAD_DIM)]
    tails += [jnp.zeros_like(tails[0])] * (len(tails) % 2)
    parts += [jnp.concatenate(tails[i : i + 2], 1) for i in range(0, len(tails), 2)]
    return jnp.concatenate(parts, 0)


def unpacked(ref, h, columns, patches):
    tiles = patches // 128
    starts = [t * columns + h * HEAD_DIM for t in range(tiles)]
    parts = [ref[at : at + HEAD_DIM].astype(jnp.float32) for at in starts]
    at = tiles * columns + h // 2 * HEAD_DIM
    tail = ref[at : at + HEAD_DIM].astype(jnp.float32)
    return jnp.concatenate(parts + [tail[:, h % 2 * 64 : h % 2 * 64 + 64]], 1)


def gather_kernel(count, *refs):
    _, row_count, width = refs[0].shape
    total = refs[0][0].astype(jnp.float32)
    for p in range(1, count):
        total = total + refs[p][0].astype(jnp.float32)
    out_ref, packed_ref = refs[-2:]
    total = total.astype(jnp.bfloat16)
    columns = width // 4
    patch = iota((row_count, 4 * row_count), 1)
    token = iota((row_count, 4 * row_count), 0)
    result = jnp.zeros((columns, 4 * row_count), jnp.float32)
    for j in range(4):
        put = jnp.where(patch == 4 * token + j, 1.0, 0.0).astype(jnp.bfloat16)
        result = result + dot(total[:, j * columns : (j + 1) * columns], put, TN)
    out_ref[...] = result.astype(jnp.bfloat16)
    packed_ref[...] = packed(result).astype(jnp.bfloat16)


def gathered(pieces, later):
    _, row_count, width = pieces[0].shape
    size = len(pieces) * row_count * width
    return pl.pallas_call(
        functools.partial(gather_kernel, len(pieces)),
        out_shape=(
            jax.ShapeDtypeStruct((width // 4, 4 * row_count), jnp.bfloat16),
            jax.ShapeDtypeStruct((packed_rows(width // 4, 4 * row_count), 128), jnp.bfloat16),
        ),
        in_specs=in_vmem(len(pieces) + 1),
        out_specs=tuple(in_vmem(2)),
        compiler_params=params(16),
        cost_estimate=pl.CostEstimate(
            flops=20_000 * size, bytes_accessed=400 * size, transcendentals=0
        ),
        name="gather_sum",
    )(*pieces, later)


def own_kernel(grad_ref, own_ref, held_ref, query_ref, key_ref, value_ref):
    columns, patches = grad_ref.shape
    rows = Rows(columns, patches)
    for h in range(columns // HEAD_DIM):
        cols = slice(h * HEAD_DIM, (h + 1) * HEAD_DIM)
        grad = grad_ref[cols]
        slope = dot(grad, held_ref[rows.head(rows.values, h), : 3 * patches], TN)
        probs = held_ref[rows.probs(h), : 3 * patches]
        wide = probs.astype(jnp.float32)
        delta = jnp.sum(wide * slope, 1, keepdims=True)
        scores = (wide * (slope - delta)).astype(jnp.bfloat16)
        query = dot(scores, held_ref[rows.head(rows.keys, h), : 3 * patches], NT) * SCALE
        query_ref[cols] = query.T.astype(jnp.bfloat16)
        key_ref[cols] = dot(own_ref[cols], scores[:, :patches], NN)
        value_ref[cols] = dot(grad, probs[:, :patches], NN)


def own_terms(grad, own, held):
    return pl.pallas_call(
        own_kernel,
        out_shape=(
            jax.ShapeDtypeStruct(grad.shape, jnp.bfloat16),
            jax.ShapeDtypeStruct(grad.shape, jnp.float32),
            jax.ShapeDtypeStruct(grad.shape, jnp.float32),
        ),
        in_specs=in_vmem(3),
        out_specs=tuple(in_vmem(3)),
        compiler_params=params(24),
        name="own_terms",
    )(grad, own, held)


def side_kernel(i, grad_ref, key_part_ref, value_part_ref, held_ref, side_ref, *refs):
    columns, patches = key_part_ref.shape
    rows = Rows(columns, patches)
    queries_at, attended_at = rows.side(i)
    key_ref, value_ref = refs[:2]
    outgoing = []
    if i == 1:
        key_hbm, value_hbm, key_ref, value_ref, sems = refs

    def send(ref, out, h):
        if i == 1:
            at = pl.ds(h * HEAD_DIM, HEAD_DIM)
            copy = pltpu.make_async_copy(ref.at[at], out.at[at], sems.at[len(outgoing)])
            copy.start()
            outgoing.append(copy)

    for h in range(columns // HEAD_DIM):
        cols = slice(h * HEAD_DIM, (h + 1) * HEAD_DIM)
        wide = unpacked(grad_ref, h, columns, patches)
        grad = wide.astype(jnp.bfloat16)
        probs = side_ref[rows.side_probs(i, h)]
        value = dot(probs, grad, NT)
        value_ref[cols] = (value_part_ref[cols] + value.T).astype(value_ref.dtype)
        send(value_ref, refs[1], h)
        slope = dot(held_ref[rows.head(rows.values, h), :patches], grad, TN)
        attended = side_ref[rows.head(attended_at, h)].astype(jnp.float32)
        delta = jnp.sum(wide * attended, 0, keepdims=True)
        scores = (probs.astype(jnp.float32) * (slope - delta)).astype(jnp.bfloat16)
        key = dot(scores, side_ref[rows.head(queries_at, h)], NT)
        key = key_part_ref[cols] + key.T
        key_ref[cols] = (key * SCALE if i == 1 else key).astype(key_ref.dtype)
        send(key_ref, refs[0], h)
    for copy in outgoing:
        copy.wait()


def side_terms(i, grad, key_part, value_part, held, side):
    kind = jnp.bfloat16 if i == 1 else jnp.float32
    shape = jax.ShapeDtypeStruct(key_part.shape, kind)
    count = 2 * (key_part.shape[0] // HEAD_DIM)
    scratch = [pltpu.VMEM(key_part.shape, kind)] * 2 + [pltpu.SemaphoreType.DMA((count,))]
    return pl.pallas_call(
        functools.partial(side_kernel, i),
        out_shape=(shape, shape),
        in_specs=in_vmem(5),
        out_specs=tuple(in_hbm(2) if i == 1 else in_vmem(2)),
        scratch_shapes=scratch if i == 1 else [],
        compiler_params=params(24),
        name="side_terms",
    )(grad, key_part, value_part, held, side)


def from_pairs(x):
    size = lax.axis_size("grp")

    def swapped(first):
        partner = {}
        for core in range(2):
            for i in range(size):
                j = i + 1 if (i - first) % 2 == 0 else i - 1
                pair = (core, j) if 0 <= j < size else (1 - core, i)
                partner[core * size + i] = pair[0] * size + pair[1]
        return lax.ppermute(x, ("core", "grp"), sorted(partner.items()))

    return swapped(0), swapped(1)


def exchanged(pieces, axes):
    count = len(pieces)
    return pieces[:1] + [
        lax.ppermute(pieces[d], axes, [(i, i ^ d) for i in range(count)]) for d in range(1, count)
    ]


def on_device(
    grad_out, destination, w_down, pre_act, w_up, queries, key_states, value_states, lengths
):
    groups = lax.axis_size("grp")
    spans = lax.axis_size("span")
    heads = lax.axis_size(("chip", "core", "span"))
    row_count = grad_out.shape[0]
    capacity, _ = padded_slots(row_count, groups)
    pieces = down_pieces(destination, grad_out, w_down, groups, spans)
    pieces, queries, key_states, value_states = lax.optimization_barrier(
        (pieces, queries, key_states, value_states)
    )
    arrived = lax.all_to_all(pieces, ("grp", "span"), split_axis=0, concat_axis=0, tiled=True)
    own = jnp.concatenate([queries.T, key_states.T, value_states.T], 0)
    even, odd = from_pairs(packed(own))
    first = lax.axis_index("grp") * row_count
    other, shares = up_pieces(arrived, pre_act, w_up, heads, capacity)
    other, odd, even = lax.optimization_barrier((other, odd, even))
    other = lax.ppermute(other, "core", [(0, 1), (1, 0)])
    shares = (other.astype(jnp.float32) + shares.astype(jnp.float32)).astype(jnp.bfloat16)
    shares, own = lax.optimization_barrier((shares, own))
    held, side, held_done = softmax_parts(lengths, first, own, odd, even)
    shares = [shares[d : d + 1] for d in range(shares.shape[0])]
    grad, grad_packed = gathered(exchanged(shares, ("chip", "span")), held_done)
    even, odd = from_pairs(grad_packed)
    grad_query, key_part, value_part = own_terms(grad, queries.T, held)
    parts = side_terms(0, odd, key_part, value_part, held, side)
    grad_key, grad_value = side_terms(1, even, *parts, held, side)
    return grad_query.T, grad_key.T, grad_value.T


def solution(mesh):
    sect, grp, span = (mesh.shape[name] for name in ("sect", "grp", "span"))
    finer = jax.sharding.Mesh(
        mesh.devices.reshape(sect // 2, 2, grp, span), ("chip", "core", "grp", "span")
    )
    split = P("grp", ("chip", "core", "span"))
    placed = (
        P("grp", "span"),
        P("grp"),
        P(("chip", "core"), "span"),
        split,
        P(None, ("chip", "core", "span")),
        split,
        split,
        split,
        P(),
    )
    return jax.shard_map(
        on_device,
        mesh=finer,
        in_specs=placed,
        out_specs=(split, split, split),
        check_vma=False,
    )
```

```python
import functools

import jax
import jax.numpy as jnp
from jax import lax
from jax.experimental import pallas as pl
from jax.experimental.pallas import tpu as pltpu
from jax.sharding import PartitionSpec as P

HEAD_DIM = 80
SCALE = HEAD_DIM**-0.5
MIB = 1024 * 1024
VMEM = pltpu.MemorySpace.VMEM
NT = (((1,), (1,)), ((), ()))
NN = (((1,), (0,)), ((), ()))
TN = (((0,), (0,)), ((), ()))


def dot(a, b, dims):
    return lax.dot_general(a, b, dims, preferred_element_type=jnp.float32)


def iota(shape, dim):
    return lax.broadcasted_iota(jnp.int32, shape, dim)


def params(mib):
    return pltpu.CompilerParams(vmem_limit_bytes=mib * MIB)


def in_vmem(count):
    return [pl.BlockSpec(memory_space=VMEM) for _ in range(count)]


def in_hbm(count):
    return [pl.BlockSpec(memory_space=pltpu.MemorySpace.HBM) for _ in range(count)]


def fetched(pairs, sems):
    copies = [pltpu.make_async_copy(a, b, sems.at[i]) for i, (a, b) in enumerate(pairs)]
    for copy in copies:
        copy.start()
    return copies


def padded_slots(row_count, groups):
    offsets = min(groups, row_count // 2)
    capacity = row_count // offsets
    return capacity, -(-(capacity + 1) // 8) * 8


def one_product(count, slots, hidden):
    return count * slots <= hidden


def down_kernel(groups, spans, capacity, slots, steps, dest_hbm, rows_hbm, weight_ref, out_hbm,
                dest_ref, rows_ref, held, total_ref, pieces_ref, sems, out_sems):
    row_count = rows_ref.shape[0]
    hidden = weight_ref.shape[0] // spans
    everything = pl.ds(0, weight_ref.shape[0])
    pairs = [(dest_hbm, dest_ref), (rows_hbm, rows_ref)]
    for at, step in steps:
        part = (everything, pl.ds(at, step))
        pairs.append((weight_ref.at[part], held.at[part]))
    copies = fetched(pairs, sems)
    copies[0].wait()
    across = jnp.broadcast_to(dest_ref[...].astype(jnp.float32), (row_count, row_count))
    down = across.T
    group_across = jnp.floor((across + 0.5) * (1.0 / row_count))
    group_down = jnp.floor((down + 0.5) * (1.0 / row_count))
    slot_down = down - group_down * row_count
    same = group_across == group_down
    earlier = iota((row_count, row_count), 0) < iota((row_count, row_count), 1)
    later = iota((row_count, row_count), 1) < iota((row_count, row_count), 0)
    rank_across = jnp.sum(jnp.where(same & earlier, 1.0, 0.0), 0, keepdims=True)
    rank_down = jnp.sum(jnp.where(same & later, 1.0, 0.0), 1, keepdims=True)
    row_of = group_across[:1] * slots + rank_across
    places = iota((groups * slots, row_count), 0).astype(jnp.float32)
    pick = jnp.where(places == row_of, 1.0, 0.0).astype(jnp.bfloat16)
    lane = iota((row_count, hidden), 1).astype(jnp.float32)
    shift = 0.0
    if one_product(groups * spans, slots, hidden):
        device = lax.axis_index("grp") * spans + lax.axis_index("span")
        shift = (device * slots).astype(jnp.float32)
    at_rank = lane == rank_down + shift
    label_row = iota((slots, hidden), 0) == capacity
    labels = []
    for g in range(groups):
        hit = at_rank & (group_down[:, :1] == g)
        labels.append(jnp.sum(jnp.where(hit, slot_down[:, :1] + 1.0, 0.0), 0, keepdims=True) - 1.0)
    copies[1].wait()
    for n, (at, step) in enumerate(steps):
        turned = rows_ref[:, at : at + step].astype(jnp.float32).T.astype(jnp.bfloat16)
        copies[2 + n].wait()
        product = dot(held[:, at : at + step], turned, NN)
        total_ref[...] = product if n == 0 else total_ref[...] + product
    outgoing = []
    for s in range(spans):
        part = total_ref[s * hidden : (s + 1) * hidden].astype(jnp.bfloat16)
        moved = dot(pick, part, NT)
        for g in range(groups):
            piece = jnp.where(label_row, labels[g], moved[g * slots : (g + 1) * slots])
            pieces_ref[s, g] = piece.astype(jnp.bfloat16)
        copy = pltpu.make_async_copy(pieces_ref.at[s], out_hbm.at[:, s], out_sems.at[s])
        copy.start()
        outgoing.append(copy)
    for copy in outgoing:
        copy.wait()


def down_pieces(dest, rows, weight, groups, spans):
    row_count = rows.shape[0]
    capacity, slots = padded_slots(row_count, groups)
    hidden = weight.shape[0] // spans
    depth = weight.shape[1]
    edges = [depth * i // 16 for i in (0, 2, 5, 10, 16)]
    steps = [(i, j - i) for i, j in zip(edges, edges[1:])]
    pieces = pl.pallas_call(
        functools.partial(down_kernel, groups, spans, capacity, slots, steps),
        out_shape=jax.ShapeDtypeStruct((groups, spans, slots, hidden), jnp.bfloat16),
        in_specs=in_hbm(3),
        out_specs=in_hbm(1)[0],
        scratch_shapes=[
            pltpu.VMEM((1, row_count), jnp.int32),
            pltpu.VMEM(rows.shape, jnp.bfloat16),
            pltpu.VMEM(weight.shape, jnp.bfloat16),
            pltpu.VMEM((weight.shape[0], row_count), jnp.float32),
            pltpu.VMEM((spans, groups, slots, hidden), jnp.bfloat16),
            pltpu.SemaphoreType.DMA((2 + len(steps),)),
            pltpu.SemaphoreType.DMA((spans,)),
        ],
        compiler_params=params(60),
        name="down_product",
    )(dest.reshape(1, row_count), rows, weight)
    return pieces.reshape(groups * spans, slots, hidden)


def up_kernel(heads, capacity, pieces_ref, pre_ref, weight_ref, send_hbm, keep_hbm, held, out_ref,
              sems, out_sems):
    row_count, hidden = pre_ref.shape
    count, slots, _ = pieces_ref.shape
    width = weight_ref.shape[2] // lax.axis_size("span")
    spans = lax.axis_size("span")
    core = lax.axis_index("core")
    chip = lax.axis_index("chip")
    chips = heads // (2 * spans)
    block = spans * width

    pairs = []
    for n in range(2 * chips):
        place = lax.bitwise_xor(chip, n % chips) * 2 + (1 - core if n < chips else core)
        pairs.append((weight_ref.at[:, place], held.at[n]))
    copies = fetched(pairs, sems)
    label_at = slice(capacity, capacity + 1)
    if one_product(count, slots, hidden):
        pieces = [pieces_ref[p].astype(jnp.float32) for p in range(count)]
        labels = functools.reduce(jnp.maximum, [x[label_at, : count * slots] for x in pieces])
        row = iota((row_count, count * slots), 0).astype(jnp.float32)
        put = jnp.where(row == labels, 1.0, 0.0).astype(jnp.bfloat16)
        total = dot(put, jnp.concatenate(pieces, 0).astype(jnp.bfloat16), NN)
    else:
        row = iota((row_count, slots), 0).astype(jnp.float32)

        def placed(p, total):
            piece = pieces_ref[p]
            labels = piece.astype(jnp.float32)[label_at, :slots]
            put = jnp.where(row == labels, 1.0, 0.0).astype(jnp.bfloat16)
            return total + dot(put, piece, NN)

        total = lax.fori_loop(0, count, placed, jnp.zeros((row_count, hidden), jnp.float32))
    pre = pre_ref[...].astype(jnp.float32)
    cdf = 0.5 * (1.0 + lax.erf(pre * 0.7071067811865476))
    slope = cdf + pre * jnp.exp(-0.5 * pre * pre) * 0.3989422804014327
    grad_pre = (total * slope).T.astype(jnp.bfloat16)
    outgoing = []
    span = lax.axis_index("span")

    def send(n, product):
        for i in range(spans):
            parts = [product[j * block + i * width : j * block + (i + 1) * width] for j in range(4)]
            part = jnp.concatenate(parts, 0).astype(jnp.bfloat16).T
            out_ref[n * spans + lax.bitwise_xor(span, i)] = part
        out_hbm = send_hbm if n < chips else keep_hbm
        source, target = pl.ds(n * spans, spans), pl.ds(n % chips * spans, spans)
        copy = pltpu.make_async_copy(out_ref.at[source], out_hbm.at[target], out_sems.at[n])
        outgoing.append(copy)
        copy.start()

    waiting = None
    for n in range(2 * chips):
        copies[n].wait()
        product = dot(held[n].reshape(4 * block, hidden), grad_pre, NN)
        if waiting is not None:
            send(n - 1, waiting)
        waiting = product
    send(2 * chips - 1, waiting)
    for copy in outgoing:
        copy.wait()


def up_pieces(pieces, pre, weight, heads, capacity):
    width = weight.shape[0] // heads
    spans = lax.axis_size("span")
    blocks = heads // spans
    return pl.pallas_call(
        functools.partial(up_kernel, heads, capacity),
        out_shape=[jax.ShapeDtypeStruct((heads // 2, pre.shape[0], width), jnp.bfloat16)] * 2,
        in_specs=in_vmem(2) + in_hbm(1),
        out_specs=in_hbm(2),
        scratch_shapes=[
            pltpu.VMEM((blocks, 4, spans * width // 4, weight.shape[1]), jnp.bfloat16),
            pltpu.VMEM((heads, pre.shape[0], width), jnp.bfloat16),
            pltpu.SemaphoreType.DMA((blocks,)),
            pltpu.SemaphoreType.DMA((blocks,)),
        ],
        compiler_params=params(52),
        cost_estimate=pl.CostEstimate(
            flops=8 * pre.shape[0] * weight.size, bytes_accessed=8 * weight.size, transcendentals=0
        ),
        name="up_product",
    )(pieces, pre, weight.reshape(4, blocks, -1, weight.shape[1]))


class Rows:
    def __init__(self, columns, patches):
        heads = columns // HEAD_DIM
        self.lanes = -(-3 * patches // 128) * 128
        self.columns, self.patches = columns, patches
        self.values, self.keys, self.probs_at = 0, columns, 2 * columns
        self.total = 2 * columns + heads * patches

    def head(self, start, h):
        return slice(start + h * HEAD_DIM, start + (h + 1) * HEAD_DIM)

    def kind(self, start):
        return slice(start, start + self.columns)

    def probs(self, h):
        return slice(self.probs_at + h * self.patches, self.probs_at + (h + 1) * self.patches)

    def side(self, i):
        start = i * self.total
        return start, start + self.columns

    def side_probs(self, i, h):
        start = i * self.total + self.probs_at + h * self.patches
        return slice(start, start + self.patches)


def softmax_kernel(lengths_ref, first_ref, own_ref, odd_ref, even_ref, held, side_ref, done_ref):
    columns, patches = own_ref.shape[0] // 3, own_ref.shape[1]
    rows = Rows(columns, patches)
    heads = columns // HEAD_DIM
    step_even = 1 - 2 * lax.rem(lax.axis_index("grp"), 2)
    offsets = (0, -step_even, step_even)
    first = first_ref[0, 0]

    def image_of(shape, dim, block):
        token = iota(shape, dim) // 4 + (first + block * (patches // 4))

        def step(i, state):
            image, bound = state
            bound = bound + lengths_ref[0, i]
            return image + jnp.where(token >= bound, 1, 0), bound

        start = (jnp.where(token < 0, -1, 0), jnp.int32(0))
        return lax.fori_loop(0, lengths_ref.shape[1], step, start)[0]

    def near(start, i, h):
        part = held[rows.head(start, h), :]
        if i == 0:
            return part[:, : 2 * patches]
        parts = [part[:, :patches], part[:, 2 * patches : 3 * patches]]
        return jnp.concatenate([x.astype(jnp.float32) for x in parts], 1).astype(jnp.bfloat16)

    across = [image_of((1, patches), 1, b).astype(jnp.float32) for b in offsets]
    down = [jnp.broadcast_to(x, (128, patches)).T[:, :1] for x in across]

    def kind(block, t, h):
        if block == 0:
            start = t * columns + h * HEAD_DIM
            return own_ref[start : start + HEAD_DIM].astype(jnp.float32)
        return unpacked((odd_ref, even_ref)[block - 1], t * heads + h, 3 * columns, patches)

    def wide(t, which, h):
        return jnp.concatenate([kind(b, t, h) for b in which], 1).astype(jnp.bfloat16)

    def softmax(queries, keys, same):
        scores = jnp.where(same, dot(queries, keys, TN) * SCALE, -jnp.inf)
        weights = jnp.exp(scores - jnp.max(scores, 1, keepdims=True))
        return weights * (1.0 / jnp.sum(weights, 1, keepdims=True))

    for h in range(heads):
        held[rows.head(rows.values, h), : 3 * patches] = wide(2, (0, 1, 2), h)
        held[rows.head(rows.keys, h), : 3 * patches] = wide(1, (0, 1, 2), h)
    same_own = down[0] == jnp.concatenate(across, 1)
    same_side = [down[b] == jnp.concatenate([across[0], across[b]], 1) for b in (1, 2)]
    for h in range(heads):
        keys = held[rows.head(rows.keys, h), : 3 * patches]
        probs = softmax(kind(0, 0, h).astype(jnp.bfloat16), keys, same_own)
        held[rows.probs(h), : 3 * patches] = probs.astype(jnp.bfloat16)
        for i, b in enumerate((1, 2)):
            queries_at, attended_at = rows.side(i)
            queries = kind(b, 0, h).astype(jnp.bfloat16)
            probs = softmax(queries, near(rows.keys, i, h), same_side[i])
            seen = dot(probs.astype(jnp.bfloat16), near(rows.values, i, h), NT)
            side_ref[rows.head(queries_at, h)] = queries
            side_ref[rows.head(attended_at, h)] = seen.T.astype(jnp.bfloat16)
            side_ref[rows.side_probs(i, h)] = probs[:, :patches].T.astype(jnp.bfloat16)
    done_ref[...] = jnp.zeros(done_ref.shape, jnp.float32)


def softmax_parts(lengths, first, own, odd, even):
    columns, patches = own.shape[0] // 3, own.shape[1]
    rows = Rows(columns, patches)
    smem = pl.BlockSpec(memory_space=pltpu.MemorySpace.SMEM)
    work = (columns // HEAD_DIM) * patches * patches
    return pl.pallas_call(
        softmax_kernel,
        out_shape=(
            jax.ShapeDtypeStruct((rows.total, rows.lanes), jnp.bfloat16),
            jax.ShapeDtypeStruct((2 * rows.total, patches), jnp.bfloat16),
            jax.ShapeDtypeStruct((8, 128), jnp.float32),
        ),
        in_specs=[smem, smem] + in_vmem(3),
        out_specs=tuple(in_vmem(3)),
        compiler_params=params(32),
        cost_estimate=pl.CostEstimate(
            flops=100_000 * work, bytes_accessed=500 * work, transcendentals=9 * work
        ),
        name="softmax_parts",
    )(lengths.reshape(1, -1), first.reshape(1, 1), own, odd, even)


def packed_rows(columns, patches):
    heads = columns // HEAD_DIM
    return patches // 128 * columns + (heads + 1) // 2 * HEAD_DIM


def packed(x):
    columns, patches = x.shape
    whole = patches // 128 * 128
    parts = [x[:, at : at + 128] for at in range(0, whole, 128)]
    tails = [x[at : at + HEAD_DIM, whole:] for at in range(0, columns, HEAD_DIM)]
    tails += [jnp.zeros_like(tails[0])] * (len(tails) % 2)
    parts += [jnp.concatenate(tails[i : i + 2], 1) for i in range(0, len(tails), 2)]
    return jnp.concatenate(parts, 0)


def unpacked(ref, h, columns, patches):
    tiles = patches // 128
    starts = [t * columns + h * HEAD_DIM for t in range(tiles)]
    parts = [ref[at : at + HEAD_DIM].astype(jnp.float32) for at in starts]
    at = tiles * columns + h // 2 * HEAD_DIM
    tail = ref[at : at + HEAD_DIM].astype(jnp.float32)
    return jnp.concatenate(parts + [tail[:, h % 2 * 64 : h % 2 * 64 + 64]], 1)


def gather_kernel(count, *refs):
    _, row_count, width = refs[0].shape
    total = refs[0][0].astype(jnp.float32)
    for p in range(1, count):
        total = total + refs[p][0].astype(jnp.float32)
    out_ref, packed_ref = refs[-2:]
    total = total.astype(jnp.bfloat16)
    columns = width // 4
    patch = iota((row_count, 4 * row_count), 1)
    token = iota((row_count, 4 * row_count), 0)
    result = jnp.zeros((columns, 4 * row_count), jnp.float32)
    for j in range(4):
        put = jnp.where(patch == 4 * token + j, 1.0, 0.0).astype(jnp.bfloat16)
        result = result + dot(total[:, j * columns : (j + 1) * columns], put, TN)
    out_ref[...] = result.astype(jnp.bfloat16)
    packed_ref[...] = packed(result).astype(jnp.bfloat16)


def gathered(pieces, later):
    _, row_count, width = pieces[0].shape
    size = len(pieces) * row_count * width
    return pl.pallas_call(
        functools.partial(gather_kernel, len(pieces)),
        out_shape=(
            jax.ShapeDtypeStruct((width // 4, 4 * row_count), jnp.bfloat16),
            jax.ShapeDtypeStruct((packed_rows(width // 4, 4 * row_count), 128), jnp.bfloat16),
        ),
        in_specs=in_vmem(len(pieces) + 1),
        out_specs=tuple(in_vmem(2)),
        compiler_params=params(16),
        cost_estimate=pl.CostEstimate(
            flops=20_000 * size, bytes_accessed=400 * size, transcendentals=0
        ),
        name="gather_sum",
    )(*pieces, later)


def own_kernel(grad_ref, own_ref, held_ref, query_ref, key_ref, value_ref):
    columns, patches = grad_ref.shape
    rows = Rows(columns, patches)
    for h in range(columns // HEAD_DIM):
        cols = slice(h * HEAD_DIM, (h + 1) * HEAD_DIM)
        grad = grad_ref[cols]
        slope = dot(grad, held_ref[rows.head(rows.values, h), : 3 * patches], TN)
        probs = held_ref[rows.probs(h), : 3 * patches]
        wide = probs.astype(jnp.float32)
        delta = jnp.sum(wide * slope, 1, keepdims=True)
        scores = (wide * (slope - delta)).astype(jnp.bfloat16)
        query = dot(scores, held_ref[rows.head(rows.keys, h), : 3 * patches], NT) * SCALE
        query_ref[cols] = query.T.astype(jnp.bfloat16)
        key_ref[cols] = dot(own_ref[cols], scores[:, :patches], NN)
        value_ref[cols] = dot(grad, probs[:, :patches], NN)


def own_terms(grad, own, held):
    return pl.pallas_call(
        own_kernel,
        out_shape=(
            jax.ShapeDtypeStruct(grad.shape, jnp.bfloat16),
            jax.ShapeDtypeStruct(grad.shape, jnp.float32),
            jax.ShapeDtypeStruct(grad.shape, jnp.float32),
        ),
        in_specs=in_vmem(3),
        out_specs=tuple(in_vmem(3)),
        compiler_params=params(24),
        name="own_terms",
    )(grad, own, held)


def side_kernel(i, grad_ref, key_part_ref, value_part_ref, held_ref, side_ref, key_ref, value_ref):
    columns, patches = key_part_ref.shape
    rows = Rows(columns, patches)
    queries_at, attended_at = rows.side(i)
    for h in range(columns // HEAD_DIM):
        cols = slice(h * HEAD_DIM, (h + 1) * HEAD_DIM)
        wide = unpacked(grad_ref, h, columns, patches)
        grad = wide.astype(jnp.bfloat16)
        slope = dot(held_ref[rows.head(rows.values, h), :patches], grad, TN)
        attended = side_ref[rows.head(attended_at, h)].astype(jnp.float32)
        delta = jnp.sum(wide * attended, 0, keepdims=True)
        probs = side_ref[rows.side_probs(i, h)]
        value = dot(probs, grad, NT)
        scores = (probs.astype(jnp.float32) * (slope - delta)).astype(jnp.bfloat16)
        key = dot(scores, side_ref[rows.head(queries_at, h)], NT)
        key = key_part_ref[cols] + key.T
        key_ref[cols] = (key * SCALE if i == 1 else key).astype(key_ref.dtype)
        value_ref[cols] = (value_part_ref[cols] + value.T).astype(value_ref.dtype)


def side_terms(i, grad, key_part, value_part, held, side):
    kind = jnp.bfloat16 if i == 1 else jnp.float32
    shape = jax.ShapeDtypeStruct(key_part.shape, kind)
    return pl.pallas_call(
        functools.partial(side_kernel, i),
        out_shape=(shape, shape),
        in_specs=in_vmem(5),
        out_specs=tuple(in_vmem(2)),
        compiler_params=params(24),
        name="side_terms",
    )(grad, key_part, value_part, held, side)


def from_pairs(x):
    size = lax.axis_size("grp")

    def swapped(first):
        partner = {}
        for core in range(2):
            for i in range(size):
                j = i + 1 if (i - first) % 2 == 0 else i - 1
                pair = (core, j) if 0 <= j < size else (1 - core, i)
                partner[core * size + i] = pair[0] * size + pair[1]
        return lax.ppermute(x, ("core", "grp"), sorted(partner.items()))

    return swapped(0), swapped(1)


def exchanged(pieces, axes):
    count = len(pieces)
    return pieces[:1] + [
        lax.ppermute(pieces[d], axes, [(i, i ^ d) for i in range(count)]) for d in range(1, count)
    ]


def on_device(
    grad_out, destination, w_down, pre_act, w_up, queries, key_states, value_states, lengths
):
    groups = lax.axis_size("grp")
    spans = lax.axis_size("span")
    heads = lax.axis_size(("chip", "core", "span"))
    row_count = grad_out.shape[0]
    capacity, _ = padded_slots(row_count, groups)
    pieces = down_pieces(destination, grad_out, w_down, groups, spans)
    pieces, queries, key_states, value_states = lax.optimization_barrier(
        (pieces, queries, key_states, value_states)
    )
    arrived = lax.all_to_all(pieces, ("grp", "span"), split_axis=0, concat_axis=0, tiled=True)
    own = jnp.concatenate([queries.T, key_states.T, value_states.T], 0)
    even, odd = from_pairs(packed(own))
    first = lax.axis_index("grp") * row_count
    other, shares = up_pieces(arrived, pre_act, w_up, heads, capacity)
    other, odd, even = lax.optimization_barrier((other, odd, even))
    other = lax.ppermute(other, "core", [(0, 1), (1, 0)])
    shares = (other.astype(jnp.float32) + shares.astype(jnp.float32)).astype(jnp.bfloat16)
    shares, own = lax.optimization_barrier((shares, own))
    held, side, held_done = softmax_parts(lengths, first, own, odd, even)
    shares = [shares[d : d + 1] for d in range(shares.shape[0])]
    grad, grad_packed = gathered(exchanged(shares, ("chip", "span")), held_done)
    even, odd = from_pairs(grad_packed)
    grad_query, key_part, value_part = own_terms(grad, queries.T, held)
    parts = side_terms(0, odd, key_part, value_part, held, side)
    grad_key, grad_value = side_terms(1, even, *parts, held, side)
    return grad_query.T, grad_key.T, grad_value.T


def solution(mesh):
    sect, grp, span = (mesh.shape[name] for name in ("sect", "grp", "span"))
    finer = jax.sharding.Mesh(
        mesh.devices.reshape(sect // 2, 2, grp, span), ("chip", "core", "grp", "span")
    )
    split = P("grp", ("chip", "core", "span"))
    placed = (
        P("grp", "span"),
        P("grp"),
        P(("chip", "core"), "span"),
        split,
        P(None, ("chip", "core", "span")),
        split,
        split,
        split,
        P(),
    )
    return jax.shard_map(
        on_device,
        mesh=finer,
        in_specs=placed,
        out_specs=(split, split, split),
        check_vma=False,
    )
```

```python
import functools

import jax
import jax.numpy as jnp
from jax import lax
from jax.experimental import pallas as pl
from jax.experimental.pallas import tpu as pltpu
from jax.sharding import PartitionSpec as P

HEAD_DIM = 80
SCALE = HEAD_DIM**-0.5
MIB = 1024 * 1024
VMEM = pltpu.MemorySpace.VMEM
NT = (((1,), (1,)), ((), ()))
NN = (((1,), (0,)), ((), ()))
TN = (((0,), (0,)), ((), ()))


def dot(a, b, dims):
    return lax.dot_general(a, b, dims, preferred_element_type=jnp.float32)


def iota(shape, dim):
    return lax.broadcasted_iota(jnp.int32, shape, dim)


def params(mib):
    return pltpu.CompilerParams(vmem_limit_bytes=mib * MIB)


def in_vmem(count):
    return [pl.BlockSpec(memory_space=VMEM) for _ in range(count)]


def in_hbm(count):
    return [pl.BlockSpec(memory_space=pltpu.MemorySpace.HBM) for _ in range(count)]


def fetched(pairs, sems):
    copies = [pltpu.make_async_copy(a, b, sems.at[i]) for i, (a, b) in enumerate(pairs)]
    for copy in copies:
        copy.start()
    return copies


def padded_slots(row_count, groups):
    offsets = min(groups, row_count // 2)
    capacity = row_count // offsets
    return capacity, -(-(capacity + 1) // 8) * 8


def one_product(count, slots, hidden):
    return count * slots <= hidden


def down_kernel(groups, spans, capacity, slots, steps, dest_hbm, rows_hbm, weight_ref, out_hbm,
                dest_ref, rows_ref, held, total_ref, pieces_ref, sems, out_sems):
    row_count = rows_ref.shape[0]
    hidden = weight_ref.shape[0] // spans
    everything = pl.ds(0, weight_ref.shape[0])
    pairs = [(dest_hbm, dest_ref), (rows_hbm, rows_ref)]
    for at, step in steps:
        part = (everything, pl.ds(at, step))
        pairs.append((weight_ref.at[part], held.at[part]))
    copies = fetched(pairs, sems)
    copies[0].wait()
    across = jnp.broadcast_to(dest_ref[...].astype(jnp.float32), (row_count, row_count))
    down = across.T
    group_across = jnp.floor((across + 0.5) * (1.0 / row_count))
    group_down = jnp.floor((down + 0.5) * (1.0 / row_count))
    slot_down = down - group_down * row_count
    same = group_across == group_down
    earlier = iota((row_count, row_count), 0) < iota((row_count, row_count), 1)
    later = iota((row_count, row_count), 1) < iota((row_count, row_count), 0)
    rank_across = jnp.sum(jnp.where(same & earlier, 1.0, 0.0), 0, keepdims=True)
    rank_down = jnp.sum(jnp.where(same & later, 1.0, 0.0), 1, keepdims=True)
    row_of = group_across[:1] * slots + rank_across
    places = iota((groups * slots, row_count), 0).astype(jnp.float32)
    pick = jnp.where(places == row_of, 1.0, 0.0).astype(jnp.bfloat16)
    lane = iota((row_count, hidden), 1).astype(jnp.float32)
    shift = 0.0
    if one_product(groups * spans, slots, hidden):
        device = lax.axis_index("grp") * spans + lax.axis_index("span")
        shift = (device * slots).astype(jnp.float32)
    at_rank = lane == rank_down + shift
    label_row = iota((slots, hidden), 0) == capacity
    labels = []
    for g in range(groups):
        hit = at_rank & (group_down[:, :1] == g)
        labels.append(jnp.sum(jnp.where(hit, slot_down[:, :1] + 1.0, 0.0), 0, keepdims=True) - 1.0)
    copies[1].wait()
    for n, (at, step) in enumerate(steps):
        turned = rows_ref[:, at : at + step].astype(jnp.float32).T.astype(jnp.bfloat16)
        copies[2 + n].wait()
        product = dot(held[:, at : at + step], turned, NN)
        total_ref[...] = product if n == 0 else total_ref[...] + product
    outgoing = []
    for s in range(spans):
        part = total_ref[s * hidden : (s + 1) * hidden].astype(jnp.bfloat16)
        moved = dot(pick, part, NT)
        for g in range(groups):
            piece = jnp.where(label_row, labels[g], moved[g * slots : (g + 1) * slots])
            pieces_ref[s, g] = piece.astype(jnp.bfloat16)
        copy = pltpu.make_async_copy(pieces_ref.at[s], out_hbm.at[:, s], out_sems.at[s])
        copy.start()
        outgoing.append(copy)
    for copy in outgoing:
        copy.wait()


def down_pieces(dest, rows, weight, groups, spans):
    row_count = rows.shape[0]
    capacity, slots = padded_slots(row_count, groups)
    hidden = weight.shape[0] // spans
    depth = weight.shape[1]
    edges = [depth * i // 16 for i in (0, 1, 4, 9, 16)]
    steps = [(i, j - i) for i, j in zip(edges, edges[1:])]
    pieces = pl.pallas_call(
        functools.partial(down_kernel, groups, spans, capacity, slots, steps),
        out_shape=jax.ShapeDtypeStruct((groups, spans, slots, hidden), jnp.bfloat16),
        in_specs=in_hbm(3),
        out_specs=in_hbm(1)[0],
        scratch_shapes=[
            pltpu.VMEM((1, row_count), jnp.int32),
            pltpu.VMEM(rows.shape, jnp.bfloat16),
            pltpu.VMEM(weight.shape, jnp.bfloat16),
            pltpu.VMEM((weight.shape[0], row_count), jnp.float32),
            pltpu.VMEM((spans, groups, slots, hidden), jnp.bfloat16),
            pltpu.SemaphoreType.DMA((2 + len(steps),)),
            pltpu.SemaphoreType.DMA((spans,)),
        ],
        compiler_params=params(60),
        name="down_product",
    )(dest.reshape(1, row_count), rows, weight)
    return pieces.reshape(groups * spans, slots, hidden)


def up_kernel(heads, capacity, pieces_ref, pre_ref, weight_ref, send_hbm, keep_hbm, held, out_ref,
              sems, out_sems):
    row_count, hidden = pre_ref.shape
    count, slots, _ = pieces_ref.shape
    width = weight_ref.shape[2] // lax.axis_size("span")
    spans = lax.axis_size("span")
    core = lax.axis_index("core")
    chip = lax.axis_index("chip")
    chips = heads // (2 * spans)
    block = spans * width

    pairs = []
    for n in range(2 * chips):
        place = lax.bitwise_xor(chip, n % chips) * 2 + (1 - core if n < chips else core)
        pairs.append((weight_ref.at[:, place], held.at[n]))
    copies = fetched(pairs, sems)
    label_at = slice(capacity, capacity + 1)
    if one_product(count, slots, hidden):
        pieces = [pieces_ref[p].astype(jnp.float32) for p in range(count)]
        labels = functools.reduce(jnp.maximum, [x[label_at, : count * slots] for x in pieces])
        row = iota((row_count, count * slots), 0).astype(jnp.float32)
        put = jnp.where(row == labels, 1.0, 0.0).astype(jnp.bfloat16)
        total = dot(put, jnp.concatenate(pieces, 0).astype(jnp.bfloat16), NN)
    else:
        row = iota((row_count, slots), 0).astype(jnp.float32)

        def placed(p, total):
            piece = pieces_ref[p]
            labels = piece.astype(jnp.float32)[label_at, :slots]
            put = jnp.where(row == labels, 1.0, 0.0).astype(jnp.bfloat16)
            return total + dot(put, piece, NN)

        total = lax.fori_loop(0, count, placed, jnp.zeros((row_count, hidden), jnp.float32))
    pre = pre_ref[...].astype(jnp.float32)
    cdf = 0.5 * (1.0 + lax.erf(pre * 0.7071067811865476))
    slope = cdf + pre * jnp.exp(-0.5 * pre * pre) * 0.3989422804014327
    grad_pre = (total * slope).T.astype(jnp.bfloat16)
    outgoing = []
    span = lax.axis_index("span")

    def send(n, product):
        for i in range(spans):
            parts = [product[j * block + i * width : j * block + (i + 1) * width] for j in range(4)]
            part = jnp.concatenate(parts, 0).astype(jnp.bfloat16).T
            out_ref[n * spans + lax.bitwise_xor(span, i)] = part
        out_hbm = send_hbm if n < chips else keep_hbm
        source, target = pl.ds(n * spans, spans), pl.ds(n % chips * spans, spans)
        copy = pltpu.make_async_copy(out_ref.at[source], out_hbm.at[target], out_sems.at[n])
        outgoing.append(copy)
        copy.start()

    waiting = None
    for n in range(2 * chips):
        copies[n].wait()
        product = dot(held[n].reshape(4 * block, hidden), grad_pre, NN)
        if waiting is not None:
            send(n - 1, waiting)
        waiting = product
    send(2 * chips - 1, waiting)
    for copy in outgoing:
        copy.wait()


def up_pieces(pieces, pre, weight, heads, capacity):
    width = weight.shape[0] // heads
    spans = lax.axis_size("span")
    blocks = heads // spans
    return pl.pallas_call(
        functools.partial(up_kernel, heads, capacity),
        out_shape=[jax.ShapeDtypeStruct((heads // 2, pre.shape[0], width), jnp.bfloat16)] * 2,
        in_specs=in_vmem(2) + in_hbm(1),
        out_specs=in_hbm(2),
        scratch_shapes=[
            pltpu.VMEM((blocks, 4, spans * width // 4, weight.shape[1]), jnp.bfloat16),
            pltpu.VMEM((heads, pre.shape[0], width), jnp.bfloat16),
            pltpu.SemaphoreType.DMA((blocks,)),
            pltpu.SemaphoreType.DMA((blocks,)),
        ],
        compiler_params=params(52),
        cost_estimate=pl.CostEstimate(
            flops=8 * pre.shape[0] * weight.size, bytes_accessed=8 * weight.size, transcendentals=0
        ),
        name="up_product",
    )(pieces, pre, weight.reshape(4, blocks, -1, weight.shape[1]))


class Rows:
    def __init__(self, columns, patches):
        heads = columns // HEAD_DIM
        self.lanes = -(-3 * patches // 128) * 128
        self.columns, self.patches = columns, patches
        self.values, self.keys, self.probs_at = 0, columns, 2 * columns
        self.total = 2 * columns + heads * patches

    def head(self, start, h):
        return slice(start + h * HEAD_DIM, start + (h + 1) * HEAD_DIM)

    def kind(self, start):
        return slice(start, start + self.columns)

    def probs(self, h):
        return slice(self.probs_at + h * self.patches, self.probs_at + (h + 1) * self.patches)

    def side(self, i):
        start = i * self.total
        return start, start + self.columns

    def side_probs(self, i, h):
        start = i * self.total + self.probs_at + h * self.patches
        return slice(start, start + self.patches)


def softmax_kernel(lengths_ref, first_ref, own_ref, odd_ref, even_ref, held, side_ref, done_ref):
    columns, patches = own_ref.shape[0] // 3, own_ref.shape[1]
    rows = Rows(columns, patches)
    heads = columns // HEAD_DIM
    step_even = 1 - 2 * lax.rem(lax.axis_index("grp"), 2)
    offsets = (0, -step_even, step_even)
    first = first_ref[0, 0]

    def image_of(shape, dim, block):
        token = iota(shape, dim) // 4 + (first + block * (patches // 4))

        def step(i, state):
            image, bound = state
            bound = bound + lengths_ref[0, i]
            return image + jnp.where(token >= bound, 1, 0), bound

        start = (jnp.where(token < 0, -1, 0), jnp.int32(0))
        return lax.fori_loop(0, lengths_ref.shape[1], step, start)[0]

    def near(start, i, h):
        part = held[rows.head(start, h), :]
        if i == 0:
            return part[:, : 2 * patches]
        parts = [part[:, :patches], part[:, 2 * patches : 3 * patches]]
        return jnp.concatenate([x.astype(jnp.float32) for x in parts], 1).astype(jnp.bfloat16)

    across = [image_of((1, patches), 1, b).astype(jnp.float32) for b in offsets]
    down = [jnp.broadcast_to(x, (128, patches)).T[:, :1] for x in across]

    def kind(block, t, h):
        if block == 0:
            start = t * columns + h * HEAD_DIM
            return own_ref[start : start + HEAD_DIM].astype(jnp.float32)
        return unpacked((odd_ref, even_ref)[block - 1], t * heads + h, 3 * columns, patches)

    def wide(t, which, h):
        return jnp.concatenate([kind(b, t, h) for b in which], 1).astype(jnp.bfloat16)

    def softmax(queries, keys, same):
        scores = jnp.where(same, dot(queries, keys, TN) * SCALE, -jnp.inf)
        weights = jnp.exp(scores - jnp.max(scores, 1, keepdims=True))
        return weights * (1.0 / jnp.sum(weights, 1, keepdims=True))

    for h in range(heads):
        held[rows.head(rows.values, h), : 3 * patches] = wide(2, (0, 1, 2), h)
        held[rows.head(rows.keys, h), : 3 * patches] = wide(1, (0, 1, 2), h)
    same_own = down[0] == jnp.concatenate(across, 1)
    same_side = [down[b] == jnp.concatenate([across[0], across[b]], 1) for b in (1, 2)]
    for h in range(heads):
        keys = held[rows.head(rows.keys, h), : 3 * patches]
        probs = softmax(kind(0, 0, h).astype(jnp.bfloat16), keys, same_own)
        held[rows.probs(h), : 3 * patches] = probs.astype(jnp.bfloat16)
        for i, b in enumerate((1, 2)):
            queries_at, attended_at = rows.side(i)
            queries = kind(b, 0, h).astype(jnp.bfloat16)
            probs = softmax(queries, near(rows.keys, i, h), same_side[i])
            seen = dot(probs.astype(jnp.bfloat16), near(rows.values, i, h), NT)
            side_ref[rows.head(queries_at, h)] = queries
            side_ref[rows.head(attended_at, h)] = seen.T.astype(jnp.bfloat16)
            side_ref[rows.side_probs(i, h)] = probs[:, :patches].T.astype(jnp.bfloat16)
    done_ref[...] = jnp.zeros(done_ref.shape, jnp.float32)


def softmax_parts(lengths, first, own, odd, even):
    columns, patches = own.shape[0] // 3, own.shape[1]
    rows = Rows(columns, patches)
    smem = pl.BlockSpec(memory_space=pltpu.MemorySpace.SMEM)
    work = (columns // HEAD_DIM) * patches * patches
    return pl.pallas_call(
        softmax_kernel,
        out_shape=(
            jax.ShapeDtypeStruct((rows.total, rows.lanes), jnp.bfloat16),
            jax.ShapeDtypeStruct((2 * rows.total, patches), jnp.bfloat16),
            jax.ShapeDtypeStruct((8, 128), jnp.float32),
        ),
        in_specs=[smem, smem] + in_vmem(3),
        out_specs=tuple(in_vmem(3)),
        compiler_params=params(32),
        cost_estimate=pl.CostEstimate(
            flops=100_000 * work, bytes_accessed=500 * work, transcendentals=9 * work
        ),
        name="softmax_parts",
    )(lengths.reshape(1, -1), first.reshape(1, 1), own, odd, even)


def packed_rows(columns, patches):
    heads = columns // HEAD_DIM
    return patches // 128 * columns + (heads + 1) // 2 * HEAD_DIM


def packed(x):
    columns, patches = x.shape
    whole = patches // 128 * 128
    parts = [x[:, at : at + 128] for at in range(0, whole, 128)]
    tails = [x[at : at + HEAD_DIM, whole:] for at in range(0, columns, HEAD_DIM)]
    tails += [jnp.zeros_like(tails[0])] * (len(tails) % 2)
    parts += [jnp.concatenate(tails[i : i + 2], 1) for i in range(0, len(tails), 2)]
    return jnp.concatenate(parts, 0)


def unpacked(ref, h, columns, patches):
    tiles = patches // 128
    starts = [t * columns + h * HEAD_DIM for t in range(tiles)]
    parts = [ref[at : at + HEAD_DIM].astype(jnp.float32) for at in starts]
    at = tiles * columns + h // 2 * HEAD_DIM
    tail = ref[at : at + HEAD_DIM].astype(jnp.float32)
    return jnp.concatenate(parts + [tail[:, h % 2 * 64 : h % 2 * 64 + 64]], 1)


def gather_kernel(count, *refs):
    _, row_count, width = refs[0].shape
    total = refs[0][0].astype(jnp.float32)
    for p in range(1, count):
        total = total + refs[p][0].astype(jnp.float32)
    out_ref, packed_ref = refs[-2:]
    total = total.astype(jnp.bfloat16)
    columns = width // 4
    patch = iota((row_count, 4 * row_count), 1)
    token = iota((row_count, 4 * row_count), 0)
    result = jnp.zeros((columns, 4 * row_count), jnp.float32)
    for j in range(4):
        put = jnp.where(patch == 4 * token + j, 1.0, 0.0).astype(jnp.bfloat16)
        result = result + dot(total[:, j * columns : (j + 1) * columns], put, TN)
    out_ref[...] = result.astype(jnp.bfloat16)
    packed_ref[...] = packed(result).astype(jnp.bfloat16)


def gathered(pieces, later):
    _, row_count, width = pieces[0].shape
    size = len(pieces) * row_count * width
    return pl.pallas_call(
        functools.partial(gather_kernel, len(pieces)),
        out_shape=(
            jax.ShapeDtypeStruct((width // 4, 4 * row_count), jnp.bfloat16),
            jax.ShapeDtypeStruct((packed_rows(width // 4, 4 * row_count), 128), jnp.bfloat16),
        ),
        in_specs=in_vmem(len(pieces) + 1),
        out_specs=tuple(in_vmem(2)),
        compiler_params=params(16),
        cost_estimate=pl.CostEstimate(
            flops=20_000 * size, bytes_accessed=400 * size, transcendentals=0
        ),
        name="gather_sum",
    )(*pieces, later)


def own_kernel(grad_ref, own_ref, held_ref, query_ref, key_ref, value_ref):
    columns, patches = grad_ref.shape
    rows = Rows(columns, patches)
    for h in range(columns // HEAD_DIM):
        cols = slice(h * HEAD_DIM, (h + 1) * HEAD_DIM)
        grad = grad_ref[cols]
        slope = dot(grad, held_ref[rows.head(rows.values, h), : 3 * patches], TN)
        probs = held_ref[rows.probs(h), : 3 * patches]
        wide = probs.astype(jnp.float32)
        delta = jnp.sum(wide * slope, 1, keepdims=True)
        scores = (wide * (slope - delta)).astype(jnp.bfloat16)
        query = dot(scores, held_ref[rows.head(rows.keys, h), : 3 * patches], NT) * SCALE
        query_ref[cols] = query.T.astype(jnp.bfloat16)
        key_ref[cols] = dot(own_ref[cols], scores[:, :patches], NN)
        value_ref[cols] = dot(grad, probs[:, :patches], NN)


def own_terms(grad, own, held):
    return pl.pallas_call(
        own_kernel,
        out_shape=(
            jax.ShapeDtypeStruct(grad.shape, jnp.bfloat16),
            jax.ShapeDtypeStruct(grad.shape, jnp.float32),
            jax.ShapeDtypeStruct(grad.shape, jnp.float32),
        ),
        in_specs=in_vmem(3),
        out_specs=tuple(in_vmem(3)),
        compiler_params=params(24),
        name="own_terms",
    )(grad, own, held)


def side_kernel(i, grad_ref, key_part_ref, value_part_ref, held_ref, side_ref, key_ref, value_ref):
    columns, patches = key_part_ref.shape
    rows = Rows(columns, patches)
    queries_at, attended_at = rows.side(i)
    for h in range(columns // HEAD_DIM):
        cols = slice(h * HEAD_DIM, (h + 1) * HEAD_DIM)
        wide = unpacked(grad_ref, h, columns, patches)
        grad = wide.astype(jnp.bfloat16)
        slope = dot(held_ref[rows.head(rows.values, h), :patches], grad, TN)
        attended = side_ref[rows.head(attended_at, h)].astype(jnp.float32)
        delta = jnp.sum(wide * attended, 0, keepdims=True)
        probs = side_ref[rows.side_probs(i, h)]
        value = dot(probs, grad, NT)
        scores = (probs.astype(jnp.float32) * (slope - delta)).astype(jnp.bfloat16)
        key = dot(scores, side_ref[rows.head(queries_at, h)], NT)
        key = key_part_ref[cols] + key.T
        key_ref[cols] = (key * SCALE if i == 1 else key).astype(key_ref.dtype)
        value_ref[cols] = (value_part_ref[cols] + value.T).astype(value_ref.dtype)


def side_terms(i, grad, key_part, value_part, held, side):
    kind = jnp.bfloat16 if i == 1 else jnp.float32
    shape = jax.ShapeDtypeStruct(key_part.shape, kind)
    return pl.pallas_call(
        functools.partial(side_kernel, i),
        out_shape=(shape, shape),
        in_specs=in_vmem(5),
        out_specs=tuple(in_vmem(2)),
        compiler_params=params(24),
        name="side_terms",
    )(grad, key_part, value_part, held, side)


def from_pairs(x):
    size = lax.axis_size("grp")

    def swapped(first):
        partner = {}
        for core in range(2):
            for i in range(size):
                j = i + 1 if (i - first) % 2 == 0 else i - 1
                pair = (core, j) if 0 <= j < size else (1 - core, i)
                partner[core * size + i] = pair[0] * size + pair[1]
        return lax.ppermute(x, ("core", "grp"), sorted(partner.items()))

    return swapped(0), swapped(1)


def exchanged(pieces, axes):
    count = len(pieces)
    return pieces[:1] + [
        lax.ppermute(pieces[d], axes, [(i, i ^ d) for i in range(count)]) for d in range(1, count)
    ]


def on_device(
    grad_out, destination, w_down, pre_act, w_up, queries, key_states, value_states, lengths
):
    groups = lax.axis_size("grp")
    spans = lax.axis_size("span")
    heads = lax.axis_size(("chip", "core", "span"))
    row_count = grad_out.shape[0]
    capacity, _ = padded_slots(row_count, groups)
    pieces = down_pieces(destination, grad_out, w_down, groups, spans)
    pieces, queries, key_states, value_states = lax.optimization_barrier(
        (pieces, queries, key_states, value_states)
    )
    arrived = lax.all_to_all(pieces, ("grp", "span"), split_axis=0, concat_axis=0, tiled=True)
    own = jnp.concatenate([queries.T, key_states.T, value_states.T], 0)
    even, odd = from_pairs(packed(own))
    first = lax.axis_index("grp") * row_count
    other, shares = up_pieces(arrived, pre_act, w_up, heads, capacity)
    other, odd, even = lax.optimization_barrier((other, odd, even))
    other = lax.ppermute(other, "core", [(0, 1), (1, 0)])
    shares = (other.astype(jnp.float32) + shares.astype(jnp.float32)).astype(jnp.bfloat16)
    shares, own = lax.optimization_barrier((shares, own))
    held, side, held_done = softmax_parts(lengths, first, own, odd, even)
    shares = [shares[d : d + 1] for d in range(shares.shape[0])]
    grad, grad_packed = gathered(exchanged(shares, ("chip", "span")), held_done)
    even, odd = from_pairs(grad_packed)
    grad_query, key_part, value_part = own_terms(grad, queries.T, held)
    parts = side_terms(0, odd, key_part, value_part, held, side)
    grad_key, grad_value = side_terms(1, even, *parts, held, side)
    return grad_query.T, grad_key.T, grad_value.T


def solution(mesh):
    sect, grp, span = (mesh.shape[name] for name in ("sect", "grp", "span"))
    finer = jax.sharding.Mesh(
        mesh.devices.reshape(sect // 2, 2, grp, span), ("chip", "core", "grp", "span")
    )
    split = P("grp", ("chip", "core", "span"))
    placed = (
        P("grp", "span"),
        P("grp"),
        P(("chip", "core"), "span"),
        split,
        P(None, ("chip", "core", "span")),
        split,
        split,
        split,
        P(),
    )
    return jax.shard_map(
        on_device,
        mesh=finer,
        in_specs=placed,
        out_specs=(split, split, split),
        check_vma=False,
    )
```
